32 devices in a mesh: dp: 8 (over z, y), tensor: 4 (over x, core).
Axes of the slice: x: 2, y: 2, z: 4, core: 2. Of those that a mesh axis runs over, the one named last changes fastest.
Arguments:
- tokens: bfloat16 [8192, 768], P('dp'), may hold values from -6 to 6
- text_states: bfloat16 [32, 77, 768], P('dp'), may hold values from -6 to 6
- clip_len: int32 [32], P('dp'), may hold values from 0 to 1024, as said below
- text_len: int32 [32], P('dp'), may hold values from 1 to 77
- timesteps: int32 [32], P('dp'), may hold values from 0 to 999
- q_weight: bfloat16 [768, 768], P(None, 'tensor'), may hold values from -0.21875 to 0.21875
- k_weight: bfloat16 [768, 768], P(None, 'tensor'), may hold values from -0.21875 to 0.21875
- v_weight: bfloat16 [768, 768], P(None, 'tensor'), may hold values from -0.21875 to 0.21875
- o_weight: bfloat16 [768, 768], P('tensor'), may hold values from -3 to 3
- cross_q: bfloat16 [768, 768], P(None, 'tensor'), may hold values from -0.21875 to 0.21875
- cross_k: bfloat16 [768, 768], P(None, 'tensor'), may hold values from -0.21875 to 0.21875
- cross_v: bfloat16 [768, 768], P(None, 'tensor'), may hold values from -0.21875 to 0.21875
- cross_o: bfloat16 [768, 768], P('tensor'), may hold values from -1.25 to 1.25
- mlp_in: bfloat16 [768, 3072], P(None, 'tensor'), may hold values from -0.3125 to 0.3125
- mlp_out: bfloat16 [3072, 768], P('tensor'), may hold values from -0.21875 to 0.21875
- mod_weight: bfloat16 [768, 6912], P(None, 'tensor'), may hold values from -0.21875 to 0.21875
- mod_bias: bfloat16 [6912], P('tensor'), may hold values from -3 to 3
- cotangent: bfloat16 [8192, 768], P('dp'), may hold values from -6 to 6
Outputs:
- mixed: bfloat16 [8192, 768], P('dp')
- token_grad: bfloat16 [8192, 768], P('dp')
- q_weight_grad: float32 [768, 768], P(None, 'tensor')
- k_weight_grad: float32 [768, 768], P(None, 'tensor')
- v_weight_grad: float32 [768, 768], P(None, 'tensor')
- o_weight_grad: float32 [768, 768], P('tensor')
- cross_q_grad: float32 [768, 768], P(None, 'tensor')
- cross_k_grad: float32 [768, 768], P(None, 'tensor')
- cross_v_grad: float32 [768, 768], P(None, 'tensor')
- cross_o_grad: float32 [768, 768], P('tensor')
- mlp_in_grad: float32 [768, 3072], P(None, 'tensor')
- mlp_out_grad: float32 [3072, 768], P('tensor')
- mod_weight_grad: float32 [768, 6912], P(None, 'tensor')
- mod_bias_grad: float32 [6912], P('tensor')
The draws below stay inside these ranges and needn't reach their ends.
Inputs may be any that keep to these rules, and one draw needn't show every extreme that they name: `clip_len`: each aligned run of 4 entries lists, in order, clip lengths of 256, 512 or 1024 frames that sum to 1024, followed by zeros for unused slots.
All inputs are finite; a program needn't handle non-finite values.
Results may differ from the reference program's by a relative error of at most 0.028.
Values may be sent and summed in bfloat16 or wider, within the bound.
No kernel may reach another device: no remote copies, remote signals or barrier semaphores. Data moves between devices by JAX's collectives and lax.ppermute only.
A program may use at most 192 MiB of HBM per device.

```python
import math
import jax
import jax.numpy as jnp
from jax import lax

D = 768
HEADS = 12
FF = 3072
TEXT_D = 768
TEXT_LEN = 77
UNIT = 256
TOK_DEV = 1024
SLOTS = 4
TOKENS = 8192
CLIPS = 32
N_DP = 8
N_TENSOR = 4


def draw_clip_len(key, part):
    key = jax.random.fold_in(key, 11)
    device_count = CLIPS // SLOTS
    remaining = jnp.full((device_count,), TOK_DEV, jnp.int32)
    columns = []
    for slot_number in range(SLOTS):
        picks = jax.random.randint(jax.random.fold_in(key, slot_number), (device_count,), 0, 3)
        allowed_count = (remaining >= UNIT).astype(jnp.int32) + (remaining >= 2 * UNIT).astype(jnp.int32) + (remaining >= 4 * UNIT).astype(jnp.int32)
        option = picks % jnp.maximum(allowed_count, 1)
        length = jnp.where(option == 0, UNIT, jnp.where(option == 1, 2 * UNIT, 4 * UNIT))
        length = jnp.where(allowed_count > 0, length, 0).astype(jnp.int32)
        if slot_number == 0:
            length = length.at[0].set(4 * UNIT)
        remaining = remaining - length
        columns.append(length)
    return jnp.stack(columns, axis=1).reshape(-1)


def draw_text_len(key, part):
    key = jax.random.fold_in(key, 23)
    lengths = jax.random.randint(key, (CLIPS,), 1, TEXT_LEN + 1)
    return lengths.at[0].set(TEXT_LEN).at[1].set(1)


def set_ends(values, rng, low, largest):
    longest = values.shape.index(max(values.shape))
    spots = []
    for shift in (0, 1):
        where = [jax.random.randint(jax.random.fold_in(rng, axis), (), 0, length) for axis, length in enumerate(values.shape)]
        where[longest] = (where[longest] + shift) % values.shape[longest]
        spots.append(tuple(where))
    return values.at[spots[0]].set(low).at[spots[1]].set(largest)


def steps_of(rng, dims, split, low, top_value):
    factor_of = 1.0
    for dim, parts in split:
        heights = jax.random.uniform(jax.random.fold_in(jax.random.fold_in(rng, 6), dim), (parts,), jnp.float32, low / len(split), top_value / len(split))
        factor_of = factor_of * jnp.repeat(jnp.exp(heights), dims[dim] // parts).reshape((-1,) + (1,) * (len(dims) - 1 - dim))
    return factor_of


def gaussian(key, dims, deviation, bound, cuts=(), kind=jnp.bfloat16):
    result = deviation * jax.random.normal(key, dims, jnp.float32)
    if cuts:
        result = result * steps_of(key, dims, cuts, -0.22, 0.18)
    return jnp.clip(result, -bound, bound).astype(kind)


def setup_inputs(seed: int = 0) -> dict:
    splits = jax.random.split(jax.random.key(seed), 19)
    return {
        "tokens": gaussian(splits[0], (TOKENS, D), 1.0, 6.0, ((0, 8),)),
        "text_states": gaussian(splits[1], (CLIPS, TEXT_LEN, TEXT_D), 1.0, 6.0, ((0, 8),)),
        "clip_len": draw_clip_len(jax.random.fold_in(splits[18], 71), 0),
        "text_len": draw_text_len(jax.random.fold_in(splits[18], 71), 0),
        "timesteps": set_ends(jax.random.randint(splits[4], (CLIPS,), 0, 1000), jax.random.fold_in(splits[4], 1), 0, 999).astype(jnp.int32),
        "q_weight": gaussian(splits[5], (D, D), D ** -0.5, 0.21875, ((1, 4),)),
        "k_weight": gaussian(splits[6], (D, D), D ** -0.5, 0.21875, ((1, 4),)),
        "v_weight": gaussian(splits[7], (D, D), D ** -0.5, 0.21875, ((1, 4),)),
        "o_weight": gaussian(splits[8], (D, D), (max(1, D // 192)) ** -0.5, 3.0, ((0, 4),)),
        "cross_q": gaussian(splits[9], (D, D), D ** -0.5, 0.21875, ((1, 4),)),
        "cross_k": gaussian(splits[10], (TEXT_D, D), TEXT_D ** -0.5, 0.21875, ((1, 4),)),
        "cross_v": gaussian(splits[11], (TEXT_D, D), TEXT_D ** -0.5, 0.21875, ((1, 4),)),
        "cross_o": gaussian(splits[12], (D, D), (max(1, D // 32)) ** -0.5, 1.25, ((0, 4),)),
        "mlp_in": gaussian(splits[13], (D, FF), (max(1, D // 2)) ** -0.5, 0.3125, ((1, 4),)),
        "mlp_out": gaussian(splits[14], (FF, D), (max(1, FF // 4)) ** -0.5, 0.21875, ((0, 4),)),
        "mod_weight": gaussian(splits[15], (D, 9 * D), D ** -0.5, 0.21875, ((1, 4),)),
        "mod_bias": gaussian(splits[16], (9 * D,), 0.5, 3.0, ((0, 4),)),
        "cotangent": gaussian(splits[17], (TOKENS, D), 1.0, 6.0, ((0, 8),)),
    }


epsilon = 1e-06
masked_score = -1000000000.0

@jax.custom_vjp
def low(v):
    return lax.optimization_barrier(v.astype(jnp.bfloat16)).astype(jnp.float32)

@jax.custom_vjp
def low_back(v):
    return v

def low_keep(v):
    return (low(v), None)

def low_pass(kept, grad):
    return (grad,)

def back_keep(v):
    return (v, None)

def back_low(kept, grad):
    return (low(grad),)
low.defvjp(low_keep, low_pass)
low_back.defvjp(back_keep, back_low)

def both_ways(values):
    return low(low_back(values))

def matmul(left_side, right_side):
    return jnp.dot(left_side, right_side, precision=lax.Precision.HIGHEST, preferred_element_type=jnp.float32)

def sinusoid(step_ids, model_width):
    half_width = model_width // 2
    ramp_index = jnp.arange(half_width).astype(jnp.float32)
    frequency = jnp.exp(ramp_index * (-math.log(10000.0) / half_width))
    angles = step_ids.astype(jnp.float32)[:, None] * frequency[None, :]
    return jnp.concatenate([jnp.cos(angles), jnp.sin(angles)], axis=1)

def layer_norm(values):
    row_mean = lax.optimization_barrier(jnp.mean(values, axis=-1, keepdims=True))
    centered = values - row_mean
    variance = lax.optimization_barrier(jnp.mean(centered * centered, axis=-1, keepdims=True))
    return centered * lax.rsqrt(variance + epsilon)

def clip_positions(lengths, token_count):
    clip_ends = jnp.cumsum(lengths)
    position = jnp.arange(token_count, dtype=jnp.int32)
    return lax.optimization_barrier(jnp.sum((position[:, None] >= clip_ends[None, :]).astype(jnp.int32), axis=1))

def masks(clip_index, slot_count, text_lengths):
    slot_range = jnp.arange(slot_count, dtype=jnp.int32)
    onehot = clip_index[:, None] == slot_range[None, :]
    self_allowed = clip_index[:, None] == clip_index[None, :]
    key_range = jnp.arange(slot_count * TEXT_LEN, dtype=jnp.int32)
    key_slot = key_range // TEXT_LEN
    key_place = key_range % TEXT_LEN
    key_limit = jnp.repeat(text_lengths, TEXT_LEN)
    cross_allowed = (clip_index[:, None] == key_slot[None, :]) & (key_place < key_limit)[None, :]
    return (onehot, self_allowed, cross_allowed)

def column_split(hidden, weight_list):
    results = [[] for member in weight_list]
    for group in range(N_TENSOR):
        copy_in = low_back(hidden)
        for member, weight in enumerate(weight_list):
            col_count = weight.shape[1] // N_TENSOR
            results[member].append(matmul(copy_in, weight[:, group * col_count:(group + 1) * col_count]))
    return [jnp.concatenate(pieces, axis=1) for pieces in results]

def row_split(hidden, weight):
    row_count = weight.shape[0] // N_TENSOR
    summed = jnp.zeros((hidden.shape[0], weight.shape[1]), jnp.float32)
    for group in range(N_TENSOR):
        partial_out = matmul(hidden[:, group * row_count:(group + 1) * row_count], weight[group * row_count:(group + 1) * row_count])
        summed = summed + low(partial_out)
    return low_back(summed)

def attention(queries, key_rows, value_rows, allowed):
    head_dim = D // HEADS
    score_scale = head_dim ** (-0.5)

    def one_head(operands):
        query_head, key_head, value_head = operands
        scores = low_back(matmul(query_head, key_head.T) * score_scale)
        scores = jnp.where(allowed, scores, masked_score)
        weights_low = low(jax.nn.softmax(scores, axis=-1))
        return matmul(weights_low, value_head)

    def by_head(array):
        return array.reshape(array.shape[0], -1, head_dim).transpose(1, 0, 2)
    heads_out = lax.map(jax.checkpoint(one_head), (by_head(queries), by_head(key_rows), by_head(value_rows)))
    return heads_out.transpose(1, 0, 2).reshape(queries.shape[0], -1)

def layer_forward(layer_in, layer_weights, text_flat, onehot, self_allowed, cross_allowed, silu_low):
    q_weight, k_weight, v_weight, o_weight, cross_q, cross_k, cross_v, cross_o, mlp_in, mlp_out, mod_weight, mod_bias = layer_weights
    modulation = low_back(matmul(silu_low, mod_weight) + mod_bias)
    per_token = matmul(onehot, modulation)
    pieces = [per_token[:, component * D:(component + 1) * D] for component in range(9)]
    shift_one, scale_one, gate_one, shift_two, scale_two, gate_two, shift_three, scale_three, gate_three = pieces
    hidden_one = low(layer_norm(layer_in) * (1.0 + scale_one) + shift_one)
    queries, key_rows, value_rows = column_split(hidden_one, [q_weight, k_weight, v_weight])
    attended = both_ways(attention(both_ways(queries), both_ways(key_rows), both_ways(value_rows), self_allowed))
    branch_one = row_split(attended, o_weight)
    after_one = layer_in + gate_one * branch_one
    hidden_two = low(layer_norm(after_one) * (1.0 + scale_two) + shift_two)
    cross_queries = column_split(hidden_two, [cross_q])[0]
    text_keys = both_ways(matmul(text_flat, cross_k))
    text_values = both_ways(matmul(text_flat, cross_v))
    crossed = both_ways(attention(both_ways(cross_queries), text_keys, text_values, cross_allowed))
    branch_two = row_split(crossed, cross_o)
    after_two = after_one + gate_two * branch_two
    hidden_three = low(layer_norm(after_two) * (1.0 + scale_three) + shift_three)
    pre_act = column_split(hidden_three, [mlp_in])[0]
    activated = low(jax.nn.gelu(low_back(pre_act), approximate=True))
    branch_three = row_split(activated, mlp_out)
    return after_two + gate_three * branch_three

def reference(tokens, text_states, clip_len, text_len, timesteps, q_weight, k_weight, v_weight, o_weight, cross_q, cross_k, cross_v, cross_o, mlp_in, mlp_out, mod_weight, mod_bias, cotangent):
    weight_args = tuple((member.astype(jnp.float32) for member in (q_weight, k_weight, v_weight, o_weight, cross_q, cross_k, cross_v, cross_o, mlp_in, mlp_out, mod_weight, mod_bias)))
    group_items = (tokens.astype(jnp.float32).reshape(N_DP, TOK_DEV, D), text_states.astype(jnp.float32).reshape(N_DP, SLOTS * TEXT_LEN, TEXT_D), clip_len.reshape(N_DP, SLOTS), text_len.reshape(N_DP, SLOTS), timesteps.reshape(N_DP, SLOTS), cotangent.astype(jnp.float32).reshape(N_DP, TOK_DEV, D))

    def one_group(grad_totals, group_item):
        group_in, text_flat, lengths, text_lengths, step_ids, group_cot = group_item
        clip_index = clip_positions(lengths, TOK_DEV)
        onehot, self_allowed, cross_allowed = masks(clip_index, SLOTS, text_lengths)
        onehot_float = onehot.astype(jnp.float32)
        silu_low = low(jax.nn.silu(sinusoid(step_ids, D)))

        def forward(layer_in, *layer_weights):
            return layer_forward(layer_in, layer_weights, text_flat, onehot_float, self_allowed, cross_allowed, silu_low)
        layer_out, pullback = jax.vjp(forward, group_in, *weight_args)
        gradients = pullback(group_cot)
        new_totals = tuple((total_part + grad_part for total_part, grad_part in zip(grad_totals, gradients[1:])))
        return (new_totals, (layer_out, gradients[0]))
    zero_totals = tuple((jnp.zeros(member.shape, jnp.float32) for member in weight_args))
    grad_totals, (layer_outs, input_grads) = lax.scan(one_group, zero_totals, group_items)
    return (layer_outs.reshape(TOKENS, D).astype(jnp.bfloat16), input_grads.reshape(TOKENS, D).astype(jnp.bfloat16), grad_totals[0], grad_totals[1], grad_totals[2], grad_totals[3], grad_totals[4], grad_totals[5], grad_totals[6], grad_totals[7], grad_totals[8], grad_totals[9], grad_totals[10], grad_totals[11])
```

```python
import math

import jax
import jax.numpy as jnp
from jax import lax
from jax.experimental import pallas as pl
from jax.experimental.pallas import tpu as pltpu
from jax.sharding import PartitionSpec as P

HEAD = 64
BLOCK = 256
EPSILON = 1e-06
MASKED = -1000000000.0
CURVE = math.sqrt(2.0 / math.pi)
CUBIC = 0.044715
F32 = jnp.float32
BF16 = jnp.bfloat16


def dot_nn(a, b):
    return lax.dot_general(a, b, (((1,), (0,)), ((), ())), preferred_element_type=F32)


def dot_nt(a, b):
    return lax.dot_general(a, b, (((1,), (1,)), ((), ())), preferred_element_type=F32)


def dot_tn(a, b):
    return lax.dot_general(a, b, (((0,), (0,)), ((), ())), preferred_element_type=F32)


def normalize(values):
    centered = values - jnp.mean(values, axis=-1, keepdims=True)
    inverse = lax.rsqrt(jnp.mean(centered * centered, axis=-1, keepdims=True) + EPSILON)
    return centered * inverse, inverse


def norm_back(grad, normed, inverse):
    first = jnp.mean(grad, axis=-1, keepdims=True)
    second = jnp.mean(grad * normed, axis=-1, keepdims=True)
    return inverse * (grad - first - normed * second)


def column_sum(values):
    return jnp.sum(values, axis=0, keepdims=True)


def three_parts(column):
    high = column.astype(BF16).astype(F32)
    rest = column - high
    middle = rest.astype(BF16).astype(F32)
    return high, middle, rest - middle


def head_slice(rows, head):
    piece = rows[:, head * HEAD : (head + 1) * HEAD]
    return jnp.concatenate([piece, jnp.zeros_like(piece)], axis=1)


def run(kernel, outs, scalars, arrays, scratch=(), flops=0, vmem=40):
    vmem_spec = pl.BlockSpec(memory_space=pltpu.VMEM)
    return pl.pallas_call(
        kernel,
        out_shape=[jax.ShapeDtypeStruct(shape, kind) for shape, kind in outs],
        in_specs=[pl.BlockSpec(memory_space=pltpu.SMEM)] + [vmem_spec] * len(arrays),
        out_specs=[vmem_spec] * len(outs),
        scratch_shapes=[pltpu.VMEM(shape, kind) for shape, kind in scratch],
        compiler_params=pltpu.CompilerParams(vmem_limit_bytes=vmem * 1024 * 1024),
        cost_estimate=pl.CostEstimate(flops=flops, bytes_accessed=8_000_000, transcendentals=0),
    )(scalars, *arrays)


SLOT, CORE, OWN, ROW, LIMIT = 0, 4, 5, 7, 8


def text_kernel(place, text, ck, cv, cq, co, packed):
    width = ck.shape[1]
    slots = text.shape[0]
    rows = text.shape[1]
    packed[0:width, :] = cq[...].astype(F32).T.astype(BF16)
    packed[width : 2 * width, :] = co[...]
    for slot in range(slots):
        keys = dot_nn(text[slot], ck[...]).astype(BF16)
        values = dot_nn(text[slot], cv[...]).astype(BF16)
        first = 2 * width + rows * (slot % 2)
        left = 2 * width * (slot // 2)
        packed[first : first + rows, left : left + 2 * width] = jnp.concatenate([keys, values], axis=1)


def self_forward(place, tokens, mod, wq, wk, wv, wo, part, h1, qa, ka, va, att):
    model = tokens.shape[1]
    blocks = tokens.shape[0] // BLOCK
    half = blocks // 2
    heads = wq.shape[1] // HEAD
    lane = lax.broadcasted_iota(jnp.int32, (BLOCK, 2 * HEAD), 1)
    keep = lane < HEAD

    def project(block, carry):
        rows = pl.ds(pl.multiple_of(block * BLOCK, BLOCK), BLOCK)
        slot = place[SLOT + block]
        normed, _ = normalize(tokens[rows, :].astype(F32))
        scale = mod[pl.ds(slot, 1), model : 2 * model]
        shift = mod[pl.ds(slot, 1), 0:model]
        hidden = (normed * (1.0 + scale) + shift).astype(BF16)
        h1[rows, :] = hidden
        q = dot_nn(hidden, wq[...]).astype(BF16).astype(F32) * (HEAD**-0.5)
        k = dot_nn(hidden, wk[...])
        v = dot_nn(hidden, wv[...])
        mine = lane == HEAD + slot
        q_more = jnp.where(mine, 1.0, 0.0)
        k_more = jnp.where((lane >= HEAD + 4) & (lane < HEAD + 7), 1.0, 0.0)
        k_more = jnp.where((lane >= HEAD) & (lane < HEAD + 4) & jnp.logical_not(mine), MASKED, k_more)
        v_more = jnp.where((lane >= HEAD) & (lane < HEAD + 3), 1.0, 0.0)
        for head in range(heads):
            qa[head, rows, :] = jnp.where(keep, head_slice(q, head), q_more).astype(BF16)
            ka[head, rows, :] = jnp.where(keep, head_slice(k, head), k_more).astype(BF16)
            va[head, rows, :] = jnp.where(keep, head_slice(v, head), v_more).astype(BF16)
        return carry

    lax.fori_loop(0, blocks, project, 0)

    def attend(block, carry):
        rows = pl.ds(pl.multiple_of(block * BLOCK, BLOCK), BLOCK)
        pieces = []
        for head in range(heads):
            queries = qa[head, rows, :]
            scores = dot_nt(queries, ka[head])
            top = jnp.max(scores, axis=1, keepdims=True)
            raised = jnp.exp(scores - top).astype(BF16)
            out = dot_nn(raised, va[head])
            total = out[:, HEAD : HEAD + 1]
            pieces.append(out[:, :HEAD] * (1.0 / total))
            high, middle, low = three_parts(-(top + jnp.log(total)))
            more = jnp.where(lane == HEAD + 4, high, jnp.where(lane == HEAD + 5, middle, low))
            spot = (lane >= HEAD + 4) & (lane < HEAD + 7)
            qa[head, rows, :] = jnp.where(spot, more, queries.astype(F32)).astype(BF16)
        attended = jnp.concatenate(pieces, axis=1).astype(BF16)
        att[rows, :] = attended
        side = lax.div(block, half) ^ place[CORE]
        out_rows = pl.ds(pl.multiple_of(lax.rem(block, half) * BLOCK, BLOCK), BLOCK)
        part[side, out_rows, :] = dot_nn(attended, wo[...]).astype(BF16)
        return carry

    lax.fori_loop(0, blocks, attend, 0)


def gather_pieces(pieces, cqt, co, width):
    for index, piece in enumerate(pieces):
        cqt[index * width : (index + 1) * width, :] = piece[0:width, :]
        co[index * width : (index + 1) * width, :] = piece[width : 2 * width, :]


def middle_kernel(
    place, tokens, cot, mod, sum_own, sum_far, p0, p1, p2, p3, win0, win1, wout0, wout1,
    x1_out, b2_out, h2_out, q2_out, cr_out, kall, vall, h3g_out, b3_out, dw_out,
    cqt, co, h3_all, act0, act1, pg0, pg1, b3g_all,
):
    model = tokens.shape[1]
    width = (p0.shape[1]) // 4
    rows_of_slot = kall.shape[1]
    count = sum_own.shape[0]
    blocks = count // BLOCK
    pieces = (p0, p1, p2, p3)
    gather_pieces(pieces, cqt, co, width)
    for slot in range(kall.shape[0]):
        first = 2 * width + rows_of_slot * (slot % 2)
        left = 2 * width * (slot // 2)
        both = [p[first : first + rows_of_slot, left : left + 2 * width] for p in pieces]
        kall[slot] = jnp.concatenate([b[:, :width] for b in both], axis=1)
        vall[slot] = jnp.concatenate([b[:, width:] for b in both], axis=1)
    lane = lax.broadcasted_iota(jnp.int32, (1, 2 * HEAD), 1)
    sides = [jnp.where(lane < HEAD, 1.0, 0.0).astype(BF16), jnp.where(lane < HEAD, 0.0, 1.0).astype(BF16)]
    key_lane = lax.broadcasted_iota(jnp.int32, (BLOCK, rows_of_slot), 1)

    def body(block, carry):
        first = pl.multiple_of(block * BLOCK, BLOCK)
        rows = pl.ds(first, BLOCK)
        group_rows = pl.ds(pl.multiple_of(place[CORE] * count + first, BLOCK), BLOCK)
        slot = place[OWN + block]

        def m(component):
            return mod[pl.ds(slot, 1), component * model : (component + 1) * model]

        branch = sum_own[rows, :].astype(F32) + sum_far[rows, :].astype(F32)
        x1 = tokens[group_rows, :].astype(F32) + m(2) * branch
        x1_out[rows, :] = x1
        normed, _ = normalize(x1)
        h2 = (normed * (1.0 + m(4)) + m(3)).astype(BF16)
        h2_out[rows, :] = h2
        q2 = dot_nt(h2, cqt[...]).astype(BF16)
        q2_out[rows, :] = q2
        allowed = key_lane < place[LIMIT + slot]
        crossed = []
        for pair in range(model // (2 * HEAD)):
            cols = slice(pair * 2 * HEAD, (pair + 1) * 2 * HEAD)
            keys = kall[slot, :, cols]
            values = vall[slot, :, cols]
            total = None
            for side in sides:
                scores = dot_nt(q2[:, cols], keys * side) * (HEAD**-0.5)
                scores = jnp.where(allowed, scores, MASKED)
                raised = jnp.exp(scores - jnp.max(scores, axis=1, keepdims=True))
                probs = raised * (1.0 / jnp.sum(raised, axis=1, keepdims=True))
                out = dot_nn(probs.astype(BF16), values * side)
                total = out if total is None else total + out
            crossed.append(total.astype(BF16))
        crossed = jnp.concatenate(crossed, axis=1)
        cr_out[rows, :] = crossed
        b2 = dot_nn(crossed, co[...])
        b2_out[rows, :] = b2
        x2 = x1 + m(5) * b2
        normed, _ = normalize(x2)
        h3 = (normed * (1.0 + m(7)) + m(6)).astype(BF16)
        h3_all[rows, :] = h3
        b3g = (cot[group_rows, :].astype(F32) * m(8)).astype(BF16)
        b3g_all[rows, :] = b3g
        b3 = jnp.zeros((BLOCK, model), F32)
        h3g = jnp.zeros((BLOCK, model), F32)
        for win, wout, act_all, pg_all in ((win0, wout0, act0, pg0), (win1, wout1, act1, pg1)):
            pre = dot_nn(h3, win[...])
            square = pre * pre
            bent = jnp.tanh(CURVE * (pre + CUBIC * (square * pre)))
            act = (0.5 * pre * (1.0 + bent)).astype(BF16)
            act_all[rows, :] = act
            slope = 0.5 * (1.0 + bent) + 0.5 * pre * (1.0 - bent * bent) * (
                CURVE * (1.0 + 3.0 * CUBIC * square)
            )
            b3 = b3 + dot_nn(act, wout[...])
            pg = (dot_nt(b3g, wout[...]) * slope).astype(BF16)
            pg_all[rows, :] = pg
            h3g = h3g + dot_nt(pg, win[...])
        b3_out[rows, :] = b3.astype(BF16)
        h3g_out[rows, :] = h3g.astype(BF16)
        return carry

    lax.fori_loop(0, blocks, body, 0)
    row = place[ROW]
    for member, (act_all, pg_all) in enumerate(((act0, pg0), (act1, pg1))):
        for start in range(0, model, BLOCK):
            cols = slice(start, start + BLOCK)
            dw_out[member, row, cols, :] = dot_tn(h3_all[:, cols], pg_all[...]).astype(BF16)
            dw_out[member, 1 - row, cols, :] = dot_tn(act_all[:, cols], b3g_all[...]).astype(BF16)


def cross_back(
    place, mod, cot, text, h3g_own, h3g_far, x1_in, b2_in, sum_own, sum_far, h2_in, q2_in, cr_in,
    kall, vall, p0, p1, p2, p3,
    b1g_out, x1g_out, dw_out, sums,
    cqt, co, dk_all, dv_all, dq_all, b2g_all,
):
    model = cot.shape[1]
    width = p0.shape[1] // 4
    rows_of_slot = kall.shape[1]
    count = sum_own.shape[0]
    blocks = count // BLOCK
    gather_pieces((p0, p1, p2, p3), cqt, co, width)
    dk_all[...] = jnp.zeros_like(dk_all)
    dv_all[...] = jnp.zeros_like(dv_all)
    lane = lax.broadcasted_iota(jnp.int32, (1, 2 * HEAD), 1)
    sides = [jnp.where(lane < HEAD, 1.0, 0.0), jnp.where(lane < HEAD, 0.0, 1.0)]
    key_row = lax.broadcasted_iota(jnp.int32, (rows_of_slot, BLOCK), 0)

    def body(block, carry):
        first = pl.multiple_of(block * BLOCK, BLOCK)
        rows = pl.ds(first, BLOCK)
        group_rows = pl.ds(pl.multiple_of(place[CORE] * count + first, BLOCK), BLOCK)
        slot = place[OWN + block]

        def m(component):
            return mod[pl.ds(slot, 1), component * model : (component + 1) * model]

        x1 = x1_in[rows, :]
        b2 = b2_in[rows, :]
        h3g = h3g_own[rows, :].astype(F32) + h3g_far[rows, :].astype(F32)
        normed, inverse = normalize(x1 + m(5) * b2)
        sums[block, 4:5, :] = column_sum(h3g)
        sums[block, 5:6, :] = column_sum(h3g * normed)
        x2g = cot[group_rows, :].astype(F32) + norm_back(h3g * (1.0 + m(7)), normed, inverse)
        sums[block, 3:4, :] = column_sum(x2g * b2)
        b2g = (x2g * m(5)).astype(BF16)
        b2g_all[rows, :] = b2g
        out_grad = dot_nt(b2g, co[...]).astype(BF16)
        q2 = q2_in[rows, :]
        allowed = key_row < place[LIMIT + slot]
        query_grads = []
        for pair in range(model // (2 * HEAD)):
            cols = slice(pair * 2 * HEAD, (pair + 1) * 2 * HEAD)
            keys = kall[slot, :, cols]
            values = vall[slot, :, cols]
            queries = q2[:, cols]
            grads = out_grad[:, cols]
            dq = dk = dv = None
            for side in sides:
                side_low = side.astype(BF16)
                key_side = keys * side_low
                scores = jnp.where(allowed, dot_nt(key_side, queries) * (HEAD**-0.5), MASKED)
                raised = jnp.exp(scores - jnp.max(scores, axis=0, keepdims=True))
                probs = raised * (1.0 / jnp.sum(raised, axis=0, keepdims=True))
                prob_grad = dot_nt(values * side_low, grads)
                row_dot = jnp.sum(probs * prob_grad, axis=0, keepdims=True)
                score_grad = (probs * (prob_grad - row_dot)).astype(BF16)
                dv_side = dot_nn(probs.astype(BF16), grads) * side
                dk_side = dot_nn(score_grad, queries) * side
                dq_side = dot_tn(score_grad, key_side)
                dv = dv_side if dv is None else dv + dv_side
                dk = dk_side if dk is None else dk + dk_side
                dq = dq_side if dq is None else dq + dq_side
            query_grads.append((dq * (HEAD**-0.5)).astype(BF16))
            dk_all[slot, :, cols] += dk * (HEAD**-0.5)
            dv_all[slot, :, cols] += dv
        query_grad = jnp.concatenate(query_grads, axis=1)
        dq_all[rows, :] = query_grad
        h2g = dot_nn(query_grad, cqt[...])
        normed, inverse = normalize(x1)
        sums[block, 1:2, :] = column_sum(h2g)
        sums[block, 2:3, :] = column_sum(h2g * normed)
        x1g = x2g + norm_back(h2g * (1.0 + m(4)), normed, inverse)
        x1g_out[rows, :] = x1g
        branch = sum_own[rows, :].astype(F32) + sum_far[rows, :].astype(F32)
        sums[block, 0:1, :] = column_sum(x1g * branch)
        b1g_out[rows, :] = (x1g * m(2)).astype(BF16)
        return carry

    lax.fori_loop(0, blocks, body, 0)
    flip = 2 * place[ROW]
    for member in range(2):
        start = (member * width // 128) * 128
        skip = member * width - start
        cols = slice(start, start + 2 * 128)
        kept = slice(skip, skip + width)
        dw_out[member, 0 ^ flip] = dot_tn(dq_all[:, cols], h2_in[...])[kept].astype(BF16)
        dk_rows = dv_rows = None
        for slot in range(kall.shape[0]):
            dk_one = dot_tn(dk_all[slot, :, cols].astype(BF16), text[slot])
            dv_one = dot_tn(dv_all[slot, :, cols].astype(BF16), text[slot])
            dk_rows = dk_one if dk_rows is None else dk_rows + dk_one
            dv_rows = dv_one if dv_rows is None else dv_rows + dv_one
        dw_out[member, 1 ^ flip] = dk_rows[kept].astype(BF16)
        dw_out[member, 2 ^ flip] = dv_rows[kept].astype(BF16)
        dw_out[member, 3 ^ flip] = dot_tn(cr_in[:, cols], b2g_all[...])[kept].astype(BF16)


def self_back(
    place, b1g_own, b1g_far, att, h1, qa, ka, va, wq, wk, wv, wo,
    part, dw_out,
    b1g, da, dq_sum, dq_all, dk_all, dv_all,
):
    count = b1g_own.shape[0]
    blocks = h1.shape[0] // BLOCK
    half = blocks // 2
    heads = wq.shape[1] // HEAD
    b1g[pl.ds(pl.multiple_of(place[CORE] * count, BLOCK), count), :] = b1g_own[...]
    b1g[pl.ds(pl.multiple_of((1 - place[CORE]) * count, BLOCK), count), :] = b1g_far[...]
    dq_sum[...] = jnp.zeros_like(dq_sum)
    lane = lax.broadcasted_iota(jnp.int32, (BLOCK, 2 * HEAD), 1)

    def prepare(block, carry):
        rows = pl.ds(pl.multiple_of(block * BLOCK, BLOCK), BLOCK)
        grads = dot_nt(b1g[rows, :], wo[...]).astype(BF16).astype(F32)
        dots = grads * att[rows, :].astype(F32)
        for head in range(heads):
            row_dot = jnp.sum(dots[:, head * HEAD : (head + 1) * HEAD], axis=1, keepdims=True)
            high, middle, low = three_parts(-row_dot)
            more = jnp.where(lane == HEAD, high, jnp.where(lane == HEAD + 1, middle, low))
            more = jnp.where(lane < HEAD + 3, more, 0.0)
            da[head, rows, :] = jnp.where(lane < HEAD, head_slice(grads, head), more).astype(BF16)
        return carry

    lax.fori_loop(0, blocks, prepare, 0)

    def by_keys(block, carry):
        rows = pl.ds(pl.multiple_of(block * BLOCK, BLOCK), BLOCK)
        dks = []
        dvs = []
        for head in range(heads):
            keys = ka[head, rows, :]
            probs = jnp.exp(dot_nt(keys, qa[head]))
            prob_grad = dot_nt(va[head, rows, :], da[head])
            score_grad = (probs * prob_grad).astype(BF16)
            dvs.append(dot_nn(probs.astype(BF16), da[head])[:, :HEAD])
            dks.append(dot_nn(score_grad, qa[head])[:, :HEAD])
            dq_sum[head] += dot_tn(score_grad, keys)
        dk_all[rows, :] = jnp.concatenate(dks, axis=1).astype(BF16)
        dv_all[rows, :] = jnp.concatenate(dvs, axis=1).astype(BF16)
        return carry

    lax.fori_loop(0, blocks, by_keys, 0)

    def leave(block, carry):
        rows = pl.ds(pl.multiple_of(block * BLOCK, BLOCK), BLOCK)
        dq = jnp.concatenate([dq_sum[head, rows, :HEAD] for head in range(heads)], axis=1)
        dq = (dq * (HEAD**-0.5)).astype(BF16)
        dq_all[rows, :] = dq
        out = dot_nt(dq, wq[...]) + dot_nt(dk_all[rows, :], wk[...]) + dot_nt(dv_all[rows, :], wv[...])
        side = lax.div(block, half) ^ place[CORE]
        out_rows = pl.ds(pl.multiple_of(lax.rem(block, half) * BLOCK, BLOCK), BLOCK)
        part[side, out_rows, :] = out.astype(BF16)
        return carry

    lax.fori_loop(0, blocks, leave, 0)
    flip = 2 * place[ROW]
    dw_out[0 ^ flip] = dot_tn(dq_all[...], h1[...]).astype(BF16)
    dw_out[1 ^ flip] = dot_tn(dk_all[...], h1[...]).astype(BF16)
    dw_out[2 ^ flip] = dot_tn(dv_all[...], h1[...]).astype(BF16)
    dw_out[3 ^ flip] = dot_tn(att[...], b1g[...]).astype(BF16)


def mixed_kernel(place, mod, cot, x1_in, b2_in, b3_own, b3_far, mixed, sums):
    model = cot.shape[1]
    count = x1_in.shape[0]
    for block in range(count // BLOCK):
        rows = slice(block * BLOCK, (block + 1) * BLOCK)
        group_rows = pl.ds(pl.multiple_of(place[CORE] * count + block * BLOCK, BLOCK), BLOCK)
        slot = place[OWN + block]
        gate_two = mod[pl.ds(slot, 1), 5 * model : 6 * model]
        gate_three = mod[pl.ds(slot, 1), 8 * model : 9 * model]
        b3 = b3_own[rows, :].astype(F32) + b3_far[rows, :].astype(F32)
        mixed[rows, :] = (x1_in[rows, :] + gate_two * b2_in[rows, :] + gate_three * b3).astype(BF16)
        sums[block] = column_sum(cot[group_rows, :].astype(F32) * b3)


def final_kernel(place, mod, tokens, h1g_own, h1g_far, x1g_in, sums_cross, sums_mixed, token_grad, slot_sums):
    model = tokens.shape[1]
    count = x1g_in.shape[0]
    slot_sums[...] = jnp.zeros_like(slot_sums)
    for block in range(count // BLOCK):
        rows = slice(block * BLOCK, (block + 1) * BLOCK)
        group_rows = pl.ds(pl.multiple_of(place[CORE] * count + block * BLOCK, BLOCK), BLOCK)
        slot = place[OWN + block]
        h1g = h1g_own[rows, :].astype(F32) + h1g_far[rows, :].astype(F32)
        normed, inverse = normalize(tokens[group_rows, :].astype(F32))
        scale = mod[pl.ds(slot, 1), model : 2 * model]
        token_grad[rows, :] = (x1g_in[rows, :] + norm_back(h1g * (1.0 + scale), normed, inverse)).astype(BF16)
        terms = [column_sum(h1g), column_sum(h1g * normed)]
        terms += [sums_cross[block, i : i + 1, :] for i in range(6)]
        terms += [sums_mixed[block]]
        for component, term in enumerate(terms):
            slot_sums[pl.ds(slot, 1), component * model : (component + 1) * model] += term


def solution(mesh):
    n_dp = mesh.shape["dp"]
    n_tensor = mesh.shape["tensor"]
    core_pairs = [(i, i ^ 1) for i in range(n_tensor)]
    far_pairs = [(i, i ^ 2) for i in range(n_tensor)]
    cross_pairs = [(i, i ^ 3) for i in range(n_tensor)]
    dp_bits = int(math.log2(n_dp))

    def core_swap(value):
        return lax.ppermute(value, "tensor", core_pairs)

    def far_swap(value):
        return lax.ppermute(value, "tensor", far_pairs)

    def dp_swap(value, bit):
        return lax.ppermute(value, "dp", [(i, i ^ (1 << bit)) for i in range(n_dp)])

    def pair_up(flag, mine, other):
        return jnp.concatenate([jnp.where(flag == 0, mine, other), jnp.where(flag == 0, other, mine)], axis=0)

    def local(
        tokens, text_states, clip_len, text_len, timesteps, q_weight, k_weight, v_weight, o_weight,
        cross_q, cross_k, cross_v, cross_o, mlp_in, mlp_out, mod_weight, mod_bias, cotangent,
    ):
        count, model = tokens.shape
        slots, text_rows = text_states.shape[:2]
        width = q_weight.shape[1]
        heads = width // HEAD
        half = count // 2
        blocks = count // BLOCK
        text_pad = -(-text_rows // 16) * 16
        tensor_at = lax.axis_index("tensor")
        dp_at = lax.axis_index("dp")
        core = tensor_at & 1
        row = dp_at & 1

        ends = jnp.cumsum(clip_len)
        starts = jnp.arange(blocks, dtype=jnp.int32) * BLOCK
        slot_of = jnp.sum((starts[:, None] >= ends[None, :]).astype(jnp.int32), axis=1)
        own_slots = lax.dynamic_slice(slot_of, (core * (blocks // 2),), (blocks // 2,))
        place = jnp.concatenate([slot_of, core[None], own_slots, row[None], text_len]).astype(jnp.int32)

        half_width = model // 2
        ramp = jnp.arange(half_width).astype(F32)
        frequency = jnp.exp(ramp * (-math.log(10000.0) / half_width))
        angles = timesteps.astype(F32)[:, None] * frequency[None, :]
        embed = jnp.concatenate([jnp.cos(angles), jnp.sin(angles)], axis=1)
        silu_low = jax.nn.silu(embed).astype(BF16)
        mod_own = dot_nn(silu_low, mod_weight) + mod_bias.astype(F32)
        mod_all = jnp.stack(
            [mod_own] + [lax.ppermute(mod_own, "tensor", p) for p in (core_pairs, far_pairs, cross_pairs)]
        )
        mod = jnp.concatenate(
            [lax.dynamic_index_in_dim(mod_all, tensor_at ^ j, 0, keepdims=False) for j in range(n_tensor)], axis=1
        )

        text = jnp.pad(text_states, ((0, 0), (0, text_pad - text_rows), (0, 0)))
        packed_rows = 2 * width + 2 * text_pad
        (p0,) = run(
            text_kernel, [((packed_rows, model), BF16)], place,
            [text, cross_k, cross_v, cross_q, cross_o], flops=2 * slots * text_pad * model * 2 * width,
        )
        p2 = far_swap(p0)
        p1 = core_swap(p0)
        p3 = core_swap(p2)
        mlp_in_far = core_swap(mlp_in)
        mlp_out_far = core_swap(mlp_out)

        part, h1, qa, ka, va, att = run(
            self_forward,
            [((2, half, model), BF16), ((count, model), BF16)]
            + [((heads, count, 2 * HEAD), BF16)] * 3 + [((count, width), BF16)],
            place, [tokens, mod, q_weight, k_weight, v_weight, o_weight],
            flops=12_000_000_000,
        )
        sum_own = (part[0].astype(F32) + core_swap(part[1]).astype(F32)).astype(BF16)
        sum_far = far_swap(sum_own)

        x1, b2, h2, q2, crossed, kall, vall, h3g_own, b3_own, dw_mlp = run(
            middle_kernel,
            [((half, model), F32)] * 2 + [((half, model), BF16)] * 3
            + [((slots, text_pad, model), BF16)] * 2 + [((half, model), BF16)] * 2
            + [((2, 2, model, model), BF16)],
            place,
            [tokens, cotangent, mod, sum_own, sum_far, p0, p1, p2, p3, mlp_in, mlp_in_far, mlp_out, mlp_out_far],
            scratch=[((model, model), BF16)] * 2 + [((half, model), BF16)] * 6,
            flops=16_000_000_000, vmem=52,
        )
        h3g_far = far_swap(h3g_own)
        dw_mlp = (dw_mlp[0].astype(F32) + core_swap(dw_mlp[1]).astype(F32)).astype(BF16)

        b1g, x1g, dw_cross, sums_cross = run(
            cross_back,
            [((half, model), BF16), ((half, model), F32), ((2, 4, width, model), BF16), ((2, 8, model), F32)],
            place,
            [mod, cotangent, text, h3g_own, h3g_far, x1, b2, sum_own, sum_far, h2, q2, crossed, kall, vall,
             p0, p1, p2, p3],
            scratch=[((model, model), BF16)] * 2 + [((slots, text_pad, model), F32)] * 2 + [((half, model), BF16)] * 2,
            flops=8_000_000_000, vmem=52,
        )
        b3_far = far_swap(b3_own)
        b1g_far = core_swap(b1g)
        dw_cross = (dw_cross[0].astype(F32) + core_swap(dw_cross[1]).astype(F32)).astype(BF16)

        part_grad, dw_self = run(
            self_back,
            [((2, half, model), BF16), ((4, width, model), BF16)],
            place, [b1g, b1g_far, att, h1, qa, ka, va, q_weight, k_weight, v_weight, o_weight],
            scratch=[((count, model), BF16), ((heads, count, 2 * HEAD), BF16), ((heads, count, 2 * HEAD), F32)]
            + [((count, width), BF16)] * 3,
            flops=20_000_000_000, vmem=52,
        )
        h1g_own = (part_grad[0].astype(F32) + core_swap(part_grad[1]).astype(F32)).astype(BF16)
        h1g_far = far_swap(h1g_own)

        mixed, sums_mixed = run(
            mixed_kernel, [((half, model), BF16), ((2, 1, model), F32)],
            place, [mod, cotangent, x1, b2, b3_own, b3_far], flops=10_000_000,
        )
        token_grad, slot_sums = run(
            final_kernel, [((half, model), BF16), ((slots, 9 * model), F32)],
            place, [mod, tokens, h1g_own, h1g_far, x1g, sums_cross, sums_mixed], flops=10_000_000,
        )
        mixed = pair_up(core, mixed, core_swap(mixed))
        token_grad = pair_up(core, token_grad, core_swap(token_grad))

        slot_sums = slot_sums + core_swap(slot_sums)
        local_cols = mod_weight.shape[1]
        slot_grad = lax.dynamic_slice_in_dim(slot_sums, tensor_at * local_cols, local_cols, 1).astype(BF16)
        gathered = jnp.concatenate([silu_low, slot_grad], axis=1)
        for bit in range(dp_bits):
            gathered = jnp.concatenate([gathered, dp_swap(gathered, bit)], axis=0)
        mod_weight_grad = dot_tn(gathered[:, :model], gathered[:, model:])
        mod_bias_grad = jnp.sum(gathered[:, model:].astype(F32), axis=0)

        def dp_sum(keep, send):
            total = (keep.astype(F32) + dp_swap(send, 0).astype(F32)).astype(BF16)
            for bit in range(1, dp_bits):
                flag = (dp_at >> bit) & 1
                size = total.shape[0] // 2
                keep = lax.dynamic_slice_in_dim(total, flag * size, size, 0)
                send = lax.dynamic_slice_in_dim(total, (1 - flag) * size, size, 0)
                total = (keep.astype(F32) + dp_swap(send, bit).astype(F32)).astype(BF16)
            for bit in reversed(range(1, dp_bits)):
                total = pair_up((dp_at >> bit) & 1, total, dp_swap(total, bit))
            other = dp_swap(total, 0)
            first = jnp.where(row == 0, total, other).astype(F32)
            second = jnp.where(row == 0, other, total).astype(F32)
            return first, second

        mlp_in_grad, mlp_out_grad = dp_sum(dw_mlp[0], dw_mlp[1])
        flat = (2, 2 * width, model)
        dw_cross = dw_cross.reshape(flat)
        dw_self = dw_self.reshape(flat)
        cross_qk, cross_vo = dp_sum(dw_cross[0], dw_cross[1])
        self_qk, self_vo = dp_sum(dw_self[0], dw_self[1])
        return (
            mixed,
            token_grad,
            self_qk[:width].T,
            self_qk[width:].T,
            self_vo[:width].T,
            self_vo[width:],
            cross_qk[:width].T,
            cross_qk[width:].T,
            cross_vo[:width].T,
            cross_vo[width:],
            mlp_in_grad,
            mlp_out_grad,
            mod_weight_grad,
            mod_bias_grad,
        )

    rows = P("dp", None)
    by_col = P(None, "tensor")
    by_row = P("tensor", None)
    return jax.shard_map(
        local,
        mesh=mesh,
        in_specs=(
            rows, P("dp", None, None), P("dp"), P("dp"), P("dp"), by_col, by_col, by_col, by_row,
            by_col, by_col, by_col, by_row, by_col, by_row, by_col, P("tensor"), rows,
        ),
        out_specs=(
            rows, rows, by_col, by_col, by_col, by_row, by_col, by_col, by_col, by_row,
            by_col, by_row, by_col, P("tensor"),
        ),
        check_vma=False,
    )
```

```python
import functools
import math

import jax
import jax.numpy as jnp
from jax import lax
from jax.experimental import pallas as pl
from jax.experimental.pallas import tpu as pltpu
from jax.sharding import PartitionSpec as P

HEAD = 64
BLOCK = 256
EPSILON = 1e-06
MASKED = -1000000000.0
CURVE = math.sqrt(2.0 / math.pi)
CUBIC = 0.044715
F32 = jnp.float32
BF16 = jnp.bfloat16


def dot_nn(a, b):
    return lax.dot_general(a, b, (((1,), (0,)), ((), ())), preferred_element_type=F32)


def dot_nt(a, b):
    return lax.dot_general(a, b, (((1,), (1,)), ((), ())), preferred_element_type=F32)


def dot_tn(a, b):
    return lax.dot_general(a, b, (((0,), (0,)), ((), ())), preferred_element_type=F32)


def normalize(values):
    centered = values - jnp.mean(values, axis=-1, keepdims=True)
    inverse = lax.rsqrt(jnp.mean(centered * centered, axis=-1, keepdims=True) + EPSILON)
    return centered * inverse, inverse


def norm_back(grad, normed, inverse):
    first = jnp.mean(grad, axis=-1, keepdims=True)
    second = jnp.mean(grad * normed, axis=-1, keepdims=True)
    return inverse * (grad - first - normed * second)


def column_sum(values):
    return jnp.sum(values, axis=0, keepdims=True)


def three_parts(column):
    high = column.astype(BF16).astype(F32)
    rest = column - high
    middle = rest.astype(BF16).astype(F32)
    return high, middle, rest - middle


def head_slice(rows, head):
    piece = rows[:, head * HEAD : (head + 1) * HEAD]
    return jnp.concatenate([piece, jnp.zeros_like(piece)], axis=1)


class View:
    def __init__(self, ref):
        self.view = ref

    def ref(self):
        return self.view


def run(kernel, outs, scalars, arrays, late=(), scratch=(), cost=1.0, vmem=16):
    in_vmem = pl.BlockSpec(memory_space=pltpu.VMEM)
    pairs = [entry if isinstance(entry, tuple) else (entry, None) for entry in late]
    n_plain = len(arrays)

    def wrapped(place, *refs):
        views = []
        for ref, (_, block) in zip(refs[n_plain:], pairs):
            views.append(View(ref if block is None else ref.at[token_rows(block(place)), :]))
        kernel(place, *refs[:n_plain], *views, *refs[n_plain + len(pairs) :])

    return pl.pallas_call(
        wrapped,
        name=getattr(kernel, "__name__", "advance"),
        out_shape=[jax.ShapeDtypeStruct(shape, kind) for shape, kind in outs],
        in_specs=[pl.BlockSpec(memory_space=pltpu.SMEM)] + [in_vmem] * (n_plain + len(pairs)),
        out_specs=[in_vmem] * len(outs),
        scratch_shapes=[pltpu.VMEM(shape, kind) for shape, kind in scratch],
        compiler_params=pltpu.CompilerParams(vmem_limit_bytes=vmem * 1024 * 1024),
        cost_estimate=pl.CostEstimate(flops=int(cost * 1_000_000_000), bytes_accessed=1000, transcendentals=0),
    )(scalars, *arrays, *[array for array, _ in pairs])


SLOT, CORE, ROW, LIMIT, END = 0, 4, 5, 6, 10
ORDER = (0, 2, 1, 3)


def block_of(place, chunk):
    return place[CORE] * 2 + chunk


def mod_row(mod, slot, component, model):
    return mod[pl.ds(slot, 1), component * model : (component + 1) * model]


def token_rows(block):
    return pl.ds(pl.multiple_of(block * BLOCK, BLOCK), BLOCK)


def text_kernel(place, text, weights, packed):
    rows = text.shape[1]
    wide = weights.shape[0]
    for slot in range(text.shape[0]):
        first = rows * (slot % 2)
        left = wide * (slot // 2)
        packed[first : first + rows, left : left + wide] = dot_nt(text[slot], weights[...]).astype(BF16)


def unpack_kernel(place, q0, o0, q1, o1, q2, o2, q3, o3, t0, t1, t2, t3, cqt, co, kall, vall):
    width = q0.shape[0]
    rows = kall.shape[1]
    for index, (query, out) in enumerate(((q0, o0), (q1, o1), (q2, o2), (q3, o3))):
        cqt[index * width : (index + 1) * width, :] = query[...]
        co[index * width : (index + 1) * width, :] = out[...]
    for slot in range(kall.shape[0]):
        first = rows * (slot % 2)
        left = 2 * width * (slot // 2)
        both = [t[first : first + rows, left : left + 2 * width] for t in (t0, t1, t2, t3)]
        kall[slot] = jnp.concatenate([b[:, :width] for b in both], axis=1)
        vall[slot] = jnp.concatenate([b[:, width:] for b in both], axis=1)


def attend_chunk(place, chunk, qa_in, ka, va, wo, part_own, part_send, qa_out, att):
    heads = ka.shape[0]
    lane = lax.broadcasted_iota(jnp.int32, (BLOCK, 2 * HEAD), 1)
    spot = (lane >= HEAD + 4) & (lane < HEAD + 7)
    for side in range(2):
        at = (2 * chunk + side) * BLOCK
        here = slice(side * BLOCK, (side + 1) * BLOCK)
        pieces = []
        for head in range(heads):
            queries = qa_in[head, at : at + BLOCK, :]
            scores = dot_nt(queries, ka[head])
            top = jnp.max(scores, axis=1, keepdims=True)
            raised = jnp.exp(scores - top).astype(BF16)
            out = dot_nn(raised, va[head])
            total = out[:, HEAD : HEAD + 1]
            pieces.append(out[:, :HEAD] * (1.0 / total))
            high, middle, low = three_parts(-(top + jnp.log(total)))
            more = jnp.where(lane == HEAD + 4, high, jnp.where(lane == HEAD + 5, middle, low))
            qa_out[head, here, :] = jnp.where(spot, more, queries.astype(F32)).astype(BF16)
        attended = jnp.concatenate(pieces, axis=1).astype(BF16)
        att[here, :] = attended
        out = dot_nn(attended, wo[...]).astype(BF16)

        @pl.when(place[CORE] == side)
        def _():
            part_own[...] = out

        @pl.when(place[CORE] != side)
        def _():
            part_send[...] = out


def self_first(place, mod, weights, tokens, wo, part_own, part_send, qa, ka, va, qa_out, att, h1):
    model = mod.shape[1] // 9
    lane = lax.broadcasted_iota(jnp.int32, (BLOCK, 2 * HEAD), 1)
    keep = lane < HEAD
    width = weights.shape[0] // 3
    tokens = tokens.ref()
    for position, block in enumerate(ORDER):
        rows = slice(position * BLOCK, (position + 1) * BLOCK)
        slot = place[SLOT + block]
        normed, _ = normalize(tokens[block * BLOCK : (block + 1) * BLOCK, :].astype(F32))
        hidden = (normed * (1.0 + mod_row(mod, slot, 1, model)) + mod_row(mod, slot, 0, model)).astype(BF16)
        h1[rows, :] = hidden
        rows_qkv = dot_nt(hidden, weights[...])
        q = rows_qkv[:, :width].astype(BF16).astype(F32) * (HEAD**-0.5)
        k = rows_qkv[:, width : 2 * width]
        v = rows_qkv[:, 2 * width :]
        mine = lane == HEAD + slot
        q_more = jnp.where(mine, 1.0, 0.0)
        k_more = jnp.where((lane >= HEAD + 4) & (lane < HEAD + 7), 1.0, 0.0)
        k_more = jnp.where((lane >= HEAD) & (lane < HEAD + 4) & jnp.logical_not(mine), MASKED, k_more)
        v_more = jnp.where((lane >= HEAD) & (lane < HEAD + 3), 1.0, 0.0)
        for head in range(ka.shape[0]):
            qa[head, rows, :] = jnp.where(keep, head_slice(q, head), q_more).astype(BF16)
            ka[head, rows, :] = jnp.where(keep, head_slice(k, head), k_more).astype(BF16)
            va[head, rows, :] = jnp.where(keep, head_slice(v, head), v_more).astype(BF16)
    attend_chunk(place, 0, qa, ka, va, wo.ref(), part_own, part_send, qa_out, att)


def self_second(place, qa, ka, va, wo, part_own, part_send, qa_out, att):
    attend_chunk(place, 1, qa, ka, va, wo.ref(), part_own, part_send, qa_out, att)


def quad_stack(rows, masks):
    return jnp.concatenate([rows * mask for mask in masks], axis=0)


def quad_masks():
    lane = lax.broadcasted_iota(jnp.int32, (1, 4 * HEAD), 1)
    return [jnp.where((lane >= u * HEAD) & (lane < (u + 1) * HEAD), 1.0, 0.0) for u in range(4)]


def quad_probs(scores, limit, text_rows):
    key_row = lax.broadcasted_iota(jnp.int32, (text_rows, 1), 0)
    bias = jnp.where(key_row < limit, 0.0, MASKED)
    probs = []
    for u in range(4):
        part = scores[u * text_rows : (u + 1) * text_rows, :] + bias
        raised = jnp.exp(part - jnp.max(part, axis=0, keepdims=True))
        probs.append(raised * (1.0 / jnp.sum(raised, axis=0, keepdims=True)))
    return probs


def middle_chunk(
    place, chunk, mod, sum_own, sum_far, cqt, co, kall, vall, tokens, cot, win0, wout0, win1, wout1, b3_before,
    h3g_out, h3_out, act0, act1, pg0, pg1, b3g_out, x1_out, b2_out, h2_out, q2_out, cr_out, b3_out,
):
    model = cqt.shape[1]
    text_rows = kall.shape[1]
    slot = place[SLOT + block_of(place, chunk)]

    def m(component):
        return mod_row(mod, slot, component, model)

    x1 = tokens.ref()[...].astype(F32) + m(2) * (sum_own[...].astype(F32) + sum_far[...].astype(F32))
    x1_out[...] = x1
    normed, _ = normalize(x1)
    h2 = (normed * (1.0 + m(4)) + m(3)).astype(BF16)
    h2_out[...] = h2
    q2 = (dot_nt(h2, cqt[...]).astype(BF16).astype(F32) * (HEAD**-0.5)).astype(BF16)
    q2_out[...] = q2
    masks = [mask.astype(BF16) for mask in quad_masks()]
    crossed = []
    for quad in range(model // (4 * HEAD)):
        cols = slice(quad * 4 * HEAD, (quad + 1) * 4 * HEAD)
        scores = dot_nt(quad_stack(kall[slot, :, cols], masks), q2[:, cols])
        probs = jnp.concatenate(quad_probs(scores, place[LIMIT + slot], text_rows), axis=0)
        crossed.append(dot_tn(probs.astype(BF16), quad_stack(vall[slot, :, cols], masks)).astype(BF16))
    crossed = jnp.concatenate(crossed, axis=1)
    cr_out[...] = crossed
    b2 = dot_nn(crossed, co[...])
    b2_out[...] = b2
    normed, _ = normalize(x1 + m(5) * b2)
    h3 = (normed * (1.0 + m(7)) + m(6)).astype(BF16)
    h3_out[...] = h3
    b3g = (cot.ref()[...].astype(F32) * m(8)).astype(BF16)
    b3g_out[...] = b3g
    b3 = h3g = None
    for win, wout, act_out, pg_out in ((win0, wout0, act0, pg0), (win1, wout1, act1, pg1)):
        win, wout = win.ref(), wout.ref()
        pre = dot_nn(h3, win[...])
        square = pre * pre
        bent = jnp.tanh(CURVE * (pre + CUBIC * (square * pre)))
        act = (0.5 * pre * (1.0 + bent)).astype(BF16)
        act_out[...] = act
        slope = 0.5 * (1.0 + bent) + 0.5 * pre * (1.0 - bent * bent) * (CURVE * (1.0 + 3.0 * CUBIC * square))
        b3_half = dot_nn(act, wout[...])
        pg = (dot_nt(b3g, wout[...]) * slope).astype(BF16)
        pg_out[...] = pg
        h3g_half = dot_nt(pg, win[...])
        b3 = b3_half if b3 is None else b3 + b3_half
        h3g = h3g_half if h3g is None else h3g + h3g_half
    b3_out[chunk * BLOCK : (chunk + 1) * BLOCK, :] = b3.astype(BF16)
    if chunk:
        b3_out[0:BLOCK, :] = b3_before.ref()[...]
    h3g_out[...] = h3g.astype(BF16)


def middle_first(place, *refs):
    middle_chunk(place, 0, *refs[:13], None, *refs[13:])


def middle_second(place, *refs):
    middle_chunk(place, 1, *refs)


def stacked(first, second):
    return jnp.concatenate([first[...], second[...]], axis=0)


def mlp_back(
    place, h3a, h3b, pg0a, pg0b, pg1a, pg1b, act0a, act0b, act1a, act1b, b3ga, b3gb,
    in_own, in_send, out_own, out_send,
):
    half = in_own.shape[1]
    grads = (stacked(pg0a, pg0b), stacked(pg1a, pg1b))
    for part in range(2):
        cols = slice(part * half, (part + 1) * half)
        rows = jnp.concatenate([h3a[:, cols], h3b[:, cols]], axis=0)
        for out, grad in ((in_send, grads[1]), (in_own, grads[0])):
            out[part ^ place[ROW]] = dot_tn(rows, grad).astype(BF16)
    grad = stacked(b3ga, b3gb)
    for out, first, second in ((out_send, act1a, act1b), (out_own, act0a, act0b)):
        for part in range(2):
            cols = slice(part * half, (part + 1) * half)
            rows = jnp.concatenate([first[:, cols], second[:, cols]], axis=0)
            out[part ^ place[ROW]] = dot_tn(rows, grad).astype(BF16)


def cross_chunk(
    place, chunk, mod, h3g_own, h3g_far, kall, vall, cqt, co, x1_in, b2_in, cot, q2_in, sum_own, sum_far,
    b1g_out, dq_out, b2g_out, dk_out, dv_out, sums, x1g_out,
):
    model = cqt.shape[1]
    text_rows = kall.shape[1]
    slot = place[SLOT + block_of(place, chunk)]

    def m(component):
        return mod_row(mod, slot, component, model)

    x1 = x1_in.ref()[...]
    b2 = b2_in.ref()[...]
    h3g = h3g_own[...].astype(F32) + h3g_far[...].astype(F32)
    normed, inverse = normalize(x1 + m(5) * b2)
    sums[4:5, :] = column_sum(h3g)
    sums[5:6, :] = column_sum(h3g * normed)
    x2g = cot.ref()[...].astype(F32) + norm_back(h3g * (1.0 + m(7)), normed, inverse)
    sums[3:4, :] = column_sum(x2g * b2)
    b2g = (x2g * m(5)).astype(BF16)
    b2g_out[...] = b2g
    out_grad = dot_nt(b2g, co[...]).astype(BF16)
    masks = quad_masks()
    low = [mask.astype(BF16) for mask in masks]
    query_grads = []
    for quad in range(model // (4 * HEAD)):
        cols = slice(quad * 4 * HEAD, (quad + 1) * 4 * HEAD)
        queries = q2_in.ref()[:, cols]
        grads = out_grad[:, cols]
        keys = quad_stack(kall[slot, :, cols], low)
        values = quad_stack(vall[slot, :, cols], low)
        probs = quad_probs(dot_nt(keys, queries), place[LIMIT + slot], text_rows)
        prob_grad = dot_nt(values, grads)
        score_grad = []
        for u in range(4):
            part = prob_grad[u * text_rows : (u + 1) * text_rows, :]
            row_dot = jnp.sum(probs[u] * part, axis=0, keepdims=True)
            score_grad.append((probs[u] * (part - row_dot)).astype(BF16))
        score_grad = jnp.concatenate(score_grad, axis=0)
        dv = dot_nn(jnp.concatenate(probs, axis=0).astype(BF16), grads)
        dk = dot_nn(score_grad, queries)
        query_grads.append((dot_tn(score_grad, keys) * (HEAD**-0.5)).astype(BF16))
        for wide, out in ((dk, dk_out), (dv, dv_out)):
            total = None
            for u in range(4):
                part = wide[u * text_rows : (u + 1) * text_rows, :] * masks[u]
                total = part if total is None else total + part
            out[:, cols] = total.astype(BF16)
    query_grad = jnp.concatenate(query_grads, axis=1)
    dq_out[...] = query_grad
    h2g = dot_nn(query_grad, cqt[...])
    normed, inverse = normalize(x1)
    sums[1:2, :] = column_sum(h2g)
    sums[2:3, :] = column_sum(h2g * normed)
    x1g = x2g + norm_back(h2g * (1.0 + m(4)), normed, inverse)
    x1g_out[...] = x1g
    branch = sum_own.ref()[...].astype(F32) + sum_far.ref()[...].astype(F32)
    sums[0:1, :] = column_sum(x1g * branch)
    sums[6:8, :] = jnp.zeros((2, model), F32)
    b1g_out[...] = (x1g * m(2)).astype(BF16)


def cross_first(place, *refs):
    cross_chunk(place, 0, *refs)


def cross_second(place, *refs):
    cross_chunk(place, 1, *refs)


def cross_weights(
    place, dqa, dqb, b2ga, b2gb, dka, dkb, dva, dvb, h2a, h2b, cra, crb, text, own, send,
):
    width = own.shape[1] // 2
    row = place[ROW]
    h2a, h2b, cra, crb, text = h2a.ref(), h2b.ref(), cra.ref(), crb.ref(), text.ref()
    hidden = stacked(h2a, h2b)
    grads = stacked(b2ga, b2gb)
    texts = [text[place[SLOT + block_of(place, chunk)]] for chunk in range(2)]
    for member, out in ((1, send), (0, own)):
        start = (member * width // 128) * 128
        skip = member * width - start
        cols = slice(start, start + 2 * 128)
        kept = slice(skip, skip + width)

        def two(first, second):
            return jnp.concatenate([first[:, cols], second[:, cols]], axis=0)

        top, bottom = slice(0, width), slice(width, 2 * width)
        out[row, top] = dot_tn(two(dqa, dqb), hidden)[kept].astype(BF16)
        out[row, bottom] = (dot_tn(dka[:, cols], texts[0]) + dot_tn(dkb[:, cols], texts[1]))[kept].astype(BF16)
        out[1 - row, top] = (dot_tn(dva[:, cols], texts[0]) + dot_tn(dvb[:, cols], texts[1]))[kept].astype(BF16)
        out[1 - row, bottom] = dot_tn(two(cra, crb), grads)[kept].astype(BF16)


def keys_back(block, first, qa, ka, va, da, dq_sum):
    rows = token_rows(block)
    dks = []
    dvs = []
    for head in range(ka.shape[0]):
        keys = ka[head, rows, :]
        probs = jnp.exp(dot_nt(keys, qa[head]))
        prob_grad = dot_nt(va[head, rows, :], da[head])
        score_grad = (probs * prob_grad).astype(BF16)
        dvs.append(dot_nn(probs.astype(BF16), da[head])[:, :HEAD])
        dks.append(dot_nn(score_grad, qa[head])[:, :HEAD])
        dq = dot_tn(score_grad, keys)
        dq_sum[head] = dq if first else dq_sum[head] + dq
    return jnp.concatenate(dks, axis=1).astype(BF16), jnp.concatenate(dvs, axis=1).astype(BF16)


def self_back_first(
    place, b1g_a, b1g_b, far_a, far_b, wo, att_a, att_b, qa_a, qa_b, ka, va,
    b1g, att, qa, da, dq_sum, dk_all, dv_all,
):
    blocks = b1g.shape[0] // BLOCK
    heads = da.shape[0]
    core = place[CORE]
    for chunk, (own, far) in enumerate(((b1g_a, far_a), (b1g_b, far_b))):
        b1g[token_rows(2 * chunk + core), :] = own[...]
        b1g[token_rows(2 * chunk + 1 - core), :] = far[...]
    wo = wo.ref()
    att[0 : 2 * BLOCK, :] = att_a.ref()[...]
    att[2 * BLOCK : 4 * BLOCK, :] = att_b.ref()[...]
    lane = lax.broadcasted_iota(jnp.int32, (BLOCK, 2 * HEAD), 1)
    for block in range(blocks):
        rows = slice(block * BLOCK, (block + 1) * BLOCK)
        grads = dot_nt(b1g[rows, :], wo[...]).astype(BF16).astype(F32)
        dots = grads * att[rows, :].astype(F32)
        for head in range(heads):
            row_dot = jnp.sum(dots[:, head * HEAD : (head + 1) * HEAD], axis=1, keepdims=True)
            high, middle, low = three_parts(-row_dot)
            more = jnp.where(lane == HEAD, high, jnp.where(lane == HEAD + 1, middle, low))
            more = jnp.where(lane < HEAD + 3, more, 0.0)
            da[head, rows, :] = jnp.where(lane < HEAD, head_slice(grads, head), more).astype(BF16)
    qa[:, 0 : 2 * BLOCK, :] = qa_a.ref()[...]
    qa[:, 2 * BLOCK : 4 * BLOCK, :] = qa_b.ref()[...]
    ka, va = ka.ref(), va.ref()
    for block in range(2):
        rows = slice(block * BLOCK, (block + 1) * BLOCK)
        dk_all[rows, :], dv_all[rows, :] = keys_back(block, block == 0, qa, ka, va, da, dq_sum)


def self_back_second(
    place, b1g, att, qa, da, dq_in, dk_in, dv_in, weights, ka, va, h1,
    part_own, part_send, dw_keep, dw_give,
    dq_sum, grad_all,
):
    blocks = b1g.shape[0] // BLOCK
    heads = da.shape[0]
    core = place[CORE]
    width = heads * HEAD
    ka, va = ka.ref(), va.ref()
    dq_sum[...] = dq_in[...]
    grad_all[0 : 2 * BLOCK, width : 2 * width] = dk_in[0 : 2 * BLOCK, :]
    grad_all[0 : 2 * BLOCK, 2 * width : 3 * width] = dv_in[0 : 2 * BLOCK, :]
    for block in range(2, blocks):
        rows = slice(block * BLOCK, (block + 1) * BLOCK)
        dk, dv = keys_back(block, False, qa, ka, va, da, dq_sum)
        grad_all[rows, width : 2 * width] = dk
        grad_all[rows, 2 * width : 3 * width] = dv
    h1 = h1.ref()
    for block in range(blocks):
        rows = slice(block * BLOCK, (block + 1) * BLOCK)
        dq = jnp.concatenate([dq_sum[head, rows, :HEAD] for head in range(heads)], axis=1)
        grad_all[rows, 0:width] = (dq * (HEAD**-0.5)).astype(BF16)
        out = dot_nn(grad_all[rows, :], weights[...]).astype(BF16)
        chunk, side = block // 2, block % 2
        out_rows = slice(chunk * BLOCK, (chunk + 1) * BLOCK)

        @pl.when(core == side)
        def _():
            part_own[out_rows, :] = out

        @pl.when(core != side)
        def _():
            part_send[out_rows, :] = out

    grads = dot_tn(grad_all[...], h1[...]).astype(BF16)
    query_key = (grads[:width], grads[width : 2 * width])
    value_out = (grads[2 * width :], dot_tn(att[...], b1g[...]).astype(BF16))
    for flag, first, second in ((0, query_key, value_out), (1, value_out, query_key)):

        @pl.when(place[ROW] == flag)
        def _():
            for index in range(2):
                rows = slice(index * width, (index + 1) * width)
                dw_keep[rows, :] = first[index]
                dw_give[rows, :] = second[index]


def mixed_kernel(place, mod, b3_own, b3_far, cot_a, cot_b, x1a, x1b, b2a, b2b, mixed, sums):
    model = mixed.shape[1]
    for chunk, (x1, b2, cot) in enumerate(((x1a, b2a, cot_a), (x1b, b2b, cot_b))):
        rows = slice(chunk * BLOCK, (chunk + 1) * BLOCK)
        block = block_of(place, chunk)
        slot = place[SLOT + block]
        b3 = b3_own[rows, :].astype(F32) + b3_far[rows, :].astype(F32)
        out = x1.ref()[...] + mod_row(mod, slot, 5, model) * b2.ref()[...] + mod_row(mod, slot, 8, model) * b3
        mixed[rows, :] = out.astype(BF16)
        sums[chunk] = column_sum(cot.ref()[...].astype(F32) * b3)


def final_kernel(
    place, mod, h1g_own, h1g_far, sums_a, sums_b, sums_mixed, tokens_a, tokens_b, x1ga, x1gb, token_grad, slot_sums,
):
    model = token_grad.shape[1]
    slot_sums[...] = jnp.zeros_like(slot_sums)
    for chunk, (x1g, sums, tokens) in enumerate(((x1ga, sums_a, tokens_a), (x1gb, sums_b, tokens_b))):
        rows = slice(chunk * BLOCK, (chunk + 1) * BLOCK)
        block = block_of(place, chunk)
        slot = place[SLOT + block]
        h1g = h1g_own[rows, :].astype(F32) + h1g_far[rows, :].astype(F32)
        normed, inverse = normalize(tokens.ref()[...].astype(F32))
        scaled = h1g * (1.0 + mod_row(mod, slot, 1, model))
        token_grad[rows, :] = (x1g.ref()[...] + norm_back(scaled, normed, inverse)).astype(BF16)
        terms = [column_sum(h1g), column_sum(h1g * normed)]
        terms += [sums[i : i + 1, :] for i in range(6)] + [sums_mixed[chunk]]
        for component, term in enumerate(terms):
            slot_sums[pl.ds(slot, 1), component * model : (component + 1) * model] += term


def advance_kernel(roles, place, *refs):
    refs = list(refs)
    values, got = {}, {}
    for role in roles:
        values[role] = refs.pop(0)
    for name in ("row", "column", "middle"):
        if any(role in roles for role in {"row": "a", "column": "bd", "middle": "c"}[name]):
            got[name] = refs.pop(0)
    outs = {role: refs.pop(0) for role in roles}
    end = place[END]
    if "a" in roles:
        outs["a"][...] = added(values["a"][...], got["row"][...])
    if "c" in roles:

        @pl.when(end == 0)
        def _():
            outs["c"][...] = added(values["c"][...], got["middle"][...])

        @pl.when(end != 0)
        def _():
            outs["c"][...] = values["c"][...]

    if "b" in roles:

        @pl.when(end == 0)
        def _():
            outs["b"][...] = added(values["b"][...], got["column"][...])

        @pl.when(end != 0)
        def _():
            outs["b"][...] = values["b"][...]

    if "d" in roles:

        @pl.when(end == 0)
        def _():
            outs["d"][...] = values["d"][...]

        @pl.when(end != 0)
        def _():
            outs["d"][...] = got["column"][...]

    if refs:

        @pl.when(end == 0)
        def _():
            refs[0][...] = outs["c"][...]

        @pl.when(end != 0)
        def _():
            refs[0][...] = outs["a"][...]


def added(first, second):
    return (first.astype(F32) + second.astype(F32)).astype(BF16)


def solution(mesh):
    n_dp = mesh.shape["dp"]
    n_tensor = mesh.shape["tensor"]
    n_col = n_dp // 2
    dp_bits = int(math.log2(n_dp))

    def tensor_swap(value, flip):
        return lax.ppermute(value, "tensor", [(i, i ^ flip) for i in range(n_tensor)])

    def core_swap(value):
        return tensor_swap(value, 1)

    def far_swap(value):
        return tensor_swap(value, 2)

    def dp_swap(value, flip):
        return lax.ppermute(value, "dp", [(i, i ^ flip) for i in range(n_dp)])

    def tie(*values):
        return lax.optimization_barrier(values) if values else ()

    def pair_up(flag, mine, other):
        return jnp.concatenate([jnp.where(flag == 0, mine, other), jnp.where(flag == 0, other, mine)], axis=0)

    def local(
        tokens, text_states, clip_len, text_len, timesteps, q_weight, k_weight, v_weight, o_weight,
        cross_q, cross_k, cross_v, cross_o, mlp_in, mlp_out, mod_weight, mod_bias, cotangent,
    ):
        count, model = tokens.shape
        slots, text_rows = text_states.shape[:2]
        width = o_weight.shape[0]
        heads = width // HEAD
        half = count // 2
        text_pad = -(-text_rows // 16) * 16
        tensor_at = lax.axis_index("tensor")
        dp_at = lax.axis_index("dp")
        core = tensor_at & 1
        row = dp_at & 1
        column = dp_at >> 1

        ends = jnp.cumsum(clip_len)
        starts = jnp.arange(count // BLOCK, dtype=jnp.int32) * BLOCK
        slot_of = jnp.sum((starts[:, None] >= ends[None, :]).astype(jnp.int32), axis=1)
        end = (column == 0) | (column == n_col - 1)
        place = jnp.concatenate([slot_of, core[None], row[None], text_len, end[None].astype(jnp.int32)])
        place = place.astype(jnp.int32)

        query_own = cross_q.T
        query_far, out_far = far_swap(query_own), far_swap(cross_o)
        text_weights = jnp.concatenate([cross_k.T, cross_v.T], axis=0)
        text = jnp.pad(text_states, ((0, 0), (0, text_pad - text_rows), (0, 0)))
        self_weights = jnp.concatenate([q_weight.T, k_weight.T, v_weight.T], axis=0)

        half_width = model // 2
        ramp = jnp.arange(half_width).astype(F32)
        frequency = jnp.exp(ramp * (-math.log(10000.0) / half_width))
        angles = timesteps.astype(F32)[:, None] * frequency[None, :]
        embed = jnp.concatenate([jnp.cos(angles), jnp.sin(angles)], axis=1)
        silu_low = jax.nn.silu(embed).astype(BF16)
        mod_own = dot_nn(silu_low, mod_weight) + mod_bias.astype(F32)
        mod_far = [tensor_swap(mod_own, flip) for flip in range(1, n_tensor)]
        (text_own,) = run(text_kernel, [((2 * text_pad, model), BF16)], place, [text, text_weights])
        text_own, self_weights, *mod_far = tie(text_own, self_weights, *mod_far)
        text_far = far_swap(text_own)
        mod_all = jnp.stack([mod_own] + mod_far)
        mod = jnp.concatenate(
            [lax.dynamic_index_in_dim(mod_all, tensor_at ^ j, 0, keepdims=False) for j in range(n_tensor)], axis=1
        )

        wide = (heads, count, 2 * HEAD)
        block_wide = (heads, 2 * BLOCK, 2 * HEAD)
        one = ((BLOCK, model), BF16)
        one_f32 = ((BLOCK, model), F32)
        attend_far = [(block_wide, BF16), ((2 * BLOCK, width), BF16)]
        own_a, send_a, qa, ka, va, qa_a, att_a, h1 = run(
            self_first, [one, one] + [(wide, BF16)] * 3 + attend_far + [((count, model), BF16)], place, [mod, self_weights], cost=0.001,
            late=[tokens, o_weight],
        )
        send_a, query_far, out_far, text_far = tie(send_a, query_far, out_far, text_far)
        query1, out1, text1 = core_swap(query_own), core_swap(cross_o), core_swap(text_own)
        send_far_a = core_swap(send_a)
        send_far_a, query1, out1, text1 = tie(send_far_a, query1, out1, text1)
        query3, out3, text3 = core_swap(query_far), core_swap(out_far), core_swap(text_far)
        sum_a = added(own_a, send_far_a)
        sum_a, qa, query3, out3, text3 = tie(sum_a, qa, query3, out3, text3)
        far_a = far_swap(sum_a)
        win1, wout1 = core_swap(mlp_in), core_swap(mlp_out)
        own_b, send_b, qa_b, att_b = run(
            self_second, [one, one] + attend_far, place, [qa, ka, va], late=[o_weight], cost=0.001
        )
        cqt, co, kall, vall = run(
            unpack_kernel, [((model, model), BF16)] * 2 + [((slots, text_pad, model), BF16)] * 2,
            place, [query_own, cross_o, query1, out1, query_far, out_far, query3, out3, text_own, text1, text_far, text3],
            cost=0.001,
        )
        send_b, cqt, far_a, win1, wout1 = tie(send_b, cqt, far_a, win1, wout1)
        sum_b = added(own_b, core_swap(send_b))
        sum_b, far_a = tie(sum_b, far_a)
        far_b = far_swap(sum_b)
        shared = [cqt, co, kall, vall]

        def chunk_rows(array, chunk):
            return (array, functools.partial(block_of, chunk=chunk))

        def middle(kernel, chunk, own, far, *before):
            return run(
                kernel, [one] * 7 + [one_f32, one_f32] + [one] * 3 + [(((chunk + 1) * BLOCK, model), BF16)], place,
                [mod, own, far] + shared, cost=7.5,
                late=[chunk_rows(tokens, chunk), chunk_rows(cotangent, chunk), mlp_in, mlp_out, win1, wout1, *before],
            )

        h3ga, h3a, act0a, act1a, pg0a, pg1a, b3ga, x1a, b2a, h2a, q2a, cra, b3a = middle(middle_first, 0, sum_a, far_a)
        h3ga, far_b = tie(h3ga, far_b)
        h3g_far_a = far_swap(h3ga)
        h3gb, h3b, act0b, act1b, pg0b, pg1b, b3gb, x1b, b2b, h2b, q2b, crb, b3 = middle(middle_second, 1, sum_b, far_b, b3a)
        h3gb, pg0b, h3g_far_a = tie(h3gb, pg0b, h3g_far_a)
        h3g_far_b = far_swap(h3gb)

        in_own, in_send, out_own, out_send = run(
            mlp_back, [((2, model // 2, model), BF16)] * 4, place,
            [h3a, h3b, pg0a, pg0b, pg1a, pg1b, act0a, act0b, act1a, act1b, b3ga, b3gb], cost=0.001,
        )

        def cross(kernel, chunk, h3g_own, h3g_far, x1, b2, own, far, q2):
            return run(
                kernel, [one] * 3 + [((text_pad, model), BF16)] * 2 + [((8, model), F32), one_f32], place,
                [mod, h3g_own, h3g_far, kall, vall, cqt, co],
                late=[x1, b2, chunk_rows(cotangent, chunk), q2, own, far], cost=4.0 if chunk else 0.001,
            )

        b1g_a, dqa, b2ga, dka, dva, sums_a, x1ga = cross(
            cross_first, 0, h3ga, h3g_far_a, x1a, b2a, sum_a, far_a, q2a
        )
        in_send, out_send, b1g_a, h3g_far_b = tie(in_send, out_send, b1g_a, h3g_far_b)
        in_got, out_got, b1g_far_a = core_swap(in_send), core_swap(out_send), core_swap(b1g_a)
        b1g_b, dqb, b2gb, dkb, dvb, sums_b, x1gb = cross(
            cross_second, 1, h3gb, h3g_far_b, x1b, b2b, sum_b, far_b, q2b
        )
        in_got, out_got, b1g_far_a, b1g_b, dqb = tie(in_got, out_got, b1g_far_a, b1g_b, dqb)
        in_keep, in_give = added(in_own[0], in_got[0]), added(in_own[1], in_got[1])
        out_keep, out_give = added(out_own[0], out_got[0]), added(out_own[1], out_got[1])

        across = [(i, i ^ 1) for i in range(n_dp)]
        neighbours = [(i, i ^ 2) for i in range(n_dp)]
        middle_pair = [(2 * a + r, 2 * b + r) for a, b in ((1, 2), (2, 1)) for r in range(2)]
        chain_rows = (model // 2, model)

        class Rounds:
            def __init__(self):
                self.values, self.column_send, self.results, self.waiting = {}, None, [], []

            def start(self, *chain):
                self.got = {}
                if n_col != 4:
                    self.waiting += [chain] if chain else []
                    return
                if chain:
                    self.values["a"] = chain[0]
                    self.got["row"] = lax.ppermute(chain[1], "dp", across)
                if "e" in self.values:
                    self.got["last"] = lax.ppermute(self.values["e"], "dp", across)
                if "b" in self.values or "d" in self.values:
                    self.got["column"] = lax.ppermute(self.column_send, "dp", neighbours)
                if "c" in self.values:
                    self.got["middle"] = lax.ppermute(self.values["c"], "dp", middle_pair)

            def finish(self, *others):
                if "last" in self.got:
                    self.results.append(tie(self.values.pop("e"), self.got.pop("last")))
                roles = "".join(role for role in "abcd" if role in self.values)
                if not roles:
                    return tie(*others)
                operands = [self.values[role] for role in roles]
                operands += [self.got[name] for name in ("row", "column", "middle") if name in self.got]
                sends = "a" in roles or "c" in roles
                both = "a" in roles and "c" in roles
                outs = run(
                    functools.partial(advance_kernel, roles), [(chain_rows, BF16)] * (len(roles) + both),
                    place, operands, cost=0.3,
                )
                done = tie(*outs, *others)
                stepped = dict(zip(roles, done))
                if sends:
                    self.column_send = done[len(roles)] if both else stepped["a" if "a" in roles else "c"]
                self.values = {{"a": "b", "b": "c", "c": "d", "d": "e"}[role]: v for role, v in stepped.items()}
                return done[len(outs) :]

            def totals(self):
                if n_col != 4:
                    self.results += [self.slowly(*chain) for chain in self.waiting]
                    self.waiting = []
                return [
                    (jnp.where(row == 0, mine, other).astype(F32), jnp.where(row == 0, other, mine).astype(F32))
                    for mine, other in self.results
                ]

            def slowly(self, keep, give):
                total = added(keep, lax.ppermute(give, "dp", across))
                for bit in range(1, dp_bits):
                    size, flag = total.shape[0] // 2, (dp_at >> bit) & 1
                    sent = lax.dynamic_slice_in_dim(total, (1 - flag) * size, size, 0)
                    total = added(lax.dynamic_slice_in_dim(total, flag * size, size, 0), dp_swap(sent, 1 << bit))
                for bit in reversed(range(1, dp_bits)):
                    total = pair_up((dp_at >> bit) & 1, total, dp_swap(total, 1 << bit))
                return total, lax.ppermute(total, "dp", across)

        rounds = Rounds()

        rounds.start(in_keep, in_give)
        b1g_far_b = core_swap(b1g_b)
        cross_dw, cross_send = run(
            cross_weights, [((2, 2 * width, model), BF16)] * 2, place,
            [dqa, dqb, b2ga, b2gb, dka, dkb, dva, dvb], late=[h2a, h2b, cra, crb, text], cost=0.001,
        )
        b1g_far_b, cross_send = tie(b1g_far_b, cross_send)
        b1g_all, att_all, qa_all, da, dq_sum, dk_all, dv_all = run(
            self_back_first,
            [((count, model), BF16), ((count, width), BF16), (wide, BF16), (wide, BF16), (wide, F32)]
            + [((count, width), BF16)] * 2,
            place, [b1g_a, b1g_b, b1g_far_a, b1g_far_b],
            late=[o_weight, att_a, att_b, qa_a, qa_b, ka, va], cost=0.001,
        )
        b1g_all, cross_send, out_give, b3 = rounds.finish(b1g_all, cross_send, out_give, b3)

        rounds.start(out_keep, out_give)
        cross_got = core_swap(cross_send)
        b3_far = far_swap(b3)
        grad_own, grad_send, self_keep, self_give = run(
            self_back_second,
            [((half, model), BF16)] * 2 + [((2 * width, model), BF16)] * 2, place,
            [b1g_all, att_all, qa_all, da, dq_sum, dk_all, dv_all, self_weights], late=[ka, va, h1],
            scratch=[(wide, F32), ((count, 3 * width), BF16)], cost=10.0,
        )
        cross_keep, cross_give = added(cross_dw[0], cross_got[0]), added(cross_dw[1], cross_got[1])
        grad_send, cross_give, self_give = rounds.finish(grad_send, cross_give, self_give)

        rounds.start(cross_keep, cross_give)
        h1g_own = added(grad_own, core_swap(grad_send))
        h1g_far = far_swap(h1g_own)
        mixed, sums_mixed = run(
            mixed_kernel, [((half, model), BF16), ((2, 1, model), F32)],
            place, [mod, b3, b3_far],
            late=[chunk_rows(cotangent, 0), chunk_rows(cotangent, 1), x1a, x1b, b2a, b2b],
        )
        self_give, h1g_own, mixed = rounds.finish(self_give, h1g_own, mixed)

        rounds.start(self_keep, self_give)
        mixed_far = core_swap(mixed)
        token_grad, slot_sums = run(
            final_kernel, [((half, model), BF16), ((slots, 9 * model), F32)],
            place, [mod, h1g_own, h1g_far, sums_a, sums_b, sums_mixed],
            late=[chunk_rows(tokens, 0), chunk_rows(tokens, 1), x1ga, x1gb],
        )
        token_far = core_swap(token_grad)
        slot_sums = slot_sums + core_swap(slot_sums)
        local_cols = mod_weight.shape[1]
        slot_grad = lax.dynamic_slice_in_dim(slot_sums, tensor_at * local_cols, local_cols, 1).astype(BF16)
        gathered = jnp.concatenate([silu_low, slot_grad], axis=1)
        gathered, mixed_far, token_far = rounds.finish(gathered, mixed_far, token_far)

        for bit in range(dp_bits):
            if bit < 3:
                rounds.start()
            got = dp_swap(gathered, 1 << bit)
            gathered = jnp.concatenate([gathered, got], axis=0)
            if bit == 0:
                mixed = pair_up(core, mixed, mixed_far)
                gathered, mixed = rounds.finish(gathered, mixed)
            elif bit == 1:
                token_grad = pair_up(core, token_grad, token_far)
                gathered, token_grad = rounds.finish(gathered, token_grad)
            elif bit == 2:
                (gathered,) = rounds.finish(gathered)

        rounds.start()
        mod_weight_grad = dot_tn(gathered[:, :model], gathered[:, model:])
        mod_bias_grad = jnp.sum(gathered[:, model:].astype(F32), axis=0)
        early = rounds.totals()
        early, mod_weight_grad = tie(early, mod_weight_grad)
        rounds.finish()
        (self_qk, self_vo) = rounds.totals()[-1]
        mlp_in_grad, mlp_out_grad, (cross_qk, cross_vo) = early[:3]
        mlp_in_grad = jnp.concatenate(mlp_in_grad, axis=0)
        mlp_out_grad = jnp.concatenate(mlp_out_grad, axis=0)

        return (
            mixed,
            token_grad,
            self_qk[:width].T,
            self_qk[width:].T,
            self_vo[:width].T,
            self_vo[width:],
            cross_qk[:width].T,
            cross_qk[width:].T,
            cross_vo[:width].T,
            cross_vo[width:],
            mlp_in_grad,
            mlp_out_grad,
            mod_weight_grad,
            mod_bias_grad,
        )

    rows = P("dp", None)
    by_col = P(None, "tensor")
    by_row = P("tensor", None)
    return jax.shard_map(
        local,
        mesh=mesh,
        in_specs=(
            rows, P("dp", None, None), P("dp"), P("dp"), P("dp"), by_col, by_col, by_col, by_row,
            by_col, by_col, by_col, by_row, by_col, by_row, by_col, P("tensor"), rows,
        ),
        out_specs=(
            rows, rows, by_col, by_col, by_col, by_row, by_col, by_col, by_col, by_row,
            by_col, by_row, by_col, P("tensor"),
        ),
        check_vma=False,
    )
```

```python
import functools
import math

import jax
import jax.numpy as jnp
from jax import lax
from jax.experimental import pallas as pl
from jax.experimental.pallas import tpu as pltpu
from jax.sharding import PartitionSpec as P

HEAD = 64
BLOCK = 256
EPSILON = 1e-06
MASKED = -1000000000.0
CURVE = math.sqrt(2.0 / math.pi)
CUBIC = 0.044715
F32 = jnp.float32
BF16 = jnp.bfloat16


def dot_nn(a, b):
    return lax.dot_general(a, b, (((1,), (0,)), ((), ())), preferred_element_type=F32)


def dot_nt(a, b):
    return lax.dot_general(a, b, (((1,), (1,)), ((), ())), preferred_element_type=F32)


def dot_tn(a, b):
    return lax.dot_general(a, b, (((0,), (0,)), ((), ())), preferred_element_type=F32)


def normalize(values):
    centered = values - jnp.mean(values, axis=-1, keepdims=True)
    inverse = lax.rsqrt(jnp.mean(centered * centered, axis=-1, keepdims=True) + EPSILON)
    return centered * inverse, inverse


def norm_back(grad, normed, inverse):
    first = jnp.mean(grad, axis=-1, keepdims=True)
    second = jnp.mean(grad * normed, axis=-1, keepdims=True)
    return inverse * (grad - first - normed * second)


def column_sum(values):
    return jnp.sum(values, axis=0, keepdims=True)


def three_parts(column):
    high = column.astype(BF16).astype(F32)
    rest = column - high
    middle = rest.astype(BF16).astype(F32)
    return high, middle, rest - middle


def head_slice(rows, head):
    piece = rows[:, head * HEAD : (head + 1) * HEAD]
    return jnp.concatenate([piece, jnp.zeros_like(piece)], axis=1)


class View:
    def __init__(self, ref):
        self.view = ref

    def ref(self):
        return self.view


def run(kernel, outs, scalars, arrays, late=(), scratch=(), cost=1.0, vmem=10):
    in_vmem = pl.BlockSpec(memory_space=pltpu.VMEM)
    pairs = [entry if isinstance(entry, tuple) else (entry, None) for entry in late]
    n_plain = len(arrays)

    def wrapped(place, *refs):
        views = []
        for ref, (_, block) in zip(refs[n_plain:], pairs):
            views.append(View(ref if block is None else ref.at[token_rows(block(place)), :]))
        kernel(place, *refs[:n_plain], *views, *refs[n_plain + len(pairs) :])

    return pl.pallas_call(
        wrapped,
        name=getattr(kernel, "__name__", "advance"),
        out_shape=[jax.ShapeDtypeStruct(shape, kind) for shape, kind in outs],
        in_specs=[pl.BlockSpec(memory_space=pltpu.SMEM)] + [in_vmem] * (n_plain + len(pairs)),
        out_specs=[in_vmem] * len(outs),
        scratch_shapes=[pltpu.VMEM(shape, kind) for shape, kind in scratch],
        compiler_params=pltpu.CompilerParams(vmem_limit_bytes=vmem * 1024 * 1024),
        cost_estimate=pl.CostEstimate(flops=int(cost * 1_000_000_000), bytes_accessed=1000, transcendentals=0),
    )(scalars, *arrays, *[array for array, _ in pairs])


SLOT, CORE, ROW, LIMIT, END = 0, 4, 5, 6, 10
ORDER = (0, 2, 1, 3)


def block_of(place, chunk):
    return place[CORE] * 2 + chunk


def mod_row(mod, slot, component, model):
    return mod[pl.ds(slot, 1), component * model : (component + 1) * model]


def token_rows(block):
    return pl.ds(pl.multiple_of(block * BLOCK, BLOCK), BLOCK)


def text_kernel(place, text, weights, packed):
    rows = text.shape[1]
    wide = weights.shape[0]
    for slot in range(text.shape[0]):
        first = rows * (slot % 2)
        left = wide * (slot // 2)
        packed[first : first + rows, left : left + wide] = dot_nt(text[slot], weights[...]).astype(BF16)


def unpack_kernel(place, q0, o0, q1, o1, part2, rest2, part3, rest3, t0, t1, t2, t3, cqt, co, kall, vall):
    width = q0.shape[0]
    half = width // 2
    rows = kall.shape[1]
    for index, (query, out) in enumerate(((q0, o0), (q1, o1))):
        cqt[index * width : (index + 1) * width, :] = query[...]
        co[index * width : (index + 1) * width, :] = out[...]
    for index, (part, rest) in enumerate(((part2, rest2), (part3, rest3))):
        for piece, row in ((part, place[ROW]), (rest, 1 - place[ROW])):
            at = pl.ds(pl.multiple_of((index + 2) * width + row * half, half), half)
            cqt[at, :] = piece[:half, :]
            co[at, :] = piece[half:, :]
    for slot in range(kall.shape[0]):
        first = rows * (slot % 2)
        left = 2 * width * (slot // 2)
        both = [t[first : first + rows, left : left + 2 * width] for t in (t0, t1, t2, t3)]
        kall[slot] = jnp.concatenate([b[:, :width] for b in both], axis=1)
        vall[slot] = jnp.concatenate([b[:, width:] for b in both], axis=1)


def attend_chunk(place, chunk, qa_in, ka, va, wo, part_own, part_send, qa_out, att):
    heads = ka.shape[0]
    lane = lax.broadcasted_iota(jnp.int32, (BLOCK, 2 * HEAD), 1)
    spot = (lane >= HEAD + 4) & (lane < HEAD + 7)
    for side in range(2):
        at = (2 * chunk + side) * BLOCK
        here = slice(side * BLOCK, (side + 1) * BLOCK)
        pieces = []
        for head in range(heads):
            queries = qa_in[head, at : at + BLOCK, :]
            scores = dot_nt(queries, ka[head])
            top = jnp.max(scores, axis=1, keepdims=True)
            raised = jnp.exp(scores - top).astype(BF16)
            out = dot_nn(raised, va[head])
            total = out[:, HEAD : HEAD + 1]
            pieces.append(out[:, :HEAD] * (1.0 / total))
            high, middle, low = three_parts(-(top + jnp.log(total)))
            more = jnp.where(lane == HEAD + 4, high, jnp.where(lane == HEAD + 5, middle, low))
            qa_out[head, here, :] = jnp.where(spot, more, queries.astype(F32)).astype(BF16)
        attended = jnp.concatenate(pieces, axis=1).astype(BF16)
        att[here, :] = attended
        out = dot_nn(attended, wo[...]).astype(BF16)

        @pl.when(place[CORE] == side)
        def _():
            part_own[...] = out

        @pl.when(place[CORE] != side)
        def _():
            part_send[...] = out


def self_first(place, mod, weights, tokens, wo, part_own, part_send, qa, ka, va, qa_out, att, h1):
    model = mod.shape[1] // 9
    lane = lax.broadcasted_iota(jnp.int32, (BLOCK, 2 * HEAD), 1)
    keep = lane < HEAD
    width = weights.shape[0] // 3
    tokens = tokens.ref()
    for position, block in enumerate(ORDER):
        rows = slice(position * BLOCK, (position + 1) * BLOCK)
        slot = place[SLOT + block]
        normed, _ = normalize(tokens[block * BLOCK : (block + 1) * BLOCK, :].astype(F32))
        hidden = (normed * (1.0 + mod_row(mod, slot, 1, model)) + mod_row(mod, slot, 0, model)).astype(BF16)
        h1[rows, :] = hidden
        rows_qkv = dot_nt(hidden, weights[...])
        q = rows_qkv[:, :width].astype(BF16).astype(F32) * (HEAD**-0.5)
        k = rows_qkv[:, width : 2 * width]
        v = rows_qkv[:, 2 * width :]
        mine = lane == HEAD + slot
        q_more = jnp.where(mine, 1.0, 0.0)
        k_more = jnp.where((lane >= HEAD + 4) & (lane < HEAD + 7), 1.0, 0.0)
        k_more = jnp.where((lane >= HEAD) & (lane < HEAD + 4) & jnp.logical_not(mine), MASKED, k_more)
        v_more = jnp.where((lane >= HEAD) & (lane < HEAD + 3), 1.0, 0.0)
        for head in range(ka.shape[0]):
            qa[head, rows, :] = jnp.where(keep, head_slice(q, head), q_more).astype(BF16)
            ka[head, rows, :] = jnp.where(keep, head_slice(k, head), k_more).astype(BF16)
            va[head, rows, :] = jnp.where(keep, head_slice(v, head), v_more).astype(BF16)
    attend_chunk(place, 0, qa, ka, va, wo.ref(), part_own, part_send, qa_out, att)


def self_second(place, qa, ka, va, wo, part_own, part_send, qa_out, att):
    attend_chunk(place, 1, qa, ka, va, wo.ref(), part_own, part_send, qa_out, att)


def quad_stack(rows, masks):
    return jnp.concatenate([rows * mask for mask in masks], axis=0)


def quad_masks():
    lane = lax.broadcasted_iota(jnp.int32, (1, 4 * HEAD), 1)
    return [jnp.where((lane >= u * HEAD) & (lane < (u + 1) * HEAD), 1.0, 0.0) for u in range(4)]


def quad_probs(scores, limit, text_rows):
    key_row = lax.broadcasted_iota(jnp.int32, (text_rows, 1), 0)
    bias = jnp.where(key_row < limit, 0.0, MASKED)
    probs = []
    for u in range(4):
        part = scores[u * text_rows : (u + 1) * text_rows, :] + bias
        raised = jnp.exp(part - jnp.max(part, axis=0, keepdims=True))
        probs.append(raised * (1.0 / jnp.sum(raised, axis=0, keepdims=True)))
    return probs


def middle_chunk(
    place, chunk, mod, sum_own, sum_far, cqt, co, kall, vall, tokens, cot, win0, wout0, win1, wout1, x2_before,
    h3g_out, h3_out, act0, act1, pg0, pg1, b3g_out, x1_out, b2_out, h2_out, q2_out, cr_out, b3_out, x2_out,
):
    model = cqt.shape[1]
    text_rows = kall.shape[1]
    slot = place[SLOT + block_of(place, chunk)]

    def m(component):
        return mod_row(mod, slot, component, model)

    x1 = tokens.ref()[...].astype(F32) + m(2) * (sum_own[...].astype(F32) + sum_far[...].astype(F32))
    x1_out[...] = x1
    normed, _ = normalize(x1)
    h2 = (normed * (1.0 + m(4)) + m(3)).astype(BF16)
    h2_out[...] = h2
    q2 = (dot_nt(h2, cqt[...]).astype(BF16).astype(F32) * (HEAD**-0.5)).astype(BF16)
    q2_out[...] = q2
    masks = [mask.astype(BF16) for mask in quad_masks()]
    crossed = []
    for quad in range(model // (4 * HEAD)):
        cols = slice(quad * 4 * HEAD, (quad + 1) * 4 * HEAD)
        scores = dot_nt(quad_stack(kall[slot, :, cols], masks), q2[:, cols])
        probs = jnp.concatenate(quad_probs(scores, place[LIMIT + slot], text_rows), axis=0)
        crossed.append(dot_tn(probs.astype(BF16), quad_stack(vall[slot, :, cols], masks)).astype(BF16))
    crossed = jnp.concatenate(crossed, axis=1)
    cr_out[...] = crossed
    b2 = dot_nn(crossed, co[...])
    b2_out[...] = b2
    x2 = x1 + m(5) * b2
    x2_out[chunk * BLOCK : (chunk + 1) * BLOCK, :] = x2
    normed, _ = normalize(x2)
    h3 = (normed * (1.0 + m(7)) + m(6)).astype(BF16)
    h3_out[...] = h3
    b3g = (cot.ref()[...].astype(F32) * m(8)).astype(BF16)
    b3g_out[...] = b3g
    b3 = h3g = None
    for win, wout, act_out, pg_out in ((win0, wout0, act0, pg0), (win1, wout1, act1, pg1)):
        win, wout = win.ref(), wout.ref()
        pre = dot_nn(h3, win[...])
        square = pre * pre
        bent = jnp.tanh(CURVE * (pre + CUBIC * (square * pre)))
        act = (0.5 * pre * (1.0 + bent)).astype(BF16)
        act_out[...] = act
        slope = 0.5 * (1.0 + bent) + 0.5 * pre * (1.0 - bent * bent) * (CURVE * (1.0 + 3.0 * CUBIC * square))
        b3_half = dot_nn(act, wout[...])
        pg = (dot_nt(b3g, wout[...]) * slope).astype(BF16)
        pg_out[...] = pg
        h3g_half = dot_nt(pg, win[...])
        b3 = b3_half if b3 is None else b3 + b3_half
        h3g = h3g_half if h3g is None else h3g + h3g_half
    b3_out[...] = b3.astype(BF16)
    if chunk:
        x2_out[0:BLOCK, :] = x2_before.ref()[...]
    h3g_out[...] = h3g.astype(BF16)


def middle_first(place, *refs):
    middle_chunk(place, 0, *refs[:13], None, *refs[13:])


def middle_second(place, *refs):
    middle_chunk(place, 1, *refs)


def stacked(first, second):
    return jnp.concatenate([first[...], second[...]], axis=0)


def mlp_back(
    place, h3a, h3b, pg0a, pg0b, pg1a, pg1b, act0a, act0b, act1a, act1b, b3ga, b3gb,
    in_own, in_send, out_own, out_send,
):
    half = in_own.shape[1]
    grads = (stacked(pg0a, pg0b), stacked(pg1a, pg1b))
    for part in range(2):
        cols = slice(part * half, (part + 1) * half)
        rows = jnp.concatenate([h3a[:, cols], h3b[:, cols]], axis=0)
        for out, grad in ((in_send, grads[1]), (in_own, grads[0])):
            out[part ^ place[ROW]] = dot_tn(rows, grad).astype(BF16)
    grad = stacked(b3ga, b3gb)
    for out, first, second in ((out_send, act1a, act1b), (out_own, act0a, act0b)):
        for part in range(2):
            cols = slice(part * half, (part + 1) * half)
            rows = jnp.concatenate([first[:, cols], second[:, cols]], axis=0)
            out[part ^ place[ROW]] = dot_tn(rows, grad).astype(BF16)


def cross_chunk(
    place, chunk, mod, h3g_own, h3g_far, kall, vall, cqt, co, x1_in, b2_in, cot, q2_in, sum_own, sum_far,
    b1g_out, dq_out, b2g_out, dk_out, dv_out, sums, x1g_out,
):
    model = cqt.shape[1]
    text_rows = kall.shape[1]
    slot = place[SLOT + block_of(place, chunk)]

    def m(component):
        return mod_row(mod, slot, component, model)

    x1 = x1_in.ref()[...]
    b2 = b2_in.ref()[...]
    h3g = h3g_own[...].astype(F32) + h3g_far[...].astype(F32)
    normed, inverse = normalize(x1 + m(5) * b2)
    sums[4:5, :] = column_sum(h3g)
    sums[5:6, :] = column_sum(h3g * normed)
    x2g = cot.ref()[...].astype(F32) + norm_back(h3g * (1.0 + m(7)), normed, inverse)
    sums[3:4, :] = column_sum(x2g * b2)
    b2g = (x2g * m(5)).astype(BF16)
    b2g_out[...] = b2g
    out_grad = dot_nt(b2g, co[...]).astype(BF16)
    masks = quad_masks()
    low = [mask.astype(BF16) for mask in masks]
    query_grads = []
    for quad in range(model // (4 * HEAD)):
        cols = slice(quad * 4 * HEAD, (quad + 1) * 4 * HEAD)
        queries = q2_in.ref()[:, cols]
        grads = out_grad[:, cols]
        keys = quad_stack(kall[slot, :, cols], low)
        values = quad_stack(vall[slot, :, cols], low)
        probs = quad_probs(dot_nt(keys, queries), place[LIMIT + slot], text_rows)
        prob_grad = dot_nt(values, grads)
        score_grad = []
        for u in range(4):
            part = prob_grad[u * text_rows : (u + 1) * text_rows, :]
            row_dot = jnp.sum(probs[u] * part, axis=0, keepdims=True)
            score_grad.append((probs[u] * (part - row_dot)).astype(BF16))
        score_grad = jnp.concatenate(score_grad, axis=0)
        dv = dot_nn(jnp.concatenate(probs, axis=0).astype(BF16), grads)
        dk = dot_nn(score_grad, queries)
        query_grads.append((dot_tn(score_grad, keys) * (HEAD**-0.5)).astype(BF16))
        for wide, out in ((dk, dk_out), (dv, dv_out)):
            total = None
            for u in range(4):
                part = wide[u * text_rows : (u + 1) * text_rows, :] * masks[u]
                total = part if total is None else total + part
            out[:, cols] = total.astype(BF16)
    query_grad = jnp.concatenate(query_grads, axis=1)
    dq_out[...] = query_grad
    h2g = dot_nn(query_grad, cqt[...])
    normed, inverse = normalize(x1)
    sums[1:2, :] = column_sum(h2g)
    sums[2:3, :] = column_sum(h2g * normed)
    x1g = x2g + norm_back(h2g * (1.0 + m(4)), normed, inverse)
    x1g_out[...] = x1g
    branch = sum_own.ref()[...].astype(F32) + sum_far.ref()[...].astype(F32)
    sums[0:1, :] = column_sum(x1g * branch)
    sums[6:8, :] = jnp.zeros((2, model), F32)
    b1g_out[...] = (x1g * m(2)).astype(BF16)


def cross_first(place, *refs):
    cross_chunk(place, 0, *refs)


def cross_second(place, *refs):
    cross_chunk(place, 1, *refs)


def cross_weights(
    place, dqa, dqb, b2ga, b2gb, dka, dkb, dva, dvb, h2a, h2b, cra, crb, text, own, send,
):
    width = own.shape[1] // 2
    row = place[ROW]
    h2a, h2b, cra, crb, text = h2a.ref(), h2b.ref(), cra.ref(), crb.ref(), text.ref()
    hidden = stacked(h2a, h2b)
    grads = stacked(b2ga, b2gb)
    texts = [text[place[SLOT + block_of(place, chunk)]] for chunk in range(2)]
    for member, out in ((1, send), (0, own)):
        start = (member * width // 128) * 128
        skip = member * width - start
        cols = slice(start, start + 2 * 128)
        kept = slice(skip, skip + width)

        def two(first, second):
            return jnp.concatenate([first[:, cols], second[:, cols]], axis=0)

        top, bottom = slice(0, width), slice(width, 2 * width)
        out[row, top] = dot_tn(two(dqa, dqb), hidden)[kept].astype(BF16)
        out[row, bottom] = (dot_tn(dka[:, cols], texts[0]) + dot_tn(dkb[:, cols], texts[1]))[kept].astype(BF16)
        out[1 - row, top] = (dot_tn(dva[:, cols], texts[0]) + dot_tn(dvb[:, cols], texts[1]))[kept].astype(BF16)
        out[1 - row, bottom] = dot_tn(two(cra, crb), grads)[kept].astype(BF16)


def keys_back(block, first, qa, ka, va, da, dq_sum):
    rows = token_rows(block)
    dks = []
    dvs = []
    for head in range(ka.shape[0]):
        keys = ka[head, rows, :]
        probs = jnp.exp(dot_nt(keys, qa[head]))
        prob_grad = dot_nt(va[head, rows, :], da[head])
        score_grad = (probs * prob_grad).astype(BF16)
        dvs.append(dot_nn(probs.astype(BF16), da[head])[:, :HEAD])
        dks.append(dot_nn(score_grad, qa[head])[:, :HEAD])
        dq = dot_tn(score_grad, keys)
        dq_sum[head] = dq if first else dq_sum[head] + dq
    return jnp.concatenate(dks, axis=1).astype(BF16), jnp.concatenate(dvs, axis=1).astype(BF16)


def self_back_first(
    place, b1g_a, b1g_b, far_a, far_b, wo, att_a, att_b, qa_a, qa_b, ka, va,
    b1g, att, qa, da, dq_sum, dk_all, dv_all,
):
    blocks = b1g.shape[0] // BLOCK
    heads = da.shape[0]
    core = place[CORE]
    for chunk, (own, far) in enumerate(((b1g_a, far_a), (b1g_b, far_b))):
        b1g[token_rows(2 * chunk + core), :] = own[...]
        b1g[token_rows(2 * chunk + 1 - core), :] = far[...]
    wo = wo.ref()
    att[0 : 2 * BLOCK, :] = att_a.ref()[...]
    att[2 * BLOCK : 4 * BLOCK, :] = att_b.ref()[...]
    lane = lax.broadcasted_iota(jnp.int32, (BLOCK, 2 * HEAD), 1)
    for block in range(blocks):
        rows = slice(block * BLOCK, (block + 1) * BLOCK)
        grads = dot_nt(b1g[rows, :], wo[...]).astype(BF16).astype(F32)
        dots = grads * att[rows, :].astype(F32)
        for head in range(heads):
            row_dot = jnp.sum(dots[:, head * HEAD : (head + 1) * HEAD], axis=1, keepdims=True)
            high, middle, low = three_parts(-row_dot)
            more = jnp.where(lane == HEAD, high, jnp.where(lane == HEAD + 1, middle, low))
            more = jnp.where(lane < HEAD + 3, more, 0.0)
            da[head, rows, :] = jnp.where(lane < HEAD, head_slice(grads, head), more).astype(BF16)
    qa[:, 0 : 2 * BLOCK, :] = qa_a.ref()[...]
    qa[:, 2 * BLOCK : 4 * BLOCK, :] = qa_b.ref()[...]
    ka, va = ka.ref(), va.ref()
    for block in range(2):
        rows = slice(block * BLOCK, (block + 1) * BLOCK)
        dk_all[rows, :], dv_all[rows, :] = keys_back(block, block == 0, qa, ka, va, da, dq_sum)


def self_back_second(
    place, b1g, att, qa, da, dq_in, dk_in, dv_in, weights, ka, va, h1,
    part_own, part_send, dw_keep, dw_give,
    dq_sum, grad_all,
):
    blocks = b1g.shape[0] // BLOCK
    heads = da.shape[0]
    core = place[CORE]
    width = heads * HEAD
    ka, va = ka.ref(), va.ref()
    dq_sum[...] = dq_in[...]
    grad_all[0 : 2 * BLOCK, width : 2 * width] = dk_in[0 : 2 * BLOCK, :]
    grad_all[0 : 2 * BLOCK, 2 * width : 3 * width] = dv_in[0 : 2 * BLOCK, :]
    for block in range(2, blocks):
        rows = slice(block * BLOCK, (block + 1) * BLOCK)
        dk, dv = keys_back(block, False, qa, ka, va, da, dq_sum)
        grad_all[rows, width : 2 * width] = dk
        grad_all[rows, 2 * width : 3 * width] = dv
    h1 = h1.ref()
    for block in range(blocks):
        rows = slice(block * BLOCK, (block + 1) * BLOCK)
        dq = jnp.concatenate([dq_sum[head, rows, :HEAD] for head in range(heads)], axis=1)
        grad_all[rows, 0:width] = (dq * (HEAD**-0.5)).astype(BF16)
        out = dot_nn(grad_all[rows, :], weights[...]).astype(BF16)
        chunk, side = block // 2, block % 2
        out_rows = slice(chunk * BLOCK, (chunk + 1) * BLOCK)

        @pl.when(core == side)
        def _():
            part_own[out_rows, :] = out

        @pl.when(core != side)
        def _():
            part_send[out_rows, :] = out

    grads = dot_tn(grad_all[...], h1[...]).astype(BF16)
    query_key = (grads[:width], grads[width : 2 * width])
    value_out = (grads[2 * width :], dot_tn(att[...], b1g[...]).astype(BF16))
    for flag, first, second in ((0, query_key, value_out), (1, value_out, query_key)):

        @pl.when(place[ROW] == flag)
        def _():
            for index in range(2):
                rows = slice(index * width, (index + 1) * width)
                dw_keep[rows, :] = first[index]
                dw_give[rows, :] = second[index]


def mixed_kernel(place, mod, b3a, b3b, far_a, far_b, x2, cot_a, cot_b, mixed, sums):
    model = mixed.shape[1]
    for chunk, (own, far, cot) in enumerate(((b3a, far_a, cot_a), (b3b, far_b, cot_b))):
        rows = slice(chunk * BLOCK, (chunk + 1) * BLOCK)
        slot = place[SLOT + block_of(place, chunk)]
        b3 = own[...].astype(F32) + far[...].astype(F32)
        mixed[rows, :] = (x2[rows, :] + mod_row(mod, slot, 8, model) * b3).astype(BF16)
        sums[chunk] = column_sum(cot.ref()[...].astype(F32) * b3)


def final_kernel(
    place, mod, h1g_own, h1g_far, sums_a, sums_b, sums_mixed, tokens_a, tokens_b, x1ga, x1gb, token_grad, slot_sums,
):
    model = token_grad.shape[1]
    slot_sums[...] = jnp.zeros_like(slot_sums)
    for chunk, (x1g, sums, tokens) in enumerate(((x1ga, sums_a, tokens_a), (x1gb, sums_b, tokens_b))):
        rows = slice(chunk * BLOCK, (chunk + 1) * BLOCK)
        block = block_of(place, chunk)
        slot = place[SLOT + block]
        h1g = h1g_own[rows, :].astype(F32) + h1g_far[rows, :].astype(F32)
        normed, inverse = normalize(tokens.ref()[...].astype(F32))
        scaled = h1g * (1.0 + mod_row(mod, slot, 1, model))
        token_grad[rows, :] = (x1g.ref()[...] + norm_back(scaled, normed, inverse)).astype(BF16)
        terms = [column_sum(h1g), column_sum(h1g * normed)]
        terms += [sums[i : i + 1, :] for i in range(6)] + [sums_mixed[chunk]]
        for component, term in enumerate(terms):
            slot_sums[pl.ds(slot, 1), component * model : (component + 1) * model] += term


def advance_kernel(roles, place, *refs):
    refs = list(refs)
    values, got = {}, {}
    for role in roles:
        values[role] = refs.pop(0)
    for name in ("row", "column", "middle"):
        if any(role in roles for role in {"row": "a", "column": "bd", "middle": "c"}[name]):
            got[name] = refs.pop(0)
    outs = {role: refs.pop(0) for role in roles}
    end = place[END]
    if "a" in roles:
        outs["a"][...] = added(values["a"][...], got["row"][...])
    if "c" in roles:

        @pl.when(end == 0)
        def _():
            outs["c"][...] = added(values["c"][...], got["middle"][...])

        @pl.when(end != 0)
        def _():
            outs["c"][...] = values["c"][...]

    if "b" in roles:

        @pl.when(end == 0)
        def _():
            outs["b"][...] = added(values["b"][...], got["column"][...])

        @pl.when(end != 0)
        def _():
            outs["b"][...] = values["b"][...]

    if "d" in roles:

        @pl.when(end == 0)
        def _():
            outs["d"][...] = values["d"][...]

        @pl.when(end != 0)
        def _():
            outs["d"][...] = got["column"][...]

    if refs:

        @pl.when(end == 0)
        def _():
            refs[0][...] = outs["c"][...]

        @pl.when(end != 0)
        def _():
            refs[0][...] = outs["a"][...]


def added(first, second):
    return (first.astype(F32) + second.astype(F32)).astype(BF16)


def solution(mesh):
    n_dp = mesh.shape["dp"]
    n_tensor = mesh.shape["tensor"]
    n_col = n_dp // 2
    dp_bits = int(math.log2(n_dp))

    def tensor_swap(value, flip):
        return lax.ppermute(value, "tensor", [(i, i ^ flip) for i in range(n_tensor)])

    def core_swap(value):
        return tensor_swap(value, 1)

    def far_swap(value):
        return tensor_swap(value, 2)

    def dp_swap(value, flip):
        return lax.ppermute(value, "dp", [(i, i ^ flip) for i in range(n_dp)])

    def tie(*values):
        return lax.optimization_barrier(values) if values else ()

    def pair_up(flag, mine, other):
        return jnp.concatenate([jnp.where(flag == 0, mine, other), jnp.where(flag == 0, other, mine)], axis=0)

    def local(
        tokens, text_states, clip_len, text_len, timesteps, q_weight, k_weight, v_weight, o_weight,
        cross_q, cross_k, cross_v, cross_o, mlp_in, mlp_out, mod_weight, mod_bias, cotangent,
    ):
        count, model = tokens.shape
        slots, text_rows = text_states.shape[:2]
        width = o_weight.shape[0]
        heads = width // HEAD
        half = count // 2
        text_pad = -(-text_rows // 16) * 16
        tensor_at = lax.axis_index("tensor")
        dp_at = lax.axis_index("dp")
        core = tensor_at & 1
        row = dp_at & 1
        column = dp_at >> 1

        ends = jnp.cumsum(clip_len)
        starts = jnp.arange(count // BLOCK, dtype=jnp.int32) * BLOCK
        slot_of = jnp.sum((starts[:, None] >= ends[None, :]).astype(jnp.int32), axis=1)
        end = (column == 0) | (column == n_col - 1)
        place = jnp.concatenate([slot_of, core[None], row[None], text_len, end[None].astype(jnp.int32)])
        place = place.astype(jnp.int32)

        query_own = cross_q.T
        part_own = jnp.concatenate(
            [lax.dynamic_slice_in_dim(w, row * (width // 2), width // 2, 0) for w in (query_own, cross_o)], axis=0
        )
        text_weights = jnp.concatenate([cross_k.T, cross_v.T], axis=0)
        text = jnp.pad(text_states, ((0, 0), (0, text_pad - text_rows), (0, 0)))
        self_weights = jnp.concatenate([q_weight.T, k_weight.T, v_weight.T], axis=0)

        half_width = model // 2
        ramp = jnp.arange(half_width).astype(F32)
        frequency = jnp.exp(ramp * (-math.log(10000.0) / half_width))
        angles = timesteps.astype(F32)[:, None] * frequency[None, :]
        embed = jnp.concatenate([jnp.cos(angles), jnp.sin(angles)], axis=1)
        silu_low = jax.nn.silu(embed).astype(BF16)
        part_far = far_swap(part_own)
        wout1 = core_swap(mlp_out)
        mod_own = dot_nn(silu_low, mod_weight) + mod_bias.astype(F32)
        mod_far = [tensor_swap(mod_own, flip) for flip in range(1, n_tensor)]
        (text_own,) = run(text_kernel, [((2 * text_pad, model), BF16)], place, [text, text_weights])
        text_own, self_weights, wout1, *mod_far = tie(text_own, self_weights, wout1, *mod_far)
        text_far = far_swap(text_own)
        query_own, out_own, text_own = tie(query_own, cross_o, text_own)
        query1, out1, text1 = core_swap(query_own), core_swap(out_own), core_swap(text_own)
        mod_all = jnp.stack([mod_own] + mod_far)
        mod = jnp.concatenate(
            [lax.dynamic_index_in_dim(mod_all, tensor_at ^ j, 0, keepdims=False) for j in range(n_tensor)], axis=1
        )

        wide = (heads, count, 2 * HEAD)
        block_wide = (heads, 2 * BLOCK, 2 * HEAD)
        one = ((BLOCK, model), BF16)
        one_f32 = ((BLOCK, model), F32)
        attend_far = [(block_wide, BF16), ((2 * BLOCK, width), BF16)]
        own_a, send_a, qa, ka, va, qa_a, att_a, h1 = run(
            self_first, [one, one] + [(wide, BF16)] * 3 + attend_far + [((count, model), BF16)], place, [mod, self_weights], cost=0.001,
            late=[tokens, o_weight],
        )
        send_a, part_far, text_far, query1, out1, text1 = tie(send_a, part_far, text_far, query1, out1, text1)
        sum_a = added(own_a, core_swap(send_a))
        sum_a, qa, part_far, text_far, win0 = tie(sum_a, qa, part_far, text_far, mlp_in)
        far_a = far_swap(sum_a)
        rest_far = dp_swap(part_far, 1)
        part3, text3, win1 = core_swap(part_far), core_swap(text_far), core_swap(win0)
        own_b, send_b, qa_b, att_b = run(
            self_second, [one, one] + attend_far, place, [qa, ka, va], late=[o_weight], cost=4.5
        )
        send_b, far_a, rest_far, part3, text3, win1 = tie(send_b, far_a, rest_far, part3, text3, win1)
        rest3 = core_swap(rest_far)
        sum_b = added(own_b, core_swap(send_b))
        sum_b, rest3 = tie(sum_b, rest3)
        far_b = far_swap(sum_b)
        cqt, co, kall, vall = run(
            unpack_kernel, [((model, model), BF16)] * 2 + [((slots, text_pad, model), BF16)] * 2,
            place,
            [query_own, out_own, query1, out1, part_far, rest_far, part3, rest3, text_own, text1, text_far, text3],
            cost=0.001,
        )
        shared = [cqt, co, kall, vall]

        def chunk_rows(array, chunk):
            return (array, functools.partial(block_of, chunk=chunk))

        def middle(kernel, chunk, own, far, *before):
            return run(
                kernel, [one] * 7 + [one_f32, one_f32] + [one] * 4 + [(((chunk + 1) * BLOCK, model), F32)], place,
                [mod, own, far] + shared, cost=7.5,
                late=[chunk_rows(tokens, chunk), chunk_rows(cotangent, chunk), mlp_in, mlp_out, win1, wout1, *before],
            )

        h3ga, h3a, act0a, act1a, pg0a, pg1a, b3ga, x1a, b2a, h2a, q2a, cra, b3a, x2a = middle(
            middle_first, 0, sum_a, far_a
        )
        h3ga, far_b = tie(h3ga, far_b)
        h3g_far_a = far_swap(h3ga)
        h3gb, h3b, act0b, act1b, pg0b, pg1b, b3gb, x1b, b2b, h2b, q2b, crb, b3b, x2 = middle(
            middle_second, 1, sum_b, far_b, x2a
        )
        h3gb, pg0b, h3g_far_a = tie(h3gb, pg0b, h3g_far_a)
        h3g_far_b = far_swap(h3gb)

        in_own, in_send, out_own, out_send = run(
            mlp_back, [((2, model // 2, model), BF16)] * 4, place,
            [h3a, h3b, pg0a, pg0b, pg1a, pg1b, act0a, act0b, act1a, act1b, b3ga, b3gb], cost=0.001,
        )

        def cross(kernel, chunk, h3g_own, h3g_far, x1, b2, own, far, q2):
            return run(
                kernel, [one] * 3 + [((text_pad, model), BF16)] * 2 + [((8, model), F32), one_f32], place,
                [mod, h3g_own, h3g_far, kall, vall, cqt, co],
                late=[x1, b2, chunk_rows(cotangent, chunk), q2, own, far], cost=4.0 if chunk else 0.001,
            )

        b1g_a, dqa, b2ga, dka, dva, sums_a, x1ga = cross(
            cross_first, 0, h3ga, h3g_far_a, x1a, b2a, sum_a, far_a, q2a
        )
        in_send, out_send, b1g_a, h3g_far_b = tie(in_send, out_send, b1g_a, h3g_far_b)
        in_got, out_got, b1g_far_a = core_swap(in_send), core_swap(out_send), core_swap(b1g_a)
        b1g_b, dqb, b2gb, dkb, dvb, sums_b, x1gb = cross(
            cross_second, 1, h3gb, h3g_far_b, x1b, b2b, sum_b, far_b, q2b
        )
        in_got, out_got, b1g_far_a, b1g_b, dqb, b3a = tie(in_got, out_got, b1g_far_a, b1g_b, dqb, b3a)
        in_keep, in_give = added(in_own[0], in_got[0]), added(in_own[1], in_got[1])
        out_keep, out_give = added(out_own[0], out_got[0]), added(out_own[1], out_got[1])

        across = [(i, i ^ 1) for i in range(n_dp)]
        neighbours = [(i, i ^ 2) for i in range(n_dp)]
        middle_pair = [(2 * a + r, 2 * b + r) for a, b in ((1, 2), (2, 1)) for r in range(2)]
        chain_rows = (model // 2, model)

        class Rounds:
            def __init__(self):
                self.values, self.column_send, self.results, self.waiting = {}, None, [], []

            def start(self, *chain):
                self.got = {}
                if n_col != 4:
                    self.waiting += [chain] if chain else []
                    return
                if chain:
                    self.values["a"] = chain[0]
                    self.got["row"] = lax.ppermute(chain[1], "dp", across)
                if "e" in self.values:
                    self.got["last"] = lax.ppermute(self.values["e"], "dp", across)
                if "b" in self.values or "d" in self.values:
                    self.got["column"] = lax.ppermute(self.column_send, "dp", neighbours)
                if "c" in self.values:
                    self.got["middle"] = lax.ppermute(self.values["c"], "dp", middle_pair)

            def finish(self, *others):
                ended = [self.got.pop("last"), self.values.pop("e")] if "last" in self.got else []
                roles = "".join(role for role in "abcd" if role in self.values)
                if not roles:
                    tied = tie(*ended, *others)
                    if ended:
                        self.results.append(tied[1::-1])
                    return tied[len(ended) :]
                operands = [self.values[role] for role in roles]
                operands += [self.got[name] for name in ("row", "column", "middle") if name in self.got]
                tied = tie(*ended, *operands, *others)
                if ended:
                    self.results.append(tied[1::-1])
                    tied = tied[2:]
                operands, others = tied[: len(operands)], tied[len(operands) :]
                sends = "a" in roles or "c" in roles
                both = "a" in roles and "c" in roles
                outs = run(
                    functools.partial(advance_kernel, roles), [(chain_rows, BF16)] * (len(roles) + both),
                    place, operands, cost=0.3,
                )
                done = tie(*outs, *others)
                stepped = dict(zip(roles, done))
                if sends:
                    self.column_send = done[len(roles)] if both else stepped["a" if "a" in roles else "c"]
                self.values = {{"a": "b", "b": "c", "c": "d", "d": "e"}[role]: v for role, v in stepped.items()}
                return done[len(outs) :]

            def total(self, number):
                mine, other = self.results[number] if n_col == 4 else self.slowly(*self.waiting[number])
                return jnp.where(row == 0, mine, other).astype(F32), jnp.where(row == 0, other, mine).astype(F32)

            def slowly(self, keep, give):
                total = added(keep, lax.ppermute(give, "dp", across))
                for bit in range(1, dp_bits):
                    size, flag = total.shape[0] // 2, (dp_at >> bit) & 1
                    sent = lax.dynamic_slice_in_dim(total, (1 - flag) * size, size, 0)
                    total = added(lax.dynamic_slice_in_dim(total, flag * size, size, 0), dp_swap(sent, 1 << bit))
                for bit in reversed(range(1, dp_bits)):
                    total = pair_up((dp_at >> bit) & 1, total, dp_swap(total, 1 << bit))
                return total, lax.ppermute(total, "dp", across)

        rounds = Rounds()

        rounds.start(in_keep, in_give)
        b1g_far_b = core_swap(b1g_b)
        b3_far_a = far_swap(b3a)
        cross_dw, cross_send = run(
            cross_weights, [((2, 2 * width, model), BF16)] * 2, place,
            [dqa, dqb, b2ga, b2gb, dka, dkb, dva, dvb], late=[h2a, h2b, cra, crb, text], cost=0.001,
        )
        b1g_far_b, cross_send = tie(b1g_far_b, cross_send)
        b1g_all, att_all, qa_all, da, dq_sum, dk_all, dv_all = run(
            self_back_first,
            [((count, model), BF16), ((count, width), BF16), (wide, BF16), (wide, BF16), (wide, F32)]
            + [((count, width), BF16)] * 2,
            place, [b1g_a, b1g_b, b1g_far_a, b1g_far_b],
            late=[o_weight, att_a, att_b, qa_a, qa_b, ka, va], cost=0.001,
        )
        b1g_all, cross_send, out_give, b3b, b3_far_a = rounds.finish(b1g_all, cross_send, out_give, b3b, b3_far_a)

        rounds.start(out_keep, out_give)
        cross_got = core_swap(cross_send)
        b3_far_b = far_swap(b3b)
        grad_own, grad_send, self_keep, self_give = run(
            self_back_second,
            [((half, model), BF16)] * 2 + [((2 * width, model), BF16)] * 2, place,
            [b1g_all, att_all, qa_all, da, dq_sum, dk_all, dv_all, self_weights], late=[ka, va, h1],
            scratch=[(wide, F32), ((count, 3 * width), BF16)], cost=10.0,
        )
        cross_keep, cross_give = added(cross_dw[0], cross_got[0]), added(cross_dw[1], cross_got[1])
        grad_send, cross_give, self_give, b3_far_b = rounds.finish(grad_send, cross_give, self_give, b3_far_b)

        rounds.start(cross_keep, cross_give)
        h1g_own = added(grad_own, core_swap(grad_send))
        h1g_far = far_swap(h1g_own)
        mixed, sums_mixed = run(
            mixed_kernel, [((half, model), BF16), ((2, 1, model), F32)],
            place, [mod, b3a, b3b, b3_far_a, b3_far_b, x2], late=[chunk_rows(cotangent, 0), chunk_rows(cotangent, 1)],
        )
        self_give, h1g_own, mixed = rounds.finish(self_give, h1g_own, mixed)

        rounds.start(self_keep, self_give)
        mixed_far = core_swap(mixed)
        token_grad, slot_sums = run(
            final_kernel, [((half, model), BF16), ((slots, 9 * model), F32)],
            place, [mod, h1g_own, h1g_far, sums_a, sums_b, sums_mixed],
            late=[chunk_rows(tokens, 0), chunk_rows(tokens, 1), x1ga, x1gb],
        )
        token_grad, slot_sums, mixed_far = rounds.finish(token_grad, slot_sums, mixed_far)

        rounds.start()
        token_far = core_swap(token_grad)
        slot_far = core_swap(slot_sums)
        mixed = pair_up(core, mixed, mixed_far)
        token_far, slot_far, mixed = rounds.finish(token_far, slot_far, mixed)

        rounds.start()
        local_cols = mod_weight.shape[1]
        slot_grad = lax.dynamic_slice_in_dim(slot_sums + slot_far, tensor_at * local_cols, local_cols, 1).astype(BF16)
        gathered = jnp.concatenate([silu_low, slot_grad], axis=1)
        gathered = jnp.concatenate([gathered, dp_swap(gathered, 1)], axis=0)
        gathered, token_far = rounds.finish(gathered, token_far)

        rounds.start()
        token_grad = pair_up(core, token_grad, token_far)
        mlp_in_grad = jnp.concatenate(rounds.total(0), axis=0)
        gathered, token_grad, mlp_in_grad = rounds.finish(gathered, token_grad, mlp_in_grad)

        rounds.start()
        if n_col == 4:
            gathered = jnp.concatenate([gathered] + [dp_swap(gathered, 2 * flip) for flip in range(1, n_col)], axis=0)
        else:
            for bit in range(1, dp_bits):
                gathered = jnp.concatenate([gathered, dp_swap(gathered, 1 << bit)], axis=0)
        mlp_out_grad = jnp.concatenate(rounds.total(1), axis=0)
        cross_qk, cross_vo = rounds.total(2)
        cross_grads = [part[rows] for part in (cross_qk, cross_vo) for rows in (slice(0, width), slice(width, None))]
        mod_weight_grad = dot_tn(gathered[:, :model], gathered[:, model:])
        mod_bias_grad = jnp.sum(gathered[:, model:].astype(F32), axis=0)
        mlp_out_grad, mod_weight_grad, mod_bias_grad, *cross_grads = rounds.finish(
            mlp_out_grad, mod_weight_grad, mod_bias_grad, *cross_grads
        )
        self_qk, self_vo = rounds.total(3)

        return (
            mixed,
            token_grad,
            self_qk[:width].T,
            self_qk[width:].T,
            self_vo[:width].T,
            self_vo[width:],
            cross_grads[0].T,
            cross_grads[1].T,
            cross_grads[2].T,
            cross_grads[3],
            mlp_in_grad,
            mlp_out_grad,
            mod_weight_grad,
            mod_bias_grad,
        )

    rows = P("dp", None)
    by_col = P(None, "tensor")
    by_row = P("tensor", None)
    return jax.shard_map(
        local,
        mesh=mesh,
        in_specs=(
            rows, P("dp", None, None), P("dp"), P("dp"), P("dp"), by_col, by_col, by_col, by_row,
            by_col, by_col, by_col, by_row, by_col, by_row, by_col, P("tensor"), rows,
        ),
        out_specs=(
            rows, rows, by_col, by_col, by_col, by_row, by_col, by_col, by_col, by_row,
            by_col, by_row, by_col, P("tensor"),
        ),
        check_vma=False,
    )
```

```python
import functools
import math

import jax
import jax.numpy as jnp
from jax import lax
from jax.experimental import pallas as pl
from jax.experimental.pallas import tpu as pltpu
from jax.sharding import PartitionSpec as P

HEAD = 64
BLOCK = 256
EPSILON = 1e-06
MASKED = -1000000000.0
CURVE = math.sqrt(2.0 / math.pi)
CUBIC = 0.044715
F32 = jnp.float32
BF16 = jnp.bfloat16


def dot_nn(a, b):
    return lax.dot_general(a, b, (((1,), (0,)), ((), ())), preferred_element_type=F32)


def dot_nt(a, b):
    return lax.dot_general(a, b, (((1,), (1,)), ((), ())), preferred_element_type=F32)


def dot_tn(a, b):
    return lax.dot_general(a, b, (((0,), (0,)), ((), ())), preferred_element_type=F32)


def normalize(values):
    centered = values - jnp.mean(values, axis=-1, keepdims=True)
    inverse = lax.rsqrt(jnp.mean(centered * centered, axis=-1, keepdims=True) + EPSILON)
    return centered * inverse, inverse


def norm_back(grad, normed, inverse):
    first = jnp.mean(grad, axis=-1, keepdims=True)
    second = jnp.mean(grad * normed, axis=-1, keepdims=True)
    return inverse * (grad - first - normed * second)


def column_sum(values):
    return jnp.sum(values, axis=0, keepdims=True)


def three_parts(column):
    high = column.astype(BF16).astype(F32)
    rest = column - high
    middle = rest.astype(BF16).astype(F32)
    return high, middle, rest - middle


def head_slice(rows, head):
    piece = rows[:, head * HEAD : (head + 1) * HEAD]
    return jnp.concatenate([piece, jnp.zeros_like(piece)], axis=1)


class View:
    def __init__(self, ref):
        self.view = ref

    def ref(self):
        return self.view


def run(kernel, outs, scalars, arrays, late=(), scratch=(), cost=0.001, vmem=10):
    in_vmem = pl.BlockSpec(memory_space=pltpu.VMEM)
    pairs = [entry if isinstance(entry, tuple) else (entry, None) for entry in late]
    n_plain = len(arrays)

    def wrapped(place, *refs):
        views = []
        for ref, (_, block) in zip(refs[n_plain:], pairs):
            views.append(View(ref if block is None else ref.at[token_rows(block(place)), :]))
        kernel(place, *refs[:n_plain], *views, *refs[n_plain + len(pairs) :])

    return pl.pallas_call(
        wrapped,
        name=getattr(kernel, "__name__", "advance"),
        out_shape=[jax.ShapeDtypeStruct(shape, kind) for shape, kind in outs],
        in_specs=[pl.BlockSpec(memory_space=pltpu.SMEM)] + [in_vmem] * (n_plain + len(pairs)),
        out_specs=[in_vmem] * len(outs),
        scratch_shapes=[pltpu.VMEM(shape, kind) for shape, kind in scratch],
        compiler_params=pltpu.CompilerParams(vmem_limit_bytes=vmem * 1024 * 1024),
        cost_estimate=pl.CostEstimate(flops=int(cost * 1_000_000_000), bytes_accessed=1000, transcendentals=0),
    )(scalars, *arrays, *[array for array, _ in pairs])


SLOT, CORE, ROW, LIMIT, END, TENSOR = 0, 4, 5, 6, 10, 11
ORDER = (0, 2, 1, 3)


def block_of(place, chunk):
    return place[CORE] * 2 + chunk


def mod_row(mod, slot, component, model):
    return mod[pl.ds(slot, 1), component * model : (component + 1) * model]


def token_rows(block):
    return pl.ds(pl.multiple_of(block * BLOCK, BLOCK), BLOCK)


def text_kernel(place, text, weights, packed):
    rows = text.shape[1]
    wide = weights.shape[0]
    for slot in range(text.shape[0]):
        first = rows * (slot % 2)
        left = wide * (slot // 2)
        packed[first : first + rows, left : left + wide] = dot_nt(text[slot], weights[...]).astype(BF16)


def unpack_kernel(place, q0, o0, q1, o1, part2, rest2, part3, rest3, t0, t1, t2, t3, cqt, co, kall, vall):
    width = q0.shape[0]
    half = width // 2
    rows = kall.shape[1]
    for index, (query, out) in enumerate(((q0, o0), (q1, o1))):
        cqt[index * width : (index + 1) * width, :] = query[...]
        co[index * width : (index + 1) * width, :] = out[...]
    for index, (part, rest) in enumerate(((part2, rest2), (part3, rest3))):
        for piece, row in ((part, place[ROW]), (rest, 1 - place[ROW])):
            at = pl.ds(pl.multiple_of((index + 2) * width + row * half, half), half)
            cqt[at, :] = piece[:half, :]
            co[at, :] = piece[half:, :]
    for slot in range(kall.shape[0]):
        first = rows * (slot % 2)
        left = 2 * width * (slot // 2)
        both = [t[first : first + rows, left : left + 2 * width] for t in (t0, t1, t2, t3)]
        kall[slot] = jnp.concatenate([b[:, :width] for b in both], axis=1)
        vall[slot] = jnp.concatenate([b[:, width:] for b in both], axis=1)


def attend_chunk(place, chunk, qa_in, ka, va, wo, part_own, part_send, qa_out, att):
    heads = ka.shape[0]
    lane = lax.broadcasted_iota(jnp.int32, (BLOCK, 2 * HEAD), 1)
    spot = (lane >= HEAD + 4) & (lane < HEAD + 7)
    for side in range(2):
        at = (2 * chunk + side) * BLOCK
        here = slice(side * BLOCK, (side + 1) * BLOCK)
        pieces = []
        for head in range(heads):
            queries = qa_in[head, at : at + BLOCK, :]
            scores = dot_nt(queries, ka[head])
            top = jnp.max(scores, axis=1, keepdims=True)
            raised = jnp.exp(scores - top).astype(BF16)
            out = dot_nn(raised, va[head])
            total = out[:, HEAD : HEAD + 1]
            pieces.append(out[:, :HEAD] * (1.0 / total))
            high, middle, low = three_parts(-(top + jnp.log(total)))
            more = jnp.where(lane == HEAD + 4, high, jnp.where(lane == HEAD + 5, middle, low))
            qa_out[head, here, :] = jnp.where(spot, more, queries.astype(F32)).astype(BF16)
        attended = jnp.concatenate(pieces, axis=1).astype(BF16)
        att[here, :] = attended
        out = dot_nn(attended, wo[...]).astype(BF16)

        @pl.when(place[CORE] == side)
        def _():
            part_own[...] = out

        @pl.when(place[CORE] != side)
        def _():
            part_send[...] = out


def self_first(place, mod, weights, tokens, wo, part_own, part_send, qa, ka, va, qa_out, att, h1):
    model = mod.shape[1] // 9
    lane = lax.broadcasted_iota(jnp.int32, (BLOCK, 2 * HEAD), 1)
    keep = lane < HEAD
    width = weights.shape[0] // 3
    tokens = tokens.ref()
    for position, block in enumerate(ORDER):
        rows = slice(position * BLOCK, (position + 1) * BLOCK)
        slot = place[SLOT + block]
        normed, _ = normalize(tokens[block * BLOCK : (block + 1) * BLOCK, :].astype(F32))
        hidden = (normed * (1.0 + mod_row(mod, slot, 1, model)) + mod_row(mod, slot, 0, model)).astype(BF16)
        h1[rows, :] = hidden
        rows_qkv = dot_nt(hidden, weights[...])
        q = rows_qkv[:, :width].astype(BF16).astype(F32) * (HEAD**-0.5)
        k = rows_qkv[:, width : 2 * width]
        v = rows_qkv[:, 2 * width :]
        mine = lane == HEAD + slot
        q_more = jnp.where(mine, 1.0, 0.0)
        k_more = jnp.where((lane >= HEAD + 4) & (lane < HEAD + 7), 1.0, 0.0)
        k_more = jnp.where((lane >= HEAD) & (lane < HEAD + 4) & jnp.logical_not(mine), MASKED, k_more)
        v_more = jnp.where((lane >= HEAD) & (lane < HEAD + 3), 1.0, 0.0)
        for head in range(ka.shape[0]):
            qa[head, rows, :] = jnp.where(keep, head_slice(q, head), q_more).astype(BF16)
            ka[head, rows, :] = jnp.where(keep, head_slice(k, head), k_more).astype(BF16)
            va[head, rows, :] = jnp.where(keep, head_slice(v, head), v_more).astype(BF16)
    attend_chunk(place, 0, qa, ka, va, wo.ref(), part_own, part_send, qa_out, att)


def self_second(place, qa, ka, va, wo, part_own, part_send, qa_out, att):
    attend_chunk(place, 1, qa, ka, va, wo.ref(), part_own, part_send, qa_out, att)


def quad_stack(rows, masks):
    return jnp.concatenate([rows * mask for mask in masks], axis=0)


def quad_masks():
    lane = lax.broadcasted_iota(jnp.int32, (1, 4 * HEAD), 1)
    return [jnp.where((lane >= u * HEAD) & (lane < (u + 1) * HEAD), 1.0, 0.0) for u in range(4)]


def quad_probs(scores, limit, text_rows):
    key_row = lax.broadcasted_iota(jnp.int32, (text_rows, 1), 0)
    bias = jnp.where(key_row < limit, 0.0, MASKED)
    probs = []
    for u in range(4):
        part = scores[u * text_rows : (u + 1) * text_rows, :] + bias
        raised = jnp.exp(part - jnp.max(part, axis=0, keepdims=True))
        probs.append(raised * (1.0 / jnp.sum(raised, axis=0, keepdims=True)))
    return probs


def middle_chunk(
    place, chunk, mod, sum_own, sum_far, cqt, co, kall, vall, tokens, cot, win0, wout0, win1, wout1, x2_before,
    h3g_out, h3_out, act0, act1, pg0, pg1, b3g_out, x1_out, b2_out, h2_out, q2_out, cr_out, b3_out, x2_out,
):
    model = cqt.shape[1]
    text_rows = kall.shape[1]
    slot = place[SLOT + block_of(place, chunk)]

    def m(component):
        return mod_row(mod, slot, component, model)

    x1 = tokens.ref()[...].astype(F32) + m(2) * (sum_own[...].astype(F32) + sum_far[...].astype(F32))
    x1_out[...] = x1
    normed, _ = normalize(x1)
    h2 = (normed * (1.0 + m(4)) + m(3)).astype(BF16)
    h2_out[...] = h2
    q2 = (dot_nt(h2, cqt[...]).astype(BF16).astype(F32) * (HEAD**-0.5)).astype(BF16)
    q2_out[...] = q2
    masks = [mask.astype(BF16) for mask in quad_masks()]
    crossed = []
    for quad in range(model // (4 * HEAD)):
        cols = slice(quad * 4 * HEAD, (quad + 1) * 4 * HEAD)
        scores = dot_nt(quad_stack(kall[slot, :, cols], masks), q2[:, cols])
        probs = jnp.concatenate(quad_probs(scores, place[LIMIT + slot], text_rows), axis=0)
        crossed.append(dot_tn(probs.astype(BF16), quad_stack(vall[slot, :, cols], masks)).astype(BF16))
    crossed = jnp.concatenate(crossed, axis=1)
    cr_out[...] = crossed
    b2 = dot_nn(crossed, co[...])
    b2_out[...] = b2
    x2 = x1 + m(5) * b2
    x2_out[chunk * BLOCK : (chunk + 1) * BLOCK, :] = x2
    normed, _ = normalize(x2)
    h3 = (normed * (1.0 + m(7)) + m(6)).astype(BF16)
    h3_out[...] = h3
    b3g = (cot.ref()[...].astype(F32) * m(8)).astype(BF16)
    b3g_out[...] = b3g
    b3 = h3g = None
    for win, wout, act_out, pg_out in ((win0, wout0, act0, pg0), (win1, wout1, act1, pg1)):
        win, wout = win.ref(), wout.ref()
        pre = dot_nn(h3, win[...])
        square = pre * pre
        bent = jnp.tanh(CURVE * (pre + CUBIC * (square * pre)))
        act = (0.5 * pre * (1.0 + bent)).astype(BF16)
        act_out[...] = act
        slope = 0.5 * (1.0 + bent) + 0.5 * pre * (1.0 - bent * bent) * (CURVE * (1.0 + 3.0 * CUBIC * square))
        b3_half = dot_nn(act, wout[...])
        pg = (dot_nt(b3g, wout[...]) * slope).astype(BF16)
        pg_out[...] = pg
        h3g_half = dot_nt(pg, win[...])
        b3 = b3_half if b3 is None else b3 + b3_half
        h3g = h3g_half if h3g is None else h3g + h3g_half
    b3_out[...] = b3.astype(BF16)
    if chunk:
        x2_out[0:BLOCK, :] = x2_before.ref()[...]
    h3g_out[...] = h3g.astype(BF16)


def middle_first(place, *refs):
    middle_chunk(place, 0, *refs[:13], None, *refs[13:])


def middle_second(place, *refs):
    middle_chunk(place, 1, *refs)


def stacked(first, second):
    return jnp.concatenate([first[...], second[...]], axis=0)


def mlp_back(
    place, h3a, h3b, pg0a, pg0b, pg1a, pg1b, act0a, act0b, act1a, act1b, b3ga, b3gb,
    in_own, in_send, out_own, out_send,
):
    half = in_own.shape[1]
    grads = (stacked(pg0a, pg0b), stacked(pg1a, pg1b))
    for part in range(2):
        cols = slice(part * half, (part + 1) * half)
        rows = jnp.concatenate([h3a[:, cols], h3b[:, cols]], axis=0)
        for out, grad in ((in_send, grads[1]), (in_own, grads[0])):
            out[part ^ place[ROW]] = dot_tn(rows, grad).astype(BF16)
    grad = stacked(b3ga, b3gb)
    for out, first, second in ((out_send, act1a, act1b), (out_own, act0a, act0b)):
        for part in range(2):
            cols = slice(part * half, (part + 1) * half)
            rows = jnp.concatenate([first[:, cols], second[:, cols]], axis=0)
            out[part ^ place[ROW]] = dot_tn(rows, grad).astype(BF16)


def cross_chunk(
    place, chunk, mod, h3g_own, h3g_far, kall, vall, cqt, co, x1_in, b2_in, cot, q2_in, sum_own, sum_far,
    b1g_out, dq_out, b2g_out, dk_out, dv_out, sums, x1g_out,
):
    model = cqt.shape[1]
    text_rows = kall.shape[1]
    slot = place[SLOT + block_of(place, chunk)]

    def m(component):
        return mod_row(mod, slot, component, model)

    x1 = x1_in.ref()[...]
    b2 = b2_in.ref()[...]
    h3g = h3g_own[...].astype(F32) + h3g_far[...].astype(F32)
    normed, inverse = normalize(x1 + m(5) * b2)
    sums[4:5, :] = column_sum(h3g)
    sums[5:6, :] = column_sum(h3g * normed)
    x2g = cot.ref()[...].astype(F32) + norm_back(h3g * (1.0 + m(7)), normed, inverse)
    sums[3:4, :] = column_sum(x2g * b2)
    b2g = (x2g * m(5)).astype(BF16)
    b2g_out[...] = b2g
    out_grad = dot_nt(b2g, co[...]).astype(BF16)
    masks = quad_masks()
    low = [mask.astype(BF16) for mask in masks]
    query_grads = []
    for quad in range(model // (4 * HEAD)):
        cols = slice(quad * 4 * HEAD, (quad + 1) * 4 * HEAD)
        queries = q2_in.ref()[:, cols]
        grads = out_grad[:, cols]
        keys = quad_stack(kall[slot, :, cols], low)
        values = quad_stack(vall[slot, :, cols], low)
        probs = quad_probs(dot_nt(keys, queries), place[LIMIT + slot], text_rows)
        prob_grad = dot_nt(values, grads)
        score_grad = []
        for u in range(4):
            part = prob_grad[u * text_rows : (u + 1) * text_rows, :]
            row_dot = jnp.sum(probs[u] * part, axis=0, keepdims=True)
            score_grad.append((probs[u] * (part - row_dot)).astype(BF16))
        score_grad = jnp.concatenate(score_grad, axis=0)
        dv = dot_nn(jnp.concatenate(probs, axis=0).astype(BF16), grads)
        dk = dot_nn(score_grad, queries)
        query_grads.append((dot_tn(score_grad, keys) * (HEAD**-0.5)).astype(BF16))
        for wide, out in ((dk, dk_out), (dv, dv_out)):
            total = None
            for u in range(4):
                part = wide[u * text_rows : (u + 1) * text_rows, :] * masks[u]
                total = part if total is None else total + part
            out[:, cols] = total.astype(BF16)
    query_grad = jnp.concatenate(query_grads, axis=1)
    dq_out[...] = query_grad
    h2g = dot_nn(query_grad, cqt[...])
    normed, inverse = normalize(x1)
    sums[1:2, :] = column_sum(h2g)
    sums[2:3, :] = column_sum(h2g * normed)
    x1g = x2g + norm_back(h2g * (1.0 + m(4)), normed, inverse)
    x1g_out[...] = x1g
    branch = sum_own.ref()[...].astype(F32) + sum_far.ref()[...].astype(F32)
    sums[0:1, :] = column_sum(x1g * branch)
    sums[6:8, :] = jnp.zeros((2, model), F32)
    b1g_out[...] = (x1g * m(2)).astype(BF16)


def cross_first(place, *refs):
    cross_chunk(place, 0, *refs)


def cross_second(place, *refs):
    cross_chunk(place, 1, *refs)


def cross_weights(
    place, dqa, dqb, b2ga, b2gb, dka, dkb, dva, dvb, h2a, h2b, cra, crb, text, own, send,
):
    width = own.shape[1] // 2
    row = place[ROW]
    h2a, h2b, cra, crb, text = h2a.ref(), h2b.ref(), cra.ref(), crb.ref(), text.ref()
    hidden = stacked(h2a, h2b)
    grads = stacked(b2ga, b2gb)
    texts = [text[place[SLOT + block_of(place, chunk)]] for chunk in range(2)]
    for member, out in ((1, send), (0, own)):
        start = (member * width // 128) * 128
        skip = member * width - start
        cols = slice(start, start + 2 * 128)
        kept = slice(skip, skip + width)

        def two(first, second):
            return jnp.concatenate([first[:, cols], second[:, cols]], axis=0)

        top, bottom = slice(0, width), slice(width, 2 * width)
        out[row, top] = dot_tn(two(dqa, dqb), hidden)[kept].astype(BF16)
        out[row, bottom] = (dot_tn(dka[:, cols], texts[0]) + dot_tn(dkb[:, cols], texts[1]))[kept].astype(BF16)
        out[1 - row, top] = (dot_tn(dva[:, cols], texts[0]) + dot_tn(dvb[:, cols], texts[1]))[kept].astype(BF16)
        out[1 - row, bottom] = dot_tn(two(cra, crb), grads)[kept].astype(BF16)


def keys_back(block, first, qa, ka, va, da, dq_sum):
    rows = token_rows(block)
    dks = []
    dvs = []
    for head in range(ka.shape[0]):
        keys = ka[head, rows, :]
        probs = jnp.exp(dot_nt(keys, qa[head]))
        prob_grad = dot_nt(va[head, rows, :], da[head])
        score_grad = (probs * prob_grad).astype(BF16)
        dvs.append(dot_nn(probs.astype(BF16), da[head])[:, :HEAD])
        dks.append(dot_nn(score_grad, qa[head])[:, :HEAD])
        dq = dot_tn(score_grad, keys)
        dq_sum[head] = dq if first else dq_sum[head] + dq
    return jnp.concatenate(dks, axis=1).astype(BF16), jnp.concatenate(dvs, axis=1).astype(BF16)


def self_back_first(
    place, b1g_a, b1g_b, far_a, far_b, wo, att_a, att_b, qa_a, qa_b, ka, va,
    b1g, att, qa, da, dq_sum, dk_all, dv_all,
):
    blocks = b1g.shape[0] // BLOCK
    heads = da.shape[0]
    core = place[CORE]
    for chunk, (own, far) in enumerate(((b1g_a, far_a), (b1g_b, far_b))):
        b1g[token_rows(2 * chunk + core), :] = own[...]
        b1g[token_rows(2 * chunk + 1 - core), :] = far[...]
    wo = wo.ref()
    att[0 : 2 * BLOCK, :] = att_a.ref()[...]
    att[2 * BLOCK : 4 * BLOCK, :] = att_b.ref()[...]
    lane = lax.broadcasted_iota(jnp.int32, (BLOCK, 2 * HEAD), 1)
    for block in range(blocks):
        rows = slice(block * BLOCK, (block + 1) * BLOCK)
        grads = dot_nt(b1g[rows, :], wo[...]).astype(BF16).astype(F32)
        dots = grads * att[rows, :].astype(F32)
        for head in range(heads):
            row_dot = jnp.sum(dots[:, head * HEAD : (head + 1) * HEAD], axis=1, keepdims=True)
            high, middle, low = three_parts(-row_dot)
            more = jnp.where(lane == HEAD, high, jnp.where(lane == HEAD + 1, middle, low))
            more = jnp.where(lane < HEAD + 3, more, 0.0)
            da[head, rows, :] = jnp.where(lane < HEAD, head_slice(grads, head), more).astype(BF16)
    qa[:, 0 : 2 * BLOCK, :] = qa_a.ref()[...]
    qa[:, 2 * BLOCK : 4 * BLOCK, :] = qa_b.ref()[...]
    ka, va = ka.ref(), va.ref()
    for block in range(2):
        rows = slice(block * BLOCK, (block + 1) * BLOCK)
        dk_all[rows, :], dv_all[rows, :] = keys_back(block, block == 0, qa, ka, va, da, dq_sum)


def self_back_second(
    place, b1g, att, qa, da, dq_in, dk_in, dv_in, weights, ka, va, h1,
    part_own, part_send, dw_keep, dw_give,
    dq_sum, grad_all,
):
    blocks = b1g.shape[0] // BLOCK
    heads = da.shape[0]
    core = place[CORE]
    width = heads * HEAD
    ka, va = ka.ref(), va.ref()
    dq_sum[...] = dq_in[...]
    grad_all[0 : 2 * BLOCK, width : 2 * width] = dk_in[0 : 2 * BLOCK, :]
    grad_all[0 : 2 * BLOCK, 2 * width : 3 * width] = dv_in[0 : 2 * BLOCK, :]
    for block in range(2, blocks):
        rows = slice(block * BLOCK, (block + 1) * BLOCK)
        dk, dv = keys_back(block, False, qa, ka, va, da, dq_sum)
        grad_all[rows, width : 2 * width] = dk
        grad_all[rows, 2 * width : 3 * width] = dv
    h1 = h1.ref()
    for block in range(blocks):
        rows = slice(block * BLOCK, (block + 1) * BLOCK)
        dq = jnp.concatenate([dq_sum[head, rows, :HEAD] for head in range(heads)], axis=1)
        grad_all[rows, 0:width] = (dq * (HEAD**-0.5)).astype(BF16)
        out = dot_nn(grad_all[rows, :], weights[...]).astype(BF16)
        chunk, side = block // 2, block % 2
        out_rows = slice(chunk * BLOCK, (chunk + 1) * BLOCK)

        @pl.when(core == side)
        def _():
            part_own[out_rows, :] = out

        @pl.when(core != side)
        def _():
            part_send[out_rows, :] = out

    grads = dot_tn(grad_all[...], h1[...]).astype(BF16)
    query_key = (grads[:width], grads[width : 2 * width])
    value_out = (grads[2 * width :], dot_tn(att[...], b1g[...]).astype(BF16))
    for flag, first, second in ((0, query_key, value_out), (1, value_out, query_key)):

        @pl.when(place[ROW] == flag)
        def _():
            for index in range(2):
                rows = slice(index * width, (index + 1) * width)
                dw_keep[rows, :] = first[index]
                dw_give[rows, :] = second[index]


def mixed_kernel(place, mod, b3a, b3b, far_a, far_b, x2, cot_a, cot_b, mixed_a, mixed_b, sums):
    model = mixed_a.shape[1]
    for chunk, (own, far, cot) in enumerate(((b3a, far_a, cot_a), (b3b, far_b, cot_b))):
        mixed = (mixed_a, mixed_b)[chunk]
        rows = slice(chunk * BLOCK, (chunk + 1) * BLOCK)
        slot = place[SLOT + block_of(place, chunk)]
        b3 = own[...].astype(F32) + far[...].astype(F32)
        mixed[...] = (x2[rows, :] + mod_row(mod, slot, 8, model) * b3).astype(BF16)
        sums[chunk] = column_sum(cot.ref()[...].astype(F32) * b3)


def final_kernel(
    place, mod, h1g_own, h1g_far, sums_a, sums_b, sums_mixed, tokens_a, tokens_b, x1ga, x1gb, grad_a, grad_b, slot_sums,
):
    model = grad_a.shape[1]
    slot_sums[...] = jnp.zeros_like(slot_sums)
    for chunk, (x1g, sums, tokens) in enumerate(((x1ga, sums_a, tokens_a), (x1gb, sums_b, tokens_b))):
        rows = slice(chunk * BLOCK, (chunk + 1) * BLOCK)
        block = block_of(place, chunk)
        slot = place[SLOT + block]
        h1g = h1g_own[rows, :].astype(F32) + h1g_far[rows, :].astype(F32)
        normed, inverse = normalize(tokens.ref()[...].astype(F32))
        scaled = h1g * (1.0 + mod_row(mod, slot, 1, model))
        (grad_a, grad_b)[chunk][...] = (x1g.ref()[...] + norm_back(scaled, normed, inverse)).astype(BF16)
        terms = [column_sum(h1g), column_sum(h1g * normed)]
        terms += [sums[i : i + 1, :] for i in range(6)] + [sums_mixed[chunk]]
        for component, term in enumerate(terms):
            slot_sums[pl.ds(slot, 1), component * model : (component + 1) * model] += term


def join_cores(place, mine_a, mine_b, other_a, other_b, out):
    for chunk, (mine, other) in enumerate(((mine_a, other_a), (mine_b, other_b))):
        out[token_rows(place[CORE] * 2 + chunk), :] = mine[...]
        out[token_rows((1 - place[CORE]) * 2 + chunk), :] = other[...]


def join_rows(place, mine, other, out):
    count = mine.shape[0]
    out[pl.ds(pl.multiple_of(place[ROW] * count, BLOCK // 2), count), :] = mine[...].astype(F32)
    out[pl.ds(pl.multiple_of((1 - place[ROW]) * count, BLOCK // 2), count), :] = other[...].astype(F32)


def join_four(place, mine, other, first, second, third, fourth):
    width = first.shape[0]
    for flag, top, bottom in ((0, mine, other), (1, other, mine)):

        @pl.when(place[ROW] == flag)
        def _():
            first[...] = top[:width, :].astype(F32)
            second[...] = top[width:, :].astype(F32)
            third[...] = bottom[:width, :].astype(F32)
            fourth[...] = bottom[width:, :].astype(F32)


def slot_kernel(place, own, far, silu, out):
    model = silu.shape[1]
    count = out.shape[1] - model
    out[:, :model] = silu[...].astype(F32)
    for index in range(own.shape[1] // count):
        cols = slice(index * count, (index + 1) * count)

        @pl.when(place[TENSOR] == index)
        def _():
            out[:, model:] = (own[:, cols] + far[:, cols]).astype(BF16).astype(F32)


def advance_kernel(roles, place, *refs):
    refs = list(refs)
    values, got = {}, {}
    for role in roles:
        values[role] = refs.pop(0)
    for name in ("row", "column", "middle"):
        if any(role in roles for role in {"row": "a", "column": "bd", "middle": "c"}[name]):
            got[name] = refs.pop(0)
    outs = {role: refs.pop(0) for role in roles}
    end = place[END]
    if "a" in roles:
        outs["a"][...] = added(values["a"][...], got["row"][...])
    if "c" in roles:

        @pl.when(end == 0)
        def _():
            outs["c"][...] = added(values["c"][...], got["middle"][...])

        @pl.when(end != 0)
        def _():
            outs["c"][...] = values["c"][...]

    if "b" in roles:

        @pl.when(end == 0)
        def _():
            outs["b"][...] = added(values["b"][...], got["column"][...])

        @pl.when(end != 0)
        def _():
            outs["b"][...] = values["b"][...]

    if "d" in roles:

        @pl.when(end == 0)
        def _():
            outs["d"][...] = values["d"][...]

        @pl.when(end != 0)
        def _():
            outs["d"][...] = got["column"][...]

    if refs:

        @pl.when(end == 0)
        def _():
            refs[0][...] = outs["c"][...]

        @pl.when(end != 0)
        def _():
            refs[0][...] = outs["a"][...]


def added(first, second):
    return (first.astype(F32) + second.astype(F32)).astype(BF16)


def solution(mesh):
    n_dp = mesh.shape["dp"]
    n_tensor = mesh.shape["tensor"]
    n_col = n_dp // 2
    dp_bits = int(math.log2(n_dp))

    def tensor_swap(value, flip):
        return lax.ppermute(value, "tensor", [(i, i ^ flip) for i in range(n_tensor)])

    def core_swap(value):
        return tensor_swap(value, 1)

    def far_swap(value):
        return tensor_swap(value, 2)

    def dp_swap(value, flip):
        return lax.ppermute(value, "dp", [(i, i ^ flip) for i in range(n_dp)])

    def tie(*values):
        return lax.optimization_barrier(values) if values else ()

    def pair_up(flag, mine, other):
        return jnp.concatenate([jnp.where(flag == 0, mine, other), jnp.where(flag == 0, other, mine)], axis=0)

    def local(
        tokens, text_states, clip_len, text_len, timesteps, q_weight, k_weight, v_weight, o_weight,
        cross_q, cross_k, cross_v, cross_o, mlp_in, mlp_out, mod_weight, mod_bias, cotangent,
    ):
        count, model = tokens.shape
        slots, text_rows = text_states.shape[:2]
        width = o_weight.shape[0]
        heads = width // HEAD
        half = count // 2
        text_pad = -(-text_rows // 16) * 16
        tensor_at = lax.axis_index("tensor")
        dp_at = lax.axis_index("dp")
        core = tensor_at & 1
        row = dp_at & 1
        column = dp_at >> 1

        ends = jnp.cumsum(clip_len)
        starts = jnp.arange(count // BLOCK, dtype=jnp.int32) * BLOCK
        slot_of = jnp.sum((starts[:, None] >= ends[None, :]).astype(jnp.int32), axis=1)
        end = (column == 0) | (column == n_col - 1)
        place = jnp.concatenate([slot_of, core[None], row[None], text_len, end[None].astype(jnp.int32), tensor_at[None]])
        place = place.astype(jnp.int32)

        query_own = cross_q.T
        part_own = jnp.concatenate(
            [lax.dynamic_slice_in_dim(w, row * (width // 2), width // 2, 0) for w in (query_own, cross_o)], axis=0
        )
        text_weights = jnp.concatenate([cross_k.T, cross_v.T], axis=0)
        text = jnp.pad(text_states, ((0, 0), (0, text_pad - text_rows), (0, 0)))
        self_weights = jnp.concatenate([q_weight.T, k_weight.T, v_weight.T], axis=0)

        half_width = model // 2
        ramp = jnp.arange(half_width).astype(F32)
        frequency = jnp.exp(ramp * (-math.log(10000.0) / half_width))
        angles = timesteps.astype(F32)[:, None] * frequency[None, :]
        embed = jnp.concatenate([jnp.cos(angles), jnp.sin(angles)], axis=1)
        silu_low = jax.nn.silu(embed).astype(BF16)
        part_far = far_swap(part_own)
        wout1 = core_swap(mlp_out)
        mod_own = dot_nn(silu_low, mod_weight) + mod_bias.astype(F32)
        mod_far = [tensor_swap(mod_own, flip) for flip in range(1, n_tensor)]
        (text_own,) = run(text_kernel, [((2 * text_pad, model), BF16)], place, [text, text_weights], cost=1.0)
        text_own, self_weights, wout1, *mod_far = tie(text_own, self_weights, wout1, *mod_far)
        text_far = far_swap(text_own)
        query_own, out_own, text_own = tie(query_own, cross_o, text_own)
        query1, out1, text1 = core_swap(query_own), core_swap(out_own), core_swap(text_own)
        mod_all = jnp.stack([mod_own] + mod_far)
        mod = jnp.concatenate(
            [lax.dynamic_index_in_dim(mod_all, tensor_at ^ j, 0, keepdims=False) for j in range(n_tensor)], axis=1
        )

        wide = (heads, count, 2 * HEAD)
        block_wide = (heads, 2 * BLOCK, 2 * HEAD)
        one = ((BLOCK, model), BF16)
        one_f32 = ((BLOCK, model), F32)
        attend_far = [(block_wide, BF16), ((2 * BLOCK, width), BF16)]
        own_a, send_a, qa, ka, va, qa_a, att_a, h1 = run(
            self_first, [one, one] + [(wide, BF16)] * 3 + attend_far + [((count, model), BF16)], place, [mod, self_weights], cost=0.001,
            late=[tokens, o_weight],
        )
        send_a, part_far, text_far, query1, out1, text1 = tie(send_a, part_far, text_far, query1, out1, text1)
        sum_a = added(own_a, core_swap(send_a))
        sum_a, qa, part_far, text_far, win0 = tie(sum_a, qa, part_far, text_far, mlp_in)
        far_a = far_swap(sum_a)
        rest_far = dp_swap(part_far, 1)
        part3, text3, win1 = core_swap(part_far), core_swap(text_far), core_swap(win0)
        own_b, send_b, qa_b, att_b = run(
            self_second, [one, one] + attend_far, place, [qa, ka, va], late=[o_weight], cost=4.5
        )
        (far_a,) = tie(far_a)
        send_b, far_a, rest_far, part3, text3, win1 = tie(send_b, far_a, rest_far, part3, text3, win1)
        rest3 = core_swap(rest_far)
        sum_b = added(own_b, core_swap(send_b))
        sum_b, rest3 = tie(sum_b, rest3)
        far_b = far_swap(sum_b)
        cqt, co, kall, vall = run(
            unpack_kernel, [((model, model), BF16)] * 2 + [((slots, text_pad, model), BF16)] * 2,
            place,
            [query_own, out_own, query1, out1, part_far, rest_far, part3, rest3, text_own, text1, text_far, text3],
            cost=0.001,
        )
        shared = [cqt, co, kall, vall]

        def chunk_rows(array, chunk):
            return (array, functools.partial(block_of, chunk=chunk))

        def middle(kernel, chunk, own, far, *before):
            return run(
                kernel, [one] * 7 + [one_f32, one_f32] + [one] * 4 + [(((chunk + 1) * BLOCK, model), F32)], place,
                [mod, own, far] + shared, cost=7.5,
                late=[chunk_rows(tokens, chunk), chunk_rows(cotangent, chunk), mlp_in, mlp_out, win1, wout1, *before],
            )

        h3ga, h3a, act0a, act1a, pg0a, pg1a, b3ga, x1a, b2a, h2a, q2a, cra, b3a, x2a = middle(
            middle_first, 0, sum_a, far_a
        )
        h3ga, far_b = tie(h3ga, far_b)
        h3g_far_a = far_swap(h3ga)
        h3gb, h3b, act0b, act1b, pg0b, pg1b, b3gb, x1b, b2b, h2b, q2b, crb, b3b, x2 = middle(
            middle_second, 1, sum_b, far_b, x2a
        )
        h3gb, pg0b, h3g_far_a = tie(h3gb, pg0b, h3g_far_a)
        h3g_far_b = far_swap(h3gb)

        in_own, in_send, out_own, out_send = run(
            mlp_back, [((2, model // 2, model), BF16)] * 4, place,
            [h3a, h3b, pg0a, pg0b, pg1a, pg1b, act0a, act0b, act1a, act1b, b3ga, b3gb], cost=0.001,
        )

        def cross(kernel, chunk, h3g_own, h3g_far, x1, b2, own, far, q2):
            return run(
                kernel, [one] * 3 + [((text_pad, model), BF16)] * 2 + [((8, model), F32), one_f32], place,
                [mod, h3g_own, h3g_far, kall, vall, cqt, co],
                late=[x1, b2, chunk_rows(cotangent, chunk), q2, own, far], cost=4.0 if chunk else 0.001,
            )

        b1g_a, dqa, b2ga, dka, dva, sums_a, x1ga = cross(
            cross_first, 0, h3ga, h3g_far_a, x1a, b2a, sum_a, far_a, q2a
        )
        in_send, out_send, b1g_a, h3g_far_b = tie(in_send, out_send, b1g_a, h3g_far_b)
        in_got, out_got, b1g_far_a = core_swap(in_send), core_swap(out_send), core_swap(b1g_a)
        b1g_b, dqb, b2gb, dkb, dvb, sums_b, x1gb = cross(
            cross_second, 1, h3gb, h3g_far_b, x1b, b2b, sum_b, far_b, q2b
        )
        in_got, out_got, b1g_far_a, b1g_b, dqb, b3a = tie(in_got, out_got, b1g_far_a, b1g_b, dqb, b3a)
        in_keep, in_give = added(in_own[0], in_got[0]), added(in_own[1], in_got[1])
        out_keep, out_give = added(out_own[0], out_got[0]), added(out_own[1], out_got[1])

        across = [(i, i ^ 1) for i in range(n_dp)]
        neighbours = [(i, i ^ 2) for i in range(n_dp)]
        middle_pair = [(2 * a + r, 2 * b + r) for a, b in ((1, 2), (2, 1)) for r in range(2)]
        chain_rows = (model // 2, model)

        class Rounds:
            def __init__(self):
                self.values, self.column_send, self.results, self.waiting = {}, None, [], []

            def start(self, *chain):
                self.got = {}
                if n_col != 4:
                    self.waiting += [chain] if chain else []
                    return
                if chain:
                    self.values["a"] = chain[0]
                    self.got["row"] = lax.ppermute(chain[1], "dp", across)
                if "e" in self.values:
                    self.got["last"] = lax.ppermute(self.values["e"], "dp", across)
                if "b" in self.values or "d" in self.values:
                    self.got["column"] = lax.ppermute(self.column_send, "dp", neighbours)
                if "c" in self.values:
                    self.got["middle"] = lax.ppermute(self.values["c"], "dp", middle_pair)

            def finish(self, *others, early=()):
                order = [name for name in ("row", "last", "column", "middle") if name in self.got]
                settled = list(early)
                for name in order:
                    settled = list(tie(self.got[name], *settled))
                tied = tie(*settled, *others)
                self.got = dict(zip(reversed(order), tied))
                others = tied[len(order) :]
                if "last" in self.got:
                    self.results.append((self.values.pop("e"), self.got.pop("last")))
                roles = "".join(role for role in "abcd" if role in self.values)
                if not roles:
                    return others
                operands = [self.values[role] for role in roles]
                operands += [self.got[name] for name in ("row", "column", "middle") if name in self.got]
                sends = "a" in roles or "c" in roles
                both = "a" in roles and "c" in roles
                outs = run(
                    functools.partial(advance_kernel, roles), [(chain_rows, BF16)] * (len(roles) + both),
                    place, operands, cost=0.3,
                )
                done = tie(*outs, *others)
                stepped = dict(zip(roles, done))
                if sends:
                    self.column_send = done[len(roles)] if both else stepped["a" if "a" in roles else "c"]
                self.values = {{"a": "b", "b": "c", "c": "d", "d": "e"}[role]: v for role, v in stepped.items()}
                return done[len(outs) :]

            def halves(self, number):
                return self.results[number] if n_col == 4 else self.slowly(*self.waiting[number])

            def whole(self, number):
                return run(join_rows, [((model, model), F32)], place, self.halves(number))[0]

            def four(self, number):
                return run(join_four, [((width, model), F32)] * 4, place, self.halves(number))

            def slowly(self, keep, give):
                total = added(keep, lax.ppermute(give, "dp", across))
                for bit in range(1, dp_bits):
                    size, flag = total.shape[0] // 2, (dp_at >> bit) & 1
                    sent = lax.dynamic_slice_in_dim(total, (1 - flag) * size, size, 0)
                    total = added(lax.dynamic_slice_in_dim(total, flag * size, size, 0), dp_swap(sent, 1 << bit))
                for bit in reversed(range(1, dp_bits)):
                    total = pair_up((dp_at >> bit) & 1, total, dp_swap(total, 1 << bit))
                return total, lax.ppermute(total, "dp", across)

        rounds = Rounds()

        rounds.start(in_keep, in_give)
        b1g_far_b = core_swap(b1g_b)
        b3_far_a = far_swap(b3a)
        cross_dw, cross_send = run(
            cross_weights, [((2, 2 * width, model), BF16)] * 2, place,
            [dqa, dqb, b2ga, b2gb, dka, dkb, dva, dvb], late=[h2a, h2b, cra, crb, text], cost=0.001,
        )
        b1g_far_b, cross_send = tie(b1g_far_b, cross_send)
        b1g_all, att_all, qa_all, da, dq_sum, dk_all, dv_all = run(
            self_back_first,
            [((count, model), BF16), ((count, width), BF16), (wide, BF16), (wide, BF16), (wide, F32)]
            + [((count, width), BF16)] * 2,
            place, [b1g_a, b1g_b, b1g_far_a, b1g_far_b],
            late=[o_weight, att_a, att_b, qa_a, qa_b, ka, va], cost=0.001,
        )
        b1g_all, cross_send, out_give, b3b, b3_far_a = rounds.finish(b1g_all, cross_send, out_give, b3b, b3_far_a)

        rounds.start(out_keep, out_give)
        cross_got = core_swap(cross_send)
        b3_far_b = far_swap(b3b)
        grad_own, grad_send, self_keep, self_give = run(
            self_back_second,
            [((half, model), BF16)] * 2 + [((2 * width, model), BF16)] * 2, place,
            [b1g_all, att_all, qa_all, da, dq_sum, dk_all, dv_all, self_weights], late=[ka, va, h1],
            scratch=[(wide, F32), ((count, 3 * width), BF16)],
        )
        cross_keep, cross_give = added(cross_dw[0], cross_got[0]), added(cross_dw[1], cross_got[1])
        grad_send, cross_give, self_give, b3_far_b = rounds.finish(grad_send, cross_give, self_give, b3_far_b)

        rounds.start(cross_keep, cross_give)
        h1g_own = added(grad_own, core_swap(grad_send))
        h1g_far = far_swap(h1g_own)
        mixed_a, mixed_b, sums_mixed = run(
            mixed_kernel, [one, one, ((2, 1, model), F32)],
            place, [mod, b3a, b3b, b3_far_a, b3_far_b, x2], late=[chunk_rows(cotangent, 0), chunk_rows(cotangent, 1)],
        )
        self_give, h1g_own, mixed_a, mixed_b = rounds.finish(self_give, h1g_own, mixed_a, mixed_b)

        rounds.start(self_keep, self_give)
        grad_a, grad_b, slot_sums = run(
            final_kernel, [one, one, ((slots, 9 * model), F32)],
            place, [mod, h1g_own, h1g_far, sums_a, sums_b, sums_mixed],
            late=[chunk_rows(tokens, 0), chunk_rows(tokens, 1), x1ga, x1gb],
        )
        grad_a, grad_b, slot_sums, mixed_a = rounds.finish(mixed_a, early=(grad_a, grad_b, slot_sums))

        rounds.start()
        slot_far = core_swap(slot_sums)
        mixed_far_a = core_swap(mixed_a)
        slot_far, mixed_far_a, mixed_b = rounds.finish(slot_far, mixed_far_a, mixed_b)

        rounds.start()
        (gathered,) = run(
            slot_kernel, [((slots, model + mod_weight.shape[1]), F32)], place, [slot_sums, slot_far, silu_low]
        )
        gathered = jnp.concatenate([gathered, dp_swap(gathered, 1)], axis=0)
        mixed_far_b = core_swap(mixed_b)
        gathered, mixed_far_b, grad_a, grad_b = rounds.finish(gathered, mixed_far_b, grad_a, grad_b)

        rounds.start()
        gathered = jnp.concatenate([gathered, dp_swap(gathered, 2)], axis=0)
        grad_far_a, grad_far_b = core_swap(grad_a), core_swap(grad_b)
        mlp_in_grad, mlp_out_grad = rounds.whole(0), rounds.whole(1)
        gathered, grad_far_a, grad_far_b, mlp_in_grad, mlp_out_grad = rounds.finish(
            gathered, grad_far_a, grad_far_b, mlp_in_grad, mlp_out_grad
        )

        rounds.start()
        for bit in range(2, dp_bits):
            gathered = jnp.concatenate([gathered, dp_swap(gathered, 1 << bit)], axis=0)
        (mixed,) = run(
            join_cores, [((count, model), BF16)], place, [mixed_a, mixed_b, mixed_far_a, mixed_far_b]
        )
        (token_grad,) = run(
            join_cores, [((count, model), BF16)], place, [grad_a, grad_b, grad_far_a, grad_far_b]
        )
        cross_grads = rounds.four(2)
        gathered_low = gathered.astype(BF16)
        mod_weight_grad = dot_tn(gathered_low[:, :model], gathered_low[:, model:])
        mod_bias_grad = jnp.sum(gathered[:, model:], axis=0)
        mixed, token_grad, mod_weight_grad, mod_bias_grad, *cross_grads = rounds.finish(
            mixed, token_grad, mod_weight_grad, mod_bias_grad, *cross_grads
        )
        self_grads = rounds.four(3)

        return (
            mixed,
            token_grad,
            self_grads[0].T,
            self_grads[1].T,
            self_grads[2].T,
            self_grads[3],
            cross_grads[0].T,
            cross_grads[1].T,
            cross_grads[2].T,
            cross_grads[3],
            mlp_in_grad,
            mlp_out_grad,
            mod_weight_grad,
            mod_bias_grad,
        )

    rows = P("dp", None)
    by_col = P(None, "tensor")
    by_row = P("tensor", None)
    return jax.shard_map(
        local,
        mesh=mesh,
        in_specs=(
            rows, P("dp", None, None), P("dp"), P("dp"), P("dp"), by_col, by_col, by_col, by_row,
            by_col, by_col, by_col, by_row, by_col, by_row, by_col, P("tensor"), rows,
        ),
        out_specs=(
            rows, rows, by_col, by_col, by_col, by_row, by_col, by_col, by_col, by_row,
            by_col, by_row, by_col, P("tensor"),
        ),
        check_vma=False,
    )
```

```python
import functools
import math

import jax
import jax.numpy as jnp
from jax import lax
from jax.experimental import pallas as pl
from jax.experimental.pallas import tpu as pltpu
from jax.sharding import PartitionSpec as P

HEAD = 64
BLOCK = 256
EPSILON = 1e-06
MASKED = -1000000000.0
CURVE = math.sqrt(2.0 / math.pi)
CUBIC = 0.044715
F32 = jnp.float32
BF16 = jnp.bfloat16


def dot_nn(a, b):
    return lax.dot_general(a, b, (((1,), (0,)), ((), ())), preferred_element_type=F32)


def dot_nt(a, b):
    return lax.dot_general(a, b, (((1,), (1,)), ((), ())), preferred_element_type=F32)


def dot_tn(a, b):
    return lax.dot_general(a, b, (((0,), (0,)), ((), ())), preferred_element_type=F32)


def normalize(values):
    centered = values - jnp.mean(values, axis=-1, keepdims=True)
    inverse = lax.rsqrt(jnp.mean(centered * centered, axis=-1, keepdims=True) + EPSILON)
    return centered * inverse, inverse


def norm_back(grad, normed, inverse):
    first = jnp.mean(grad, axis=-1, keepdims=True)
    second = jnp.mean(grad * normed, axis=-1, keepdims=True)
    return inverse * (grad - first - normed * second)


def column_sum(values):
    return jnp.sum(values, axis=0, keepdims=True)


def three_parts(column):
    high = column.astype(BF16).astype(F32)
    rest = column - high
    middle = rest.astype(BF16).astype(F32)
    return high, middle, rest - middle


def head_slice(rows, head):
    piece = rows[:, head * HEAD : (head + 1) * HEAD]
    return jnp.concatenate([piece, jnp.zeros_like(piece)], axis=1)


class View:
    def __init__(self, ref):
        self.view = ref

    def ref(self):
        return self.view


class Place:
    def __init__(self, ref):
        self.ref = ref

    def __getitem__(self, index):
        return self.ref[0, index]


def run(kernel, outs, scalars, arrays, late=(), scratch=(), cost=0.001, vmem=10):
    in_vmem = pl.BlockSpec(memory_space=pltpu.VMEM)
    pairs = [entry if isinstance(entry, tuple) else (entry, None) for entry in late]
    n_plain = len(arrays)

    def wrapped(place, *refs):
        place = Place(place)
        views = []
        for ref, (_, block) in zip(refs[n_plain:], pairs):
            views.append(View(ref if block is None else ref.at[token_rows(block(place)), :]))
        kernel(place, *refs[:n_plain], *views, *refs[n_plain + len(pairs) :])

    return pl.pallas_call(
        wrapped,
        name=getattr(kernel, "__name__", "advance"),
        out_shape=[jax.ShapeDtypeStruct(shape, kind) for shape, kind in outs],
        in_specs=[in_vmem] * (1 + n_plain + len(pairs)),
        out_specs=[in_vmem] * len(outs),
        scratch_shapes=[pltpu.VMEM(shape, kind) for shape, kind in scratch],
        compiler_params=pltpu.CompilerParams(vmem_limit_bytes=vmem * 1024 * 1024),
        cost_estimate=pl.CostEstimate(flops=int(cost * 1_000_000_000), bytes_accessed=1000, transcendentals=0),
    )(scalars, *arrays, *[array for array, _ in pairs])


SLOT, CORE, ROW, END, TENSOR, OWN, FAR, LIMIT = 0, 4, 5, 6, 7, 8, 10, 12
ORDER = (0, 2, 1, 3)


def block_of(place, chunk):
    return place[CORE] * 2 + chunk


def mod_row(mod, slot, component, model):
    return mod[pl.ds(slot, 1), component * model : (component + 1) * model]


def token_rows(block):
    return pl.ds(pl.multiple_of(block * BLOCK, BLOCK), BLOCK)


def text_kernel(place, text, weights, packed):
    rows = text.shape[1]
    wide = weights.shape[0]
    for slot in range(text.shape[0]):
        first = rows * (slot % 2)
        left = wide * (slot // 2)
        packed[first : first + rows, left : left + wide] = dot_nt(text[slot], weights[...]).astype(BF16)


def unpack_kernel(place, q0, o0, q1, o1, part2, rest2, part3, rest3, t0, t1, t2, t3, cqt, co, kall, vall):
    width = q0.shape[0]
    half = width // 2
    rows = kall.shape[1]
    for index, (query, out) in enumerate(((q0, o0), (q1, o1))):
        cqt[index * width : (index + 1) * width, :] = query[...]
        co[index * width : (index + 1) * width, :] = out[...]
    for index, (part, rest) in enumerate(((part2, rest2), (part3, rest3))):
        for piece, row in ((part, place[ROW]), (rest, 1 - place[ROW])):
            at = pl.ds(pl.multiple_of((index + 2) * width + row * half, half), half)
            cqt[at, :] = piece[:half, :]
            co[at, :] = piece[half:, :]
    for slot in range(kall.shape[0]):
        first = rows * (slot % 2)
        left = 2 * width * (slot // 2)
        both = [t[first : first + rows, left : left + 2 * width] for t in (t0, t1, t2, t3)]
        kall[slot] = jnp.concatenate([b[:, :width] for b in both], axis=1)
        vall[slot] = jnp.concatenate([b[:, width:] for b in both], axis=1)


def attend_chunk(place, chunk, qa_in, ka, va, wo, part_own, part_send, qa_out, att):
    heads = ka.shape[0]
    lane = lax.broadcasted_iota(jnp.int32, (BLOCK, 2 * HEAD), 1)
    spot = (lane >= HEAD + 4) & (lane < HEAD + 7)
    for side in range(2):
        at = (2 * chunk + side) * BLOCK
        here = slice(side * BLOCK, (side + 1) * BLOCK)
        pieces = []
        for head in range(heads):
            queries = qa_in[head, at : at + BLOCK, :]
            scores = dot_nt(queries, ka[head])
            top = jnp.max(scores, axis=1, keepdims=True)
            raised = jnp.exp(scores - top).astype(BF16)
            out = dot_nn(raised, va[head])
            total = out[:, HEAD : HEAD + 1]
            pieces.append(out[:, :HEAD] * (1.0 / total))
            high, middle, low = three_parts(-(top + jnp.log(total)))
            more = jnp.where(lane == HEAD + 4, high, jnp.where(lane == HEAD + 5, middle, low))
            qa_out[head, here, :] = jnp.where(spot, more, queries.astype(F32)).astype(BF16)
        attended = jnp.concatenate(pieces, axis=1).astype(BF16)
        att[here, :] = attended
        out = dot_nn(attended, wo[...]).astype(BF16)

        @pl.when(place[CORE] == side)
        def _():
            part_own[...] = out

        @pl.when(place[CORE] != side)
        def _():
            part_send[...] = out


def self_first(place, mod, weights, tokens, wo, part_own, part_send, qa, ka, va, qa_out, att, h1):
    model = mod.shape[1] // 9
    lane = lax.broadcasted_iota(jnp.int32, (BLOCK, 2 * HEAD), 1)
    keep = lane < HEAD
    width = weights.shape[0] // 3
    tokens = tokens.ref()
    for position, block in enumerate(ORDER):
        rows = slice(position * BLOCK, (position + 1) * BLOCK)
        slot = place[SLOT + block]
        normed, _ = normalize(tokens[block * BLOCK : (block + 1) * BLOCK, :].astype(F32))
        hidden = (normed * (1.0 + mod_row(mod, slot, 1, model)) + mod_row(mod, slot, 0, model)).astype(BF16)
        h1[rows, :] = hidden
        rows_qkv = dot_nt(hidden, weights[...])
        q = rows_qkv[:, :width].astype(BF16).astype(F32) * (HEAD**-0.5)
        k = rows_qkv[:, width : 2 * width]
        v = rows_qkv[:, 2 * width :]
        mine = lane == HEAD + slot
        q_more = jnp.where(mine, 1.0, 0.0)
        k_more = jnp.where((lane >= HEAD + 4) & (lane < HEAD + 7), 1.0, 0.0)
        k_more = jnp.where((lane >= HEAD) & (lane < HEAD + 4) & jnp.logical_not(mine), MASKED, k_more)
        v_more = jnp.where((lane >= HEAD) & (lane < HEAD + 3), 1.0, 0.0)
        for head in range(ka.shape[0]):
            qa[head, rows, :] = jnp.where(keep, head_slice(q, head), q_more).astype(BF16)
            ka[head, rows, :] = jnp.where(keep, head_slice(k, head), k_more).astype(BF16)
            va[head, rows, :] = jnp.where(keep, head_slice(v, head), v_more).astype(BF16)
    attend_chunk(place, 0, qa, ka, va, wo.ref(), part_own, part_send, qa_out, att)


def self_second(place, qa, ka, va, wo, part_own, part_send, qa_out, att):
    attend_chunk(place, 1, qa, ka, va, wo.ref(), part_own, part_send, qa_out, att)


def quad_stack(rows, masks):
    return jnp.concatenate([rows * mask for mask in masks], axis=0)


def quad_masks():
    lane = lax.broadcasted_iota(jnp.int32, (1, 4 * HEAD), 1)
    return [jnp.where((lane >= u * HEAD) & (lane < (u + 1) * HEAD), 1.0, 0.0) for u in range(4)]


def quad_probs(scores, limit, text_rows):
    key_row = lax.broadcasted_iota(jnp.int32, (text_rows, 1), 0)
    bias = jnp.where(key_row < limit, 0.0, MASKED)
    probs = []
    for u in range(4):
        part = scores[u * text_rows : (u + 1) * text_rows, :] + bias
        raised = jnp.exp(part - jnp.max(part, axis=0, keepdims=True))
        probs.append(raised * (1.0 / jnp.sum(raised, axis=0, keepdims=True)))
    return probs


def middle_chunk(
    place, chunk, mod, sum_own, sum_far, cqt, co, kall, vall, tokens, cot, win0, wout0, win1, wout1, x2_before,
    h3g_out, h3_out, act0, act1, pg0, pg1, b3g_out, x1_out, b2_out, h2_out, q2_out, cr_out, b3_out, x2_out,
):
    model = cqt.shape[1]
    text_rows = kall.shape[1]
    slot = place[OWN + chunk]

    def m(component):
        return mod_row(mod, slot, component, model)

    x1 = tokens.ref()[...].astype(F32) + m(2) * (sum_own[...].astype(F32) + sum_far[...].astype(F32))
    x1_out[...] = x1
    normed, _ = normalize(x1)
    h2 = (normed * (1.0 + m(4)) + m(3)).astype(BF16)
    h2_out[...] = h2
    q2 = (dot_nt(h2, cqt[...]).astype(BF16).astype(F32) * (HEAD**-0.5)).astype(BF16)
    q2_out[...] = q2
    masks = [mask.astype(BF16) for mask in quad_masks()]
    crossed = []
    for quad in range(model // (4 * HEAD)):
        cols = slice(quad * 4 * HEAD, (quad + 1) * 4 * HEAD)
        scores = dot_nt(quad_stack(kall[slot, :, cols], masks), q2[:, cols])
        probs = jnp.concatenate(quad_probs(scores, place[LIMIT + chunk], text_rows), axis=0)
        crossed.append(dot_tn(probs.astype(BF16), quad_stack(vall[slot, :, cols], masks)).astype(BF16))
    crossed = jnp.concatenate(crossed, axis=1)
    cr_out[...] = crossed
    b2 = dot_nn(crossed, co[...])
    b2_out[...] = b2
    x2 = x1 + m(5) * b2
    x2_out[chunk * BLOCK : (chunk + 1) * BLOCK, :] = x2
    normed, _ = normalize(x2)
    h3 = (normed * (1.0 + m(7)) + m(6)).astype(BF16)
    h3_out[...] = h3
    b3g = (cot.ref()[...].astype(F32) * m(8)).astype(BF16)
    b3g_out[...] = b3g
    b3 = h3g = None
    for win, wout, act_out, pg_out in ((win0, wout0, act0, pg0), (win1, wout1, act1, pg1)):
        win, wout = win.ref(), wout.ref()
        pre = dot_nn(h3, win[...])
        square = pre * pre
        bent = jnp.tanh(CURVE * (pre + CUBIC * (square * pre)))
        act = (0.5 * pre * (1.0 + bent)).astype(BF16)
        act_out[...] = act
        slope = 0.5 * (1.0 + bent) + 0.5 * pre * (1.0 - bent * bent) * (CURVE * (1.0 + 3.0 * CUBIC * square))
        b3_half = dot_nn(act, wout[...])
        pg = (dot_nt(b3g, wout[...]) * slope).astype(BF16)
        pg_out[...] = pg
        h3g_half = dot_nt(pg, win[...])
        b3 = b3_half if b3 is None else b3 + b3_half
        h3g = h3g_half if h3g is None else h3g + h3g_half
    b3_out[...] = b3.astype(BF16)
    if chunk:
        x2_out[0:BLOCK, :] = x2_before.ref()[...]
    h3g_out[...] = h3g.astype(BF16)


def middle_first(place, *refs):
    middle_chunk(place, 0, *refs[:13], None, *refs[13:])


def middle_second(place, *refs):
    middle_chunk(place, 1, *refs)


def stacked(first, second):
    return jnp.concatenate([first[...], second[...]], axis=0)


def mlp_back(
    place, h3a, h3b, pg0a, pg0b, pg1a, pg1b, act0a, act0b, act1a, act1b, b3ga, b3gb,
    in_own, in_send, out_own, out_send,
):
    half = in_own.shape[1]
    grads = (stacked(pg0a, pg0b), stacked(pg1a, pg1b))
    for part in range(2):
        cols = slice(part * half, (part + 1) * half)
        rows = jnp.concatenate([h3a[:, cols], h3b[:, cols]], axis=0)
        for out, grad in ((in_send, grads[1]), (in_own, grads[0])):
            out[part ^ place[ROW]] = dot_tn(rows, grad).astype(BF16)
    grad = stacked(b3ga, b3gb)
    for out, first, second in ((out_send, act1a, act1b), (out_own, act0a, act0b)):
        for part in range(2):
            cols = slice(part * half, (part + 1) * half)
            rows = jnp.concatenate([first[:, cols], second[:, cols]], axis=0)
            out[part ^ place[ROW]] = dot_tn(rows, grad).astype(BF16)


def cross_chunk(
    place, chunk, mod, h3g_own, h3g_far, kall, vall, cqt, co, x1_in, b2_in, cot, q2_in, sum_own, sum_far,
    b1g_out, dq_out, b2g_out, dk_out, dv_out, sums, x1g_out,
):
    model = cqt.shape[1]
    text_rows = kall.shape[1]
    slot = place[OWN + chunk]

    def m(component):
        return mod_row(mod, slot, component, model)

    x1 = x1_in.ref()[...]
    b2 = b2_in.ref()[...]
    h3g = h3g_own[...].astype(F32) + h3g_far[...].astype(F32)
    normed, inverse = normalize(x1 + m(5) * b2)
    sums[4:5, :] = column_sum(h3g)
    sums[5:6, :] = column_sum(h3g * normed)
    x2g = cot.ref()[...].astype(F32) + norm_back(h3g * (1.0 + m(7)), normed, inverse)
    sums[3:4, :] = column_sum(x2g * b2)
    b2g = (x2g * m(5)).astype(BF16)
    b2g_out[...] = b2g
    out_grad = dot_nt(b2g, co[...]).astype(BF16)
    masks = quad_masks()
    low = [mask.astype(BF16) for mask in masks]
    query_grads = []
    for quad in range(model // (4 * HEAD)):
        cols = slice(quad * 4 * HEAD, (quad + 1) * 4 * HEAD)
        queries = q2_in.ref()[:, cols]
        grads = out_grad[:, cols]
        keys = quad_stack(kall[slot, :, cols], low)
        values = quad_stack(vall[slot, :, cols], low)
        probs = quad_probs(dot_nt(keys, queries), place[LIMIT + chunk], text_rows)
        prob_grad = dot_nt(values, grads)
        score_grad = []
        for u in range(4):
            part = prob_grad[u * text_rows : (u + 1) * text_rows, :]
            row_dot = jnp.sum(probs[u] * part, axis=0, keepdims=True)
            score_grad.append((probs[u] * (part - row_dot)).astype(BF16))
        score_grad = jnp.concatenate(score_grad, axis=0)
        dv = dot_nn(jnp.concatenate(probs, axis=0).astype(BF16), grads)
        dk = dot_nn(score_grad, queries)
        query_grads.append((dot_tn(score_grad, keys) * (HEAD**-0.5)).astype(BF16))
        for wide, out in ((dk, dk_out), (dv, dv_out)):
            total = None
            for u in range(4):
                part = wide[u * text_rows : (u + 1) * text_rows, :] * masks[u]
                total = part if total is None else total + part
            out[:, cols] = total.astype(BF16)
    query_grad = jnp.concatenate(query_grads, axis=1)
    dq_out[...] = query_grad
    h2g = dot_nn(query_grad, cqt[...])
    normed, inverse = normalize(x1)
    sums[1:2, :] = column_sum(h2g)
    sums[2:3, :] = column_sum(h2g * normed)
    x1g = x2g + norm_back(h2g * (1.0 + m(4)), normed, inverse)
    x1g_out[...] = x1g
    branch = sum_own.ref()[...].astype(F32) + sum_far.ref()[...].astype(F32)
    sums[0:1, :] = column_sum(x1g * branch)
    sums[6:8, :] = jnp.zeros((2, model), F32)
    b1g_out[...] = (x1g * m(2)).astype(BF16)


def cross_first(place, *refs):
    cross_chunk(place, 0, *refs)


def cross_second(place, *refs):
    cross_chunk(place, 1, *refs)


def cross_weights(
    place, dqa, dqb, b2ga, b2gb, dka, dkb, dva, dvb, h2a, h2b, cra, crb, text, own, send,
):
    width = own.shape[1] // 2
    row = place[ROW]
    h2a, h2b, cra, crb, text = h2a.ref(), h2b.ref(), cra.ref(), crb.ref(), text.ref()
    hidden = stacked(h2a, h2b)
    grads = stacked(b2ga, b2gb)
    texts = [text[place[OWN + chunk]] for chunk in range(2)]
    for member, out in ((1, send), (0, own)):
        start = (member * width // 128) * 128
        skip = member * width - start
        cols = slice(start, start + 2 * 128)
        kept = slice(skip, skip + width)

        def two(first, second):
            return jnp.concatenate([first[:, cols], second[:, cols]], axis=0)

        top, bottom = slice(0, width), slice(width, 2 * width)
        out[row, top] = dot_tn(two(dqa, dqb), hidden)[kept].astype(BF16)
        out[row, bottom] = (dot_tn(dka[:, cols], texts[0]) + dot_tn(dkb[:, cols], texts[1]))[kept].astype(BF16)
        out[1 - row, top] = (dot_tn(dva[:, cols], texts[0]) + dot_tn(dvb[:, cols], texts[1]))[kept].astype(BF16)
        out[1 - row, bottom] = dot_tn(two(cra, crb), grads)[kept].astype(BF16)


def keys_back(block, first, qa, ka, va, da, dq_sum):
    rows = token_rows(block)
    dks = []
    dvs = []
    for head in range(ka.shape[0]):
        keys = ka[head, rows, :]
        probs = jnp.exp(dot_nt(keys, qa[head]))
        prob_grad = dot_nt(va[head, rows, :], da[head])
        score_grad = (probs * prob_grad).astype(BF16)
        dvs.append(dot_nn(probs.astype(BF16), da[head])[:, :HEAD])
        dks.append(dot_nn(score_grad, qa[head])[:, :HEAD])
        dq = dot_tn(score_grad, keys)
        dq_sum[head] = dq if first else dq_sum[head] + dq
    return jnp.concatenate(dks, axis=1).astype(BF16), jnp.concatenate(dvs, axis=1).astype(BF16)


def self_back_first(
    place, b1g_a, b1g_b, far_a, far_b, wo, att_a, att_b, qa_a, qa_b, ka, va,
    b1g, att, qa, da, dq_sum, dk_all, dv_all,
):
    blocks = b1g.shape[0] // BLOCK
    heads = da.shape[0]
    core = place[CORE]
    for chunk, (own, far) in enumerate(((b1g_a, far_a), (b1g_b, far_b))):
        b1g[token_rows(2 * chunk + core), :] = own[...]
        b1g[token_rows(2 * chunk + 1 - core), :] = far[...]
    wo = wo.ref()
    att[0 : 2 * BLOCK, :] = att_a.ref()[...]
    att[2 * BLOCK : 4 * BLOCK, :] = att_b.ref()[...]
    lane = lax.broadcasted_iota(jnp.int32, (BLOCK, 2 * HEAD), 1)
    for block in range(blocks):
        rows = slice(block * BLOCK, (block + 1) * BLOCK)
        grads = dot_nt(b1g[rows, :], wo[...]).astype(BF16).astype(F32)
        dots = grads * att[rows, :].astype(F32)
        for head in range(heads):
            row_dot = jnp.sum(dots[:, head * HEAD : (head + 1) * HEAD], axis=1, keepdims=True)
            high, middle, low = three_parts(-row_dot)
            more = jnp.where(lane == HEAD, high, jnp.where(lane == HEAD + 1, middle, low))
            more = jnp.where(lane < HEAD + 3, more, 0.0)
            da[head, rows, :] = jnp.where(lane < HEAD, head_slice(grads, head), more).astype(BF16)
    qa[:, 0 : 2 * BLOCK, :] = qa_a.ref()[...]
    qa[:, 2 * BLOCK : 4 * BLOCK, :] = qa_b.ref()[...]
    ka, va = ka.ref(), va.ref()
    for block in range(2):
        rows = slice(block * BLOCK, (block + 1) * BLOCK)
        dk_all[rows, :], dv_all[rows, :] = keys_back(block, block == 0, qa, ka, va, da, dq_sum)


def self_back_second(
    place, b1g, att, qa, da, dq_in, dk_in, dv_in, weights, ka, va, h1,
    part_own, part_send, dw_keep, dw_give,
    dq_sum, grad_all,
):
    blocks = b1g.shape[0] // BLOCK
    heads = da.shape[0]
    core = place[CORE]
    width = heads * HEAD
    ka, va = ka.ref(), va.ref()
    dq_sum[...] = dq_in[...]
    grad_all[0 : 2 * BLOCK, width : 2 * width] = dk_in[0 : 2 * BLOCK, :]
    grad_all[0 : 2 * BLOCK, 2 * width : 3 * width] = dv_in[0 : 2 * BLOCK, :]
    for block in range(2, blocks):
        rows = slice(block * BLOCK, (block + 1) * BLOCK)
        dk, dv = keys_back(block, False, qa, ka, va, da, dq_sum)
        grad_all[rows, width : 2 * width] = dk
        grad_all[rows, 2 * width : 3 * width] = dv
    h1 = h1.ref()
    for block in range(blocks):
        rows = slice(block * BLOCK, (block + 1) * BLOCK)
        dq = jnp.concatenate([dq_sum[head, rows, :HEAD] for head in range(heads)], axis=1)
        grad_all[rows, 0:width] = (dq * (HEAD**-0.5)).astype(BF16)
        out = dot_nn(grad_all[rows, :], weights[...]).astype(BF16)
        chunk, side = block // 2, block % 2
        out_rows = slice(chunk * BLOCK, (chunk + 1) * BLOCK)

        @pl.when(core == side)
        def _():
            part_own[out_rows, :] = out

        @pl.when(core != side)
        def _():
            part_send[out_rows, :] = out

    grads = dot_tn(grad_all[...], h1[...]).astype(BF16)
    query_key = (grads[:width], grads[width : 2 * width])
    value_out = (grads[2 * width :], dot_tn(att[...], b1g[...]).astype(BF16))
    for flag, first, second in ((0, query_key, value_out), (1, value_out, query_key)):

        @pl.when(place[ROW] == flag)
        def _():
            for index in range(2):
                rows = slice(index * width, (index + 1) * width)
                dw_keep[rows, :] = first[index]
                dw_give[rows, :] = second[index]


def mixed_kernel(place, mod, b3a, b3b, far_a, far_b, x2, cot_a, cot_b, mixed_a, mixed_b, sums):
    model = mixed_a.shape[1]
    for chunk, (own, far, cot) in enumerate(((b3a, far_a, cot_a), (b3b, far_b, cot_b))):
        mixed = (mixed_a, mixed_b)[chunk]
        rows = slice(chunk * BLOCK, (chunk + 1) * BLOCK)
        slot = place[OWN + chunk]
        b3 = own[...].astype(F32) + far[...].astype(F32)
        mixed[...] = (x2[rows, :] + mod_row(mod, slot, 8, model) * b3).astype(BF16)
        sums[chunk] = column_sum(cot.ref()[...].astype(F32) * b3)


def final_kernel(
    place, mod, h1g_own, h1g_far, sums_a, sums_b, sums_mixed, tokens_a, tokens_b, x1ga, x1gb, grad_a, grad_b, slot_sums,
):
    model = grad_a.shape[1]
    slot_sums[...] = jnp.zeros_like(slot_sums)
    for chunk, (x1g, sums, tokens) in enumerate(((x1ga, sums_a, tokens_a), (x1gb, sums_b, tokens_b))):
        rows = slice(chunk * BLOCK, (chunk + 1) * BLOCK)
        slot = place[OWN + chunk]
        h1g = h1g_own[rows, :].astype(F32) + h1g_far[rows, :].astype(F32)
        normed, inverse = normalize(tokens.ref()[...].astype(F32))
        scaled = h1g * (1.0 + mod_row(mod, slot, 1, model))
        (grad_a, grad_b)[chunk][...] = (x1g.ref()[...] + norm_back(scaled, normed, inverse)).astype(BF16)
        terms = [column_sum(h1g), column_sum(h1g * normed)]
        terms += [sums[i : i + 1, :] for i in range(6)] + [sums_mixed[chunk]]
        for component, term in enumerate(terms):
            slot_sums[pl.ds(slot, 1), component * model : (component + 1) * model] += term


def join_cores(place, mine_a, mine_b, other_a, other_b, out):
    for chunk, (mine, other) in enumerate(((mine_a, other_a), (mine_b, other_b))):
        out[token_rows(place[CORE] * 2 + chunk), :] = mine[...]
        out[token_rows((1 - place[CORE]) * 2 + chunk), :] = other[...]


def join_rows(place, mine, other, out):
    count = mine.shape[0]
    out[pl.ds(pl.multiple_of(place[ROW] * count, BLOCK // 2), count), :] = mine[...].astype(F32)
    out[pl.ds(pl.multiple_of((1 - place[ROW]) * count, BLOCK // 2), count), :] = other[...].astype(F32)


def join_four(place, mine, other, first, second, third, fourth):
    width = first.shape[0]
    for flag, top, bottom in ((0, mine, other), (1, other, mine)):

        @pl.when(place[ROW] == flag)
        def _():
            first[...] = top[:width, :].astype(F32)
            second[...] = top[width:, :].astype(F32)
            third[...] = bottom[:width, :].astype(F32)
            fourth[...] = bottom[width:, :].astype(F32)


def slot_kernel(place, own, far, silu, out):
    model = silu.shape[1]
    count = out.shape[1] - model
    out[:, :model] = silu[...].astype(F32)
    for index in range(own.shape[1] // count):
        cols = slice(index * count, (index + 1) * count)

        @pl.when(place[TENSOR] == index)
        def _():
            out[:, model:] = (own[:, cols] + far[:, cols]).astype(BF16).astype(F32)


def advance_kernel(roles, place, *refs):
    refs = list(refs)
    values, got = {}, {}
    for role in roles:
        values[role] = refs.pop(0)
    for name in ("row", "column", "middle"):
        if any(role in roles for role in {"row": "a", "column": "bd", "middle": "c"}[name]):
            got[name] = refs.pop(0)
    outs = {role: refs.pop(0) for role in roles}
    end = place[END]
    if "a" in roles:
        outs["a"][...] = added(values["a"][...], got["row"][...])
    if "c" in roles:

        @pl.when(end == 0)
        def _():
            outs["c"][...] = added(values["c"][...], got["middle"][...])

        @pl.when(end != 0)
        def _():
            outs["c"][...] = values["c"][...]

    if "b" in roles:

        @pl.when(end == 0)
        def _():
            outs["b"][...] = added(values["b"][...], got["column"][...])

        @pl.when(end != 0)
        def _():
            outs["b"][...] = values["b"][...]

    if "d" in roles:

        @pl.when(end == 0)
        def _():
            outs["d"][...] = values["d"][...]

        @pl.when(end != 0)
        def _():
            outs["d"][...] = got["column"][...]

    if refs:

        @pl.when(end == 0)
        def _():
            refs[0][...] = outs["c"][...]

        @pl.when(end != 0)
        def _():
            refs[0][...] = outs["a"][...]


def added(first, second):
    return (first.astype(F32) + second.astype(F32)).astype(BF16)


def solution(mesh):
    n_dp = mesh.shape["dp"]
    n_tensor = mesh.shape["tensor"]
    n_col = n_dp // 2
    dp_bits = int(math.log2(n_dp))

    def tensor_swap(value, flip):
        return lax.ppermute(value, "tensor", [(i, i ^ flip) for i in range(n_tensor)])

    def core_swap(value):
        return tensor_swap(value, 1)

    def far_swap(value):
        return tensor_swap(value, 2)

    def dp_swap(value, flip):
        return lax.ppermute(value, "dp", [(i, i ^ flip) for i in range(n_dp)])

    def tie(*values):
        return lax.optimization_barrier(values) if values else ()

    def pair_up(flag, mine, other):
        return jnp.concatenate([jnp.where(flag == 0, mine, other), jnp.where(flag == 0, other, mine)], axis=0)

    def local(
        tokens, text_states, clip_len, text_len, timesteps, q_weight, k_weight, v_weight, o_weight,
        cross_q, cross_k, cross_v, cross_o, mlp_in, mlp_out, mod_weight, mod_bias, cotangent,
    ):
        count, model = tokens.shape
        slots, text_rows = text_states.shape[:2]
        width = o_weight.shape[0]
        heads = width // HEAD
        half = count // 2
        text_pad = -(-text_rows // 16) * 16
        tensor_at = lax.axis_index("tensor")
        dp_at = lax.axis_index("dp")
        core = tensor_at & 1
        row = dp_at & 1
        column = dp_at >> 1

        ends = jnp.cumsum(clip_len)
        starts = jnp.arange(count // BLOCK, dtype=jnp.int32) * BLOCK
        slot_of = jnp.sum((starts[:, None] >= ends[None, :]).astype(jnp.int32), axis=1)
        end = (column == 0) | (column == n_col - 1)
        own_slots = lax.dynamic_slice_in_dim(slot_of, core * 2, 2, 0)
        far_slots = lax.dynamic_slice_in_dim(slot_of, (1 - core) * 2, 2, 0)
        limits = jnp.sum(jnp.where(own_slots[:, None] == jnp.arange(slots)[None, :], text_len[None, :], 0), axis=1)
        single = jnp.stack([core, row, end.astype(jnp.int32), tensor_at])
        place = jnp.concatenate([slot_of, single, own_slots, far_slots, limits])
        place = jnp.pad(place[None, :], ((0, 7), (0, 128 - place.shape[0])))
        place = place.astype(jnp.int32)

        query_own = cross_q.T
        part_own = jnp.concatenate(
            [lax.dynamic_slice_in_dim(w, row * (width // 2), width // 2, 0) for w in (query_own, cross_o)], axis=0
        )
        text_weights = jnp.concatenate([cross_k.T, cross_v.T], axis=0)
        text = jnp.pad(text_states, ((0, 0), (0, text_pad - text_rows), (0, 0)))
        self_weights = jnp.concatenate([q_weight.T, k_weight.T, v_weight.T], axis=0)

        half_width = model // 2
        ramp = jnp.arange(half_width).astype(F32)
        frequency = jnp.exp(ramp * (-math.log(10000.0) / half_width))
        angles = timesteps.astype(F32)[:, None] * frequency[None, :]
        embed = jnp.concatenate([jnp.cos(angles), jnp.sin(angles)], axis=1)
        silu_low = jax.nn.silu(embed).astype(BF16)
        part_far = far_swap(part_own)
        wout1 = core_swap(mlp_out)
        mod_own = dot_nn(silu_low, mod_weight) + mod_bias.astype(F32)
        mod_far = [tensor_swap(mod_own, flip) for flip in range(1, n_tensor)]
        (text_own,) = run(text_kernel, [((2 * text_pad, model), BF16)], place, [text, text_weights], cost=1.0)
        text_own, self_weights, wout1, *mod_far = tie(text_own, self_weights, wout1, *mod_far)
        text_far = far_swap(text_own)
        query_own, out_own, text_own = tie(query_own, cross_o, text_own)
        query1, out1, text1 = core_swap(query_own), core_swap(out_own), core_swap(text_own)
        mod_all = jnp.stack([mod_own] + mod_far)
        mod = jnp.concatenate(
            [lax.dynamic_index_in_dim(mod_all, tensor_at ^ j, 0, keepdims=False) for j in range(n_tensor)], axis=1
        )

        wide = (heads, count, 2 * HEAD)
        block_wide = (heads, 2 * BLOCK, 2 * HEAD)
        one = ((BLOCK, model), BF16)
        one_f32 = ((BLOCK, model), F32)
        attend_far = [(block_wide, BF16), ((2 * BLOCK, width), BF16)]
        own_a, send_a, qa, ka, va, qa_a, att_a, h1 = run(
            self_first, [one, one] + [(wide, BF16)] * 3 + attend_far + [((count, model), BF16)], place, [mod, self_weights], cost=0.001,
            late=[tokens, o_weight],
        )
        send_a, part_far, text_far, query1, out1, text1 = tie(send_a, part_far, text_far, query1, out1, text1)
        sum_a = added(own_a, core_swap(send_a))
        sum_a, qa, part_far, text_far, win0 = tie(sum_a, qa, part_far, text_far, mlp_in)
        far_a = far_swap(sum_a)
        rest_far = dp_swap(part_far, 1)
        part3, text3, win1 = core_swap(part_far), core_swap(text_far), core_swap(win0)
        own_b, send_b, qa_b, att_b = run(
            self_second, [one, one] + attend_far, place, [qa, ka, va], late=[o_weight]
        )
        (far_a,) = tie(far_a)
        send_b, far_a, rest_far, part3, text3, win1 = tie(send_b, far_a, rest_far, part3, text3, win1)
        rest3 = core_swap(rest_far)
        sum_b = added(own_b, core_swap(send_b))
        sum_b, rest3 = tie(sum_b, rest3)
        far_b = far_swap(sum_b)
        cqt, co, kall, vall = run(
            unpack_kernel, [((model, model), BF16)] * 2 + [((slots, text_pad, model), BF16)] * 2,
            place,
            [query_own, out_own, query1, out1, part_far, rest_far, part3, rest3, text_own, text1, text_far, text3],
            cost=0.001,
        )
        shared = [cqt, co, kall, vall]

        def chunk_rows(array, chunk):
            return (array, functools.partial(block_of, chunk=chunk))

        def middle(kernel, chunk, own, far, *before):
            return run(
                kernel, [one] * 7 + [one_f32, one_f32] + [one] * 4 + [(((chunk + 1) * BLOCK, model), F32)], place,
                [mod, own, far] + shared, cost=7.5,
                late=[chunk_rows(tokens, chunk), chunk_rows(cotangent, chunk), mlp_in, mlp_out, win1, wout1, *before],
            )

        h3ga, h3a, act0a, act1a, pg0a, pg1a, b3ga, x1a, b2a, h2a, q2a, cra, b3a, x2a = middle(
            middle_first, 0, sum_a, far_a
        )
        h3ga, far_b = tie(h3ga, far_b)
        h3g_far_a = far_swap(h3ga)
        h3gb, h3b, act0b, act1b, pg0b, pg1b, b3gb, x1b, b2b, h2b, q2b, crb, b3b, x2 = middle(
            middle_second, 1, sum_b, far_b, x2a
        )
        h3gb, pg0b, h3g_far_a = tie(h3gb, pg0b, h3g_far_a)
        h3g_far_b = far_swap(h3gb)

        in_own, in_send, out_own, out_send = run(
            mlp_back, [((2, model // 2, model), BF16)] * 4, place,
            [h3a, h3b, pg0a, pg0b, pg1a, pg1b, act0a, act0b, act1a, act1b, b3ga, b3gb], cost=0.001,
        )

        def cross(kernel, chunk, h3g_own, h3g_far, x1, b2, own, far, q2):
            return run(
                kernel, [one] * 3 + [((text_pad, model), BF16)] * 2 + [((8, model), F32), one_f32], place,
                [mod, h3g_own, h3g_far, kall, vall, cqt, co],
                late=[x1, b2, chunk_rows(cotangent, chunk), q2, own, far], cost=4.0 if chunk else 0.001,
            )

        b1g_a, dqa, b2ga, dka, dva, sums_a, x1ga = cross(
            cross_first, 0, h3ga, h3g_far_a, x1a, b2a, sum_a, far_a, q2a
        )
        in_send, out_send, b1g_a, h3g_far_b = tie(in_send, out_send, b1g_a, h3g_far_b)
        in_got, out_got, b1g_far_a = core_swap(in_send), core_swap(out_send), core_swap(b1g_a)
        b1g_b, dqb, b2gb, dkb, dvb, sums_b, x1gb = cross(
            cross_second, 1, h3gb, h3g_far_b, x1b, b2b, sum_b, far_b, q2b
        )
        in_got, out_got, b1g_far_a, b1g_b, dqb, b3a = tie(in_got, out_got, b1g_far_a, b1g_b, dqb, b3a)
        in_keep, in_give = added(in_own[0], in_got[0]), added(in_own[1], in_got[1])
        out_keep, out_give = added(out_own[0], out_got[0]), added(out_own[1], out_got[1])

        across = [(i, i ^ 1) for i in range(n_dp)]
        neighbours = [(i, i ^ 2) for i in range(n_dp)]
        middle_pair = [(2 * a + r, 2 * b + r) for a, b in ((1, 2), (2, 1)) for r in range(2)]
        chain_rows = (model // 2, model)

        class Rounds:
            def __init__(self):
                self.values, self.column_send, self.results, self.waiting = {}, None, [], []

            def start(self, *chain):
                self.got = {}
                if n_col != 4:
                    self.waiting += [chain] if chain else []
                    return
                if chain:
                    self.values["a"] = chain[0]
                    self.got["row"] = lax.ppermute(chain[1], "dp", across)
                if "e" in self.values:
                    self.got["last"] = lax.ppermute(self.values["e"], "dp", across)
                if "b" in self.values or "d" in self.values:
                    self.got["column"] = lax.ppermute(self.column_send, "dp", neighbours)
                if "c" in self.values:
                    self.got["middle"] = lax.ppermute(self.values["c"], "dp", middle_pair)

            def finish(self, *others, early=()):
                order = [name for name in ("row", "last", "column", "middle") if name in self.got]
                settled = list(early)
                for name in order:
                    settled = list(tie(self.got[name], *settled))
                tied = tie(*settled, *others)
                self.got = dict(zip(reversed(order), tied))
                others = tied[len(order) :]
                if "last" in self.got:
                    self.results.append((self.values.pop("e"), self.got.pop("last")))
                roles = "".join(role for role in "abcd" if role in self.values)
                if not roles:
                    return others
                operands = [self.values[role] for role in roles]
                operands += [self.got[name] for name in ("row", "column", "middle") if name in self.got]
                sends = "a" in roles or "c" in roles
                both = "a" in roles and "c" in roles
                outs = run(
                    functools.partial(advance_kernel, roles), [(chain_rows, BF16)] * (len(roles) + both),
                    place, operands, cost=0.3,
                )
                done = tie(*outs, *others)
                stepped = dict(zip(roles, done))
                if sends:
                    self.column_send = done[len(roles)] if both else stepped["a" if "a" in roles else "c"]
                self.values = {{"a": "b", "b": "c", "c": "d", "d": "e"}[role]: v for role, v in stepped.items()}
                return done[len(outs) :]

            def halves(self, number):
                return self.results[number] if n_col == 4 else self.slowly(*self.waiting[number])

            def whole(self, number):
                return run(join_rows, [((model, model), F32)], place, self.halves(number))[0]

            def four(self, number):
                return run(join_four, [((width, model), F32)] * 4, place, self.halves(number))

            def slowly(self, keep, give):
                total = added(keep, lax.ppermute(give, "dp", across))
                for bit in range(1, dp_bits):
                    size, flag = total.shape[0] // 2, (dp_at >> bit) & 1
                    sent = lax.dynamic_slice_in_dim(total, (1 - flag) * size, size, 0)
                    total = added(lax.dynamic_slice_in_dim(total, flag * size, size, 0), dp_swap(sent, 1 << bit))
                for bit in reversed(range(1, dp_bits)):
                    total = pair_up((dp_at >> bit) & 1, total, dp_swap(total, 1 << bit))
                return total, lax.ppermute(total, "dp", across)

        rounds = Rounds()

        rounds.start(in_keep, in_give)
        b1g_far_b = core_swap(b1g_b)
        b3_far_a = far_swap(b3a)
        cross_dw, cross_send = run(
            cross_weights, [((2, 2 * width, model), BF16)] * 2, place,
            [dqa, dqb, b2ga, b2gb, dka, dkb, dva, dvb], late=[h2a, h2b, cra, crb, text], cost=0.001,
        )
        b1g_far_b, cross_send = tie(b1g_far_b, cross_send)
        b1g_all, att_all, qa_all, da, dq_sum, dk_all, dv_all = run(
            self_back_first,
            [((count, model), BF16), ((count, width), BF16), (wide, BF16), (wide, BF16), (wide, F32)]
            + [((count, width), BF16)] * 2,
            place, [b1g_a, b1g_b, b1g_far_a, b1g_far_b],
            late=[o_weight, att_a, att_b, qa_a, qa_b, ka, va], cost=0.001,
        )
        b1g_all, cross_send, out_give, b3b, b3_far_a = rounds.finish(b1g_all, cross_send, out_give, b3b, b3_far_a)

        rounds.start(out_keep, out_give)
        cross_got = core_swap(cross_send)
        b3_far_b = far_swap(b3b)
        grad_own, grad_send, self_keep, self_give = run(
            self_back_second,
            [((half, model), BF16)] * 2 + [((2 * width, model), BF16)] * 2, place,
            [b1g_all, att_all, qa_all, da, dq_sum, dk_all, dv_all, self_weights], late=[ka, va, h1],
            scratch=[(wide, F32), ((count, 3 * width), BF16)],
        )
        cross_keep, cross_give = added(cross_dw[0], cross_got[0]), added(cross_dw[1], cross_got[1])
        grad_send, cross_give, self_give, b3_far_b = rounds.finish(grad_send, cross_give, self_give, b3_far_b)

        rounds.start(cross_keep, cross_give)
        h1g_own = added(grad_own, core_swap(grad_send))
        h1g_far = far_swap(h1g_own)
        mixed_a, mixed_b, sums_mixed = run(
            mixed_kernel, [one, one, ((2, 1, model), F32)],
            place, [mod, b3a, b3b, b3_far_a, b3_far_b, x2], late=[chunk_rows(cotangent, 0), chunk_rows(cotangent, 1)],
        )
        self_give, h1g_own, mixed_a, mixed_b = rounds.finish(self_give, h1g_own, mixed_a, mixed_b)

        rounds.start(self_keep, self_give)
        grad_a, grad_b, slot_sums = run(
            final_kernel, [one, one, ((slots, 9 * model), F32)],
            place, [mod, h1g_own, h1g_far, sums_a, sums_b, sums_mixed],
            late=[chunk_rows(tokens, 0), chunk_rows(tokens, 1), x1ga, x1gb],
        )
        grad_a, grad_b, slot_sums, mixed_a = rounds.finish(mixed_a, early=(grad_a, grad_b, slot_sums))

        rounds.start()
        slot_far = core_swap(slot_sums)
        mixed_far_a = core_swap(mixed_a)
        slot_far, mixed_far_a, mixed_b = rounds.finish(slot_far, mixed_far_a, mixed_b)

        rounds.start()
        (gathered,) = run(
            slot_kernel, [((slots, model + mod_weight.shape[1]), F32)], place, [slot_sums, slot_far, silu_low]
        )
        gathered = jnp.concatenate([gathered, dp_swap(gathered, 1)], axis=0)
        mixed_far_b = core_swap(mixed_b)
        gathered, mixed_far_b, grad_a, grad_b = rounds.finish(gathered, mixed_far_b, grad_a, grad_b)

        rounds.start()
        gathered = jnp.concatenate([gathered, dp_swap(gathered, 2)], axis=0)
        grad_far_a, grad_far_b = core_swap(grad_a), core_swap(grad_b)
        mlp_in_grad, mlp_out_grad = rounds.whole(0), rounds.whole(1)
        gathered, grad_far_a, grad_far_b, mlp_in_grad, mlp_out_grad = rounds.finish(
            gathered, grad_far_a, grad_far_b, mlp_in_grad, mlp_out_grad
        )

        rounds.start()
        for bit in range(2, dp_bits):
            gathered = jnp.concatenate([gathered, dp_swap(gathered, 1 << bit)], axis=0)
        (mixed,) = run(
            join_cores, [((count, model), BF16)], place, [mixed_a, mixed_b, mixed_far_a, mixed_far_b]
        )
        (token_grad,) = run(
            join_cores, [((count, model), BF16)], place, [grad_a, grad_b, grad_far_a, grad_far_b]
        )
        cross_grads = rounds.four(2)
        gathered_low = gathered.astype(BF16)
        mod_weight_grad = dot_tn(gathered_low[:, :model], gathered_low[:, model:])
        mod_bias_grad = jnp.sum(gathered[:, model:], axis=0)
        mixed, token_grad, mod_weight_grad, mod_bias_grad, *cross_grads = rounds.finish(
            mixed, token_grad, mod_weight_grad, mod_bias_grad, *cross_grads
        )
        self_grads = rounds.four(3)

        return (
            mixed,
            token_grad,
            self_grads[0].T,
            self_grads[1].T,
            self_grads[2].T,
            self_grads[3],
            cross_grads[0].T,
            cross_grads[1].T,
            cross_grads[2].T,
            cross_grads[3],
            mlp_in_grad,
            mlp_out_grad,
            mod_weight_grad,
            mod_bias_grad,
        )

    rows = P("dp", None)
    by_col = P(None, "tensor")
    by_row = P("tensor", None)
    return jax.shard_map(
        local,
        mesh=mesh,
        in_specs=(
            rows, P("dp", None, None), P("dp"), P("dp"), P("dp"), by_col, by_col, by_col, by_row,
            by_col, by_col, by_col, by_row, by_col, by_row, by_col, P("tensor"), rows,
        ),
        out_specs=(
            rows, rows, by_col, by_col, by_col, by_row, by_col, by_col, by_col, by_row,
            by_col, by_row, by_col, P("tensor"),
        ),
        check_vma=False,
    )
```

```python
import functools
import math

import jax
import jax.numpy as jnp
from jax import lax
from jax.experimental import pallas as pl
from jax.experimental.pallas import tpu as pltpu
from jax.sharding import PartitionSpec as P

HEAD = 64
BLOCK = 256
EPSILON = 1e-06
MASKED = -1000000000.0
CURVE = math.sqrt(2.0 / math.pi)
CUBIC = 0.044715
F32 = jnp.float32
BF16 = jnp.bfloat16


def dot_nn(a, b):
    return lax.dot_general(a, b, (((1,), (0,)), ((), ())), preferred_element_type=F32)


def dot_nt(a, b):
    return lax.dot_general(a, b, (((1,), (1,)), ((), ())), preferred_element_type=F32)


def dot_tn(a, b):
    return lax.dot_general(a, b, (((0,), (0,)), ((), ())), preferred_element_type=F32)


def normalize(values):
    centered = values - jnp.mean(values, axis=-1, keepdims=True)
    inverse = lax.rsqrt(jnp.mean(centered * centered, axis=-1, keepdims=True) + EPSILON)
    return centered * inverse, inverse


def norm_back(grad, normed, inverse):
    first = jnp.mean(grad, axis=-1, keepdims=True)
    second = jnp.mean(grad * normed, axis=-1, keepdims=True)
    return inverse * (grad - first - normed * second)


def column_sum(values):
    return jnp.sum(values, axis=0, keepdims=True)


def three_parts(column):
    high = column.astype(BF16).astype(F32)
    rest = column - high
    middle = rest.astype(BF16).astype(F32)
    return high, middle, rest - middle


def head_slice(rows, head):
    piece = rows[:, head * HEAD : (head + 1) * HEAD]
    return jnp.concatenate([piece, jnp.zeros_like(piece)], axis=1)


class View:
    def __init__(self, ref):
        self.view = ref

    def ref(self):
        return self.view


class Place:
    def __init__(self, ref):
        self.ref = ref

    def __getitem__(self, index):
        return self.ref[0, index]


def run(kernel, outs, scalars, arrays, late=(), scratch=(), cost=0.001, vmem=10):
    in_vmem = pl.BlockSpec(memory_space=pltpu.VMEM)
    pairs = [entry if isinstance(entry, tuple) else (entry, None) for entry in late]
    n_plain = len(arrays)

    def wrapped(place, *refs):
        place = Place(place)
        views = []
        for ref, (_, block) in zip(refs[n_plain:], pairs):
            views.append(View(ref if block is None else ref.at[token_rows(block(place)), :]))
        kernel(place, *refs[:n_plain], *views, *refs[n_plain + len(pairs) :])

    return pl.pallas_call(
        wrapped,
        name=getattr(kernel, "__name__", "advance"),
        out_shape=[jax.ShapeDtypeStruct(shape, kind) for shape, kind in outs],
        in_specs=[in_vmem] * (1 + n_plain + len(pairs)),
        out_specs=[in_vmem] * len(outs),
        scratch_shapes=[pltpu.VMEM(shape, kind) for shape, kind in scratch],
        compiler_params=pltpu.CompilerParams(vmem_limit_bytes=vmem * 1024 * 1024),
        cost_estimate=pl.CostEstimate(flops=int(cost * 1_000_000_000), bytes_accessed=1000, transcendentals=0),
    )(scalars, *arrays, *[array for array, _ in pairs])


SLOT, CORE, ROW, END, TENSOR, OWN, FAR, LIMIT = 0, 4, 5, 6, 7, 8, 10, 12
ORDER = (0, 2, 1, 3)


def block_of(place, chunk):
    return place[CORE] * 2 + chunk


def mod_row(mod, slot, component, model):
    return mod[pl.ds(slot, 1), component * model : (component + 1) * model]


def quad_cols(quad):
    return pl.ds(pl.multiple_of(quad * 4 * HEAD, 4 * HEAD), 4 * HEAD)


def token_rows(block):
    return pl.ds(pl.multiple_of(block * BLOCK, BLOCK), BLOCK)


def text_kernel(place, text, weights, packed):
    rows = text.shape[1]
    wide = weights.shape[0]
    for slot in range(text.shape[0]):
        first = rows * (slot % 2)
        left = wide * (slot // 2)
        packed[first : first + rows, left : left + wide] = dot_nt(text[slot], weights[...]).astype(BF16)


def unpack_kernel(place, q0, o0, q1, o1, part2, rest2, part3, rest3, t0, t1, t2, t3, cqt, co, kall, vall):
    width = q0.shape[0]
    half = width // 2
    rows = kall.shape[1]
    for index, (query, out) in enumerate(((q0, o0), (q1, o1))):
        cqt[index * width : (index + 1) * width, :] = query[...]
        co[index * width : (index + 1) * width, :] = out[...]
    for index, (part, rest) in enumerate(((part2, rest2), (part3, rest3))):
        for piece, row in ((part, place[ROW]), (rest, 1 - place[ROW])):
            at = pl.ds(pl.multiple_of((index + 2) * width + row * half, half), half)
            cqt[at, :] = piece[:half, :]
            co[at, :] = piece[half:, :]
    for slot in range(kall.shape[0]):
        first = rows * (slot % 2)
        left = 2 * width * (slot // 2)
        both = [t[first : first + rows, left : left + 2 * width] for t in (t0, t1, t2, t3)]
        kall[slot] = jnp.concatenate([b[:, :width] for b in both], axis=1)
        vall[slot] = jnp.concatenate([b[:, width:] for b in both], axis=1)


def attend_chunk(place, chunk, qa_in, ka, va, wo, part_own, part_send, qa_out, att):
    heads = ka.shape[0]
    lane = lax.broadcasted_iota(jnp.int32, (BLOCK, 2 * HEAD), 1)
    spot = (lane >= HEAD + 4) & (lane < HEAD + 7)

    @pl.loop(0, 2)
    def _(side):
        at = token_rows(2 * chunk + side)
        here = token_rows(side)
        pieces = []
        for head in range(heads):
            queries = qa_in[head, at, :]
            scores = dot_nt(queries, ka[head])
            top = jnp.max(scores, axis=1, keepdims=True)
            raised = jnp.exp(scores - top).astype(BF16)
            out = dot_nn(raised, va[head])
            total = out[:, HEAD : HEAD + 1]
            pieces.append(out[:, :HEAD] * (1.0 / total))
            high, middle, low = three_parts(-(top + jnp.log(total)))
            more = jnp.where(lane == HEAD + 4, high, jnp.where(lane == HEAD + 5, middle, low))
            qa_out[head, here, :] = jnp.where(spot, more, queries.astype(F32)).astype(BF16)
        attended = jnp.concatenate(pieces, axis=1).astype(BF16)
        att[here, :] = attended
        out = dot_nn(attended, wo[...]).astype(BF16)

        @pl.when(place[CORE] == side)
        def _():
            part_own[...] = out

        @pl.when(place[CORE] != side)
        def _():
            part_send[...] = out


def self_first(place, mod, weights, tokens, wo, part_own, part_send, qa, ka, va, qa_out, att, h1):
    model = mod.shape[1] // 9
    lane = lax.broadcasted_iota(jnp.int32, (BLOCK, 2 * HEAD), 1)
    keep = lane < HEAD
    width = weights.shape[0] // 3
    tokens = tokens.ref()
    slots = [place[SLOT + block] for block in ORDER]

    @pl.loop(0, len(ORDER))
    def _(position):
        rows = token_rows(position)
        first = jnp.where(position == 0, slots[0], slots[1])
        slot = jnp.where(position < 2, first, jnp.where(position == 2, slots[2], slots[3]))
        block = lax.rem(position, 2) * 2 + lax.div(position, 2)
        normed, _ = normalize(tokens[token_rows(block), :].astype(F32))
        hidden = (normed * (1.0 + mod_row(mod, slot, 1, model)) + mod_row(mod, slot, 0, model)).astype(BF16)
        h1[rows, :] = hidden
        rows_qkv = dot_nt(hidden, weights[...])
        q = rows_qkv[:, :width].astype(BF16).astype(F32) * (HEAD**-0.5)
        k = rows_qkv[:, width : 2 * width]
        v = rows_qkv[:, 2 * width :]
        mine = lane == HEAD + slot
        q_more = jnp.where(mine, 1.0, 0.0)
        k_more = jnp.where((lane >= HEAD + 4) & (lane < HEAD + 7), 1.0, 0.0)
        k_more = jnp.where((lane >= HEAD) & (lane < HEAD + 4) & jnp.logical_not(mine), MASKED, k_more)
        v_more = jnp.where((lane >= HEAD) & (lane < HEAD + 3), 1.0, 0.0)
        for head in range(ka.shape[0]):
            qa[head, rows, :] = jnp.where(keep, head_slice(q, head), q_more).astype(BF16)
            ka[head, rows, :] = jnp.where(keep, head_slice(k, head), k_more).astype(BF16)
            va[head, rows, :] = jnp.where(keep, head_slice(v, head), v_more).astype(BF16)
    attend_chunk(place, 0, qa, ka, va, wo.ref(), part_own, part_send, qa_out, att)


def self_second(place, qa, ka, va, wo, part_own, part_send, qa_out, att):
    attend_chunk(place, 1, qa, ka, va, wo.ref(), part_own, part_send, qa_out, att)


def quad_stack(rows, masks):
    return jnp.concatenate([rows * mask for mask in masks], axis=0)


def quad_masks():
    lane = lax.broadcasted_iota(jnp.int32, (1, 4 * HEAD), 1)
    return [jnp.where((lane >= u * HEAD) & (lane < (u + 1) * HEAD), 1.0, 0.0) for u in range(4)]


def quad_probs(scores, limit, text_rows):
    key_row = lax.broadcasted_iota(jnp.int32, (text_rows, 1), 0)
    bias = jnp.where(key_row < limit, 0.0, MASKED)
    probs = []
    for u in range(4):
        part = scores[u * text_rows : (u + 1) * text_rows, :] + bias
        raised = jnp.exp(part - jnp.max(part, axis=0, keepdims=True))
        probs.append(raised * (1.0 / jnp.sum(raised, axis=0, keepdims=True)))
    return probs


def middle_chunk(
    place, chunk, mod, sum_own, sum_far, cqt, co, kall, vall, tokens, cot, win0, wout0, win1, wout1, x2_before,
    h3g_out, h3_out, act0, act1, pg0, pg1, b3g_out, x1_out, b2_out, h2_out, q2_out, cr_out, b3_out, x2_out,
):
    model = cqt.shape[1]
    text_rows = kall.shape[1]
    slot = place[OWN + chunk]

    def m(component):
        return mod_row(mod, slot, component, model)

    x1 = tokens.ref()[...].astype(F32) + m(2) * (sum_own[...].astype(F32) + sum_far[...].astype(F32))
    x1_out[...] = x1
    normed, _ = normalize(x1)
    h2 = (normed * (1.0 + m(4)) + m(3)).astype(BF16)
    h2_out[...] = h2
    q2 = (dot_nt(h2, cqt[...]).astype(BF16).astype(F32) * (HEAD**-0.5)).astype(BF16)
    q2_out[...] = q2
    masks = [mask.astype(BF16) for mask in quad_masks()]
    limit = place[LIMIT + chunk]

    @pl.loop(0, model // (4 * HEAD))
    def _(quad):
        cols = quad_cols(quad)
        scores = dot_nt(quad_stack(kall[slot, :, cols], masks), q2_out[:, cols])
        probs = jnp.concatenate(quad_probs(scores, limit, text_rows), axis=0)
        cr_out[:, cols] = dot_tn(probs.astype(BF16), quad_stack(vall[slot, :, cols], masks)).astype(BF16)

    b2 = dot_nn(cr_out[...], co[...])
    b2_out[...] = b2
    x2 = x1 + m(5) * b2
    x2_out[chunk * BLOCK : (chunk + 1) * BLOCK, :] = x2
    normed, _ = normalize(x2)
    h3 = (normed * (1.0 + m(7)) + m(6)).astype(BF16)
    h3_out[...] = h3
    b3g = (cot.ref()[...].astype(F32) * m(8)).astype(BF16)
    b3g_out[...] = b3g
    b3 = h3g = None
    for win, wout, act_out, pg_out in ((win0, wout0, act0, pg0), (win1, wout1, act1, pg1)):
        win, wout = win.ref(), wout.ref()
        pre = dot_nn(h3, win[...])
        square = pre * pre
        bent = jnp.tanh(CURVE * (pre + CUBIC * (square * pre)))
        act = (0.5 * pre * (1.0 + bent)).astype(BF16)
        act_out[...] = act
        slope = 0.5 * (1.0 + bent) + 0.5 * pre * (1.0 - bent * bent) * (CURVE * (1.0 + 3.0 * CUBIC * square))
        b3_half = dot_nn(act, wout[...])
        pg = (dot_nt(b3g, wout[...]) * slope).astype(BF16)
        pg_out[...] = pg
        h3g_half = dot_nt(pg, win[...])
        b3 = b3_half if b3 is None else b3 + b3_half
        h3g = h3g_half if h3g is None else h3g + h3g_half
    b3_out[...] = b3.astype(BF16)
    if chunk:
        x2_out[0:BLOCK, :] = x2_before.ref()[...]
    h3g_out[...] = h3g.astype(BF16)


def middle_first(place, *refs):
    middle_chunk(place, 0, *refs[:13], None, *refs[13:])


def middle_second(place, *refs):
    middle_chunk(place, 1, *refs)


def stacked(first, second):
    return jnp.concatenate([first[...], second[...]], axis=0)


def mlp_back(
    place, h3a, h3b, pg0a, pg0b, pg1a, pg1b, act0a, act0b, act1a, act1b, b3ga, b3gb,
    in_own, in_send, out_own, out_send,
):
    half = in_own.shape[1]
    grads = (stacked(pg0a, pg0b), stacked(pg1a, pg1b))
    grad = stacked(b3ga, b3gb)

    @pl.loop(0, 2)
    def _(part):
        cols = pl.ds(pl.multiple_of(part * half, half), half)
        kept = part ^ place[ROW]
        rows = jnp.concatenate([h3a[:, cols], h3b[:, cols]], axis=0)
        in_send[kept] = dot_tn(rows, grads[1]).astype(BF16)
        in_own[kept] = dot_tn(rows, grads[0]).astype(BF16)
        out_send[kept] = dot_tn(jnp.concatenate([act1a[:, cols], act1b[:, cols]], axis=0), grad).astype(BF16)
        out_own[kept] = dot_tn(jnp.concatenate([act0a[:, cols], act0b[:, cols]], axis=0), grad).astype(BF16)


def cross_chunk(
    place, chunk, mod, h3g_own, h3g_far, kall, vall, cqt, co, x1_in, b2_in, cot, q2_in, sum_own, sum_far,
    b1g_out, dq_out, b2g_out, dk_out, dv_out, sums, x1g_out, out_grad,
):
    model = cqt.shape[1]
    text_rows = kall.shape[1]
    slot = place[OWN + chunk]

    def m(component):
        return mod_row(mod, slot, component, model)

    x1 = x1_in.ref()[...]
    b2 = b2_in.ref()[...]
    h3g = h3g_own[...].astype(F32) + h3g_far[...].astype(F32)
    normed, inverse = normalize(x1 + m(5) * b2)
    sums[4:5, :] = column_sum(h3g)
    sums[5:6, :] = column_sum(h3g * normed)
    x2g = cot.ref()[...].astype(F32) + norm_back(h3g * (1.0 + m(7)), normed, inverse)
    sums[3:4, :] = column_sum(x2g * b2)
    b2g = (x2g * m(5)).astype(BF16)
    b2g_out[...] = b2g
    out_grad[...] = dot_nt(b2g, co[...]).astype(BF16)
    masks = quad_masks()
    low = [mask.astype(BF16) for mask in masks]
    limit = place[LIMIT + chunk]

    @pl.loop(0, model // (4 * HEAD))
    def _(quad):
        cols = quad_cols(quad)
        queries = q2_in.ref()[:, cols]
        grads = out_grad[:, cols]
        keys = quad_stack(kall[slot, :, cols], low)
        values = quad_stack(vall[slot, :, cols], low)
        probs = quad_probs(dot_nt(keys, queries), limit, text_rows)
        prob_grad = dot_nt(values, grads)
        score_grad = []
        for u in range(4):
            part = prob_grad[u * text_rows : (u + 1) * text_rows, :]
            row_dot = jnp.sum(probs[u] * part, axis=0, keepdims=True)
            score_grad.append((probs[u] * (part - row_dot)).astype(BF16))
        score_grad = jnp.concatenate(score_grad, axis=0)
        dv = dot_nn(jnp.concatenate(probs, axis=0).astype(BF16), grads)
        dk = dot_nn(score_grad, queries)
        dq_out[:, cols] = (dot_tn(score_grad, keys) * (HEAD**-0.5)).astype(BF16)
        for wide, out in ((dk, dk_out), (dv, dv_out)):
            total = None
            for u in range(4):
                part = wide[u * text_rows : (u + 1) * text_rows, :] * masks[u]
                total = part if total is None else total + part
            out[:, cols] = total.astype(BF16)
    h2g = dot_nn(dq_out[...], cqt[...])
    normed, inverse = normalize(x1)
    sums[1:2, :] = column_sum(h2g)
    sums[2:3, :] = column_sum(h2g * normed)
    x1g = x2g + norm_back(h2g * (1.0 + m(4)), normed, inverse)
    x1g_out[...] = x1g
    branch = sum_own.ref()[...].astype(F32) + sum_far.ref()[...].astype(F32)
    sums[0:1, :] = column_sum(x1g * branch)
    sums[6:8, :] = jnp.zeros((2, model), F32)
    b1g_out[...] = (x1g * m(2)).astype(BF16)


def cross_first(place, *refs):
    cross_chunk(place, 0, *refs)


def cross_second(place, *refs):
    cross_chunk(place, 1, *refs)


def cross_weights(
    place, dqa, dqb, b2ga, b2gb, dka, dkb, dva, dvb, h2a, h2b, cra, crb, text, own, send,
):
    width = own.shape[1] // 2
    row = place[ROW]
    h2a, h2b, cra, crb, text = h2a.ref(), h2b.ref(), cra.ref(), crb.ref(), text.ref()
    hidden = stacked(h2a, h2b)
    grads = stacked(b2ga, b2gb)
    texts = [text[place[OWN + chunk]] for chunk in range(2)]
    for member, out in ((1, send), (0, own)):
        start = (member * width // 128) * 128
        skip = member * width - start
        cols = slice(start, start + 2 * 128)
        kept = slice(skip, skip + width)

        def two(first, second):
            return jnp.concatenate([first[:, cols], second[:, cols]], axis=0)

        top, bottom = slice(0, width), slice(width, 2 * width)
        out[row, top] = dot_tn(two(dqa, dqb), hidden)[kept].astype(BF16)
        out[row, bottom] = (dot_tn(dka[:, cols], texts[0]) + dot_tn(dkb[:, cols], texts[1]))[kept].astype(BF16)
        out[1 - row, top] = (dot_tn(dva[:, cols], texts[0]) + dot_tn(dvb[:, cols], texts[1]))[kept].astype(BF16)
        out[1 - row, bottom] = dot_tn(two(cra, crb), grads)[kept].astype(BF16)


def keys_back(block, qa, ka, va, da, dq_sum):
    rows = token_rows(block)
    dks = []
    dvs = []
    for head in range(ka.shape[0]):
        keys = ka[head, rows, :]
        probs = jnp.exp(dot_nt(keys, qa[head]))
        prob_grad = dot_nt(va[head, rows, :], da[head])
        score_grad = (probs * prob_grad).astype(BF16)
        dvs.append(dot_nn(probs.astype(BF16), da[head])[:, :HEAD])
        dks.append(dot_nn(score_grad, qa[head])[:, :HEAD])
        dq = dot_tn(score_grad, keys)
        dq_sum[head] += dq
    return jnp.concatenate(dks, axis=1).astype(BF16), jnp.concatenate(dvs, axis=1).astype(BF16)


def self_back_first(
    place, b1g_a, b1g_b, far_a, far_b, wo, att_a, att_b, qa_a, qa_b, ka, va,
    b1g, att, qa, da, dq_sum, dk_all, dv_all,
):
    blocks = b1g.shape[0] // BLOCK
    heads = da.shape[0]
    core = place[CORE]
    for chunk, (own, far) in enumerate(((b1g_a, far_a), (b1g_b, far_b))):
        b1g[token_rows(2 * chunk + core), :] = own[...]
        b1g[token_rows(2 * chunk + 1 - core), :] = far[...]
    wo = wo.ref()
    att[0 : 2 * BLOCK, :] = att_a.ref()[...]
    att[2 * BLOCK : 4 * BLOCK, :] = att_b.ref()[...]
    lane = lax.broadcasted_iota(jnp.int32, (BLOCK, 2 * HEAD), 1)

    @pl.loop(0, blocks)
    def _(block):
        rows = token_rows(block)
        grads = dot_nt(b1g[rows, :], wo[...]).astype(BF16).astype(F32)
        dots = grads * att[rows, :].astype(F32)
        for head in range(heads):
            row_dot = jnp.sum(dots[:, head * HEAD : (head + 1) * HEAD], axis=1, keepdims=True)
            high, middle, low = three_parts(-row_dot)
            more = jnp.where(lane == HEAD, high, jnp.where(lane == HEAD + 1, middle, low))
            more = jnp.where(lane < HEAD + 3, more, 0.0)
            da[head, rows, :] = jnp.where(lane < HEAD, head_slice(grads, head), more).astype(BF16)
    qa[:, 0 : 2 * BLOCK, :] = qa_a.ref()[...]
    qa[:, 2 * BLOCK : 4 * BLOCK, :] = qa_b.ref()[...]
    ka, va = ka.ref(), va.ref()
    dq_sum[...] = jnp.zeros_like(dq_sum)

    @pl.loop(0, 2)
    def _(block):
        rows = token_rows(block)
        dk_all[rows, :], dv_all[rows, :] = keys_back(block, qa, ka, va, da, dq_sum)


def self_back_second(
    place, b1g, att, qa, da, dq_in, dk_in, dv_in, weights, ka, va, h1,
    part_own, part_send, dw_keep, dw_give,
    dq_sum, grad_all,
):
    blocks = b1g.shape[0] // BLOCK
    heads = da.shape[0]
    core = place[CORE]
    width = heads * HEAD
    ka, va = ka.ref(), va.ref()
    dq_sum[...] = dq_in[...]
    grad_all[0 : 2 * BLOCK, width : 2 * width] = dk_in[0 : 2 * BLOCK, :]
    grad_all[0 : 2 * BLOCK, 2 * width : 3 * width] = dv_in[0 : 2 * BLOCK, :]

    @pl.loop(2, blocks)
    def _(block):
        rows = token_rows(block)
        dk, dv = keys_back(block, qa, ka, va, da, dq_sum)
        grad_all[rows, width : 2 * width] = dk
        grad_all[rows, 2 * width : 3 * width] = dv
    h1 = h1.ref()

    @pl.loop(0, blocks)
    def _(block):
        rows = token_rows(block)
        dq = jnp.concatenate([dq_sum[head, rows, :HEAD] for head in range(heads)], axis=1)
        grad_all[rows, 0:width] = (dq * (HEAD**-0.5)).astype(BF16)
        out = dot_nn(grad_all[rows, :], weights[...]).astype(BF16)
        side = lax.rem(block, 2)
        out_rows = token_rows(lax.div(block, 2))

        @pl.when(core == side)
        def _():
            part_own[out_rows, :] = out

        @pl.when(core != side)
        def _():
            part_send[out_rows, :] = out

    grads = dot_tn(grad_all[...], h1[...]).astype(BF16)
    query_key = (grads[:width], grads[width : 2 * width])
    value_out = (grads[2 * width :], dot_tn(att[...], b1g[...]).astype(BF16))
    for flag, first, second in ((0, query_key, value_out), (1, value_out, query_key)):

        @pl.when(place[ROW] == flag)
        def _():
            for index in range(2):
                rows = slice(index * width, (index + 1) * width)
                dw_keep[rows, :] = first[index]
                dw_give[rows, :] = second[index]


def mixed_kernel(place, mod, b3a, b3b, far_a, far_b, x2, cot_a, cot_b, mixed_a, mixed_b, sums):
    model = mixed_a.shape[1]
    for chunk, (own, far, cot) in enumerate(((b3a, far_a, cot_a), (b3b, far_b, cot_b))):
        mixed = (mixed_a, mixed_b)[chunk]
        rows = slice(chunk * BLOCK, (chunk + 1) * BLOCK)
        slot = place[OWN + chunk]
        b3 = own[...].astype(F32) + far[...].astype(F32)
        mixed[...] = (x2[rows, :] + mod_row(mod, slot, 8, model) * b3).astype(BF16)
        sums[chunk] = column_sum(cot.ref()[...].astype(F32) * b3)


def final_kernel(
    place, mod, h1g_own, h1g_far, sums_a, sums_b, sums_mixed, tokens_a, tokens_b, x1ga, x1gb, grad_a, grad_b, slot_sums,
):
    model = grad_a.shape[1]
    slot_sums[...] = jnp.zeros_like(slot_sums)
    for chunk, (x1g, sums, tokens) in enumerate(((x1ga, sums_a, tokens_a), (x1gb, sums_b, tokens_b))):
        rows = slice(chunk * BLOCK, (chunk + 1) * BLOCK)
        slot = place[OWN + chunk]
        h1g = h1g_own[rows, :].astype(F32) + h1g_far[rows, :].astype(F32)
        normed, inverse = normalize(tokens.ref()[...].astype(F32))
        scaled = h1g * (1.0 + mod_row(mod, slot, 1, model))
        (grad_a, grad_b)[chunk][...] = (x1g.ref()[...] + norm_back(scaled, normed, inverse)).astype(BF16)
        terms = [column_sum(h1g), column_sum(h1g * normed)]
        terms += [sums[i : i + 1, :] for i in range(6)] + [sums_mixed[chunk]]
        for component, term in enumerate(terms):
            slot_sums[pl.ds(slot, 1), component * model : (component + 1) * model] += term


def join_cores(place, mine_a, mine_b, other_a, other_b, out):
    for chunk, (mine, other) in enumerate(((mine_a, other_a), (mine_b, other_b))):
        out[token_rows(place[CORE] * 2 + chunk), :] = mine[...]
        out[token_rows((1 - place[CORE]) * 2 + chunk), :] = other[...]


def join_rows(place, mine, other, out):
    count = mine.shape[0]
    out[pl.ds(pl.multiple_of(place[ROW] * count, BLOCK // 2), count), :] = mine[...].astype(F32)
    out[pl.ds(pl.multiple_of((1 - place[ROW]) * count, BLOCK // 2), count), :] = other[...].astype(F32)


def join_four(place, mine, other, first, second, third, fourth):
    width = first.shape[0]
    for flag, top, bottom in ((0, mine, other), (1, other, mine)):

        @pl.when(place[ROW] == flag)
        def _():
            first[...] = top[:width, :].astype(F32)
            second[...] = top[width:, :].astype(F32)
            third[...] = bottom[:width, :].astype(F32)
            fourth[...] = bottom[width:, :].astype(F32)


def slot_kernel(place, own, far, silu, out):
    model = silu.shape[1]
    count = out.shape[1] - model
    out[:, :model] = silu[...].astype(F32)
    for index in range(own.shape[1] // count):
        cols = slice(index * count, (index + 1) * count)

        @pl.when(place[TENSOR] == index)
        def _():
            out[:, model:] = (own[:, cols] + far[:, cols]).astype(BF16).astype(F32)


def advance_kernel(roles, place, *refs):
    refs = list(refs)
    values, got = {}, {}
    for role in roles:
        values[role] = refs.pop(0)
    for name in ("row", "column", "middle"):
        if any(role in roles for role in {"row": "a", "column": "bd", "middle": "c"}[name]):
            got[name] = refs.pop(0)
    outs = {role: refs.pop(0) for role in roles}
    end = place[END]
    if "a" in roles:
        outs["a"][...] = added(values["a"][...], got["row"][...])
    if "c" in roles:

        @pl.when(end == 0)
        def _():
            outs["c"][...] = added(values["c"][...], got["middle"][...])

        @pl.when(end != 0)
        def _():
            outs["c"][...] = values["c"][...]

    if "b" in roles:

        @pl.when(end == 0)
        def _():
            outs["b"][...] = added(values["b"][...], got["column"][...])

        @pl.when(end != 0)
        def _():
            outs["b"][...] = values["b"][...]

    if "d" in roles:

        @pl.when(end == 0)
        def _():
            outs["d"][...] = values["d"][...]

        @pl.when(end != 0)
        def _():
            outs["d"][...] = got["column"][...]

    if refs:

        @pl.when(end == 0)
        def _():
            refs[0][...] = outs["c"][...]

        @pl.when(end != 0)
        def _():
            refs[0][...] = outs["a"][...]


def added(first, second):
    return (first.astype(F32) + second.astype(F32)).astype(BF16)


def solution(mesh):
    n_dp = mesh.shape["dp"]
    n_tensor = mesh.shape["tensor"]
    n_col = n_dp // 2
    dp_bits = int(math.log2(n_dp))

    def tensor_swap(value, flip):
        return lax.ppermute(value, "tensor", [(i, i ^ flip) for i in range(n_tensor)])

    def core_swap(value):
        return tensor_swap(value, 1)

    def far_swap(value):
        return tensor_swap(value, 2)

    def dp_swap(value, flip):
        return lax.ppermute(value, "dp", [(i, i ^ flip) for i in range(n_dp)])

    def tie(*values):
        return lax.optimization_barrier(values) if values else ()

    def pair_up(flag, mine, other):
        return jnp.concatenate([jnp.where(flag == 0, mine, other), jnp.where(flag == 0, other, mine)], axis=0)

    def local(
        tokens, text_states, clip_len, text_len, timesteps, q_weight, k_weight, v_weight, o_weight,
        cross_q, cross_k, cross_v, cross_o, mlp_in, mlp_out, mod_weight, mod_bias, cotangent,
    ):
        count, model = tokens.shape
        slots, text_rows = text_states.shape[:2]
        width = o_weight.shape[0]
        heads = width // HEAD
        half = count // 2
        text_pad = -(-text_rows // 16) * 16
        tensor_at = lax.axis_index("tensor")
        dp_at = lax.axis_index("dp")
        core = tensor_at & 1
        row = dp_at & 1
        column = dp_at >> 1

        ends = jnp.cumsum(clip_len)
        starts = jnp.arange(count // BLOCK, dtype=jnp.int32) * BLOCK
        slot_of = jnp.sum((starts[:, None] >= ends[None, :]).astype(jnp.int32), axis=1)
        end = (column == 0) | (column == n_col - 1)
        own_slots = lax.dynamic_slice_in_dim(slot_of, core * 2, 2, 0)
        far_slots = lax.dynamic_slice_in_dim(slot_of, (1 - core) * 2, 2, 0)
        limits = jnp.sum(jnp.where(own_slots[:, None] == jnp.arange(slots)[None, :], text_len[None, :], 0), axis=1)
        single = jnp.stack([core, row, end.astype(jnp.int32), tensor_at])
        place = jnp.concatenate([slot_of, single, own_slots, far_slots, limits])
        place = jnp.pad(place[None, :], ((0, 7), (0, 128 - place.shape[0])))
        place = place.astype(jnp.int32)

        query_own = cross_q.T
        part_own = jnp.concatenate(
            [lax.dynamic_slice_in_dim(w, row * (width // 2), width // 2, 0) for w in (query_own, cross_o)], axis=0
        )
        text_weights = jnp.concatenate([cross_k.T, cross_v.T], axis=0)
        text = jnp.pad(text_states, ((0, 0), (0, text_pad - text_rows), (0, 0)))
        self_weights = jnp.concatenate([q_weight.T, k_weight.T, v_weight.T], axis=0)

        half_width = model // 2
        ramp = jnp.arange(half_width).astype(F32)
        frequency = jnp.exp(ramp * (-math.log(10000.0) / half_width))
        angles = timesteps.astype(F32)[:, None] * frequency[None, :]
        embed = jnp.concatenate([jnp.cos(angles), jnp.sin(angles)], axis=1)
        silu_low = jax.nn.silu(embed).astype(BF16)
        part_far = far_swap(part_own)
        wout1 = core_swap(mlp_out)
        mod_own = dot_nn(silu_low, mod_weight) + mod_bias.astype(F32)
        mod_far = [tensor_swap(mod_own, flip) for flip in range(1, n_tensor)]
        (text_own,) = run(text_kernel, [((2 * text_pad, model), BF16)], place, [text, text_weights], cost=1.0)
        text_own, self_weights, wout1, *mod_far = tie(text_own, self_weights, wout1, *mod_far)
        text_far = far_swap(text_own)
        query_own, out_own, text_own = tie(query_own, cross_o, text_own)
        query1, out1, text1 = core_swap(query_own), core_swap(out_own), core_swap(text_own)
        mod_all = jnp.stack([mod_own] + mod_far)
        mod = jnp.concatenate(
            [lax.dynamic_index_in_dim(mod_all, tensor_at ^ j, 0, keepdims=False) for j in range(n_tensor)], axis=1
        )

        wide = (heads, count, 2 * HEAD)
        block_wide = (heads, 2 * BLOCK, 2 * HEAD)
        one = ((BLOCK, model), BF16)
        one_f32 = ((BLOCK, model), F32)
        attend_far = [(block_wide, BF16), ((2 * BLOCK, width), BF16)]
        own_a, send_a, qa, ka, va, qa_a, att_a, h1 = run(
            self_first, [one, one] + [(wide, BF16)] * 3 + attend_far + [((count, model), BF16)], place, [mod, self_weights], cost=0.001,
            late=[tokens, o_weight],
        )
        send_a, part_far, text_far, query1, out1, text1 = tie(send_a, part_far, text_far, query1, out1, text1)
        sum_a = added(own_a, core_swap(send_a))
        sum_a, qa, part_far, text_far, win0 = tie(sum_a, qa, part_far, text_far, mlp_in)
        far_a = far_swap(sum_a)
        rest_far = dp_swap(part_far, 1)
        part3, text3, win1 = core_swap(part_far), core_swap(text_far), core_swap(win0)
        own_b, send_b, qa_b, att_b = run(
            self_second, [one, one] + attend_far, place, [qa, ka, va], late=[o_weight]
        )
        (far_a,) = tie(far_a)
        send_b, far_a, rest_far, part3, text3, win1 = tie(send_b, far_a, rest_far, part3, text3, win1)
        rest3 = core_swap(rest_far)
        sum_b = added(own_b, core_swap(send_b))
        sum_b, rest3 = tie(sum_b, rest3)
        far_b = far_swap(sum_b)
        cqt, co, kall, vall = run(
            unpack_kernel, [((model, model), BF16)] * 2 + [((slots, text_pad, model), BF16)] * 2,
            place,
            [query_own, out_own, query1, out1, part_far, rest_far, part3, rest3, text_own, text1, text_far, text3],
            cost=0.001,
        )
        shared = [cqt, co, kall, vall]

        def chunk_rows(array, chunk):
            return (array, functools.partial(block_of, chunk=chunk))

        def middle(kernel, chunk, own, far, *before):
            return run(
                kernel, [one] * 7 + [one_f32, one_f32] + [one] * 4 + [(((chunk + 1) * BLOCK, model), F32)], place,
                [mod, own, far] + shared, cost=7.5,
                late=[chunk_rows(tokens, chunk), chunk_rows(cotangent, chunk), mlp_in, mlp_out, win1, wout1, *before],
            )

        h3ga, h3a, act0a, act1a, pg0a, pg1a, b3ga, x1a, b2a, h2a, q2a, cra, b3a, x2a = middle(
            middle_first, 0, sum_a, far_a
        )
        h3ga, far_b = tie(h3ga, far_b)
        h3g_far_a = far_swap(h3ga)
        h3gb, h3b, act0b, act1b, pg0b, pg1b, b3gb, x1b, b2b, h2b, q2b, crb, b3b, x2 = middle(
            middle_second, 1, sum_b, far_b, x2a
        )
        h3gb, pg0b, h3g_far_a = tie(h3gb, pg0b, h3g_far_a)
        h3g_far_b = far_swap(h3gb)

        in_own, in_send, out_own, out_send = run(
            mlp_back, [((2, model // 2, model), BF16)] * 4, place,
            [h3a, h3b, pg0a, pg0b, pg1a, pg1b, act0a, act0b, act1a, act1b, b3ga, b3gb], cost=0.001,
        )

        def cross(kernel, chunk, h3g_own, h3g_far, x1, b2, own, far, q2):
            return run(
                kernel, [one] * 3 + [((text_pad, model), BF16)] * 2 + [((8, model), F32), one_f32], place,
                [mod, h3g_own, h3g_far, kall, vall, cqt, co],
                late=[x1, b2, chunk_rows(cotangent, chunk), q2, own, far], scratch=[one],
                cost=4.0 if chunk else 0.001,
            )

        b1g_a, dqa, b2ga, dka, dva, sums_a, x1ga = cross(
            cross_first, 0, h3ga, h3g_far_a, x1a, b2a, sum_a, far_a, q2a
        )
        in_send, out_send, b1g_a, h3g_far_b = tie(in_send, out_send, b1g_a, h3g_far_b)
        in_got, out_got, b1g_far_a = core_swap(in_send), core_swap(out_send), core_swap(b1g_a)
        b1g_b, dqb, b2gb, dkb, dvb, sums_b, x1gb = cross(
            cross_second, 1, h3gb, h3g_far_b, x1b, b2b, sum_b, far_b, q2b
        )
        in_got, out_got, b1g_far_a, b1g_b, dqb, b3a = tie(in_got, out_got, b1g_far_a, b1g_b, dqb, b3a)
        in_keep, in_give = added(in_own[0], in_got[0]), added(in_own[1], in_got[1])
        out_keep, out_give = added(out_own[0], out_got[0]), added(out_own[1], out_got[1])

        across = [(i, i ^ 1) for i in range(n_dp)]
        neighbours = [(i, i ^ 2) for i in range(n_dp)]
        middle_pair = [(2 * a + r, 2 * b + r) for a, b in ((1, 2), (2, 1)) for r in range(2)]
        chain_rows = (model // 2, model)

        class Rounds:
            def __init__(self):
                self.values, self.column_send, self.results, self.waiting = {}, None, [], []

            def start(self, *chain):
                self.got = {}
                if n_col != 4:
                    self.waiting += [chain] if chain else []
                    return
                if chain:
                    self.values["a"] = chain[0]
                    self.got["row"] = lax.ppermute(chain[1], "dp", across)
                if "e" in self.values:
                    self.got["last"] = lax.ppermute(self.values["e"], "dp", across)
                if "b" in self.values or "d" in self.values:
                    self.got["column"] = lax.ppermute(self.column_send, "dp", neighbours)
                if "c" in self.values:
                    self.got["middle"] = lax.ppermute(self.values["c"], "dp", middle_pair)

            def finish(self, *others, early=()):
                order = [name for name in ("row", "last", "column", "middle") if name in self.got]
                settled = list(early)
                for name in order:
                    settled = list(tie(self.got[name], *settled))
                tied = tie(*settled, *others)
                self.got = dict(zip(reversed(order), tied))
                others = tied[len(order) :]
                if "last" in self.got:
                    self.results.append((self.values.pop("e"), self.got.pop("last")))
                roles = "".join(role for role in "abcd" if role in self.values)
                if not roles:
                    return others
                operands = [self.values[role] for role in roles]
                operands += [self.got[name] for name in ("row", "column", "middle") if name in self.got]
                sends = "a" in roles or "c" in roles
                both = "a" in roles and "c" in roles
                outs = run(
                    functools.partial(advance_kernel, roles), [(chain_rows, BF16)] * (len(roles) + both),
                    place, operands, cost=0.3,
                )
                done = tie(*outs, *others)
                stepped = dict(zip(roles, done))
                if sends:
                    self.column_send = done[len(roles)] if both else stepped["a" if "a" in roles else "c"]
                self.values = {{"a": "b", "b": "c", "c": "d", "d": "e"}[role]: v for role, v in stepped.items()}
                return done[len(outs) :]

            def halves(self, number):
                return self.results[number] if n_col == 4 else self.slowly(*self.waiting[number])

            def whole(self, number):
                return run(join_rows, [((model, model), F32)], place, self.halves(number))[0]

            def four(self, number):
                return run(join_four, [((width, model), F32)] * 4, place, self.halves(number))

            def slowly(self, keep, give):
                total = added(keep, lax.ppermute(give, "dp", across))
                for bit in range(1, dp_bits):
                    size, flag = total.shape[0] // 2, (dp_at >> bit) & 1
                    sent = lax.dynamic_slice_in_dim(total, (1 - flag) * size, size, 0)
                    total = added(lax.dynamic_slice_in_dim(total, flag * size, size, 0), dp_swap(sent, 1 << bit))
                for bit in reversed(range(1, dp_bits)):
                    total = pair_up((dp_at >> bit) & 1, total, dp_swap(total, 1 << bit))
                return total, lax.ppermute(total, "dp", across)

        rounds = Rounds()

        rounds.start(in_keep, in_give)
        b1g_far_b = core_swap(b1g_b)
        b3_far_a = far_swap(b3a)
        cross_dw, cross_send = run(
            cross_weights, [((2, 2 * width, model), BF16)] * 2, place,
            [dqa, dqb, b2ga, b2gb, dka, dkb, dva, dvb], late=[h2a, h2b, cra, crb, text], cost=0.001,
        )
        b1g_far_b, cross_send = tie(b1g_far_b, cross_send)
        b1g_all, att_all, qa_all, da, dq_sum, dk_all, dv_all = run(
            self_back_first,
            [((count, model), BF16), ((count, width), BF16), (wide, BF16), (wide, BF16), (wide, F32)]
            + [((count, width), BF16)] * 2,
            place, [b1g_a, b1g_b, b1g_far_a, b1g_far_b],
            late=[o_weight, att_a, att_b, qa_a, qa_b, ka, va], cost=0.001,
        )
        b1g_all, cross_send, out_give, b3b, b3_far_a = rounds.finish(b1g_all, cross_send, out_give, b3b, b3_far_a)

        rounds.start(out_keep, out_give)
        cross_got = core_swap(cross_send)
        b3_far_b = far_swap(b3b)
        grad_own, grad_send, self_keep, self_give = run(
            self_back_second,
            [((half, model), BF16)] * 2 + [((2 * width, model), BF16)] * 2, place,
            [b1g_all, att_all, qa_all, da, dq_sum, dk_all, dv_all, self_weights], late=[ka, va, h1],
            scratch=[(wide, F32), ((count, 3 * width), BF16)],
        )
        cross_keep, cross_give = added(cross_dw[0], cross_got[0]), added(cross_dw[1], cross_got[1])
        grad_send, cross_give, self_give, b3_far_b = rounds.finish(grad_send, cross_give, self_give, b3_far_b)

        rounds.start(cross_keep, cross_give)
        h1g_own = added(grad_own, core_swap(grad_send))
        h1g_far = far_swap(h1g_own)
        mixed_a, mixed_b, sums_mixed = run(
            mixed_kernel, [one, one, ((2, 1, model), F32)],
            place, [mod, b3a, b3b, b3_far_a, b3_far_b, x2], late=[chunk_rows(cotangent, 0), chunk_rows(cotangent, 1)],
        )
        self_give, h1g_own, mixed_a, mixed_b = rounds.finish(self_give, h1g_own, mixed_a, mixed_b)

        rounds.start(self_keep, self_give)
        grad_a, grad_b, slot_sums = run(
            final_kernel, [one, one, ((slots, 9 * model), F32)],
            place, [mod, h1g_own, h1g_far, sums_a, sums_b, sums_mixed],
            late=[chunk_rows(tokens, 0), chunk_rows(tokens, 1), x1ga, x1gb],
        )
        grad_a, grad_b, slot_sums, mixed_a = rounds.finish(mixed_a, early=(grad_a, grad_b, slot_sums))

        rounds.start()
        slot_far = core_swap(slot_sums)
        mixed_far_a = core_swap(mixed_a)
        slot_far, mixed_far_a, mixed_b = rounds.finish(slot_far, mixed_far_a, mixed_b)

        rounds.start()
        (gathered,) = run(
            slot_kernel, [((slots, model + mod_weight.shape[1]), F32)], place, [slot_sums, slot_far, silu_low]
        )
        gathered = jnp.concatenate([gathered, dp_swap(gathered, 1)], axis=0)
        mixed_far_b = core_swap(mixed_b)
        gathered, mixed_far_b, grad_a, grad_b = rounds.finish(gathered, mixed_far_b, grad_a, grad_b)

        rounds.start()
        gathered = jnp.concatenate([gathered, dp_swap(gathered, 2)], axis=0)
        grad_far_a, grad_far_b = core_swap(grad_a), core_swap(grad_b)
        mlp_in_grad, mlp_out_grad = rounds.whole(0), rounds.whole(1)
        gathered, grad_far_a, grad_far_b, mlp_in_grad, mlp_out_grad = rounds.finish(
            gathered, grad_far_a, grad_far_b, mlp_in_grad, mlp_out_grad
        )

        rounds.start()
        for bit in range(2, dp_bits):
            gathered = jnp.concatenate([gathered, dp_swap(gathered, 1 << bit)], axis=0)
        (mixed,) = run(
            join_cores, [((count, model), BF16)], place, [mixed_a, mixed_b, mixed_far_a, mixed_far_b]
        )
        (token_grad,) = run(
            join_cores, [((count, model), BF16)], place, [grad_a, grad_b, grad_far_a, grad_far_b]
        )
        cross_grads = rounds.four(2)
        gathered_low = gathered.astype(BF16)
        mod_weight_grad = dot_tn(gathered_low[:, :model], gathered_low[:, model:])
        mod_bias_grad = jnp.sum(gathered[:, model:], axis=0)
        mixed, token_grad, mod_weight_grad, mod_bias_grad, *cross_grads = rounds.finish(
            mixed, token_grad, mod_weight_grad, mod_bias_grad, *cross_grads
        )
        self_grads = rounds.four(3)

        return (
            mixed,
            token_grad,
            self_grads[0].T,
            self_grads[1].T,
            self_grads[2].T,
            self_grads[3],
            cross_grads[0].T,
            cross_grads[1].T,
            cross_grads[2].T,
            cross_grads[3],
            mlp_in_grad,
            mlp_out_grad,
            mod_weight_grad,
            mod_bias_grad,
        )

    rows = P("dp", None)
    by_col = P(None, "tensor")
    by_row = P("tensor", None)
    return jax.shard_map(
        local,
        mesh=mesh,
        in_specs=(
            rows, P("dp", None, None), P("dp"), P("dp"), P("dp"), by_col, by_col, by_col, by_row,
            by_col, by_col, by_col, by_row, by_col, by_row, by_col, P("tensor"), rows,
        ),
        out_specs=(
            rows, rows, by_col, by_col, by_col, by_row, by_col, by_col, by_col, by_row,
            by_col, by_row, by_col, P("tensor"),
        ),
        check_vma=False,
    )
```

```python
import functools
import math

import jax
import jax.numpy as jnp
from jax import lax
from jax.experimental import pallas as pl
from jax.experimental.pallas import tpu as pltpu
from jax.sharding import PartitionSpec as P

HEAD = 64
BLOCK = 256
EPSILON = 1e-06
MASKED = -1000000000.0
CURVE = math.sqrt(2.0 / math.pi)
CUBIC = 0.044715
F32 = jnp.float32
BF16 = jnp.bfloat16


def dot_nn(a, b):
    return lax.dot_general(a, b, (((1,), (0,)), ((), ())), preferred_element_type=F32)


def dot_nt(a, b):
    return lax.dot_general(a, b, (((1,), (1,)), ((), ())), preferred_element_type=F32)


def dot_tn(a, b):
    return lax.dot_general(a, b, (((0,), (0,)), ((), ())), preferred_element_type=F32)


def normalize(values):
    centered = values - jnp.mean(values, axis=-1, keepdims=True)
    inverse = lax.rsqrt(jnp.mean(centered * centered, axis=-1, keepdims=True) + EPSILON)
    return centered * inverse, inverse


def norm_back(grad, normed, inverse):
    first = jnp.mean(grad, axis=-1, keepdims=True)
    second = jnp.mean(grad * normed, axis=-1, keepdims=True)
    return inverse * (grad - first - normed * second)


def column_sum(values):
    return jnp.sum(values, axis=0, keepdims=True)


def three_parts(column):
    high = column.astype(BF16).astype(F32)
    rest = column - high
    middle = rest.astype(BF16).astype(F32)
    return high, middle, rest - middle


def head_slice(rows, head):
    piece = rows[:, head * HEAD : (head + 1) * HEAD]
    return jnp.concatenate([piece, jnp.zeros_like(piece)], axis=1)


class View:
    def __init__(self, ref):
        self.view = ref

    def ref(self):
        return self.view


class Place:
    def __init__(self, ref):
        self.ref = ref

    def __getitem__(self, index):
        return self.ref[0, index]


def run(kernel, outs, scalars, arrays, late=(), scratch=(), cost=0.001, vmem=10):
    in_vmem = pl.BlockSpec(memory_space=pltpu.VMEM)
    pairs = [entry if isinstance(entry, tuple) else (entry, None) for entry in late]
    n_plain = len(arrays)

    def wrapped(place, *refs):
        place = Place(place)
        views = []
        for ref, (_, block) in zip(refs[n_plain:], pairs):
            views.append(View(ref if block is None else ref.at[token_rows(block(place)), :]))
        kernel(place, *refs[:n_plain], *views, *refs[n_plain + len(pairs) :])

    return pl.pallas_call(
        wrapped,
        name=getattr(kernel, "__name__", "advance"),
        out_shape=[jax.ShapeDtypeStruct(shape, kind) for shape, kind in outs],
        in_specs=[in_vmem] * (1 + n_plain + len(pairs)),
        out_specs=[in_vmem] * len(outs),
        scratch_shapes=[pltpu.VMEM(shape, kind) for shape, kind in scratch],
        compiler_params=pltpu.CompilerParams(vmem_limit_bytes=vmem * 1024 * 1024),
        cost_estimate=pl.CostEstimate(flops=int(cost * 1_000_000_000), bytes_accessed=1000, transcendentals=0),
    )(scalars, *arrays, *[array for array, _ in pairs])


SLOT, CORE, ROW, END, TENSOR, OWN, FAR, LIMIT = 0, 4, 5, 6, 7, 8, 10, 12
ORDER = (0, 2, 1, 3)


def block_of(place, chunk):
    return place[CORE] * 2 + chunk


def mod_row(mod, slot, component, model):
    return mod[pl.ds(slot, 1), component * model : (component + 1) * model]


def quad_cols(quad):
    if isinstance(quad, int):
        return slice(quad * 4 * HEAD, (quad + 1) * 4 * HEAD)
    return pl.ds(pl.multiple_of(quad * 4 * HEAD, 4 * HEAD), 4 * HEAD)


def token_rows(block):
    return pl.ds(pl.multiple_of(block * BLOCK, BLOCK), BLOCK)


def text_kernel(place, text, weights, packed):
    rows = text.shape[1]
    wide = weights.shape[0]
    for slot in range(text.shape[0]):
        first = rows * (slot % 2)
        left = wide * (slot // 2)
        packed[first : first + rows, left : left + wide] = dot_nt(text[slot], weights[...]).astype(BF16)


def unpack_kernel(place, q0, o0, q1, o1, part2, rest2, part3, rest3, t0, t1, t2, t3, cqt, co, kall, vall):
    width = q0.shape[0]
    half = width // 2
    rows = kall.shape[1]
    for index, (query, out) in enumerate(((q0, o0), (q1, o1))):
        cqt[index * width : (index + 1) * width, :] = query[...]
        co[index * width : (index + 1) * width, :] = out[...]
    for index, (part, rest) in enumerate(((part2, rest2), (part3, rest3))):
        for piece, row in ((part, place[ROW]), (rest, 1 - place[ROW])):
            at = pl.ds(pl.multiple_of((index + 2) * width + row * half, half), half)
            cqt[at, :] = piece[:half, :]
            co[at, :] = piece[half:, :]
    for slot in range(kall.shape[0]):
        first = rows * (slot % 2)
        left = 2 * width * (slot // 2)
        both = [t[first : first + rows, left : left + 2 * width] for t in (t0, t1, t2, t3)]
        kall[slot] = jnp.concatenate([b[:, :width] for b in both], axis=1)
        vall[slot] = jnp.concatenate([b[:, width:] for b in both], axis=1)


def attend_chunk(place, chunk, qa_in, ka, va, wo, part_own, part_send, qa_out, att):
    heads = ka.shape[0]
    lane = lax.broadcasted_iota(jnp.int32, (BLOCK, 2 * HEAD), 1)
    spot = (lane >= HEAD + 4) & (lane < HEAD + 7)

    @pl.loop(0, 2)
    def _(side):
        at = token_rows(2 * chunk + side)
        here = token_rows(side)
        pieces = []
        for head in range(heads):
            queries = qa_in[head, at, :]
            scores = dot_nt(queries, ka[head])
            top = jnp.max(scores, axis=1, keepdims=True)
            raised = jnp.exp(scores - top).astype(BF16)
            out = dot_nn(raised, va[head])
            total = out[:, HEAD : HEAD + 1]
            pieces.append(out[:, :HEAD] * (1.0 / total))
            high, middle, low = three_parts(-(top + jnp.log(total)))
            more = jnp.where(lane == HEAD + 4, high, jnp.where(lane == HEAD + 5, middle, low))
            qa_out[head, here, :] = jnp.where(spot, more, queries.astype(F32)).astype(BF16)
        attended = jnp.concatenate(pieces, axis=1).astype(BF16)
        att[here, :] = attended
        out = dot_nn(attended, wo[...]).astype(BF16)

        @pl.when(place[CORE] == side)
        def _():
            part_own[...] = out

        @pl.when(place[CORE] != side)
        def _():
            part_send[...] = out


def self_first(place, mod, weights, tokens, wo, part_own, part_send, qa, ka, va, qa_out, att, h1):
    model = mod.shape[1] // 9
    lane = lax.broadcasted_iota(jnp.int32, (BLOCK, 2 * HEAD), 1)
    keep = lane < HEAD
    width = weights.shape[0] // 3
    tokens = tokens.ref()
    slots = [place[SLOT + block] for block in ORDER]

    @pl.loop(0, len(ORDER))
    def _(position):
        rows = token_rows(position)
        first = jnp.where(position == 0, slots[0], slots[1])
        slot = jnp.where(position < 2, first, jnp.where(position == 2, slots[2], slots[3]))
        block = lax.rem(position, 2) * 2 + lax.div(position, 2)
        normed, _ = normalize(tokens[token_rows(block), :].astype(F32))
        hidden = (normed * (1.0 + mod_row(mod, slot, 1, model)) + mod_row(mod, slot, 0, model)).astype(BF16)
        h1[rows, :] = hidden
        rows_qkv = dot_nt(hidden, weights[...])
        q = rows_qkv[:, :width].astype(BF16).astype(F32) * (HEAD**-0.5)
        k = rows_qkv[:, width : 2 * width]
        v = rows_qkv[:, 2 * width :]
        mine = lane == HEAD + slot
        q_more = jnp.where(mine, 1.0, 0.0)
        k_more = jnp.where((lane >= HEAD + 4) & (lane < HEAD + 7), 1.0, 0.0)
        k_more = jnp.where((lane >= HEAD) & (lane < HEAD + 4) & jnp.logical_not(mine), MASKED, k_more)
        v_more = jnp.where((lane >= HEAD) & (lane < HEAD + 3), 1.0, 0.0)
        for head in range(ka.shape[0]):
            qa[head, rows, :] = jnp.where(keep, head_slice(q, head), q_more).astype(BF16)
            ka[head, rows, :] = jnp.where(keep, head_slice(k, head), k_more).astype(BF16)
            va[head, rows, :] = jnp.where(keep, head_slice(v, head), v_more).astype(BF16)
    attend_chunk(place, 0, qa, ka, va, wo.ref(), part_own, part_send, qa_out, att)


def self_second(place, qa, ka, va, wo, part_own, part_send, qa_out, att):
    attend_chunk(place, 1, qa, ka, va, wo.ref(), part_own, part_send, qa_out, att)


def quad_stack(rows, masks):
    return jnp.concatenate([rows * mask for mask in masks], axis=0)


def quad_masks():
    lane = lax.broadcasted_iota(jnp.int32, (1, 4 * HEAD), 1)
    return [jnp.where((lane >= u * HEAD) & (lane < (u + 1) * HEAD), 1.0, 0.0) for u in range(4)]


def quad_probs(scores, limit, text_rows):
    key_row = lax.broadcasted_iota(jnp.int32, (text_rows, 1), 0)
    bias = jnp.where(key_row < limit, 0.0, MASKED)
    probs = []
    for u in range(4):
        part = scores[u * text_rows : (u + 1) * text_rows, :] + bias
        raised = jnp.exp(part - jnp.max(part, axis=0, keepdims=True))
        probs.append(raised * (1.0 / jnp.sum(raised, axis=0, keepdims=True)))
    return probs


def middle_chunk(
    place, chunk, mod, sum_own, sum_far, cqt, co, kall, vall, tokens, cot, win0, wout0, win1, wout1, x2_before,
    h3g_out, h3_out, act0, act1, pg0, pg1, b3g_out, x1_out, b2_out, h2_out, q2_out, cr_out, b3_out, x2_out,
):
    model = cqt.shape[1]
    text_rows = kall.shape[1]
    slot = place[OWN + chunk]

    def m(component):
        return mod_row(mod, slot, component, model)

    x1 = tokens.ref()[...].astype(F32) + m(2) * (sum_own[...].astype(F32) + sum_far[...].astype(F32))
    x1_out[...] = x1
    normed, _ = normalize(x1)
    h2 = (normed * (1.0 + m(4)) + m(3)).astype(BF16)
    h2_out[...] = h2
    q2 = (dot_nt(h2, cqt[...]).astype(BF16).astype(F32) * (HEAD**-0.5)).astype(BF16)
    q2_out[...] = q2
    masks = [mask.astype(BF16) for mask in quad_masks()]
    limit = place[LIMIT + chunk]

    crossed = []
    for quad in range(model // (4 * HEAD)):
        cols = quad_cols(quad)
        scores = dot_nt(quad_stack(kall[slot, :, cols], masks), q2[:, cols])
        probs = jnp.concatenate(quad_probs(scores, limit, text_rows), axis=0)
        crossed.append(dot_tn(probs.astype(BF16), quad_stack(vall[slot, :, cols], masks)).astype(BF16))
    crossed = jnp.concatenate(crossed, axis=1)
    cr_out[...] = crossed
    b2 = dot_nn(crossed, co[...])
    b2_out[...] = b2
    x2 = x1 + m(5) * b2
    x2_out[chunk * BLOCK : (chunk + 1) * BLOCK, :] = x2
    normed, _ = normalize(x2)
    h3 = (normed * (1.0 + m(7)) + m(6)).astype(BF16)
    h3_out[...] = h3
    b3g = (cot.ref()[...].astype(F32) * m(8)).astype(BF16)
    b3g_out[...] = b3g
    b3 = h3g = None
    for win, wout, act_out, pg_out in ((win0, wout0, act0, pg0), (win1, wout1, act1, pg1)):
        win, wout = win.ref(), wout.ref()
        pre = dot_nn(h3, win[...])
        square = pre * pre
        bent = jnp.tanh(CURVE * (pre + CUBIC * (square * pre)))
        act = (0.5 * pre * (1.0 + bent)).astype(BF16)
        act_out[...] = act
        slope = 0.5 * (1.0 + bent) + 0.5 * pre * (1.0 - bent * bent) * (CURVE * (1.0 + 3.0 * CUBIC * square))
        b3_half = dot_nn(act, wout[...])
        pg = (dot_nt(b3g, wout[...]) * slope).astype(BF16)
        pg_out[...] = pg
        h3g_half = dot_nt(pg, win[...])
        b3 = b3_half if b3 is None else b3 + b3_half
        h3g = h3g_half if h3g is None else h3g + h3g_half
    b3_out[...] = b3.astype(BF16)
    if chunk:
        x2_out[0:BLOCK, :] = x2_before.ref()[...]
    h3g_out[...] = h3g.astype(BF16)


def middle_first(place, *refs):
    middle_chunk(place, 0, *refs[:13], None, *refs[13:])


def middle_second(place, *refs):
    middle_chunk(place, 1, *refs)


def stacked(first, second):
    return jnp.concatenate([first[...], second[...]], axis=0)


def mlp_back(
    place, h3a, h3b, pg0a, pg0b, pg1a, pg1b, act0a, act0b, act1a, act1b, b3ga, b3gb,
    in_own, in_send, out_own, out_send,
):
    half = in_own.shape[1]
    grads = (stacked(pg0a, pg0b), stacked(pg1a, pg1b))
    grad = stacked(b3ga, b3gb)

    @pl.loop(0, 2)
    def _(part):
        cols = pl.ds(pl.multiple_of(part * half, half), half)
        kept = part ^ place[ROW]
        rows = jnp.concatenate([h3a[:, cols], h3b[:, cols]], axis=0)
        in_send[kept] = dot_tn(rows, grads[1]).astype(BF16)
        in_own[kept] = dot_tn(rows, grads[0]).astype(BF16)
        out_send[kept] = dot_tn(jnp.concatenate([act1a[:, cols], act1b[:, cols]], axis=0), grad).astype(BF16)
        out_own[kept] = dot_tn(jnp.concatenate([act0a[:, cols], act0b[:, cols]], axis=0), grad).astype(BF16)


def cross_chunk(
    place, chunk, mod, h3g_own, h3g_far, kall, vall, cqt, co, x1_in, b2_in, cot, q2_in, sum_own, sum_far,
    b1g_out, dq_out, b2g_out, dk_out, dv_out, sums, x1g_out, out_grad,
):
    model = cqt.shape[1]
    text_rows = kall.shape[1]
    slot = place[OWN + chunk]

    def m(component):
        return mod_row(mod, slot, component, model)

    x1 = x1_in.ref()[...]
    b2 = b2_in.ref()[...]
    h3g = h3g_own[...].astype(F32) + h3g_far[...].astype(F32)
    normed, inverse = normalize(x1 + m(5) * b2)
    sums[4:5, :] = column_sum(h3g)
    sums[5:6, :] = column_sum(h3g * normed)
    x2g = cot.ref()[...].astype(F32) + norm_back(h3g * (1.0 + m(7)), normed, inverse)
    sums[3:4, :] = column_sum(x2g * b2)
    b2g = (x2g * m(5)).astype(BF16)
    b2g_out[...] = b2g
    out_grad[...] = dot_nt(b2g, co[...]).astype(BF16)
    masks = quad_masks()
    low = [mask.astype(BF16) for mask in masks]
    limit = place[LIMIT + chunk]

    def by_quad(quad):
        cols = quad_cols(quad)
        queries = q2_in.ref()[:, cols]
        grads = out_grad[:, cols]
        keys = quad_stack(kall[slot, :, cols], low)
        values = quad_stack(vall[slot, :, cols], low)
        probs = quad_probs(dot_nt(keys, queries), limit, text_rows)
        prob_grad = dot_nt(values, grads)
        score_grad = []
        for u in range(4):
            part = prob_grad[u * text_rows : (u + 1) * text_rows, :]
            row_dot = jnp.sum(probs[u] * part, axis=0, keepdims=True)
            score_grad.append((probs[u] * (part - row_dot)).astype(BF16))
        score_grad = jnp.concatenate(score_grad, axis=0)
        dv = dot_nn(jnp.concatenate(probs, axis=0).astype(BF16), grads)
        dk = dot_nn(score_grad, queries)
        dq_out[:, cols] = (dot_tn(score_grad, keys) * (HEAD**-0.5)).astype(BF16)
        for wide, out in ((dk, dk_out), (dv, dv_out)):
            total = None
            for u in range(4):
                part = wide[u * text_rows : (u + 1) * text_rows, :] * masks[u]
                total = part if total is None else total + part
            out[:, cols] = total.astype(BF16)
    if chunk:
        for quad in range(model // (4 * HEAD)):
            by_quad(quad)
    else:
        pl.loop(0, model // (4 * HEAD))(by_quad)
    h2g = dot_nn(dq_out[...], cqt[...])
    normed, inverse = normalize(x1)
    sums[1:2, :] = column_sum(h2g)
    sums[2:3, :] = column_sum(h2g * normed)
    x1g = x2g + norm_back(h2g * (1.0 + m(4)), normed, inverse)
    x1g_out[...] = x1g
    branch = sum_own.ref()[...].astype(F32) + sum_far.ref()[...].astype(F32)
    sums[0:1, :] = column_sum(x1g * branch)
    sums[6:8, :] = jnp.zeros((2, model), F32)
    b1g_out[...] = (x1g * m(2)).astype(BF16)


def cross_first(place, *refs):
    cross_chunk(place, 0, *refs)


def cross_second(place, *refs):
    cross_chunk(place, 1, *refs)


def cross_weights(
    place, dqa, dqb, b2ga, b2gb, dka, dkb, dva, dvb, h2a, h2b, cra, crb, text, own, send,
):
    width = own.shape[1] // 2
    row = place[ROW]
    h2a, h2b, cra, crb, text = h2a.ref(), h2b.ref(), cra.ref(), crb.ref(), text.ref()
    slots = [place[OWN + chunk] for chunk in range(2)]

    @pl.loop(0, h2a.shape[1] // BLOCK)
    def _(part):
        to = token_rows(part)
        hidden = jnp.concatenate([h2a[:, to], h2b[:, to]], axis=0)
        grads = jnp.concatenate([b2ga[:, to], b2gb[:, to]], axis=0)
        texts = [text[slot, :, to] for slot in slots]
        for member, out in ((1, send), (0, own)):
            start = (member * width // 128) * 128
            skip = member * width - start
            cols = slice(start, start + 2 * 128)
            kept = slice(skip, skip + width)

            def two(first, second):
                return jnp.concatenate([first[:, cols], second[:, cols]], axis=0)

            top, bottom = slice(0, width), slice(width, 2 * width)
            out[row, top, to] = dot_tn(two(dqa, dqb), hidden)[kept].astype(BF16)
            out[row, bottom, to] = (dot_tn(dka[:, cols], texts[0]) + dot_tn(dkb[:, cols], texts[1]))[kept].astype(BF16)
            out[1 - row, top, to] = (dot_tn(dva[:, cols], texts[0]) + dot_tn(dvb[:, cols], texts[1]))[kept].astype(
                BF16
            )
            out[1 - row, bottom, to] = dot_tn(two(cra, crb), grads)[kept].astype(BF16)


def keys_back(block, qa, ka, va, da, dq_sum):
    rows = token_rows(block)
    dks = []
    dvs = []
    for head in range(ka.shape[0]):
        keys = ka[head, rows, :]
        probs = jnp.exp(dot_nt(keys, qa[head]))
        prob_grad = dot_nt(va[head, rows, :], da[head])
        score_grad = (probs * prob_grad).astype(BF16)
        dvs.append(dot_nn(probs.astype(BF16), da[head])[:, :HEAD])
        dks.append(dot_nn(score_grad, qa[head])[:, :HEAD])
        dq = dot_tn(score_grad, keys)
        dq_sum[head] += dq
    return jnp.concatenate(dks, axis=1).astype(BF16), jnp.concatenate(dvs, axis=1).astype(BF16)


def self_back_first(
    place, b1g_a, b1g_b, far_a, far_b, wo, att_a, att_b, qa_a, qa_b, ka, va,
    b1g, att, qa, da, dq_sum, dk_all, dv_all,
):
    blocks = b1g.shape[0] // BLOCK
    heads = da.shape[0]
    core = place[CORE]
    for chunk, (own, far) in enumerate(((b1g_a, far_a), (b1g_b, far_b))):
        b1g[token_rows(2 * chunk + core), :] = own[...]
        b1g[token_rows(2 * chunk + 1 - core), :] = far[...]
    wo = wo.ref()
    att[0 : 2 * BLOCK, :] = att_a.ref()[...]
    att[2 * BLOCK : 4 * BLOCK, :] = att_b.ref()[...]
    lane = lax.broadcasted_iota(jnp.int32, (BLOCK, 2 * HEAD), 1)

    @pl.loop(0, blocks)
    def _(block):
        rows = token_rows(block)
        grads = dot_nt(b1g[rows, :], wo[...]).astype(BF16).astype(F32)
        dots = grads * att[rows, :].astype(F32)
        for head in range(heads):
            row_dot = jnp.sum(dots[:, head * HEAD : (head + 1) * HEAD], axis=1, keepdims=True)
            high, middle, low = three_parts(-row_dot)
            more = jnp.where(lane == HEAD, high, jnp.where(lane == HEAD + 1, middle, low))
            more = jnp.where(lane < HEAD + 3, more, 0.0)
            da[head, rows, :] = jnp.where(lane < HEAD, head_slice(grads, head), more).astype(BF16)
    qa[:, 0 : 2 * BLOCK, :] = qa_a.ref()[...]
    qa[:, 2 * BLOCK : 4 * BLOCK, :] = qa_b.ref()[...]
    ka, va = ka.ref(), va.ref()
    dq_sum[...] = jnp.zeros_like(dq_sum)

    @pl.loop(0, 2)
    def _(block):
        rows = token_rows(block)
        dk_all[rows, :], dv_all[rows, :] = keys_back(block, qa, ka, va, da, dq_sum)


def self_back_second(
    place, b1g, att, qa, da, dq_in, dk_in, dv_in, weights, ka, va, h1,
    part_own, part_send, dw_keep, dw_give,
    dq_sum, grad_all,
):
    blocks = b1g.shape[0] // BLOCK
    heads = da.shape[0]
    core = place[CORE]
    width = heads * HEAD
    ka, va = ka.ref(), va.ref()
    dq_sum[...] = dq_in[...]
    grad_all[0 : 2 * BLOCK, width : 2 * width] = dk_in[0 : 2 * BLOCK, :]
    grad_all[0 : 2 * BLOCK, 2 * width : 3 * width] = dv_in[0 : 2 * BLOCK, :]

    @pl.loop(2, blocks)
    def _(block):
        rows = token_rows(block)
        dk, dv = keys_back(block, qa, ka, va, da, dq_sum)
        grad_all[rows, width : 2 * width] = dk
        grad_all[rows, 2 * width : 3 * width] = dv
    h1 = h1.ref()

    @pl.loop(0, blocks)
    def _(block):
        rows = token_rows(block)
        dq = jnp.concatenate([dq_sum[head, rows, :HEAD] for head in range(heads)], axis=1)
        grad_all[rows, 0:width] = (dq * (HEAD**-0.5)).astype(BF16)
        out = dot_nn(grad_all[rows, :], weights[...]).astype(BF16)
        side = lax.rem(block, 2)
        out_rows = token_rows(lax.div(block, 2))

        @pl.when(core == side)
        def _():
            part_own[out_rows, :] = out

        @pl.when(core != side)
        def _():
            part_send[out_rows, :] = out

    @pl.loop(0, h1.shape[1] // BLOCK)
    def _(part):
        cols = token_rows(part)
        grads = dot_tn(grad_all[...], h1[:, cols]).astype(BF16)
        query_key = (grads[:width], grads[width : 2 * width])
        value_out = (grads[2 * width :], dot_tn(att[...], b1g[:, cols]).astype(BF16))
        for flag, first, second in ((0, query_key, value_out), (1, value_out, query_key)):

            @pl.when(place[ROW] == flag)
            def _():
                for index in range(2):
                    rows = slice(index * width, (index + 1) * width)
                    dw_keep[rows, cols] = first[index]
                    dw_give[rows, cols] = second[index]


def mixed_kernel(place, mod, b3a, b3b, far_a, far_b, x2, cot_a, cot_b, mixed_a, mixed_b, sums):
    model = mixed_a.shape[1]
    for chunk, (own, far, cot) in enumerate(((b3a, far_a, cot_a), (b3b, far_b, cot_b))):
        mixed = (mixed_a, mixed_b)[chunk]
        rows = slice(chunk * BLOCK, (chunk + 1) * BLOCK)
        slot = place[OWN + chunk]
        b3 = own[...].astype(F32) + far[...].astype(F32)
        mixed[...] = (x2[rows, :] + mod_row(mod, slot, 8, model) * b3).astype(BF16)
        sums[chunk] = column_sum(cot.ref()[...].astype(F32) * b3)


def final_kernel(
    place, mod, h1g_own, h1g_far, sums_a, sums_b, sums_mixed, tokens_a, tokens_b, x1ga, x1gb, grad_a, grad_b, slot_sums,
):
    model = grad_a.shape[1]
    slot_sums[...] = jnp.zeros_like(slot_sums)
    for chunk, (x1g, sums, tokens) in enumerate(((x1ga, sums_a, tokens_a), (x1gb, sums_b, tokens_b))):
        rows = slice(chunk * BLOCK, (chunk + 1) * BLOCK)
        slot = place[OWN + chunk]
        h1g = h1g_own[rows, :].astype(F32) + h1g_far[rows, :].astype(F32)
        normed, inverse = normalize(tokens.ref()[...].astype(F32))
        scaled = h1g * (1.0 + mod_row(mod, slot, 1, model))
        (grad_a, grad_b)[chunk][...] = (x1g.ref()[...] + norm_back(scaled, normed, inverse)).astype(BF16)
        terms = [column_sum(h1g), column_sum(h1g * normed)]
        terms += [sums[i : i + 1, :] for i in range(6)] + [sums_mixed[chunk]]
        for component, term in enumerate(terms):
            slot_sums[pl.ds(slot, 1), component * model : (component + 1) * model] += term


def join_cores(place, mine_a, mine_b, other_a, other_b, out):
    for chunk, (mine, other) in enumerate(((mine_a, other_a), (mine_b, other_b))):
        out[token_rows(place[CORE] * 2 + chunk), :] = mine[...]
        out[token_rows((1 - place[CORE]) * 2 + chunk), :] = other[...]


def join_rows(place, mine, other, out):
    count = mine.shape[0]
    out[pl.ds(pl.multiple_of(place[ROW] * count, BLOCK // 2), count), :] = mine[...].astype(F32)
    out[pl.ds(pl.multiple_of((1 - place[ROW]) * count, BLOCK // 2), count), :] = other[...].astype(F32)


def join_four(place, mine, other, first, second, third, fourth):
    width = first.shape[0]
    for flag, top, bottom in ((0, mine, other), (1, other, mine)):

        @pl.when(place[ROW] == flag)
        def _():
            first[...] = top[:width, :].astype(F32)
            second[...] = top[width:, :].astype(F32)
            third[...] = bottom[:width, :].astype(F32)
            fourth[...] = bottom[width:, :].astype(F32)


def slot_kernel(place, own, far, silu, out):
    model = silu.shape[1]
    count = out.shape[1] - model
    out[:, :model] = silu[...].astype(F32)
    for index in range(own.shape[1] // count):
        cols = slice(index * count, (index + 1) * count)

        @pl.when(place[TENSOR] == index)
        def _():
            out[:, model:] = (own[:, cols] + far[:, cols]).astype(BF16).astype(F32)


def advance_kernel(roles, place, *refs):
    refs = list(refs)
    values, got = {}, {}
    for role in roles:
        values[role] = refs.pop(0)
    for name in ("row", "column", "middle"):
        if any(role in roles for role in {"row": "a", "column": "bd", "middle": "c"}[name]):
            got[name] = refs.pop(0)
    outs = {role: refs.pop(0) for role in roles}
    end = place[END]
    if "a" in roles:
        outs["a"][...] = added(values["a"][...], got["row"][...])
    if "c" in roles:

        @pl.when(end == 0)
        def _():
            outs["c"][...] = added(values["c"][...], got["middle"][...])

        @pl.when(end != 0)
        def _():
            outs["c"][...] = values["c"][...]

    if "b" in roles:

        @pl.when(end == 0)
        def _():
            outs["b"][...] = added(values["b"][...], got["column"][...])

        @pl.when(end != 0)
        def _():
            outs["b"][...] = values["b"][...]

    if "d" in roles:

        @pl.when(end == 0)
        def _():
            outs["d"][...] = values["d"][...]

        @pl.when(end != 0)
        def _():
            outs["d"][...] = got["column"][...]

    if refs:

        @pl.when(end == 0)
        def _():
            refs[0][...] = outs["c"][...]

        @pl.when(end != 0)
        def _():
            refs[0][...] = outs["a"][...]


def added(first, second):
    return (first.astype(F32) + second.astype(F32)).astype(BF16)


def solution(mesh):
    n_dp = mesh.shape["dp"]
    n_tensor = mesh.shape["tensor"]
    n_col = n_dp // 2
    dp_bits = int(math.log2(n_dp))

    def tensor_swap(value, flip):
        return lax.ppermute(value, "tensor", [(i, i ^ flip) for i in range(n_tensor)])

    def core_swap(value):
        return tensor_swap(value, 1)

    def far_swap(value):
        return tensor_swap(value, 2)

    def dp_swap(value, flip):
        return lax.ppermute(value, "dp", [(i, i ^ flip) for i in range(n_dp)])

    def tie(*values):
        return lax.optimization_barrier(values) if values else ()

    def pair_up(flag, mine, other):
        return jnp.concatenate([jnp.where(flag == 0, mine, other), jnp.where(flag == 0, other, mine)], axis=0)

    def local(
        tokens, text_states, clip_len, text_len, timesteps, q_weight, k_weight, v_weight, o_weight,
        cross_q, cross_k, cross_v, cross_o, mlp_in, mlp_out, mod_weight, mod_bias, cotangent,
    ):
        count, model = tokens.shape
        slots, text_rows = text_states.shape[:2]
        width = o_weight.shape[0]
        heads = width // HEAD
        half = count // 2
        text_pad = -(-text_rows // 16) * 16
        tensor_at = lax.axis_index("tensor")
        dp_at = lax.axis_index("dp")
        core = tensor_at & 1
        row = dp_at & 1
        column = dp_at >> 1

        ends = jnp.cumsum(clip_len)
        starts = jnp.arange(count // BLOCK, dtype=jnp.int32) * BLOCK
        slot_of = jnp.sum((starts[:, None] >= ends[None, :]).astype(jnp.int32), axis=1)
        end = (column == 0) | (column == n_col - 1)
        own_slots = lax.dynamic_slice_in_dim(slot_of, core * 2, 2, 0)
        far_slots = lax.dynamic_slice_in_dim(slot_of, (1 - core) * 2, 2, 0)
        limits = jnp.sum(jnp.where(own_slots[:, None] == jnp.arange(slots)[None, :], text_len[None, :], 0), axis=1)
        single = jnp.stack([core, row, end.astype(jnp.int32), tensor_at])
        place = jnp.concatenate([slot_of, single, own_slots, far_slots, limits])
        place = jnp.pad(place[None, :], ((0, 7), (0, 128 - place.shape[0])))
        place = place.astype(jnp.int32)

        query_own = cross_q.T
        part_own = jnp.concatenate(
            [lax.dynamic_slice_in_dim(w, row * (width // 2), width // 2, 0) for w in (query_own, cross_o)], axis=0
        )
        text_weights = jnp.concatenate([cross_k.T, cross_v.T], axis=0)
        text = jnp.pad(text_states, ((0, 0), (0, text_pad - text_rows), (0, 0)))
        self_weights = jnp.concatenate([q_weight.T, k_weight.T, v_weight.T], axis=0)

        half_width = model // 2
        ramp = jnp.arange(half_width).astype(F32)
        frequency = jnp.exp(ramp * (-math.log(10000.0) / half_width))
        angles = timesteps.astype(F32)[:, None] * frequency[None, :]
        embed = jnp.concatenate([jnp.cos(angles), jnp.sin(angles)], axis=1)
        silu_low = jax.nn.silu(embed).astype(BF16)
        part_far = far_swap(part_own)
        wout1 = core_swap(mlp_out)
        mod_own = dot_nn(silu_low, mod_weight) + mod_bias.astype(F32)
        mod_far = [tensor_swap(mod_own, flip) for flip in range(1, n_tensor)]
        (text_own,) = run(text_kernel, [((2 * text_pad, model), BF16)], place, [text, text_weights], cost=1.0)
        text_own, self_weights, wout1, *mod_far = tie(text_own, self_weights, wout1, *mod_far)
        text_far = far_swap(text_own)
        query_own, out_own, text_own = tie(query_own, cross_o, text_own)
        query1, out1, text1 = core_swap(query_own), core_swap(out_own), core_swap(text_own)
        mod_all = jnp.stack([mod_own] + mod_far)
        mod = jnp.concatenate(
            [lax.dynamic_index_in_dim(mod_all, tensor_at ^ j, 0, keepdims=False) for j in range(n_tensor)], axis=1
        )

        wide = (heads, count, 2 * HEAD)
        block_wide = (heads, 2 * BLOCK, 2 * HEAD)
        one = ((BLOCK, model), BF16)
        one_f32 = ((BLOCK, model), F32)
        attend_far = [(block_wide, BF16), ((2 * BLOCK, width), BF16)]
        own_a, send_a, qa, ka, va, qa_a, att_a, h1 = run(
            self_first, [one, one] + [(wide, BF16)] * 3 + attend_far + [((count, model), BF16)], place, [mod, self_weights], cost=0.001,
            late=[tokens, o_weight],
        )
        send_a, part_far, text_far, query1, out1, text1 = tie(send_a, part_far, text_far, query1, out1, text1)
        sum_a = added(own_a, core_swap(send_a))
        sum_a, qa, part_far, text_far, win0 = tie(sum_a, qa, part_far, text_far, mlp_in)
        far_a = far_swap(sum_a)
        rest_far = dp_swap(part_far, 1)
        part3, text3, win1 = core_swap(part_far), core_swap(text_far), core_swap(win0)
        own_b, send_b, qa_b, att_b = run(
            self_second, [one, one] + attend_far, place, [qa, ka, va], late=[o_weight]
        )
        (far_a,) = tie(far_a)
        send_b, far_a, rest_far, part3, text3, win1 = tie(send_b, far_a, rest_far, part3, text3, win1)
        rest3 = core_swap(rest_far)
        sum_b = added(own_b, core_swap(send_b))
        sum_b, rest3 = tie(sum_b, rest3)
        far_b = far_swap(sum_b)
        cqt, co, kall, vall = run(
            unpack_kernel, [((model, model), BF16)] * 2 + [((slots, text_pad, model), BF16)] * 2,
            place,
            [query_own, out_own, query1, out1, part_far, rest_far, part3, rest3, text_own, text1, text_far, text3],
            cost=0.001,
        )
        shared = [cqt, co, kall, vall]

        def chunk_rows(array, chunk):
            return (array, functools.partial(block_of, chunk=chunk))

        def middle(kernel, chunk, own, far, *before):
            return run(
                kernel, [one] * 7 + [one_f32, one_f32] + [one] * 4 + [(((chunk + 1) * BLOCK, model), F32)], place,
                [mod, own, far] + shared, cost=7.5,
                late=[chunk_rows(tokens, chunk), chunk_rows(cotangent, chunk), mlp_in, mlp_out, win1, wout1, *before],
            )

        h3ga, h3a, act0a, act1a, pg0a, pg1a, b3ga, x1a, b2a, h2a, q2a, cra, b3a, x2a = middle(
            middle_first, 0, sum_a, far_a
        )
        h3ga, far_b = tie(h3ga, far_b)
        h3g_far_a = far_swap(h3ga)
        h3gb, h3b, act0b, act1b, pg0b, pg1b, b3gb, x1b, b2b, h2b, q2b, crb, b3b, x2 = middle(
            middle_second, 1, sum_b, far_b, x2a
        )
        h3gb, pg0b, h3g_far_a = tie(h3gb, pg0b, h3g_far_a)
        h3g_far_b = far_swap(h3gb)

        in_own, in_send, out_own, out_send = run(
            mlp_back, [((2, model // 2, model), BF16)] * 4, place,
            [h3a, h3b, pg0a, pg0b, pg1a, pg1b, act0a, act0b, act1a, act1b, b3ga, b3gb], cost=0.001,
        )

        def cross(kernel, chunk, h3g_own, h3g_far, x1, b2, own, far, q2):
            return run(
                kernel, [one] * 3 + [((text_pad, model), BF16)] * 2 + [((8, model), F32), one_f32], place,
                [mod, h3g_own, h3g_far, kall, vall, cqt, co],
                late=[x1, b2, chunk_rows(cotangent, chunk), q2, own, far], scratch=[one],
                cost=4.0 if chunk else 0.001,
            )

        b1g_a, dqa, b2ga, dka, dva, sums_a, x1ga = cross(
            cross_first, 0, h3ga, h3g_far_a, x1a, b2a, sum_a, far_a, q2a
        )
        in_send, out_send, b1g_a, h3g_far_b = tie(in_send, out_send, b1g_a, h3g_far_b)
        in_got, b1g_far_a = core_swap(in_send), core_swap(b1g_a)
        b1g_b, dqb, b2gb, dkb, dvb, sums_b, x1gb = cross(
            cross_second, 1, h3gb, h3g_far_b, x1b, b2b, sum_b, far_b, q2b
        )
        in_got, out_send, b1g_far_a, b1g_b, dqb, b3a = tie(in_got, out_send, b1g_far_a, b1g_b, dqb, b3a)
        in_keep, in_give = added(in_own[0], in_got[0]), added(in_own[1], in_got[1])

        across = [(i, i ^ 1) for i in range(n_dp)]
        neighbours = [(i, i ^ 2) for i in range(n_dp)]
        middle_pair = [(2 * a + r, 2 * b + r) for a, b in ((1, 2), (2, 1)) for r in range(2)]
        chain_rows = (model // 2, model)

        class Rounds:
            def __init__(self):
                self.values, self.column_send, self.results, self.waiting = {}, None, [], []

            def start(self, *chain):
                self.got = {}
                if n_col != 4:
                    self.waiting += [chain] if chain else []
                    return
                if chain:
                    self.values["a"] = chain[0]
                    self.got["row"] = lax.ppermute(chain[1], "dp", across)
                if "e" in self.values:
                    self.got["last"] = lax.ppermute(self.values["e"], "dp", across)
                if "b" in self.values or "d" in self.values:
                    self.got["column"] = lax.ppermute(self.column_send, "dp", neighbours)
                if "c" in self.values:
                    self.got["middle"] = lax.ppermute(self.values["c"], "dp", middle_pair)

            def finish(self, *others, early=()):
                order = [name for name in ("row", "last", "column", "middle") if name in self.got]
                settled = list(early)
                for name in order:
                    settled = list(tie(self.got[name], *settled))
                tied = tie(*settled, *others)
                self.got = dict(zip(reversed(order), tied))
                others = tied[len(order) :]
                if "last" in self.got:
                    self.results.append((self.values.pop("e"), self.got.pop("last")))
                roles = "".join(role for role in "abcd" if role in self.values)
                if not roles:
                    return others
                operands = [self.values[role] for role in roles]
                operands += [self.got[name] for name in ("row", "column", "middle") if name in self.got]
                sends = "a" in roles or "c" in roles
                both = "a" in roles and "c" in roles
                outs = run(
                    functools.partial(advance_kernel, roles), [(chain_rows, BF16)] * (len(roles) + both),
                    place, operands, cost=0.3,
                )
                done = tie(*outs, *others)
                stepped = dict(zip(roles, done))
                if sends:
                    self.column_send = done[len(roles)] if both else stepped["a" if "a" in roles else "c"]
                self.values = {{"a": "b", "b": "c", "c": "d", "d": "e"}[role]: v for role, v in stepped.items()}
                return done[len(outs) :]

            def halves(self, number):
                return self.results[number] if n_col == 4 else self.slowly(*self.waiting[number])

            def whole(self, number):
                return run(join_rows, [((model, model), F32)], place, self.halves(number))[0]

            def four(self, number):
                return run(join_four, [((width, model), F32)] * 4, place, self.halves(number))

            def slowly(self, keep, give):
                total = added(keep, lax.ppermute(give, "dp", across))
                for bit in range(1, dp_bits):
                    size, flag = total.shape[0] // 2, (dp_at >> bit) & 1
                    sent = lax.dynamic_slice_in_dim(total, (1 - flag) * size, size, 0)
                    total = added(lax.dynamic_slice_in_dim(total, flag * size, size, 0), dp_swap(sent, 1 << bit))
                for bit in reversed(range(1, dp_bits)):
                    total = pair_up((dp_at >> bit) & 1, total, dp_swap(total, 1 << bit))
                return total, lax.ppermute(total, "dp", across)

        rounds = Rounds()

        rounds.start(in_keep, in_give)
        b1g_far_b, out_got = core_swap(b1g_b), core_swap(out_send)
        out_keep, out_give = added(out_own[0], out_got[0]), added(out_own[1], out_got[1])
        b3_far_a = far_swap(b3a)
        cross_dw, cross_send = run(
            cross_weights, [((2, 2 * width, model), BF16)] * 2, place,
            [dqa, dqb, b2ga, b2gb, dka, dkb, dva, dvb], late=[h2a, h2b, cra, crb, text], cost=0.001,
        )
        b1g_far_b, cross_send = tie(b1g_far_b, cross_send)
        b1g_all, att_all, qa_all, da, dq_sum, dk_all, dv_all = run(
            self_back_first,
            [((count, model), BF16), ((count, width), BF16), (wide, BF16), (wide, BF16), (wide, F32)]
            + [((count, width), BF16)] * 2,
            place, [b1g_a, b1g_b, b1g_far_a, b1g_far_b],
            late=[o_weight, att_a, att_b, qa_a, qa_b, ka, va], cost=0.001,
        )
        b1g_all, cross_send, out_give, b3b, b3_far_a = rounds.finish(b1g_all, cross_send, out_give, b3b, b3_far_a)

        rounds.start(out_keep, out_give)
        cross_got = core_swap(cross_send)
        b3_far_b = far_swap(b3b)
        grad_own, grad_send, self_keep, self_give = run(
            self_back_second,
            [((half, model), BF16)] * 2 + [((2 * width, model), BF16)] * 2, place,
            [b1g_all, att_all, qa_all, da, dq_sum, dk_all, dv_all, self_weights], late=[ka, va, h1],
            scratch=[(wide, F32), ((count, 3 * width), BF16)],
        )
        cross_keep, cross_give = added(cross_dw[0], cross_got[0]), added(cross_dw[1], cross_got[1])
        grad_send, cross_give, self_give, b3_far_b = rounds.finish(grad_send, cross_give, self_give, b3_far_b)

        rounds.start(cross_keep, cross_give)
        h1g_own = added(grad_own, core_swap(grad_send))
        h1g_far = far_swap(h1g_own)
        mixed_a, mixed_b, sums_mixed = run(
            mixed_kernel, [one, one, ((2, 1, model), F32)],
            place, [mod, b3a, b3b, b3_far_a, b3_far_b, x2], late=[chunk_rows(cotangent, 0), chunk_rows(cotangent, 1)],
        )
        self_give, h1g_own, mixed_a, mixed_b = rounds.finish(self_give, h1g_own, mixed_a, mixed_b)

        rounds.start(self_keep, self_give)
        grad_a, grad_b, slot_sums = run(
            final_kernel, [one, one, ((slots, 9 * model), F32)],
            place, [mod, h1g_own, h1g_far, sums_a, sums_b, sums_mixed],
            late=[chunk_rows(tokens, 0), chunk_rows(tokens, 1), x1ga, x1gb],
        )
        grad_a, grad_b, slot_sums, mixed_a = rounds.finish(mixed_a, early=(grad_a, grad_b, slot_sums))

        rounds.start()
        slot_far = core_swap(slot_sums)
        mixed_far_a = core_swap(mixed_a)
        slot_far, mixed_far_a, mixed_b = rounds.finish(slot_far, mixed_far_a, mixed_b)

        rounds.start()
        (gathered,) = run(
            slot_kernel, [((slots, model + mod_weight.shape[1]), F32)], place, [slot_sums, slot_far, silu_low]
        )
        gathered = jnp.concatenate([gathered, dp_swap(gathered, 1)], axis=0)
        mixed_far_b = core_swap(mixed_b)
        gathered, mixed_far_b, grad_a, grad_b = rounds.finish(gathered, mixed_far_b, grad_a, grad_b)

        rounds.start()
        gathered = jnp.concatenate([gathered, dp_swap(gathered, 2)], axis=0)
        grad_far_a, grad_far_b = core_swap(grad_a), core_swap(grad_b)
        mlp_in_grad, mlp_out_grad = rounds.whole(0), rounds.whole(1)
        gathered, grad_far_a, grad_far_b, mlp_in_grad, mlp_out_grad = rounds.finish(
            gathered, grad_far_a, grad_far_b, mlp_in_grad, mlp_out_grad
        )

        rounds.start()
        for bit in range(2, dp_bits):
            gathered = jnp.concatenate([gathered, dp_swap(gathered, 1 << bit)], axis=0)
        (mixed,) = run(
            join_cores, [((count, model), BF16)], place, [mixed_a, mixed_b, mixed_far_a, mixed_far_b]
        )
        (token_grad,) = run(
            join_cores, [((count, model), BF16)], place, [grad_a, grad_b, grad_far_a, grad_far_b]
        )
        cross_grads = rounds.four(2)
        gathered_low = gathered.astype(BF16)
        mod_weight_grad = dot_tn(gathered_low[:, :model], gathered_low[:, model:])
        mod_bias_grad = jnp.sum(gathered[:, model:], axis=0)
        mixed, token_grad, mod_weight_grad, mod_bias_grad, *cross_grads = rounds.finish(
            mixed, token_grad, mod_weight_grad, mod_bias_grad, *cross_grads
        )
        self_grads = rounds.four(3)

        return (
            mixed,
            token_grad,
            self_grads[0].T,
            self_grads[1].T,
            self_grads[2].T,
            self_grads[3],
            cross_grads[0].T,
            cross_grads[1].T,
            cross_grads[2].T,
            cross_grads[3],
            mlp_in_grad,
            mlp_out_grad,
            mod_weight_grad,
            mod_bias_grad,
        )

    rows = P("dp", None)
    by_col = P(None, "tensor")
    by_row = P("tensor", None)
    return jax.shard_map(
        local,
        mesh=mesh,
        in_specs=(
            rows, P("dp", None, None), P("dp"), P("dp"), P("dp"), by_col, by_col, by_col, by_row,
            by_col, by_col, by_col, by_row, by_col, by_row, by_col, P("tensor"), rows,
        ),
        out_specs=(
            rows, rows, by_col, by_col, by_col, by_row, by_col, by_col, by_col, by_row,
            by_col, by_row, by_col, P("tensor"),
        ),
        check_vma=False,
    )
```

```python
import functools
import math

import jax
import jax.numpy as jnp
from jax import lax
from jax.experimental import pallas as pl
from jax.experimental.pallas import tpu as pltpu
from jax.sharding import PartitionSpec as P

HEAD = 64
BLOCK = 256
EPSILON = 1e-06
MASKED = -1000000000.0
CURVE = math.sqrt(2.0 / math.pi)
CUBIC = 0.044715
F32 = jnp.float32
BF16 = jnp.bfloat16


def dot_nn(a, b):
    return lax.dot_general(a, b, (((1,), (0,)), ((), ())), preferred_element_type=F32)


def dot_nt(a, b):
    return lax.dot_general(a, b, (((1,), (1,)), ((), ())), preferred_element_type=F32)


def dot_tn(a, b):
    return lax.dot_general(a, b, (((0,), (0,)), ((), ())), preferred_element_type=F32)


def normalize(values):
    centered = values - jnp.mean(values, axis=-1, keepdims=True)
    inverse = lax.rsqrt(jnp.mean(centered * centered, axis=-1, keepdims=True) + EPSILON)
    return centered * inverse, inverse


def norm_back(grad, normed, inverse):
    first = jnp.mean(grad, axis=-1, keepdims=True)
    second = jnp.mean(grad * normed, axis=-1, keepdims=True)
    return inverse * (grad - first - normed * second)


def column_sum(values):
    return jnp.sum(values, axis=0, keepdims=True)


def three_parts(column):
    high = column.astype(BF16).astype(F32)
    rest = column - high
    middle = rest.astype(BF16).astype(F32)
    return high, middle, rest - middle


def head_slice(rows, head):
    piece = rows[:, head * HEAD : (head + 1) * HEAD]
    return jnp.concatenate([piece, jnp.zeros_like(piece)], axis=1)


class View:
    def __init__(self, ref):
        self.view = ref

    def ref(self):
        return self.view


class Place:
    def __init__(self, ref):
        self.ref = ref

    def __getitem__(self, index):
        return self.ref[0, index]


def run(kernel, outs, scalars, arrays, late=(), scratch=(), cost=0.001, vmem=10):
    in_vmem = pl.BlockSpec(memory_space=pltpu.VMEM)
    pairs = [entry if isinstance(entry, tuple) else (entry, None) for entry in late]
    n_plain = len(arrays)

    def wrapped(place, *refs):
        place = Place(place)
        views = []
        for ref, (_, block) in zip(refs[n_plain:], pairs):
            views.append(View(ref if block is None else ref.at[token_rows(block(place)), :]))
        kernel(place, *refs[:n_plain], *views, *refs[n_plain + len(pairs) :])

    return pl.pallas_call(
        wrapped,
        name=getattr(kernel, "__name__", "advance"),
        out_shape=[jax.ShapeDtypeStruct(shape, kind) for shape, kind in outs],
        in_specs=[in_vmem] * (1 + n_plain + len(pairs)),
        out_specs=[in_vmem] * len(outs),
        scratch_shapes=[pltpu.VMEM(shape, kind) for shape, kind in scratch],
        compiler_params=pltpu.CompilerParams(vmem_limit_bytes=vmem * 1024 * 1024),
        cost_estimate=pl.CostEstimate(flops=int(cost * 1_000_000_000), bytes_accessed=1000, transcendentals=0),
    )(scalars, *arrays, *[array for array, _ in pairs])


SLOT, CORE, ROW, END, TENSOR, OWN, FAR, LIMIT = 0, 4, 5, 6, 7, 8, 10, 12
ORDER = (0, 2, 1, 3)


def block_of(place, chunk):
    return place[CORE] * 2 + chunk


def mod_row(mod, slot, component, model):
    return mod[pl.ds(slot, 1), component * model : (component + 1) * model]


def quad_cols(quad):
    if isinstance(quad, int):
        return slice(quad * 4 * HEAD, (quad + 1) * 4 * HEAD)
    return pl.ds(pl.multiple_of(quad * 4 * HEAD, 4 * HEAD), 4 * HEAD)


def token_rows(block):
    return pl.ds(pl.multiple_of(block * BLOCK, BLOCK), BLOCK)


def text_kernel(place, text, weights, packed):
    rows = text.shape[1]
    wide = weights.shape[0]
    for slot in range(text.shape[0]):
        first = rows * (slot % 2)
        left = wide * (slot // 2)
        packed[first : first + rows, left : left + wide] = dot_nt(text[slot], weights[...]).astype(BF16)


def unpack_kernel(place, q0, o0, q1, o1, part2, rest2, part3, rest3, t0, t1, t2, t3, cqt, co, kall, vall):
    width = q0.shape[0]
    half = width // 2
    rows = kall.shape[1]
    for index, (query, out) in enumerate(((q0, o0), (q1, o1))):
        cqt[index * width : (index + 1) * width, :] = query[...]
        co[index * width : (index + 1) * width, :] = out[...]
    for index, (part, rest) in enumerate(((part2, rest2), (part3, rest3))):
        for piece, row in ((part, place[ROW]), (rest, 1 - place[ROW])):
            at = pl.ds(pl.multiple_of((index + 2) * width + row * half, half), half)
            cqt[at, :] = piece[:half, :]
            co[at, :] = piece[half:, :]
    for slot in range(kall.shape[0]):
        first = rows * (slot % 2)
        left = 2 * width * (slot // 2)
        both = [t[first : first + rows, left : left + 2 * width] for t in (t0, t1, t2, t3)]
        kall[slot] = jnp.concatenate([b[:, :width] for b in both], axis=1)
        vall[slot] = jnp.concatenate([b[:, width:] for b in both], axis=1)


def attend_chunk(place, chunk, qa_in, ka, va, wo, part_own, part_send, qa_out, att):
    heads = ka.shape[0]
    lane = lax.broadcasted_iota(jnp.int32, (BLOCK, 2 * HEAD), 1)
    spot = (lane >= HEAD + 4) & (lane < HEAD + 7)

    @pl.loop(0, 2)
    def _(side):
        at = token_rows(2 * chunk + side)
        here = token_rows(side)
        pieces = []
        for head in range(heads):
            queries = qa_in[head, at, :]
            scores = dot_nt(queries, ka[head])
            top = jnp.max(scores, axis=1, keepdims=True)
            raised = jnp.exp(scores - top).astype(BF16)
            out = dot_nn(raised, va[head])
            total = out[:, HEAD : HEAD + 1]
            pieces.append(out[:, :HEAD] * (1.0 / total))
            high, middle, low = three_parts(-(top + jnp.log(total)))
            more = jnp.where(lane == HEAD + 4, high, jnp.where(lane == HEAD + 5, middle, low))
            qa_out[head, here, :] = jnp.where(spot, more, queries.astype(F32)).astype(BF16)
        attended = jnp.concatenate(pieces, axis=1).astype(BF16)
        att[here, :] = attended
        out = dot_nn(attended, wo[...]).astype(BF16)

        @pl.when(place[CORE] == side)
        def _():
            part_own[...] = out

        @pl.when(place[CORE] != side)
        def _():
            part_send[...] = out


def self_first(place, mod, weights, tokens, wo, part_own, part_send, qa, ka, va, qa_out, att, h1):
    model = mod.shape[1] // 9
    lane = lax.broadcasted_iota(jnp.int32, (BLOCK, 2 * HEAD), 1)
    keep = lane < HEAD
    width = weights.shape[0] // 3
    tokens = tokens.ref()
    slots = [place[SLOT + block] for block in ORDER]

    @pl.loop(0, len(ORDER))
    def _(position):
        rows = token_rows(position)
        first = jnp.where(position == 0, slots[0], slots[1])
        slot = jnp.where(position < 2, first, jnp.where(position == 2, slots[2], slots[3]))
        block = lax.rem(position, 2) * 2 + lax.div(position, 2)
        normed, _ = normalize(tokens[token_rows(block), :].astype(F32))
        hidden = (normed * (1.0 + mod_row(mod, slot, 1, model)) + mod_row(mod, slot, 0, model)).astype(BF16)
        h1[rows, :] = hidden
        rows_qkv = dot_nt(hidden, weights[...])
        q = rows_qkv[:, :width].astype(BF16).astype(F32) * (HEAD**-0.5)
        k = rows_qkv[:, width : 2 * width]
        v = rows_qkv[:, 2 * width :]
        mine = lane == HEAD + slot
        q_more = jnp.where(mine, 1.0, 0.0)
        k_more = jnp.where((lane >= HEAD + 4) & (lane < HEAD + 7), 1.0, 0.0)
        k_more = jnp.where((lane >= HEAD) & (lane < HEAD + 4) & jnp.logical_not(mine), MASKED, k_more)
        v_more = jnp.where((lane >= HEAD) & (lane < HEAD + 3), 1.0, 0.0)
        for head in range(ka.shape[0]):
            qa[head, rows, :] = jnp.where(keep, head_slice(q, head), q_more).astype(BF16)
            ka[head, rows, :] = jnp.where(keep, head_slice(k, head), k_more).astype(BF16)
            va[head, rows, :] = jnp.where(keep, head_slice(v, head), v_more).astype(BF16)
    attend_chunk(place, 0, qa, ka, va, wo.ref(), part_own, part_send, qa_out, att)


def self_second(place, qa, ka, va, wo, part_own, part_send, qa_out, att):
    attend_chunk(place, 1, qa, ka, va, wo.ref(), part_own, part_send, qa_out, att)


def quad_stack(rows, masks):
    return jnp.concatenate([rows * mask for mask in masks], axis=0)


def quad_masks():
    lane = lax.broadcasted_iota(jnp.int32, (1, 4 * HEAD), 1)
    return [jnp.where((lane >= u * HEAD) & (lane < (u + 1) * HEAD), 1.0, 0.0) for u in range(4)]


def quad_probs(scores, limit, text_rows):
    key_row = lax.broadcasted_iota(jnp.int32, (text_rows, 1), 0)
    bias = jnp.where(key_row < limit, 0.0, MASKED)
    probs = []
    for u in range(4):
        part = scores[u * text_rows : (u + 1) * text_rows, :] + bias
        raised = jnp.exp(part - jnp.max(part, axis=0, keepdims=True))
        probs.append(raised * (1.0 / jnp.sum(raised, axis=0, keepdims=True)))
    return probs


def middle_chunk(
    place, chunk, mod, sum_own, sum_far, cqt, co, kall, vall, tokens, cot, win0, wout0, win1, wout1, x2_before,
    h3g_out, h3_out, act0, act1, pg0, pg1, b3g_out, x1_out, b2_out, h2_out, q2_out, cr_out, b3_out, x2_out,
):
    model = cqt.shape[1]
    text_rows = kall.shape[1]
    slot = place[OWN + chunk]

    def m(component):
        return mod_row(mod, slot, component, model)

    x1 = tokens.ref()[...].astype(F32) + m(2) * (sum_own[...].astype(F32) + sum_far[...].astype(F32))
    x1_out[...] = x1
    normed, _ = normalize(x1)
    h2 = (normed * (1.0 + m(4)) + m(3)).astype(BF16)
    h2_out[...] = h2
    q2 = (dot_nt(h2, cqt[...]).astype(BF16).astype(F32) * (HEAD**-0.5)).astype(BF16)
    q2_out[...] = q2
    masks = [mask.astype(BF16) for mask in quad_masks()]
    limit = place[LIMIT + chunk]


    def by_quad(quad):
        cols = quad_cols(quad)
        scores = dot_nt(quad_stack(kall[slot, :, cols], masks), q2_out[:, cols])
        probs = jnp.concatenate(quad_probs(scores, limit, text_rows), axis=0)
        cr_out[:, cols] = dot_tn(probs.astype(BF16), quad_stack(vall[slot, :, cols], masks)).astype(BF16)

    if chunk == 1:
        pl.loop(0, model // (4 * HEAD))(by_quad)
    else:
        for quad in range(model // (4 * HEAD)):
            by_quad(quad)
    b2 = dot_nn(cr_out[...], co[...])
    b2_out[...] = b2
    x2 = x1 + m(5) * b2
    x2_out[chunk * BLOCK : (chunk + 1) * BLOCK, :] = x2
    normed, _ = normalize(x2)
    h3 = (normed * (1.0 + m(7)) + m(6)).astype(BF16)
    h3_out[...] = h3
    b3g = (cot.ref()[...].astype(F32) * m(8)).astype(BF16)
    b3g_out[...] = b3g
    b3 = h3g = None
    for win, wout, act_out, pg_out in ((win0, wout0, act0, pg0), (win1, wout1, act1, pg1)):
        win, wout = win.ref(), wout.ref()
        pre = dot_nn(h3, win[...])
        square = pre * pre
        bent = jnp.tanh(CURVE * (pre + CUBIC * (square * pre)))
        act = (0.5 * pre * (1.0 + bent)).astype(BF16)
        act_out[...] = act
        slope = 0.5 * (1.0 + bent) + 0.5 * pre * (1.0 - bent * bent) * (CURVE * (1.0 + 3.0 * CUBIC * square))
        b3_half = dot_nn(act, wout[...])
        pg = (dot_nt(b3g, wout[...]) * slope).astype(BF16)
        pg_out[...] = pg
        h3g_half = dot_nt(pg, win[...])
        b3 = b3_half if b3 is None else b3 + b3_half
        h3g = h3g_half if h3g is None else h3g + h3g_half
    b3_out[...] = b3.astype(BF16)
    if chunk:
        x2_out[0:BLOCK, :] = x2_before.ref()[...]
    h3g_out[...] = h3g.astype(BF16)


def middle_first(place, *refs):
    middle_chunk(place, 0, *refs[:13], None, *refs[13:])


def middle_second(place, *refs):
    middle_chunk(place, 1, *refs)


def stacked(first, second):
    return jnp.concatenate([first[...], second[...]], axis=0)


def mlp_back(
    place, h3a, h3b, pg0a, pg0b, pg1a, pg1b, act0a, act0b, act1a, act1b, b3ga, b3gb,
    in_own, in_send, out_own, out_send,
):
    half = in_own.shape[1]
    grads = (stacked(pg0a, pg0b), stacked(pg1a, pg1b))
    for part in range(2):
        cols = slice(part * half, (part + 1) * half)
        rows = jnp.concatenate([h3a[:, cols], h3b[:, cols]], axis=0)
        for out, grad in ((in_send, grads[1]), (in_own, grads[0])):
            out[part ^ place[ROW]] = dot_tn(rows, grad).astype(BF16)
    grad = stacked(b3ga, b3gb)
    for out, first, second in ((out_send, act1a, act1b), (out_own, act0a, act0b)):
        for part in range(2):
            cols = slice(part * half, (part + 1) * half)
            rows = jnp.concatenate([first[:, cols], second[:, cols]], axis=0)
            out[part ^ place[ROW]] = dot_tn(rows, grad).astype(BF16)


def cross_chunk(
    place, chunk, mod, h3g_own, h3g_far, kall, vall, cqt, co, x1_in, b2_in, cot, q2_in, sum_own, sum_far,
    b1g_out, dq_out, b2g_out, dk_out, dv_out, sums, x1g_out, out_grad,
):
    model = cqt.shape[1]
    text_rows = kall.shape[1]
    slot = place[OWN + chunk]

    def m(component):
        return mod_row(mod, slot, component, model)

    x1 = x1_in.ref()[...]
    b2 = b2_in.ref()[...]
    h3g = h3g_own[...].astype(F32) + h3g_far[...].astype(F32)
    normed, inverse = normalize(x1 + m(5) * b2)
    sums[4:5, :] = column_sum(h3g)
    sums[5:6, :] = column_sum(h3g * normed)
    x2g = cot.ref()[...].astype(F32) + norm_back(h3g * (1.0 + m(7)), normed, inverse)
    sums[3:4, :] = column_sum(x2g * b2)
    b2g = (x2g * m(5)).astype(BF16)
    b2g_out[...] = b2g
    out_grad[...] = dot_nt(b2g, co[...]).astype(BF16)
    masks = quad_masks()
    low = [mask.astype(BF16) for mask in masks]
    limit = place[LIMIT + chunk]

    def by_quad(quad):
        cols = quad_cols(quad)
        queries = q2_in.ref()[:, cols]
        grads = out_grad[:, cols]
        keys = quad_stack(kall[slot, :, cols], low)
        values = quad_stack(vall[slot, :, cols], low)
        probs = quad_probs(dot_nt(keys, queries), limit, text_rows)
        prob_grad = dot_nt(values, grads)
        score_grad = []
        for u in range(4):
            part = prob_grad[u * text_rows : (u + 1) * text_rows, :]
            row_dot = jnp.sum(probs[u] * part, axis=0, keepdims=True)
            score_grad.append((probs[u] * (part - row_dot)).astype(BF16))
        score_grad = jnp.concatenate(score_grad, axis=0)
        dv = dot_nn(jnp.concatenate(probs, axis=0).astype(BF16), grads)
        dk = dot_nn(score_grad, queries)
        dq_out[:, cols] = (dot_tn(score_grad, keys) * (HEAD**-0.5)).astype(BF16)
        for wide, out in ((dk, dk_out), (dv, dv_out)):
            total = None
            for u in range(4):
                part = wide[u * text_rows : (u + 1) * text_rows, :] * masks[u]
                total = part if total is None else total + part
            out[:, cols] = total.astype(BF16)
    if chunk:
        for quad in range(model // (4 * HEAD)):
            by_quad(quad)
    else:
        pl.loop(0, model // (4 * HEAD))(by_quad)
    h2g = dot_nn(dq_out[...], cqt[...])
    normed, inverse = normalize(x1)
    sums[1:2, :] = column_sum(h2g)
    sums[2:3, :] = column_sum(h2g * normed)
    x1g = x2g + norm_back(h2g * (1.0 + m(4)), normed, inverse)
    x1g_out[...] = x1g
    branch = sum_own.ref()[...].astype(F32) + sum_far.ref()[...].astype(F32)
    sums[0:1, :] = column_sum(x1g * branch)
    sums[6:8, :] = jnp.zeros((2, model), F32)
    b1g_out[...] = (x1g * m(2)).astype(BF16)


def cross_first(place, *refs):
    cross_chunk(place, 0, *refs)


def cross_second(place, *refs):
    cross_chunk(place, 1, *refs)


def cross_weights(
    place, dqa, dqb, b2ga, b2gb, dka, dkb, dva, dvb, h2a, h2b, cra, crb, text, own, send,
):
    width = own.shape[1] // 2
    row = place[ROW]
    h2a, h2b, cra, crb, text = h2a.ref(), h2b.ref(), cra.ref(), crb.ref(), text.ref()
    slots = [place[OWN + chunk] for chunk in range(2)]

    @pl.loop(0, h2a.shape[1] // BLOCK)
    def _(part):
        to = token_rows(part)
        hidden = jnp.concatenate([h2a[:, to], h2b[:, to]], axis=0)
        grads = jnp.concatenate([b2ga[:, to], b2gb[:, to]], axis=0)
        texts = [text[slot, :, to] for slot in slots]
        for member, out in ((1, send), (0, own)):
            start = (member * width // 128) * 128
            skip = member * width - start
            cols = slice(start, start + 2 * 128)
            kept = slice(skip, skip + width)

            def two(first, second):
                return jnp.concatenate([first[:, cols], second[:, cols]], axis=0)

            top, bottom = slice(0, width), slice(width, 2 * width)
            out[row, top, to] = dot_tn(two(dqa, dqb), hidden)[kept].astype(BF16)
            out[row, bottom, to] = (dot_tn(dka[:, cols], texts[0]) + dot_tn(dkb[:, cols], texts[1]))[kept].astype(BF16)
            out[1 - row, top, to] = (dot_tn(dva[:, cols], texts[0]) + dot_tn(dvb[:, cols], texts[1]))[kept].astype(
                BF16
            )
            out[1 - row, bottom, to] = dot_tn(two(cra, crb), grads)[kept].astype(BF16)


def keys_back(block, qa, ka, va, da, dq_sum):
    rows = token_rows(block)
    dks = []
    dvs = []
    for head in range(ka.shape[0]):
        keys = ka[head, rows, :]
        probs = jnp.exp(dot_nt(keys, qa[head]))
        prob_grad = dot_nt(va[head, rows, :], da[head])
        score_grad = (probs * prob_grad).astype(BF16)
        dvs.append(dot_nn(probs.astype(BF16), da[head])[:, :HEAD])
        dks.append(dot_nn(score_grad, qa[head])[:, :HEAD])
        dq = dot_tn(score_grad, keys)
        dq_sum[head] += dq
    return jnp.concatenate(dks, axis=1).astype(BF16), jnp.concatenate(dvs, axis=1).astype(BF16)


def self_back_first(
    place, b1g_a, b1g_b, far_a, far_b, wo, att_a, att_b, qa_a, qa_b, ka, va,
    b1g, att, qa, da, dq_sum, dk_all, dv_all,
):
    blocks = b1g.shape[0] // BLOCK
    heads = da.shape[0]
    core = place[CORE]
    for chunk, (own, far) in enumerate(((b1g_a, far_a), (b1g_b, far_b))):
        b1g[token_rows(2 * chunk + core), :] = own[...]
        b1g[token_rows(2 * chunk + 1 - core), :] = far[...]
    wo = wo.ref()
    att[0 : 2 * BLOCK, :] = att_a.ref()[...]
    att[2 * BLOCK : 4 * BLOCK, :] = att_b.ref()[...]
    lane = lax.broadcasted_iota(jnp.int32, (BLOCK, 2 * HEAD), 1)

    @pl.loop(0, blocks)
    def _(block):
        rows = token_rows(block)
        grads = dot_nt(b1g[rows, :], wo[...]).astype(BF16).astype(F32)
        dots = grads * att[rows, :].astype(F32)
        for head in range(heads):
            row_dot = jnp.sum(dots[:, head * HEAD : (head + 1) * HEAD], axis=1, keepdims=True)
            high, middle, low = three_parts(-row_dot)
            more = jnp.where(lane == HEAD, high, jnp.where(lane == HEAD + 1, middle, low))
            more = jnp.where(lane < HEAD + 3, more, 0.0)
            da[head, rows, :] = jnp.where(lane < HEAD, head_slice(grads, head), more).astype(BF16)
    qa[:, 0 : 2 * BLOCK, :] = qa_a.ref()[...]
    qa[:, 2 * BLOCK : 4 * BLOCK, :] = qa_b.ref()[...]
    ka, va = ka.ref(), va.ref()
    dq_sum[...] = jnp.zeros_like(dq_sum)

    @pl.loop(0, 2)
    def _(block):
        rows = token_rows(block)
        dk_all[rows, :], dv_all[rows, :] = keys_back(block, qa, ka, va, da, dq_sum)


def self_back_second(
    place, b1g, att, qa, da, dq_in, dk_in, dv_in, weights, ka, va, h1,
    part_own, part_send, dw_keep, dw_give,
    dq_sum, grad_all,
):
    blocks = b1g.shape[0] // BLOCK
    heads = da.shape[0]
    core = place[CORE]
    width = heads * HEAD
    ka, va = ka.ref(), va.ref()
    dq_sum[...] = dq_in[...]
    grad_all[0 : 2 * BLOCK, width : 2 * width] = dk_in[0 : 2 * BLOCK, :]
    grad_all[0 : 2 * BLOCK, 2 * width : 3 * width] = dv_in[0 : 2 * BLOCK, :]

    @pl.loop(2, blocks)
    def _(block):
        rows = token_rows(block)
        dk, dv = keys_back(block, qa, ka, va, da, dq_sum)
        grad_all[rows, width : 2 * width] = dk
        grad_all[rows, 2 * width : 3 * width] = dv
    h1 = h1.ref()

    @pl.loop(0, blocks)
    def _(block):
        rows = token_rows(block)
        dq = jnp.concatenate([dq_sum[head, rows, :HEAD] for head in range(heads)], axis=1)
        grad_all[rows, 0:width] = (dq * (HEAD**-0.5)).astype(BF16)
        out = dot_nn(grad_all[rows, :], weights[...]).astype(BF16)
        side = lax.rem(block, 2)
        out_rows = token_rows(lax.div(block, 2))

        @pl.when(core == side)
        def _():
            part_own[out_rows, :] = out

        @pl.when(core != side)
        def _():
            part_send[out_rows, :] = out

    @pl.loop(0, h1.shape[1] // BLOCK)
    def _(part):
        cols = token_rows(part)
        grads = dot_tn(grad_all[...], h1[:, cols]).astype(BF16)
        query_key = (grads[:width], grads[width : 2 * width])
        value_out = (grads[2 * width :], dot_tn(att[...], b1g[:, cols]).astype(BF16))
        for flag, first, second in ((0, query_key, value_out), (1, value_out, query_key)):

            @pl.when(place[ROW] == flag)
            def _():
                for index in range(2):
                    rows = slice(index * width, (index + 1) * width)
                    dw_keep[rows, cols] = first[index]
                    dw_give[rows, cols] = second[index]


def mixed_kernel(place, mod, b3a, b3b, far_a, far_b, x2, cot_a, cot_b, mixed_a, mixed_b, sums):
    model = mixed_a.shape[1]
    for chunk, (own, far, cot) in enumerate(((b3a, far_a, cot_a), (b3b, far_b, cot_b))):
        mixed = (mixed_a, mixed_b)[chunk]
        rows = slice(chunk * BLOCK, (chunk + 1) * BLOCK)
        slot = place[OWN + chunk]
        b3 = own[...].astype(F32) + far[...].astype(F32)
        mixed[...] = (x2[rows, :] + mod_row(mod, slot, 8, model) * b3).astype(BF16)
        sums[chunk] = column_sum(cot.ref()[...].astype(F32) * b3)


def final_kernel(
    place, mod, h1g_own, h1g_far, sums_a, sums_b, sums_mixed, tokens_a, tokens_b, x1ga, x1gb, grad_a, grad_b, slot_sums,
):
    model = grad_a.shape[1]
    slot_sums[...] = jnp.zeros_like(slot_sums)
    for chunk, (x1g, sums, tokens) in enumerate(((x1ga, sums_a, tokens_a), (x1gb, sums_b, tokens_b))):
        rows = slice(chunk * BLOCK, (chunk + 1) * BLOCK)
        slot = place[OWN + chunk]
        h1g = h1g_own[rows, :].astype(F32) + h1g_far[rows, :].astype(F32)
        normed, inverse = normalize(tokens.ref()[...].astype(F32))
        scaled = h1g * (1.0 + mod_row(mod, slot, 1, model))
        (grad_a, grad_b)[chunk][...] = (x1g.ref()[...] + norm_back(scaled, normed, inverse)).astype(BF16)
        terms = [column_sum(h1g), column_sum(h1g * normed)]
        terms += [sums[i : i + 1, :] for i in range(6)] + [sums_mixed[chunk]]
        for component, term in enumerate(terms):
            slot_sums[pl.ds(slot, 1), component * model : (component + 1) * model] += term


def join_cores(place, mine_a, mine_b, other_a, other_b, out):
    for chunk, (mine, other) in enumerate(((mine_a, other_a), (mine_b, other_b))):
        out[token_rows(place[CORE] * 2 + chunk), :] = mine[...]
        out[token_rows((1 - place[CORE]) * 2 + chunk), :] = other[...]


def join_rows(place, mine, other, out):
    count = mine.shape[0]
    out[pl.ds(pl.multiple_of(place[ROW] * count, BLOCK // 2), count), :] = mine[...].astype(F32)
    out[pl.ds(pl.multiple_of((1 - place[ROW]) * count, BLOCK // 2), count), :] = other[...].astype(F32)


def join_four(place, mine, other, first, second, third, fourth):
    width = first.shape[0]
    for flag, top, bottom in ((0, mine, other), (1, other, mine)):

        @pl.when(place[ROW] == flag)
        def _():
            first[...] = top[:width, :].astype(F32)
            second[...] = top[width:, :].astype(F32)
            third[...] = bottom[:width, :].astype(F32)
            fourth[...] = bottom[width:, :].astype(F32)


def slot_kernel(place, own, far, silu, out):
    model = silu.shape[1]
    count = out.shape[1] - model
    out[:, :model] = silu[...].astype(F32)
    for index in range(own.shape[1] // count):
        cols = slice(index * count, (index + 1) * count)

        @pl.when(place[TENSOR] == index)
        def _():
            out[:, model:] = (own[:, cols] + far[:, cols]).astype(BF16).astype(F32)


def advance_kernel(roles, place, *refs):
    refs = list(refs)
    values, got = {}, {}
    for role in roles:
        values[role] = refs.pop(0)
    for name in ("row", "column", "middle"):
        if any(role in roles for role in {"row": "a", "column": "bd", "middle": "c"}[name]):
            got[name] = refs.pop(0)
    outs = {role: refs.pop(0) for role in roles}
    end = place[END]
    if "a" in roles:
        outs["a"][...] = added(values["a"][...], got["row"][...])
    if "c" in roles:

        @pl.when(end == 0)
        def _():
            outs["c"][...] = added(values["c"][...], got["middle"][...])

        @pl.when(end != 0)
        def _():
            outs["c"][...] = values["c"][...]

    if "b" in roles:

        @pl.when(end == 0)
        def _():
            outs["b"][...] = added(values["b"][...], got["column"][...])

        @pl.when(end != 0)
        def _():
            outs["b"][...] = values["b"][...]

    if "d" in roles:

        @pl.when(end == 0)
        def _():
            outs["d"][...] = values["d"][...]

        @pl.when(end != 0)
        def _():
            outs["d"][...] = got["column"][...]

    if refs:

        @pl.when(end == 0)
        def _():
            refs[0][...] = outs["c"][...]

        @pl.when(end != 0)
        def _():
            refs[0][...] = outs["a"][...]


def added(first, second):
    return (first.astype(F32) + second.astype(F32)).astype(BF16)


def solution(mesh):
    n_dp = mesh.shape["dp"]
    n_tensor = mesh.shape["tensor"]
    n_col = n_dp // 2
    dp_bits = int(math.log2(n_dp))

    def tensor_swap(value, flip):
        return lax.ppermute(value, "tensor", [(i, i ^ flip) for i in range(n_tensor)])

    def core_swap(value):
        return tensor_swap(value, 1)

    def far_swap(value):
        return tensor_swap(value, 2)

    def dp_swap(value, flip):
        return lax.ppermute(value, "dp", [(i, i ^ flip) for i in range(n_dp)])

    def tie(*values):
        return lax.optimization_barrier(values) if values else ()

    def pair_up(flag, mine, other):
        return jnp.concatenate([jnp.where(flag == 0, mine, other), jnp.where(flag == 0, other, mine)], axis=0)

    def local(
        tokens, text_states, clip_len, text_len, timesteps, q_weight, k_weight, v_weight, o_weight,
        cross_q, cross_k, cross_v, cross_o, mlp_in, mlp_out, mod_weight, mod_bias, cotangent,
    ):
        count, model = tokens.shape
        slots, text_rows = text_states.shape[:2]
        width = o_weight.shape[0]
        heads = width // HEAD
        half = count // 2
        text_pad = -(-text_rows // 16) * 16
        tensor_at = lax.axis_index("tensor")
        dp_at = lax.axis_index("dp")
        core = tensor_at & 1
        row = dp_at & 1
        column = dp_at >> 1

        ends = jnp.cumsum(clip_len)
        starts = jnp.arange(count // BLOCK, dtype=jnp.int32) * BLOCK
        slot_of = jnp.sum((starts[:, None] >= ends[None, :]).astype(jnp.int32), axis=1)
        end = (column == 0) | (column == n_col - 1)
        own_slots = lax.dynamic_slice_in_dim(slot_of, core * 2, 2, 0)
        far_slots = lax.dynamic_slice_in_dim(slot_of, (1 - core) * 2, 2, 0)
        limits = jnp.sum(jnp.where(own_slots[:, None] == jnp.arange(slots)[None, :], text_len[None, :], 0), axis=1)
        single = jnp.stack([core, row, end.astype(jnp.int32), tensor_at])
        place = jnp.concatenate([slot_of, single, own_slots, far_slots, limits])
        place = jnp.pad(place[None, :], ((0, 7), (0, 128 - place.shape[0])))
        place = place.astype(jnp.int32)

        query_own = cross_q.T
        part_own = jnp.concatenate(
            [lax.dynamic_slice_in_dim(w, row * (width // 2), width // 2, 0) for w in (query_own, cross_o)], axis=0
        )
        text_weights = jnp.concatenate([cross_k.T, cross_v.T], axis=0)
        text = jnp.pad(text_states, ((0, 0), (0, text_pad - text_rows), (0, 0)))
        self_weights = jnp.concatenate([q_weight.T, k_weight.T, v_weight.T], axis=0)

        half_width = model // 2
        ramp = jnp.arange(half_width).astype(F32)
        frequency = jnp.exp(ramp * (-math.log(10000.0) / half_width))
        angles = timesteps.astype(F32)[:, None] * frequency[None, :]
        embed = jnp.concatenate([jnp.cos(angles), jnp.sin(angles)], axis=1)
        silu_low = jax.nn.silu(embed).astype(BF16)
        part_far = far_swap(part_own)
        wout1 = core_swap(mlp_out)
        mod_own = dot_nn(silu_low, mod_weight) + mod_bias.astype(F32)
        mod_far = [tensor_swap(mod_own, flip) for flip in range(1, n_tensor)]
        (text_own,) = run(text_kernel, [((2 * text_pad, model), BF16)], place, [text, text_weights], cost=1.0)
        text_own, self_weights, wout1, *mod_far = tie(text_own, self_weights, wout1, *mod_far)
        text_far = far_swap(text_own)
        query_own, out_own, text_own = tie(query_own, cross_o, text_own)
        query1, out1, text1 = core_swap(query_own), core_swap(out_own), core_swap(text_own)
        mod_all = jnp.stack([mod_own] + mod_far)
        mod = jnp.concatenate(
            [lax.dynamic_index_in_dim(mod_all, tensor_at ^ j, 0, keepdims=False) for j in range(n_tensor)], axis=1
        )

        wide = (heads, count, 2 * HEAD)
        block_wide = (heads, 2 * BLOCK, 2 * HEAD)
        one = ((BLOCK, model), BF16)
        one_f32 = ((BLOCK, model), F32)
        attend_far = [(block_wide, BF16), ((2 * BLOCK, width), BF16)]
        own_a, send_a, qa, ka, va, qa_a, att_a, h1 = run(
            self_first, [one, one] + [(wide, BF16)] * 3 + attend_far + [((count, model), BF16)], place, [mod, self_weights], cost=0.001,
            late=[tokens, o_weight],
        )
        send_a, part_far, text_far, query1, out1, text1 = tie(send_a, part_far, text_far, query1, out1, text1)
        sum_a = added(own_a, core_swap(send_a))
        sum_a, qa, part_far, text_far, win0 = tie(sum_a, qa, part_far, text_far, mlp_in)
        far_a = far_swap(sum_a)
        rest_far = dp_swap(part_far, 1)
        part3, text3, win1 = core_swap(part_far), core_swap(text_far), core_swap(win0)
        own_b, send_b, qa_b, att_b = run(
            self_second, [one, one] + attend_far, place, [qa, ka, va], late=[o_weight]
        )
        (far_a,) = tie(far_a)
        send_b, far_a, rest_far, part3, text3, win1 = tie(send_b, far_a, rest_far, part3, text3, win1)
        rest3 = core_swap(rest_far)
        sum_b = added(own_b, core_swap(send_b))
        sum_b, rest3 = tie(sum_b, rest3)
        far_b = far_swap(sum_b)
        cqt, co, kall, vall = run(
            unpack_kernel, [((model, model), BF16)] * 2 + [((slots, text_pad, model), BF16)] * 2,
            place,
            [query_own, out_own, query1, out1, part_far, rest_far, part3, rest3, text_own, text1, text_far, text3],
            cost=0.001,
        )
        shared = [cqt, co, kall, vall]

        def chunk_rows(array, chunk):
            return (array, functools.partial(block_of, chunk=chunk))

        def middle(kernel, chunk, own, far, *before):
            return run(
                kernel, [one] * 7 + [one_f32, one_f32] + [one] * 4 + [(((chunk + 1) * BLOCK, model), F32)], place,
                [mod, own, far] + shared, cost=7.5,
                late=[chunk_rows(tokens, chunk), chunk_rows(cotangent, chunk), mlp_in, mlp_out, win1, wout1, *before],
            )

        h3ga, h3a, act0a, act1a, pg0a, pg1a, b3ga, x1a, b2a, h2a, q2a, cra, b3a, x2a = middle(
            middle_first, 0, sum_a, far_a
        )
        h3ga, far_b = tie(h3ga, far_b)
        h3g_far_a = far_swap(h3ga)
        h3gb, h3b, act0b, act1b, pg0b, pg1b, b3gb, x1b, b2b, h2b, q2b, crb, b3b, x2 = middle(
            middle_second, 1, sum_b, far_b, x2a
        )
        h3gb, pg0b, h3g_far_a = tie(h3gb, pg0b, h3g_far_a)
        h3g_far_b = far_swap(h3gb)

        in_own, in_send, out_own, out_send = run(
            mlp_back, [((2, model // 2, model), BF16)] * 4, place,
            [h3a, h3b, pg0a, pg0b, pg1a, pg1b, act0a, act0b, act1a, act1b, b3ga, b3gb], cost=0.001,
        )

        def cross(kernel, chunk, h3g_own, h3g_far, x1, b2, own, far, q2):
            return run(
                kernel, [one] * 3 + [((text_pad, model), BF16)] * 2 + [((8, model), F32), one_f32], place,
                [mod, h3g_own, h3g_far, kall, vall, cqt, co],
                late=[x1, b2, chunk_rows(cotangent, chunk), q2, own, far], scratch=[one],
                cost=4.0 if chunk else 0.001,
            )

        b1g_a, dqa, b2ga, dka, dva, sums_a, x1ga = cross(
            cross_first, 0, h3ga, h3g_far_a, x1a, b2a, sum_a, far_a, q2a
        )
        in_send, out_send, b1g_a, h3g_far_b = tie(in_send, out_send, b1g_a, h3g_far_b)
        in_got, b1g_far_a = core_swap(in_send), core_swap(b1g_a)
        b1g_b, dqb, b2gb, dkb, dvb, sums_b, x1gb = cross(
            cross_second, 1, h3gb, h3g_far_b, x1b, b2b, sum_b, far_b, q2b
        )
        in_got, out_send, b1g_far_a, b1g_b, dqb, b3a = tie(in_got, out_send, b1g_far_a, b1g_b, dqb, b3a)
        in_keep, in_give = added(in_own[0], in_got[0]), added(in_own[1], in_got[1])

        across = [(i, i ^ 1) for i in range(n_dp)]
        neighbours = [(i, i ^ 2) for i in range(n_dp)]
        middle_pair = [(2 * a + r, 2 * b + r) for a, b in ((1, 2), (2, 1)) for r in range(2)]
        chain_rows = (model // 2, model)

        class Rounds:
            def __init__(self):
                self.values, self.column_send, self.results, self.waiting = {}, None, [], []

            def start(self, *chain):
                self.got = {}
                if n_col != 4:
                    self.waiting += [chain] if chain else []
                    return
                if chain:
                    self.values["a"] = chain[0]
                    self.got["row"] = lax.ppermute(chain[1], "dp", across)
                if "e" in self.values:
                    self.got["last"] = lax.ppermute(self.values["e"], "dp", across)
                if "b" in self.values or "d" in self.values:
                    self.got["column"] = lax.ppermute(self.column_send, "dp", neighbours)
                if "c" in self.values:
                    self.got["middle"] = lax.ppermute(self.values["c"], "dp", middle_pair)

            def finish(self, *others, early=()):
                order = [name for name in ("row", "last", "column", "middle") if name in self.got]
                settled = list(early)
                for name in order:
                    settled = list(tie(self.got[name], *settled))
                tied = tie(*settled, *others)
                self.got = dict(zip(reversed(order), tied))
                others = tied[len(order) :]
                if "last" in self.got:
                    self.results.append((self.values.pop("e"), self.got.pop("last")))
                roles = "".join(role for role in "abcd" if role in self.values)
                if not roles:
                    return others
                operands = [self.values[role] for role in roles]
                operands += [self.got[name] for name in ("row", "column", "middle") if name in self.got]
                sends = "a" in roles or "c" in roles
                both = "a" in roles and "c" in roles
                outs = run(
                    functools.partial(advance_kernel, roles), [(chain_rows, BF16)] * (len(roles) + both),
                    place, operands, cost=0.3,
                )
                done = tie(*outs, *others)
                stepped = dict(zip(roles, done))
                if sends:
                    self.column_send = done[len(roles)] if both else stepped["a" if "a" in roles else "c"]
                self.values = {{"a": "b", "b": "c", "c": "d", "d": "e"}[role]: v for role, v in stepped.items()}
                return done[len(outs) :]

            def halves(self, number):
                return self.results[number] if n_col == 4 else self.slowly(*self.waiting[number])

            def whole(self, number):
                return run(join_rows, [((model, model), F32)], place, self.halves(number))[0]

            def four(self, number):
                return run(join_four, [((width, model), F32)] * 4, place, self.halves(number))

            def slowly(self, keep, give):
                total = added(keep, lax.ppermute(give, "dp", across))
                for bit in range(1, dp_bits):
                    size, flag = total.shape[0] // 2, (dp_at >> bit) & 1
                    sent = lax.dynamic_slice_in_dim(total, (1 - flag) * size, size, 0)
                    total = added(lax.dynamic_slice_in_dim(total, flag * size, size, 0), dp_swap(sent, 1 << bit))
                for bit in reversed(range(1, dp_bits)):
                    total = pair_up((dp_at >> bit) & 1, total, dp_swap(total, 1 << bit))
                return total, lax.ppermute(total, "dp", across)

        rounds = Rounds()

        rounds.start(in_keep, in_give)
        b1g_far_b, out_got = core_swap(b1g_b), core_swap(out_send)
        out_keep, out_give = added(out_own[0], out_got[0]), added(out_own[1], out_got[1])
        b3_far_a = far_swap(b3a)
        cross_dw, cross_send = run(
            cross_weights, [((2, 2 * width, model), BF16)] * 2, place,
            [dqa, dqb, b2ga, b2gb, dka, dkb, dva, dvb], late=[h2a, h2b, cra, crb, text], cost=0.001,
        )
        b1g_far_b, cross_send = tie(b1g_far_b, cross_send)
        b1g_all, att_all, qa_all, da, dq_sum, dk_all, dv_all = run(
            self_back_first,
            [((count, model), BF16), ((count, width), BF16), (wide, BF16), (wide, BF16), (wide, F32)]
            + [((count, width), BF16)] * 2,
            place, [b1g_a, b1g_b, b1g_far_a, b1g_far_b],
            late=[o_weight, att_a, att_b, qa_a, qa_b, ka, va], cost=0.001,
        )
        b1g_all, cross_send, out_give, b3b, b3_far_a = rounds.finish(b1g_all, cross_send, out_give, b3b, b3_far_a)

        rounds.start(out_keep, out_give)
        cross_got = core_swap(cross_send)
        b3_far_b = far_swap(b3b)
        grad_own, grad_send, self_keep, self_give = run(
            self_back_second,
            [((half, model), BF16)] * 2 + [((2 * width, model), BF16)] * 2, place,
            [b1g_all, att_all, qa_all, da, dq_sum, dk_all, dv_all, self_weights], late=[ka, va, h1],
            scratch=[(wide, F32), ((count, 3 * width), BF16)],
        )
        cross_keep, cross_give = added(cross_dw[0], cross_got[0]), added(cross_dw[1], cross_got[1])
        grad_send, cross_give, self_give, b3_far_b = rounds.finish(grad_send, cross_give, self_give, b3_far_b)

        rounds.start(cross_keep, cross_give)
        h1g_own = added(grad_own, core_swap(grad_send))
        h1g_far = far_swap(h1g_own)
        mixed_a, mixed_b, sums_mixed = run(
            mixed_kernel, [one, one, ((2, 1, model), F32)],
            place, [mod, b3a, b3b, b3_far_a, b3_far_b, x2], late=[chunk_rows(cotangent, 0), chunk_rows(cotangent, 1)],
        )
        self_give, h1g_own, mixed_a, mixed_b = rounds.finish(self_give, h1g_own, mixed_a, mixed_b)

        rounds.start(self_keep, self_give)
        grad_a, grad_b, slot_sums = run(
            final_kernel, [one, one, ((slots, 9 * model), F32)],
            place, [mod, h1g_own, h1g_far, sums_a, sums_b, sums_mixed],
            late=[chunk_rows(tokens, 0), chunk_rows(tokens, 1), x1ga, x1gb],
        )
        grad_a, grad_b, slot_sums, mixed_a = rounds.finish(mixed_a, early=(grad_a, grad_b, slot_sums))

        rounds.start()
        slot_far = core_swap(slot_sums)
        mixed_far_a = core_swap(mixed_a)
        slot_far, mixed_far_a, mixed_b = rounds.finish(slot_far, mixed_far_a, mixed_b)

        rounds.start()
        (gathered,) = run(
            slot_kernel, [((slots, model + mod_weight.shape[1]), F32)], place, [slot_sums, slot_far, silu_low]
        )
        gathered = jnp.concatenate([gathered, dp_swap(gathered, 1)], axis=0)
        mixed_far_b = core_swap(mixed_b)
        gathered, mixed_far_b, grad_a, grad_b = rounds.finish(gathered, mixed_far_b, grad_a, grad_b)

        rounds.start()
        gathered = jnp.concatenate([gathered, dp_swap(gathered, 2)], axis=0)
        grad_far_a, grad_far_b = core_swap(grad_a), core_swap(grad_b)
        mlp_in_grad, mlp_out_grad = rounds.whole(0), rounds.whole(1)
        gathered, grad_far_a, grad_far_b, mlp_in_grad, mlp_out_grad = rounds.finish(
            gathered, grad_far_a, grad_far_b, mlp_in_grad, mlp_out_grad
        )

        rounds.start()
        for bit in range(2, dp_bits):
            gathered = jnp.concatenate([gathered, dp_swap(gathered, 1 << bit)], axis=0)
        (mixed,) = run(
            join_cores, [((count, model), BF16)], place, [mixed_a, mixed_b, mixed_far_a, mixed_far_b]
        )
        (token_grad,) = run(
            join_cores, [((count, model), BF16)], place, [grad_a, grad_b, grad_far_a, grad_far_b]
        )
        cross_grads = rounds.four(2)
        gathered_low = gathered.astype(BF16)
        mod_weight_grad = dot_tn(gathered_low[:, :model], gathered_low[:, model:])
        mod_bias_grad = jnp.sum(gathered[:, model:], axis=0)
        mixed, token_grad, mod_weight_grad, mod_bias_grad, *cross_grads = rounds.finish(
            mixed, token_grad, mod_weight_grad, mod_bias_grad, *cross_grads
        )
        self_grads = rounds.four(3)

        return (
            mixed,
            token_grad,
            self_grads[0].T,
            self_grads[1].T,
            self_grads[2].T,
            self_grads[3],
            cross_grads[0].T,
            cross_grads[1].T,
            cross_grads[2].T,
            cross_grads[3],
            mlp_in_grad,
            mlp_out_grad,
            mod_weight_grad,
            mod_bias_grad,
        )

    rows = P("dp", None)
    by_col = P(None, "tensor")
    by_row = P("tensor", None)
    return jax.shard_map(
        local,
        mesh=mesh,
        in_specs=(
            rows, P("dp", None, None), P("dp"), P("dp"), P("dp"), by_col, by_col, by_col, by_row,
            by_col, by_col, by_col, by_row, by_col, by_row, by_col, P("tensor"), rows,
        ),
        out_specs=(
            rows, rows, by_col, by_col, by_col, by_row, by_col, by_col, by_col, by_row,
            by_col, by_row, by_col, P("tensor"),
        ),
        check_vma=False,
    )
```

```python
import functools
import math

import jax
import jax.numpy as jnp
from jax import lax
from jax.experimental import pallas as pl
from jax.experimental.pallas import tpu as pltpu
from jax.sharding import PartitionSpec as P

HEAD = 64
BLOCK = 256
EPSILON = 1e-06
MASKED = -1000000000.0
CURVE = math.sqrt(2.0 / math.pi)
CUBIC = 0.044715
F32 = jnp.float32
BF16 = jnp.bfloat16


def dot_nn(a, b):
    return lax.dot_general(a, b, (((1,), (0,)), ((), ())), preferred_element_type=F32)


def dot_nt(a, b):
    return lax.dot_general(a, b, (((1,), (1,)), ((), ())), preferred_element_type=F32)


def dot_tn(a, b):
    return lax.dot_general(a, b, (((0,), (0,)), ((), ())), preferred_element_type=F32)


def normalize(values):
    centered = values - jnp.mean(values, axis=-1, keepdims=True)
    inverse = lax.rsqrt(jnp.mean(centered * centered, axis=-1, keepdims=True) + EPSILON)
    return centered * inverse, inverse


def norm_back(grad, normed, inverse):
    first = jnp.mean(grad, axis=-1, keepdims=True)
    second = jnp.mean(grad * normed, axis=-1, keepdims=True)
    return inverse * (grad - first - normed * second)


def column_sum(values):
    return jnp.sum(values, axis=0, keepdims=True)


def three_parts(column):
    high = column.astype(BF16).astype(F32)
    rest = column - high
    middle = rest.astype(BF16).astype(F32)
    return high, middle, rest - middle


def head_slice(rows, head):
    piece = rows[:, head * HEAD : (head + 1) * HEAD]
    return jnp.concatenate([piece, jnp.zeros_like(piece)], axis=1)


class View:
    def __init__(self, ref):
        self.view = ref

    def ref(self):
        return self.view


class Place:
    def __init__(self, ref):
        self.ref = ref

    def __getitem__(self, index):
        return self.ref[0, index]


def run(kernel, outs, scalars, arrays, late=(), scratch=(), cost=0.001, vmem=10):
    in_vmem = pl.BlockSpec(memory_space=pltpu.VMEM)
    pairs = [entry if isinstance(entry, tuple) else (entry, None) for entry in late]
    n_plain = len(arrays)

    def wrapped(place, *refs):
        place = Place(place)
        views = []
        for ref, (_, block) in zip(refs[n_plain:], pairs):
            views.append(View(ref if block is None else ref.at[token_rows(block(place)), :]))
        kernel(place, *refs[:n_plain], *views, *refs[n_plain + len(pairs) :])

    return pl.pallas_call(
        wrapped,
        name=getattr(kernel, "__name__", "advance"),
        out_shape=[jax.ShapeDtypeStruct(shape, kind) for shape, kind in outs],
        in_specs=[in_vmem] * (1 + n_plain + len(pairs)),
        out_specs=[in_vmem] * len(outs),
        scratch_shapes=[pltpu.VMEM(shape, kind) for shape, kind in scratch],
        compiler_params=pltpu.CompilerParams(vmem_limit_bytes=vmem * 1024 * 1024),
        cost_estimate=pl.CostEstimate(flops=int(cost * 1_000_000_000), bytes_accessed=1000, transcendentals=0),
    )(scalars, *arrays, *[array for array, _ in pairs])


SLOT, CORE, ROW, END, TENSOR, OWN, FAR, LIMIT = 0, 4, 5, 6, 7, 8, 10, 12
ORDER = (0, 2, 1, 3)


def block_of(place, chunk):
    return place[CORE] * 2 + chunk


def mod_row(mod, slot, component, model):
    return mod[pl.ds(slot, 1), component * model : (component + 1) * model]


def quad_cols(quad):
    if isinstance(quad, int):
        return slice(quad * 4 * HEAD, (quad + 1) * 4 * HEAD)
    return pl.ds(pl.multiple_of(quad * 4 * HEAD, 4 * HEAD), 4 * HEAD)


def token_rows(block):
    return pl.ds(pl.multiple_of(block * BLOCK, BLOCK), BLOCK)


def text_kernel(place, text, weights, packed):
    rows = text.shape[1]
    wide = weights.shape[0]
    for slot in range(text.shape[0]):
        first = rows * (slot % 2)
        left = wide * (slot // 2)
        packed[first : first + rows, left : left + wide] = dot_nt(text[slot], weights[...]).astype(BF16)


def unpack_kernel(place, q0, o0, q1, o1, part2, rest2, part3, rest3, t0, t1, t2, t3, cqt, co, kall, vall):
    width = q0.shape[0]
    half = width // 2
    rows = kall.shape[1]
    for index, (query, out) in enumerate(((q0, o0), (q1, o1))):
        cqt[index * width : (index + 1) * width, :] = query[...]
        co[index * width : (index + 1) * width, :] = out[...]
    for index, (part, rest) in enumerate(((part2, rest2), (part3, rest3))):
        for piece, row in ((part, place[ROW]), (rest, 1 - place[ROW])):
            at = pl.ds(pl.multiple_of((index + 2) * width + row * half, half), half)
            cqt[at, :] = piece[:half, :]
            co[at, :] = piece[half:, :]
    for slot in range(kall.shape[0]):
        first = rows * (slot % 2)
        left = 2 * width * (slot // 2)
        both = [t[first : first + rows, left : left + 2 * width] for t in (t0, t1, t2, t3)]
        kall[slot] = jnp.concatenate([b[:, :width] for b in both], axis=1)
        vall[slot] = jnp.concatenate([b[:, width:] for b in both], axis=1)


def attend_chunk(place, chunk, qa_in, ka, va, wo, part_own, part_send, qa_out, att):
    heads = ka.shape[0]
    lane = lax.broadcasted_iota(jnp.int32, (BLOCK, 2 * HEAD), 1)
    spot = (lane >= HEAD + 4) & (lane < HEAD + 7)

    @pl.loop(0, 2)
    def _(side):
        at = token_rows(2 * chunk + side)
        here = token_rows(side)
        pieces = []
        for head in range(heads):
            queries = qa_in[head, at, :]
            scores = dot_nt(queries, ka[head])
            top = jnp.max(scores, axis=1, keepdims=True)
            raised = jnp.exp(scores - top).astype(BF16)
            out = dot_nn(raised, va[head])
            total = out[:, HEAD : HEAD + 1]
            pieces.append(out[:, :HEAD] * (1.0 / total))
            high, middle, low = three_parts(-(top + jnp.log(total)))
            more = jnp.where(lane == HEAD + 4, high, jnp.where(lane == HEAD + 5, middle, low))
            qa_out[head, here, :] = jnp.where(spot, more, queries.astype(F32)).astype(BF16)
        attended = jnp.concatenate(pieces, axis=1).astype(BF16)
        att[here, :] = attended
        out = dot_nn(attended, wo[...]).astype(BF16)

        @pl.when(place[CORE] == side)
        def _():
            part_own[...] = out

        @pl.when(place[CORE] != side)
        def _():
            part_send[...] = out


def self_first(place, mod, weights, tokens, wo, part_own, part_send, qa, ka, va, qa_out, att, h1):
    model = mod.shape[1] // 9
    lane = lax.broadcasted_iota(jnp.int32, (BLOCK, 2 * HEAD), 1)
    keep = lane < HEAD
    width = weights.shape[0] // 3
    tokens = tokens.ref()
    slots = [place[SLOT + block] for block in ORDER]

    @pl.loop(0, len(ORDER))
    def _(position):
        rows = token_rows(position)
        first = jnp.where(position == 0, slots[0], slots[1])
        slot = jnp.where(position < 2, first, jnp.where(position == 2, slots[2], slots[3]))
        block = lax.rem(position, 2) * 2 + lax.div(position, 2)
        normed, _ = normalize(tokens[token_rows(block), :].astype(F32))
        hidden = (normed * (1.0 + mod_row(mod, slot, 1, model)) + mod_row(mod, slot, 0, model)).astype(BF16)
        h1[rows, :] = hidden
        rows_qkv = dot_nt(hidden, weights[...])
        q = rows_qkv[:, :width].astype(BF16).astype(F32) * (HEAD**-0.5)
        k = rows_qkv[:, width : 2 * width]
        v = rows_qkv[:, 2 * width :]
        mine = lane == HEAD + slot
        q_more = jnp.where(mine, 1.0, 0.0)
        k_more = jnp.where((lane >= HEAD + 4) & (lane < HEAD + 7), 1.0, 0.0)
        k_more = jnp.where((lane >= HEAD) & (lane < HEAD + 4) & jnp.logical_not(mine), MASKED, k_more)
        v_more = jnp.where((lane >= HEAD) & (lane < HEAD + 3), 1.0, 0.0)
        for head in range(ka.shape[0]):
            qa[head, rows, :] = jnp.where(keep, head_slice(q, head), q_more).astype(BF16)
            ka[head, rows, :] = jnp.where(keep, head_slice(k, head), k_more).astype(BF16)
            va[head, rows, :] = jnp.where(keep, head_slice(v, head), v_more).astype(BF16)
    attend_chunk(place, 0, qa, ka, va, wo.ref(), part_own, part_send, qa_out, att)


def self_second(place, qa, ka, va, wo, part_own, part_send, qa_out, att):
    attend_chunk(place, 1, qa, ka, va, wo.ref(), part_own, part_send, qa_out, att)


def quad_stack(rows, masks):
    return jnp.concatenate([rows * mask for mask in masks], axis=0)


def quad_masks():
    lane = lax.broadcasted_iota(jnp.int32, (1, 4 * HEAD), 1)
    return [jnp.where((lane >= u * HEAD) & (lane < (u + 1) * HEAD), 1.0, 0.0) for u in range(4)]


def quad_probs(scores, limit, text_rows):
    key_row = lax.broadcasted_iota(jnp.int32, (text_rows, 1), 0)
    bias = jnp.where(key_row < limit, 0.0, MASKED)
    probs = []
    for u in range(4):
        part = scores[u * text_rows : (u + 1) * text_rows, :] + bias
        raised = jnp.exp(part - jnp.max(part, axis=0, keepdims=True))
        probs.append(raised * (1.0 / jnp.sum(raised, axis=0, keepdims=True)))
    return probs


def middle_chunk(
    place, chunk, mod, sum_own, sum_far, cqt, co, kall, vall, tokens, cot, win0, wout0, win1, wout1, x2_before,
    h3g_out, h3_out, act0, act1, pg0, pg1, b3g_out, x1_out, b2_out, h2_out, q2_out, cr_out, b3_out, x2_out,
):
    model = cqt.shape[1]
    text_rows = kall.shape[1]
    slot = place[OWN + chunk]

    def m(component):
        return mod_row(mod, slot, component, model)

    x1 = tokens.ref()[...].astype(F32) + m(2) * (sum_own[...].astype(F32) + sum_far[...].astype(F32))
    x1_out[...] = x1
    normed, _ = normalize(x1)
    h2 = (normed * (1.0 + m(4)) + m(3)).astype(BF16)
    h2_out[...] = h2
    q2 = (dot_nt(h2, cqt[...]).astype(BF16).astype(F32) * (HEAD**-0.5)).astype(BF16)
    q2_out[...] = q2
    masks = [mask.astype(BF16) for mask in quad_masks()]
    limit = place[LIMIT + chunk]


    def by_quad(quad):
        cols = quad_cols(quad)
        scores = dot_nt(quad_stack(kall[slot, :, cols], masks), q2_out[:, cols])
        probs = jnp.concatenate(quad_probs(scores, limit, text_rows), axis=0)
        cr_out[:, cols] = dot_tn(probs.astype(BF16), quad_stack(vall[slot, :, cols], masks)).astype(BF16)

    if chunk == 1:
        pl.loop(0, model // (4 * HEAD))(by_quad)
    else:
        for quad in range(model // (4 * HEAD)):
            by_quad(quad)
    b2 = dot_nn(cr_out[...], co[...])
    b2_out[...] = b2
    x2 = x1 + m(5) * b2
    x2_out[chunk * BLOCK : (chunk + 1) * BLOCK, :] = x2
    normed, _ = normalize(x2)
    h3 = (normed * (1.0 + m(7)) + m(6)).astype(BF16)
    h3_out[...] = h3
    b3g = (cot.ref()[...].astype(F32) * m(8)).astype(BF16)
    b3g_out[...] = b3g
    b3 = h3g = None
    for win, wout, act_out, pg_out in ((win0, wout0, act0, pg0), (win1, wout1, act1, pg1)):
        win, wout = win.ref(), wout.ref()
        pre = dot_nn(h3, win[...])
        square = pre * pre
        bent = jnp.tanh(CURVE * (pre + CUBIC * (square * pre)))
        act = (0.5 * pre * (1.0 + bent)).astype(BF16)
        act_out[...] = act
        slope = 0.5 * (1.0 + bent) + 0.5 * pre * (1.0 - bent * bent) * (CURVE * (1.0 + 3.0 * CUBIC * square))
        b3_half = dot_nn(act, wout[...])
        pg = (dot_nt(b3g, wout[...]) * slope).astype(BF16)
        pg_out[...] = pg
        h3g_half = dot_nt(pg, win[...])
        b3 = b3_half if b3 is None else b3 + b3_half
        h3g = h3g_half if h3g is None else h3g + h3g_half
    b3_out[...] = b3.astype(BF16)
    if chunk:
        x2_out[0:BLOCK, :] = x2_before.ref()[...]
    h3g_out[...] = h3g.astype(BF16)


def middle_first(place, *refs):
    middle_chunk(place, 0, *refs[:13], None, *refs[13:])


def middle_second(place, *refs):
    middle_chunk(place, 1, *refs)


def stacked(first, second):
    return jnp.concatenate([first[...], second[...]], axis=0)


def mlp_back(
    place, h3a, h3b, pg0a, pg0b, pg1a, pg1b, act0a, act0b, act1a, act1b, b3ga, b3gb,
    in_own, in_send, out_own, out_send,
):
    half = in_own.shape[1]
    grads = (stacked(pg0a, pg0b), stacked(pg1a, pg1b))
    for part in range(2):
        cols = slice(part * half, (part + 1) * half)
        rows = jnp.concatenate([h3a[:, cols], h3b[:, cols]], axis=0)
        for out, grad in ((in_send, grads[1]), (in_own, grads[0])):
            out[part ^ place[ROW]] = dot_tn(rows, grad).astype(BF16)
    grad = stacked(b3ga, b3gb)
    for out, first, second in ((out_send, act1a, act1b), (out_own, act0a, act0b)):
        for part in range(2):
            cols = slice(part * half, (part + 1) * half)
            rows = jnp.concatenate([first[:, cols], second[:, cols]], axis=0)
            out[part ^ place[ROW]] = dot_tn(rows, grad).astype(BF16)


def cross_chunk(
    place, chunk, mod, h3g_own, h3g_far, kall, vall, cqt, co, x1_in, b2_in, cot, q2_in, sum_own, sum_far,
    b1g_out, dq_out, b2g_out, dk_out, dv_out, sums, x1g_out, out_grad,
):
    model = cqt.shape[1]
    text_rows = kall.shape[1]
    slot = place[OWN + chunk]

    def m(component):
        return mod_row(mod, slot, component, model)

    x1 = x1_in.ref()[...]
    b2 = b2_in.ref()[...]
    h3g = h3g_own[...].astype(F32) + h3g_far[...].astype(F32)
    normed, inverse = normalize(x1 + m(5) * b2)
    sums[4:5, :] = column_sum(h3g)
    sums[5:6, :] = column_sum(h3g * normed)
    x2g = cot.ref()[...].astype(F32) + norm_back(h3g * (1.0 + m(7)), normed, inverse)
    sums[3:4, :] = column_sum(x2g * b2)
    b2g = (x2g * m(5)).astype(BF16)
    b2g_out[...] = b2g
    out_grad[...] = dot_nt(b2g, co[...]).astype(BF16)
    masks = quad_masks()
    low = [mask.astype(BF16) for mask in masks]
    limit = place[LIMIT + chunk]

    def by_quad(quad):
        cols = quad_cols(quad)
        queries = q2_in.ref()[:, cols]
        grads = out_grad[:, cols]
        keys = quad_stack(kall[slot, :, cols], low)
        values = quad_stack(vall[slot, :, cols], low)
        probs = quad_probs(dot_nt(keys, queries), limit, text_rows)
        prob_grad = dot_nt(values, grads)
        score_grad = []
        for u in range(4):
            part = prob_grad[u * text_rows : (u + 1) * text_rows, :]
            row_dot = jnp.sum(probs[u] * part, axis=0, keepdims=True)
            score_grad.append((probs[u] * (part - row_dot)).astype(BF16))
        score_grad = jnp.concatenate(score_grad, axis=0)
        dv = dot_nn(jnp.concatenate(probs, axis=0).astype(BF16), grads)
        dk = dot_nn(score_grad, queries)
        dq_out[:, cols] = (dot_tn(score_grad, keys) * (HEAD**-0.5)).astype(BF16)
        for wide, out in ((dk, dk_out), (dv, dv_out)):
            total = None
            for u in range(4):
                part = wide[u * text_rows : (u + 1) * text_rows, :] * masks[u]
                total = part if total is None else total + part
            out[:, cols] = total.astype(BF16)
    for quad in range(model // (4 * HEAD)):
        by_quad(quad)
    h2g = dot_nn(dq_out[...], cqt[...])
    normed, inverse = normalize(x1)
    sums[1:2, :] = column_sum(h2g)
    sums[2:3, :] = column_sum(h2g * normed)
    x1g = x2g + norm_back(h2g * (1.0 + m(4)), normed, inverse)
    x1g_out[...] = x1g
    branch = sum_own.ref()[...].astype(F32) + sum_far.ref()[...].astype(F32)
    sums[0:1, :] = column_sum(x1g * branch)
    sums[6:8, :] = jnp.zeros((2, model), F32)
    b1g_out[...] = (x1g * m(2)).astype(BF16)


def cross_first(place, *refs):
    cross_chunk(place, 0, *refs)


def cross_second(place, *refs):
    cross_chunk(place, 1, *refs)


def cross_weights(
    place, dqa, dqb, b2ga, b2gb, dka, dkb, dva, dvb, h2a, h2b, cra, crb, text, own, send,
):
    width = own.shape[1] // 2
    row = place[ROW]
    h2a, h2b, cra, crb, text = h2a.ref(), h2b.ref(), cra.ref(), crb.ref(), text.ref()
    slots = [place[OWN + chunk] for chunk in range(2)]

    @pl.loop(0, h2a.shape[1] // BLOCK)
    def _(part):
        to = token_rows(part)
        hidden = jnp.concatenate([h2a[:, to], h2b[:, to]], axis=0)
        grads = jnp.concatenate([b2ga[:, to], b2gb[:, to]], axis=0)
        texts = [text[slot, :, to] for slot in slots]
        for member, out in ((1, send), (0, own)):
            start = (member * width // 128) * 128
            skip = member * width - start
            cols = slice(start, start + 2 * 128)
            kept = slice(skip, skip + width)

            def two(first, second):
                return jnp.concatenate([first[:, cols], second[:, cols]], axis=0)

            top, bottom = slice(0, width), slice(width, 2 * width)
            out[row, top, to] = dot_tn(two(dqa, dqb), hidden)[kept].astype(BF16)
            out[row, bottom, to] = (dot_tn(dka[:, cols], texts[0]) + dot_tn(dkb[:, cols], texts[1]))[kept].astype(BF16)
            out[1 - row, top, to] = (dot_tn(dva[:, cols], texts[0]) + dot_tn(dvb[:, cols], texts[1]))[kept].astype(
                BF16
            )
            out[1 - row, bottom, to] = dot_tn(two(cra, crb), grads)[kept].astype(BF16)


def keys_back(block, qa, ka, va, da, dq_sum):
    rows = token_rows(block)
    dks = []
    dvs = []
    for head in range(ka.shape[0]):
        keys = ka[head, rows, :]
        probs = jnp.exp(dot_nt(keys, qa[head]))
        prob_grad = dot_nt(va[head, rows, :], da[head])
        score_grad = (probs * prob_grad).astype(BF16)
        dvs.append(dot_nn(probs.astype(BF16), da[head])[:, :HEAD])
        dks.append(dot_nn(score_grad, qa[head])[:, :HEAD])
        dq = dot_tn(score_grad, keys)
        dq_sum[head] += dq
    return jnp.concatenate(dks, axis=1).astype(BF16), jnp.concatenate(dvs, axis=1).astype(BF16)


def self_back_first(
    place, b1g_a, b1g_b, far_a, far_b, wo, att_a, att_b, qa_a, qa_b, ka, va,
    b1g, att, qa, da, dq_sum, dk_all, dv_all,
):
    blocks = b1g.shape[0] // BLOCK
    heads = da.shape[0]
    core = place[CORE]
    for chunk, (own, far) in enumerate(((b1g_a, far_a), (b1g_b, far_b))):
        b1g[token_rows(2 * chunk + core), :] = own[...]
        b1g[token_rows(2 * chunk + 1 - core), :] = far[...]
    wo = wo.ref()
    att[0 : 2 * BLOCK, :] = att_a.ref()[...]
    att[2 * BLOCK : 4 * BLOCK, :] = att_b.ref()[...]
    lane = lax.broadcasted_iota(jnp.int32, (BLOCK, 2 * HEAD), 1)

    @pl.loop(0, blocks)
    def _(block):
        rows = token_rows(block)
        grads = dot_nt(b1g[rows, :], wo[...]).astype(BF16).astype(F32)
        dots = grads * att[rows, :].astype(F32)
        for head in range(heads):
            row_dot = jnp.sum(dots[:, head * HEAD : (head + 1) * HEAD], axis=1, keepdims=True)
            high, middle, low = three_parts(-row_dot)
            more = jnp.where(lane == HEAD, high, jnp.where(lane == HEAD + 1, middle, low))
            more = jnp.where(lane < HEAD + 3, more, 0.0)
            da[head, rows, :] = jnp.where(lane < HEAD, head_slice(grads, head), more).astype(BF16)
    qa[:, 0 : 2 * BLOCK, :] = qa_a.ref()[...]
    qa[:, 2 * BLOCK : 4 * BLOCK, :] = qa_b.ref()[...]
    ka, va = ka.ref(), va.ref()
    dq_sum[...] = jnp.zeros_like(dq_sum)

    @pl.loop(0, 2)
    def _(block):
        rows = token_rows(block)
        dk_all[rows, :], dv_all[rows, :] = keys_back(block, qa, ka, va, da, dq_sum)


def self_back_second(
    place, b1g, att, qa, da, dq_in, dk_in, dv_in, weights, ka, va, h1,
    part_own, part_send, dw_keep, dw_give,
    dq_sum, grad_all,
):
    blocks = b1g.shape[0] // BLOCK
    heads = da.shape[0]
    core = place[CORE]
    width = heads * HEAD
    ka, va = ka.ref(), va.ref()
    dq_sum[...] = dq_in[...]
    grad_all[0 : 2 * BLOCK, width : 2 * width] = dk_in[0 : 2 * BLOCK, :]
    grad_all[0 : 2 * BLOCK, 2 * width : 3 * width] = dv_in[0 : 2 * BLOCK, :]

    @pl.loop(2, blocks)
    def _(block):
        rows = token_rows(block)
        dk, dv = keys_back(block, qa, ka, va, da, dq_sum)
        grad_all[rows, width : 2 * width] = dk
        grad_all[rows, 2 * width : 3 * width] = dv
    h1 = h1.ref()

    @pl.loop(0, blocks)
    def _(block):
        rows = token_rows(block)
        dq = jnp.concatenate([dq_sum[head, rows, :HEAD] for head in range(heads)], axis=1)
        grad_all[rows, 0:width] = (dq * (HEAD**-0.5)).astype(BF16)
        out = dot_nn(grad_all[rows, :], weights[...]).astype(BF16)
        side = lax.rem(block, 2)
        out_rows = token_rows(lax.div(block, 2))

        @pl.when(core == side)
        def _():
            part_own[out_rows, :] = out

        @pl.when(core != side)
        def _():
            part_send[out_rows, :] = out

    @pl.loop(0, h1.shape[1] // BLOCK)
    def _(part):
        cols = token_rows(part)
        grads = dot_tn(grad_all[...], h1[:, cols]).astype(BF16)
        query_key = (grads[:width], grads[width : 2 * width])
        value_out = (grads[2 * width :], dot_tn(att[...], b1g[:, cols]).astype(BF16))
        for flag, first, second in ((0, query_key, value_out), (1, value_out, query_key)):

            @pl.when(place[ROW] == flag)
            def _():
                for index in range(2):
                    rows = slice(index * width, (index + 1) * width)
                    dw_keep[rows, cols] = first[index]
                    dw_give[rows, cols] = second[index]


def mixed_kernel(place, mod, b3a, b3b, far_a, far_b, x2, cot_a, cot_b, mixed_a, mixed_b, sums):
    model = mixed_a.shape[1]
    for chunk, (own, far, cot) in enumerate(((b3a, far_a, cot_a), (b3b, far_b, cot_b))):
        mixed = (mixed_a, mixed_b)[chunk]
        rows = slice(chunk * BLOCK, (chunk + 1) * BLOCK)
        slot = place[OWN + chunk]
        b3 = own[...].astype(F32) + far[...].astype(F32)
        mixed[...] = (x2[rows, :] + mod_row(mod, slot, 8, model) * b3).astype(BF16)
        sums[chunk] = column_sum(cot.ref()[...].astype(F32) * b3)


def final_kernel(
    place, mod, h1g_own, h1g_far, sums_a, sums_b, sums_mixed, tokens_a, tokens_b, x1ga, x1gb, grad_a, grad_b, slot_sums,
):
    model = grad_a.shape[1]
    slot_sums[...] = jnp.zeros_like(slot_sums)
    for chunk, (x1g, sums, tokens) in enumerate(((x1ga, sums_a, tokens_a), (x1gb, sums_b, tokens_b))):
        rows = slice(chunk * BLOCK, (chunk + 1) * BLOCK)
        slot = place[OWN + chunk]
        h1g = h1g_own[rows, :].astype(F32) + h1g_far[rows, :].astype(F32)
        normed, inverse = normalize(tokens.ref()[...].astype(F32))
        scaled = h1g * (1.0 + mod_row(mod, slot, 1, model))
        (grad_a, grad_b)[chunk][...] = (x1g.ref()[...] + norm_back(scaled, normed, inverse)).astype(BF16)
        terms = [column_sum(h1g), column_sum(h1g * normed)]
        terms += [sums[i : i + 1, :] for i in range(6)] + [sums_mixed[chunk]]
        for component, term in enumerate(terms):
            slot_sums[pl.ds(slot, 1), component * model : (component + 1) * model] += term


def join_cores(place, mine_a, mine_b, other_a, other_b, out):
    for chunk, (mine, other) in enumerate(((mine_a, other_a), (mine_b, other_b))):
        out[token_rows(place[CORE] * 2 + chunk), :] = mine[...]
        out[token_rows((1 - place[CORE]) * 2 + chunk), :] = other[...]


def join_rows(place, mine, other, out):
    count = mine.shape[0]
    out[pl.ds(pl.multiple_of(place[ROW] * count, BLOCK // 2), count), :] = mine[...].astype(F32)
    out[pl.ds(pl.multiple_of((1 - place[ROW]) * count, BLOCK // 2), count), :] = other[...].astype(F32)


def join_four(place, mine, other, first, second, third, fourth):
    width = first.shape[0]
    for flag, top, bottom in ((0, mine, other), (1, other, mine)):

        @pl.when(place[ROW] == flag)
        def _():
            first[...] = top[:width, :].astype(F32)
            second[...] = top[width:, :].astype(F32)
            third[...] = bottom[:width, :].astype(F32)
            fourth[...] = bottom[width:, :].astype(F32)


def slot_kernel(place, own, far, silu, out):
    model = silu.shape[1]
    count = out.shape[1] - model
    out[:, :model] = silu[...].astype(F32)
    for index in range(own.shape[1] // count):
        cols = slice(index * count, (index + 1) * count)

        @pl.when(place[TENSOR] == index)
        def _():
            out[:, model:] = (own[:, cols] + far[:, cols]).astype(BF16).astype(F32)


def advance_kernel(roles, place, *refs):
    refs = list(refs)
    values, got = {}, {}
    for role in roles:
        values[role] = refs.pop(0)
    for name in ("row", "column", "middle"):
        if any(role in roles for role in {"row": "a", "column": "bd", "middle": "c"}[name]):
            got[name] = refs.pop(0)
    outs = {role: refs.pop(0) for role in roles}
    end = place[END]
    if "a" in roles:
        outs["a"][...] = added(values["a"][...], got["row"][...])
    if "c" in roles:

        @pl.when(end == 0)
        def _():
            outs["c"][...] = added(values["c"][...], got["middle"][...])

        @pl.when(end != 0)
        def _():
            outs["c"][...] = values["c"][...]

    if "b" in roles:

        @pl.when(end == 0)
        def _():
            outs["b"][...] = added(values["b"][...], got["column"][...])

        @pl.when(end != 0)
        def _():
            outs["b"][...] = values["b"][...]

    if "d" in roles:

        @pl.when(end == 0)
        def _():
            outs["d"][...] = values["d"][...]

        @pl.when(end != 0)
        def _():
            outs["d"][...] = got["column"][...]

    if refs:

        @pl.when(end == 0)
        def _():
            refs[0][...] = outs["c"][...]

        @pl.when(end != 0)
        def _():
            refs[0][...] = outs["a"][...]


def added(first, second):
    return (first.astype(F32) + second.astype(F32)).astype(BF16)


def solution(mesh):
    n_dp = mesh.shape["dp"]
    n_tensor = mesh.shape["tensor"]
    n_col = n_dp // 2
    dp_bits = int(math.log2(n_dp))

    def tensor_swap(value, flip):
        return lax.ppermute(value, "tensor", [(i, i ^ flip) for i in range(n_tensor)])

    def core_swap(value):
        return tensor_swap(value, 1)

    def far_swap(value):
        return tensor_swap(value, 2)

    def dp_swap(value, flip):
        return lax.ppermute(value, "dp", [(i, i ^ flip) for i in range(n_dp)])

    def tie(*values):
        return lax.optimization_barrier(values) if values else ()

    def pair_up(flag, mine, other):
        return jnp.concatenate([jnp.where(flag == 0, mine, other), jnp.where(flag == 0, other, mine)], axis=0)

    def local(
        tokens, text_states, clip_len, text_len, timesteps, q_weight, k_weight, v_weight, o_weight,
        cross_q, cross_k, cross_v, cross_o, mlp_in, mlp_out, mod_weight, mod_bias, cotangent,
    ):
        count, model = tokens.shape
        slots, text_rows = text_states.shape[:2]
        width = o_weight.shape[0]
        heads = width // HEAD
        half = count // 2
        text_pad = -(-text_rows // 16) * 16
        tensor_at = lax.axis_index("tensor")
        dp_at = lax.axis_index("dp")
        core = tensor_at & 1
        row = dp_at & 1
        column = dp_at >> 1

        ends = jnp.cumsum(clip_len)
        starts = jnp.arange(count // BLOCK, dtype=jnp.int32) * BLOCK
        slot_of = jnp.sum((starts[:, None] >= ends[None, :]).astype(jnp.int32), axis=1)
        end = (column == 0) | (column == n_col - 1)
        own_slots = lax.dynamic_slice_in_dim(slot_of, core * 2, 2, 0)
        far_slots = lax.dynamic_slice_in_dim(slot_of, (1 - core) * 2, 2, 0)
        limits = jnp.sum(jnp.where(own_slots[:, None] == jnp.arange(slots)[None, :], text_len[None, :], 0), axis=1)
        single = jnp.stack([core, row, end.astype(jnp.int32), tensor_at])
        place = jnp.concatenate([slot_of, single, own_slots, far_slots, limits])
        place = jnp.pad(place[None, :], ((0, 7), (0, 128 - place.shape[0])))
        place = place.astype(jnp.int32)

        query_own = cross_q.T
        part_own = jnp.concatenate(
            [lax.dynamic_slice_in_dim(w, row * (width // 2), width // 2, 0) for w in (query_own, cross_o)], axis=0
        )
        text_weights = jnp.concatenate([cross_k.T, cross_v.T], axis=0)
        text = jnp.pad(text_states, ((0, 0), (0, text_pad - text_rows), (0, 0)))
        self_weights = jnp.concatenate([q_weight.T, k_weight.T, v_weight.T], axis=0)

        half_width = model // 2
        ramp = jnp.arange(half_width).astype(F32)
        frequency = jnp.exp(ramp * (-math.log(10000.0) / half_width))
        angles = timesteps.astype(F32)[:, None] * frequency[None, :]
        embed = jnp.concatenate([jnp.cos(angles), jnp.sin(angles)], axis=1)
        silu_low = jax.nn.silu(embed).astype(BF16)
        part_far = far_swap(part_own)
        wout1 = core_swap(mlp_out)
        mod_own = dot_nn(silu_low, mod_weight) + mod_bias.astype(F32)
        mod_far = [tensor_swap(mod_own, flip) for flip in range(1, n_tensor)]
        (text_own,) = run(text_kernel, [((2 * text_pad, model), BF16)], place, [text, text_weights], cost=1.0)
        text_own, self_weights, wout1, *mod_far = tie(text_own, self_weights, wout1, *mod_far)
        text_far = far_swap(text_own)
        query_own, out_own, text_own = tie(query_own, cross_o, text_own)
        query1, out1, text1 = core_swap(query_own), core_swap(out_own), core_swap(text_own)
        mod_all = jnp.stack([mod_own] + mod_far)
        mod = jnp.concatenate(
            [lax.dynamic_index_in_dim(mod_all, tensor_at ^ j, 0, keepdims=False) for j in range(n_tensor)], axis=1
        )

        wide = (heads, count, 2 * HEAD)
        block_wide = (heads, 2 * BLOCK, 2 * HEAD)
        one = ((BLOCK, model), BF16)
        one_f32 = ((BLOCK, model), F32)
        attend_far = [(block_wide, BF16), ((2 * BLOCK, width), BF16)]
        own_a, send_a, qa, ka, va, qa_a, att_a, h1 = run(
            self_first, [one, one] + [(wide, BF16)] * 3 + attend_far + [((count, model), BF16)], place, [mod, self_weights], cost=0.001,
            late=[tokens, o_weight],
        )
        send_a, part_far, text_far, query1, out1, text1 = tie(send_a, part_far, text_far, query1, out1, text1)
        sum_a = added(own_a, core_swap(send_a))
        sum_a, qa, part_far, text_far, win0 = tie(sum_a, qa, part_far, text_far, mlp_in)
        far_a = far_swap(sum_a)
        rest_far = dp_swap(part_far, 1)
        part3, text3, win1 = core_swap(part_far), core_swap(text_far), core_swap(win0)
        own_b, send_b, qa_b, att_b = run(
            self_second, [one, one] + attend_far, place, [qa, ka, va], late=[o_weight]
        )
        (far_a,) = tie(far_a)
        send_b, far_a, rest_far, part3, text3, win1 = tie(send_b, far_a, rest_far, part3, text3, win1)
        rest3 = core_swap(rest_far)
        sum_b = added(own_b, core_swap(send_b))
        sum_b, rest3 = tie(sum_b, rest3)
        far_b = far_swap(sum_b)
        cqt, co, kall, vall = run(
            unpack_kernel, [((model, model), BF16)] * 2 + [((slots, text_pad, model), BF16)] * 2,
            place,
            [query_own, out_own, query1, out1, part_far, rest_far, part3, rest3, text_own, text1, text_far, text3],
            cost=0.001,
        )
        shared = [cqt, co, kall, vall]

        def chunk_rows(array, chunk):
            return (array, functools.partial(block_of, chunk=chunk))

        def middle(kernel, chunk, own, far, *before):
            return run(
                kernel, [one] * 7 + [one_f32, one_f32] + [one] * 4 + [(((chunk + 1) * BLOCK, model), F32)], place,
                [mod, own, far] + shared, cost=7.5,
                late=[chunk_rows(tokens, chunk), chunk_rows(cotangent, chunk), mlp_in, mlp_out, win1, wout1, *before],
            )

        h3ga, h3a, act0a, act1a, pg0a, pg1a, b3ga, x1a, b2a, h2a, q2a, cra, b3a, x2a = middle(
            middle_first, 0, sum_a, far_a
        )
        h3ga, far_b = tie(h3ga, far_b)
        h3g_far_a = far_swap(h3ga)
        h3gb, h3b, act0b, act1b, pg0b, pg1b, b3gb, x1b, b2b, h2b, q2b, crb, b3b, x2 = middle(
            middle_second, 1, sum_b, far_b, x2a
        )
        h3gb, pg0b, h3g_far_a = tie(h3gb, pg0b, h3g_far_a)
        h3g_far_b = far_swap(h3gb)

        in_own, in_send, out_own, out_send = run(
            mlp_back, [((2, model // 2, model), BF16)] * 4, place,
            [h3a, h3b, pg0a, pg0b, pg1a, pg1b, act0a, act0b, act1a, act1b, b3ga, b3gb], cost=0.001,
        )

        def cross(kernel, chunk, h3g_own, h3g_far, x1, b2, own, far, q2):
            return run(
                kernel, [one] * 3 + [((text_pad, model), BF16)] * 2 + [((8, model), F32), one_f32], place,
                [mod, h3g_own, h3g_far, kall, vall, cqt, co],
                late=[x1, b2, chunk_rows(cotangent, chunk), q2, own, far], scratch=[one],
                cost=4.0 if chunk else 0.001,
            )

        b1g_a, dqa, b2ga, dka, dva, sums_a, x1ga = cross(
            cross_first, 0, h3ga, h3g_far_a, x1a, b2a, sum_a, far_a, q2a
        )
        in_send, out_send, b1g_a, h3g_far_b = tie(in_send, out_send, b1g_a, h3g_far_b)
        in_got, b1g_far_a = core_swap(in_send), core_swap(b1g_a)
        b1g_b, dqb, b2gb, dkb, dvb, sums_b, x1gb = cross(
            cross_second, 1, h3gb, h3g_far_b, x1b, b2b, sum_b, far_b, q2b
        )
        in_got, out_send, b1g_far_a, b1g_b, dqb, b3a = tie(in_got, out_send, b1g_far_a, b1g_b, dqb, b3a)
        in_keep, in_give = added(in_own[0], in_got[0]), added(in_own[1], in_got[1])

        across = [(i, i ^ 1) for i in range(n_dp)]
        neighbours = [(i, i ^ 2) for i in range(n_dp)]
        middle_pair = [(2 * a + r, 2 * b + r) for a, b in ((1, 2), (2, 1)) for r in range(2)]
        chain_rows = (model // 2, model)

        class Rounds:
            def __init__(self):
                self.values, self.column_send, self.results, self.waiting = {}, None, [], []

            def start(self, *chain):
                self.got = {}
                if n_col != 4:
                    self.waiting += [chain] if chain else []
                    return
                if chain:
                    self.values["a"] = chain[0]
                    self.got["row"] = lax.ppermute(chain[1], "dp", across)
                if "e" in self.values:
                    self.got["last"] = lax.ppermute(self.values["e"], "dp", across)
                if "b" in self.values or "d" in self.values:
                    self.got["column"] = lax.ppermute(self.column_send, "dp", neighbours)
                if "c" in self.values:
                    self.got["middle"] = lax.ppermute(self.values["c"], "dp", middle_pair)

            def finish(self, *others, early=()):
                order = [name for name in ("row", "last", "column", "middle") if name in self.got]
                settled = list(early)
                for name in order:
                    settled = list(tie(self.got[name], *settled))
                tied = tie(*settled, *others)
                self.got = dict(zip(reversed(order), tied))
                others = tied[len(order) :]
                if "last" in self.got:
                    self.results.append((self.values.pop("e"), self.got.pop("last")))
                roles = "".join(role for role in "abcd" if role in self.values)
                if not roles:
                    return others
                operands = [self.values[role] for role in roles]
                operands += [self.got[name] for name in ("row", "column", "middle") if name in self.got]
                sends = "a" in roles or "c" in roles
                both = "a" in roles and "c" in roles
                outs = run(
                    functools.partial(advance_kernel, roles), [(chain_rows, BF16)] * (len(roles) + both),
                    place, operands, cost=0.3,
                )
                done = tie(*outs, *others)
                stepped = dict(zip(roles, done))
                if sends:
                    self.column_send = done[len(roles)] if both else stepped["a" if "a" in roles else "c"]
                self.values = {{"a": "b", "b": "c", "c": "d", "d": "e"}[role]: v for role, v in stepped.items()}
                return done[len(outs) :]

            def halves(self, number):
                return self.results[number] if n_col == 4 else self.slowly(*self.waiting[number])

            def whole(self, number):
                return run(join_rows, [((model, model), F32)], place, self.halves(number))[0]

            def four(self, number):
                return run(join_four, [((width, model), F32)] * 4, place, self.halves(number))

            def slowly(self, keep, give):
                total = added(keep, lax.ppermute(give, "dp", across))
                for bit in range(1, dp_bits):
                    size, flag = total.shape[0] // 2, (dp_at >> bit) & 1
                    sent = lax.dynamic_slice_in_dim(total, (1 - flag) * size, size, 0)
                    total = added(lax.dynamic_slice_in_dim(total, flag * size, size, 0), dp_swap(sent, 1 << bit))
                for bit in reversed(range(1, dp_bits)):
                    total = pair_up((dp_at >> bit) & 1, total, dp_swap(total, 1 << bit))
                return total, lax.ppermute(total, "dp", across)

        rounds = Rounds()

        rounds.start(in_keep, in_give)
        b1g_far_b, out_got = core_swap(b1g_b), core_swap(out_send)
        out_keep, out_give = added(out_own[0], out_got[0]), added(out_own[1], out_got[1])
        b3_far_a = far_swap(b3a)
        cross_dw, cross_send = run(
            cross_weights, [((2, 2 * width, model), BF16)] * 2, place,
            [dqa, dqb, b2ga, b2gb, dka, dkb, dva, dvb], late=[h2a, h2b, cra, crb, text], cost=0.001,
        )
        b1g_far_b, cross_send = tie(b1g_far_b, cross_send)
        b1g_all, att_all, qa_all, da, dq_sum, dk_all, dv_all = run(
            self_back_first,
            [((count, model), BF16), ((count, width), BF16), (wide, BF16), (wide, BF16), (wide, F32)]
            + [((count, width), BF16)] * 2,
            place, [b1g_a, b1g_b, b1g_far_a, b1g_far_b],
            late=[o_weight, att_a, att_b, qa_a, qa_b, ka, va], cost=0.001,
        )
        b1g_all, cross_send, out_give, b3b, b3_far_a = rounds.finish(b1g_all, cross_send, out_give, b3b, b3_far_a)

        rounds.start(out_keep, out_give)
        cross_got = core_swap(cross_send)
        b3_far_b = far_swap(b3b)
        grad_own, grad_send, self_keep, self_give = run(
            self_back_second,
            [((half, model), BF16)] * 2 + [((2 * width, model), BF16)] * 2, place,
            [b1g_all, att_all, qa_all, da, dq_sum, dk_all, dv_all, self_weights], late=[ka, va, h1],
            scratch=[(wide, F32), ((count, 3 * width), BF16)],
        )
        cross_keep, cross_give = added(cross_dw[0], cross_got[0]), added(cross_dw[1], cross_got[1])
        grad_send, cross_give, self_give, b3_far_b = rounds.finish(grad_send, cross_give, self_give, b3_far_b)

        rounds.start(cross_keep, cross_give)
        h1g_own = added(grad_own, core_swap(grad_send))
        h1g_far = far_swap(h1g_own)
        mixed_a, mixed_b, sums_mixed = run(
            mixed_kernel, [one, one, ((2, 1, model), F32)],
            place, [mod, b3a, b3b, b3_far_a, b3_far_b, x2], late=[chunk_rows(cotangent, 0), chunk_rows(cotangent, 1)],
        )
        self_give, h1g_own, mixed_a, mixed_b = rounds.finish(self_give, h1g_own, mixed_a, mixed_b)

        rounds.start(self_keep, self_give)
        grad_a, grad_b, slot_sums = run(
            final_kernel, [one, one, ((slots, 9 * model), F32)],
            place, [mod, h1g_own, h1g_far, sums_a, sums_b, sums_mixed],
            late=[chunk_rows(tokens, 0), chunk_rows(tokens, 1), x1ga, x1gb],
        )
        grad_a, grad_b, slot_sums, mixed_a = rounds.finish(mixed_a, early=(grad_a, grad_b, slot_sums))

        rounds.start()
        slot_far = core_swap(slot_sums)
        mixed_far_a = core_swap(mixed_a)
        slot_far, mixed_far_a, mixed_b = rounds.finish(slot_far, mixed_far_a, mixed_b)

        rounds.start()
        (gathered,) = run(
            slot_kernel, [((slots, model + mod_weight.shape[1]), F32)], place, [slot_sums, slot_far, silu_low]
        )
        gathered = jnp.concatenate([gathered, dp_swap(gathered, 1)], axis=0)
        mixed_far_b = core_swap(mixed_b)
        gathered, mixed_far_b, grad_a, grad_b = rounds.finish(gathered, mixed_far_b, grad_a, grad_b)

        rounds.start()
        gathered = jnp.concatenate([gathered, dp_swap(gathered, 2)], axis=0)
        grad_far_a, grad_far_b = core_swap(grad_a), core_swap(grad_b)
        mlp_in_grad, mlp_out_grad = rounds.whole(0), rounds.whole(1)
        gathered, grad_far_a, grad_far_b, mlp_in_grad, mlp_out_grad = rounds.finish(
            gathered, grad_far_a, grad_far_b, mlp_in_grad, mlp_out_grad
        )

        rounds.start()
        for bit in range(2, dp_bits):
            gathered = jnp.concatenate([gathered, dp_swap(gathered, 1 << bit)], axis=0)
        (mixed,) = run(
            join_cores, [((count, model), BF16)], place, [mixed_a, mixed_b, mixed_far_a, mixed_far_b]
        )
        (token_grad,) = run(
            join_cores, [((count, model), BF16)], place, [grad_a, grad_b, grad_far_a, grad_far_b]
        )
        cross_grads = rounds.four(2)
        gathered_low = gathered.astype(BF16)
        mod_weight_grad = dot_tn(gathered_low[:, :model], gathered_low[:, model:])
        mod_bias_grad = jnp.sum(gathered[:, model:], axis=0)
        mixed, token_grad, mod_weight_grad, mod_bias_grad, *cross_grads = rounds.finish(
            mixed, token_grad, mod_weight_grad, mod_bias_grad, *cross_grads
        )
        self_grads = rounds.four(3)

        return (
            mixed,
            token_grad,
            self_grads[0].T,
            self_grads[1].T,
            self_grads[2].T,
            self_grads[3],
            cross_grads[0].T,
            cross_grads[1].T,
            cross_grads[2].T,
            cross_grads[3],
            mlp_in_grad,
            mlp_out_grad,
            mod_weight_grad,
            mod_bias_grad,
        )

    rows = P("dp", None)
    by_col = P(None, "tensor")
    by_row = P("tensor", None)
    return jax.shard_map(
        local,
        mesh=mesh,
        in_specs=(
            rows, P("dp", None, None), P("dp"), P("dp"), P("dp"), by_col, by_col, by_col, by_row,
            by_col, by_col, by_col, by_row, by_col, by_row, by_col, P("tensor"), rows,
        ),
        out_specs=(
            rows, rows, by_col, by_col, by_col, by_row, by_col, by_col, by_col, by_row,
            by_col, by_row, by_col, P("tensor"),
        ),
        check_vma=False,
    )
```
